32 devices in a mesh: seq: 8 (over y, x, core), fsdp: 4 (over z).
Axes of the slice: x: 2, y: 2, z: 4, core: 2. Of those that a mesh axis runs over, the one named last changes fastest.
Arguments:
- tokens: bfloat16 [4, 2048, 2048], P('fsdp', 'seq'), may hold values from -6 to 6
- cotangent: bfloat16 [4, 2048, 2048], P('fsdp', 'seq'), may hold values from -6 to 6
- starts: int32 [4, 4], P('fsdp'), may hold values from 0 to 2047, as said below
- adapter_ids: int32 [4, 4], P('fsdp'), may hold values from 0 to 7
- w_qkv: bfloat16 [2048, 6144], P('fsdp'), may hold values from -0.125 to 0.125
- w_out: bfloat16 [2048, 2048], P('fsdp'), may hold values from -0.5 to 0.5
- w_gu: bfloat16 [2048, 16384], P('fsdp'), may hold values from -0.125 to 0.125
- w_down: bfloat16 [8192, 2048], P('fsdp'), may hold values from -0.0625 to 0.0625
- a_qkv: bfloat16 [2048, 384], P('fsdp'), may hold values from -0.125 to 0.125
- b_qkv: bfloat16 [384, 2048], P(None, 'fsdp'), may hold values from -1.5 to 1.5
- a_out: bfloat16 [2048, 128], P('fsdp'), may hold values from -0.125 to 0.125
- b_out: bfloat16 [128, 2048], P(None, 'fsdp'), may hold values from -6 to 6
- a_gu: bfloat16 [2048, 256], P('fsdp'), may hold values from -0.125 to 0.125
- b_gu: bfloat16 [256, 8192], P(None, 'fsdp'), may hold values from -1.5 to 1.5
- a_down: bfloat16 [8192, 128], P('fsdp'), may hold values from -0.0625 to 0.0625
- b_down: bfloat16 [128, 2048], P(None, 'fsdp'), may hold values from -1.5 to 1.5
Outputs:
- activations: float32 [4, 2048, 2048], P('fsdp', 'seq')
- input_grad: float32 [4, 2048, 2048], P('fsdp', 'seq')
- g_a_qkv: float32 [2048, 384], P('fsdp')
- g_b_qkv: float32 [384, 2048], P(None, 'fsdp')
- g_a_out: float32 [2048, 128], P('fsdp')
- g_b_out: float32 [128, 2048], P(None, 'fsdp')
- g_a_gu: float32 [2048, 256], P('fsdp')
- g_b_gu: float32 [256, 8192], P(None, 'fsdp')
- g_a_down: float32 [8192, 128], P('fsdp')
- g_b_down: float32 [128, 2048], P(None, 'fsdp')
The draws below stay inside these ranges and needn't reach their ends.
Inputs may be any that keep to these rules, and one draw needn't show every extreme that they name: starts[f, 0] is 0 and each row rises strictly, every start a token of the stream; in every stream one document begins within the first 256 tokens and ends within the last 256.
All inputs are finite; a program needn't handle non-finite values.
Results may differ from the reference program's by a relative error of at most 0.02.
The reference program's roundings to bfloat16 on the way count: a program that leaves them out, or rounds other values in their place, can miss the bound.
Values may be sent and summed in bfloat16 or wider, within the bound.
No kernel may reach another device: no remote copies, remote signals or barrier semaphores. Data moves between devices by JAX's collectives and lax.ppermute only.
A program may use at most 384 MiB of HBM per device.

```python
import jax
import jax.numpy as jnp
from jax import lax

HEADS = 16
HEAD_DIM = 128
D = 2048
FF = 8192
RANK = 16
ADAPTERS = 8
NDOC = 4
TOK_DEV = 256
STREAM = 2048
N_FSDP = 4


def draw_starts(key, part):
    key = jax.random.fold_in(key, 11)

    def one_stream(stream_key):
        pick_key, head_key, tail_key = jax.random.split(stream_key, 3)
        longest = jax.random.randint(pick_key, (), 0, NDOC)
        opening = jnp.where(longest == 0, 0, longest + jax.random.randint(head_key, (), 0, TOK_DEV - NDOC))
        closing = STREAM - NDOC - jax.random.randint(tail_key, (), 0, TOK_DEV - NDOC)
        order = jnp.arange(NDOC, dtype=jnp.int32)
        before = order * opening // jnp.maximum(longest, 1)
        after = closing + (order - longest - 1) * (STREAM - closing) // jnp.maximum(NDOC - 1 - longest, 1)
        return jnp.where(order < longest, before, jnp.where(order == longest, opening, after)).astype(jnp.int32)
    return jax.vmap(one_stream)(jax.random.split(key, N_FSDP))


def touch_ends(entries, key, least, largest):
    extent = entries.shape
    place = [jax.random.randint(jax.random.fold_in(key, axis), (), 0, extent[axis]) for axis in range(len(extent))]
    entries = entries.at[tuple(place)].set(least)
    longest = extent.index(max(extent))
    place[longest] = (place[longest] + 1) % extent[longest]
    return entries.at[tuple(place)].set(largest)


def steps_of(key, extent, cuts, low, largest):
    gain = 1.0
    for axis_at, shards_of in cuts:
        draws = jax.random.uniform(jax.random.fold_in(jax.random.fold_in(key, 6), axis_at), (shards_of,), jnp.float32, low / len(cuts), largest / len(cuts))
        gain = gain * jnp.repeat(jnp.exp(draws), extent[axis_at] // shards_of).reshape((-1,) + (1,) * (len(extent) - 1 - axis_at))
    return gain


def normal_values(rng, dims, scale, most, cuts=(), kind=jnp.bfloat16):
    loudness = steps_of(rng, dims, cuts, -0.22, 0.18) if cuts else 1.0
    values = jax.random.normal(rng, dims, jnp.float32) * scale * loudness
    return jnp.minimum(jnp.maximum(values, -most), most).astype(kind)


def setup_inputs(seed: int = 0) -> dict:
    streams_of = jax.random.split(jax.random.key(seed), 17)
    tokens = normal_values(streams_of[0], (N_FSDP, STREAM, D), 1.0, 6.0, ((0, 4), (1, 8)))
    cotangent = normal_values(streams_of[1], (N_FSDP, STREAM, D), 1.0, 6.0, ((0, 4), (1, 8)))
    starts = draw_starts(jax.random.fold_in(streams_of[16], 71), 0)
    adapter_ids = touch_ends(jax.random.randint(streams_of[3], (N_FSDP, NDOC), 0, ADAPTERS), jax.random.fold_in(streams_of[3], 1), 0, ADAPTERS - 1).astype(jnp.int32)
    w_qkv = normal_values(streams_of[4], (D, 3 * D), D ** -0.5, 0.125, ((0, 4),))
    w_out = normal_values(streams_of[5], (D, D), (D // 16) ** -0.5, 0.5, ((0, 4),))
    w_gu = normal_values(streams_of[6], (D, 2 * FF), D ** -0.5, 0.125, ((0, 4),))
    w_down = normal_values(streams_of[7], (FF, D), FF ** -0.5, 0.0625, ((0, 4),))
    a_qkv = normal_values(streams_of[8], (D, 3 * ADAPTERS * RANK), D ** -0.5, 0.125, ((0, 4),))
    b_qkv = normal_values(streams_of[9], (3 * ADAPTERS * RANK, D), RANK ** -0.5, 1.5, ((1, 4),))
    a_out = normal_values(streams_of[10], (D, ADAPTERS * RANK), D ** -0.5, 0.125, ((0, 4),))
    b_out = normal_values(streams_of[11], (ADAPTERS * RANK, D), 1 ** -0.5, 6.0, ((1, 4),))
    a_gu = normal_values(streams_of[12], (D, 2 * ADAPTERS * RANK), D ** -0.5, 0.125, ((0, 4),))
    b_gu = normal_values(streams_of[13], (2 * ADAPTERS * RANK, FF), RANK ** -0.5, 1.5, ((1, 4),))
    a_down = normal_values(streams_of[14], (FF, ADAPTERS * RANK), FF ** -0.5, 0.0625, ((0, 4),))
    b_down = normal_values(streams_of[15], (ADAPTERS * RANK, D), RANK ** -0.5, 1.5, ((1, 4),))
    return dict(tokens=tokens, cotangent=cotangent, starts=starts, adapter_ids=adapter_ids, w_qkv=w_qkv, w_out=w_out, w_gu=w_gu, w_down=w_down, a_qkv=a_qkv, b_qkv=b_qkv, a_out=a_out, b_out=b_out, a_gu=a_gu, b_gu=b_gu, a_down=a_down, b_down=b_down)


@jax.custom_vjp
def low(v):
    return lax.optimization_barrier(v.astype(jnp.bfloat16)).astype(jnp.float32)

@jax.custom_vjp
def low_back(v):
    return v

def low_keep(v):
    return (low(v), None)

def low_pass(kept, grad):
    return (grad,)

def back_keep(v):
    return (v, None)

def back_low(kept, grad):
    return (low(grad),)
low.defvjp(low_keep, low_pass)
low_back.defvjp(back_keep, back_low)

def matmul(left, right):
    return jnp.dot(left, right, precision=lax.Precision.HIGHEST, preferred_element_type=jnp.float32)

def layer_norm(values):
    centre = values - lax.optimization_barrier(jnp.mean(values, axis=-1, keepdims=True))
    spread = lax.optimization_barrier(jnp.mean(centre * centre, axis=-1, keepdims=True))
    return centre * lax.rsqrt(spread + 1e-05)

def doc_tables(places, first, chosen):
    within = first[None, :] <= places[:, None]
    begin = lax.optimization_barrier(jnp.max(jnp.where(within, first[None, :], 0), axis=1)).astype(jnp.int32)
    latest = lax.optimization_barrier(jnp.sum(within.astype(jnp.int32), axis=1)) - 1
    doc_order = jnp.arange(first.shape[0], dtype=jnp.int32)
    which = lax.optimization_barrier(jnp.sum(jnp.where(doc_order[None, :] == latest[:, None], chosen[None, :], 0), axis=1))
    return (begin, which.astype(jnp.int32))

def rope_tables(position, head_dim):
    freqs = 10000.0 ** (-(jnp.arange(0, head_dim, 2, dtype=jnp.float32) / head_dim))
    angles = position.astype(jnp.float32)[:, None] * freqs[None, :]
    cosine = jnp.concatenate([jnp.cos(angles), jnp.cos(angles)], axis=-1)
    sine = jnp.concatenate([jnp.sin(angles), jnp.sin(angles)], axis=-1)
    return (cosine, sine)

def rotate(values, cosine, sine):
    half_dim = values.shape[-1] // 2
    turned = jnp.concatenate([-values[..., half_dim:], values[..., :half_dim]], axis=-1)
    return values * cosine[:, None, :] + turned * sine[:, None, :]

def adapter(inputs, down, up, select, segments):
    latent = low_back(low(matmul(inputs, down))) * jnp.tile(select, (1, segments))
    span = up.shape[0] // segments
    pieces = [matmul(latent[:, seg * span:(seg + 1) * span], up[seg * span:(seg + 1) * span]) for seg in range(segments)]
    return jnp.concatenate(pieces, axis=1)

def attention(queries, keys_all, values_all, begin):
    length = queries.shape[0]
    block_rows = min(512, length)
    block_count = length // block_rows
    score_scale = HEAD_DIM ** (-0.5)
    key_places = jnp.arange(length, dtype=jnp.int32)

    @jax.checkpoint
    def one_block(block_index):
        start = (block_index * block_rows).astype(jnp.int32)
        query_block = lax.dynamic_slice_in_dim(queries, start, block_rows, 0)
        rows = start + jnp.arange(block_rows, dtype=jnp.int32)
        row_begin = lax.dynamic_slice_in_dim(begin, start, block_rows, 0)
        allowed = (key_places[None, :] <= rows[:, None]) & (key_places[None, :] >= row_begin[:, None])
        scores = low_back(score_scale * jnp.einsum('qhd,khd->hqk', query_block, keys_all, precision=lax.Precision.HIGHEST))
        scores = jnp.where(allowed[None], scores, -1e+30)
        row_top = lax.optimization_barrier(jnp.max(scores, axis=-1, keepdims=True))
        expd = jnp.exp(scores - row_top)
        probs = expd / lax.optimization_barrier(jnp.sum(expd, axis=-1, keepdims=True))
        mixed = jnp.einsum('hqk,khd->qhd', low(probs), values_all, precision=lax.Precision.HIGHEST)
        return mixed.reshape(block_rows, -1)
    return lax.map(one_block, jnp.arange(block_count, dtype=jnp.int32)).reshape(length, -1)

def forward(stream, adapters, first, chosen, frozen):
    a_qkv, b_qkv, a_out, b_out, a_gu, b_gu, a_down, b_down = adapters
    w_qkv, w_out, w_gu, w_down = frozen
    length, width = stream.shape
    places = jnp.arange(length, dtype=jnp.int32)
    begin, which = doc_tables(places, first, chosen)
    columns = jnp.arange(ADAPTERS * RANK, dtype=jnp.int32) // RANK
    select = (columns[None, :] == which[:, None]).astype(jnp.float32)
    cosine, sine = rope_tables(places - begin, HEAD_DIM)
    first_norm = low(layer_norm(stream))
    qkv = matmul(first_norm, w_qkv) + adapter(first_norm, a_qkv, b_qkv, select, 3)
    q_pre = low_back(qkv[:, :width])
    k_pre = low_back(qkv[:, width:2 * width])
    values = low_back(low(qkv[:, 2 * width:]))
    queries = low_back(low(rotate(q_pre.reshape(length, HEADS, HEAD_DIM), cosine, sine)))
    key_rot = low_back(low(rotate(k_pre.reshape(length, HEADS, HEAD_DIM), cosine, sine)))
    mixed = attention(queries, key_rot, values.reshape(length, HEADS, HEAD_DIM), begin)
    mixed = low_back(low(mixed))
    attn_branch = low_back(matmul(mixed, w_out) + adapter(mixed, a_out, b_out, select, 1))
    second = stream + attn_branch
    second_norm = low(layer_norm(second))
    gate_up = matmul(second_norm, w_gu) + adapter(second_norm, a_gu, b_gu, select, 2)
    gate = low_back(gate_up[:, :FF])
    upper = low_back(gate_up[:, FF:])
    hidden = low(jax.nn.silu(gate) * upper)
    ff_branch = low_back(matmul(hidden, w_down) + adapter(hidden, a_down, b_down, select, 1))
    return second + ff_branch

def reference(tokens, cotangent, starts, adapter_ids, w_qkv, w_out, w_gu, w_down, a_qkv, b_qkv, a_out, b_out, a_gu, b_gu, a_down, b_down):
    frozen = tuple((weight.astype(jnp.float32) for weight in (w_qkv, w_out, w_gu, w_down)))
    adapters = tuple((factor.astype(jnp.float32) for factor in (a_qkv, b_qkv, a_out, b_out, a_gu, b_gu, a_down, b_down)))

    def one_stream(totals, inputs):
        stream, stream_cot, first, chosen = inputs

        def run(stream_in, adapt_in):
            return forward(stream_in, adapt_in, first, chosen, frozen)
        result, pull = jax.vjp(run, stream.astype(jnp.float32), adapters)
        stream_grad, adapt_grad = pull(stream_cot.astype(jnp.float32))
        totals = tuple((acc + part for acc, part in zip(totals, adapt_grad)))
        return (totals, (result, stream_grad))
    zeros = tuple((jnp.zeros_like(factor) for factor in adapters))
    totals, (results, grads) = lax.scan(one_stream, zeros, (tokens, cotangent, starts, adapter_ids))
    return (results, grads, totals[0], totals[1], totals[2], totals[3], totals[4], totals[5], totals[6], totals[7])
```

```python
import functools

import jax
import jax.numpy as jnp
from jax import lax
from jax.experimental import pallas as pl
from jax.experimental.pallas import tpu as pltpu
from jax.sharding import PartitionSpec as P

HEAD_DIM = 128
RANK = 16


def layer_norm(values):
    centre = values - jnp.mean(values, axis=-1, keepdims=True)
    spread = jnp.mean(centre * centre, axis=-1, keepdims=True)
    factor = lax.rsqrt(spread + 1e-05)
    return (centre * factor, factor)


def norm_back(normed, factor, upstream):
    upstream_mean = jnp.mean(upstream, axis=-1, keepdims=True)
    cross_mean = jnp.mean(upstream * normed, axis=-1, keepdims=True)
    return factor * (upstream - upstream_mean - normed * cross_mean)


def doc_tables(places, first, chosen):
    within = first[None, :] <= places[:, None]
    begin = jnp.max(jnp.where(within, first[None, :], 0), axis=1)
    latest = jnp.sum(within.astype(jnp.int32), axis=1) - 1
    doc_order = jnp.arange(first.shape[0], dtype=jnp.int32)
    which = jnp.sum(jnp.where(doc_order[None, :] == latest[:, None], chosen[None, :], 0), axis=1)
    return (begin, which)


def rope_tables(position, head_dim):
    freqs = 10000.0 ** (-(jnp.arange(0, head_dim, 2, dtype=jnp.float32) / head_dim))
    angles = position.astype(jnp.float32)[:, None] * freqs[None, :]
    cosine = jnp.concatenate([jnp.cos(angles), jnp.cos(angles)], axis=-1)
    sine = jnp.concatenate([jnp.sin(angles), jnp.sin(angles)], axis=-1)
    return (cosine, sine)


def rotate(values, cosine, sine):
    half_dim = values.shape[-1] // 2
    turned = jnp.concatenate([-values[..., half_dim:], values[..., :half_dim]], axis=-1)
    return values * cosine[:, None, :] + turned * sine[:, None, :]


def rotate_back(upstream, cosine, sine):
    half_dim = upstream.shape[-1] // 2
    scaled = upstream * sine[:, None, :]
    return upstream * cosine[:, None, :] + jnp.concatenate(
        [scaled[..., half_dim:], -scaled[..., :half_dim]], axis=-1
    )


def inner_rows(left, right):
    return lax.dot_general(
        left, right, (((0,), (0,)), ((), ())), preferred_element_type=jnp.float32
    )


def inner_cols(left, right):
    return lax.dot_general(
        left, right, (((1,), (1,)), ((), ())), preferred_element_type=jnp.float32
    )


def adapter_fwd(inputs, down, up, select, segments):
    latent = jnp.dot(inputs, down, preferred_element_type=jnp.float32).astype(
        jnp.bfloat16
    ) * jnp.tile(select, (1, segments))
    span = up.shape[0] // segments
    pieces = [
        jnp.dot(
            latent[:, seg * span : (seg + 1) * span],
            up[seg * span : (seg + 1) * span],
            preferred_element_type=jnp.float32,
        )
        for seg in range(segments)
    ]
    return (latent, jnp.concatenate(pieces, axis=1))


def adapter_back(inputs, latent, upstream, down, up, select, segments):
    span = up.shape[0] // segments
    out_span = up.shape[1]
    grad_up = jnp.concatenate(
        [
            inner_rows(
                latent[:, seg * span : (seg + 1) * span],
                upstream[:, seg * out_span : (seg + 1) * out_span],
            )
            for seg in range(segments)
        ],
        axis=0,
    )
    latent_grad = jnp.concatenate(
        [
            inner_cols(
                upstream[:, seg * out_span : (seg + 1) * out_span],
                up[seg * span : (seg + 1) * span],
            )
            for seg in range(segments)
        ],
        axis=1,
    )
    latent_grad = (latent_grad * jnp.tile(select, (1, segments)).astype(jnp.float32)).astype(
        jnp.bfloat16
    )
    grad_down = inner_rows(inputs, latent_grad)
    back = inner_cols(latent_grad, down)
    return (grad_down, grad_up, back)


def frozen_fwd(inputs, weight):
    return (
        jnp.dot(
            inputs,
            lax.all_gather(weight, "fsdp", axis=0, tiled=True),
            preferred_element_type=jnp.float32,
        ),
        weight,
    )


def frozen_bwd(upstream, weight):
    return inner_cols(upstream, lax.all_gather(weight, "fsdp", axis=0, tiled=True))


def attend(query_h, key_h, value_h, begin, head_dim):
    length, local_width = query_h.shape
    local_heads = local_width // head_dim
    block_rows = min(512, length)
    block_count = length // block_rows
    score_scale = head_dim ** (-0.5)
    query_all = query_h.reshape(length, local_heads, head_dim)
    key_all = key_h.reshape(length, local_heads, head_dim)
    value_all = value_h.reshape(length, local_heads, head_dim)
    key_places = jnp.arange(length, dtype=jnp.int32)

    def one_block(block_index):
        start = block_index * block_rows
        query_block = lax.dynamic_slice_in_dim(query_all, start, block_rows, 0)
        rows = start + jnp.arange(block_rows, dtype=jnp.int32)
        row_begin = lax.dynamic_slice_in_dim(begin, start, block_rows, 0)
        allowed = (key_places[None, :] <= rows[:, None]) & (
            key_places[None, :] >= row_begin[:, None]
        )
        scores = (
            jnp.einsum("qhd,khd->hqk", query_block, key_all, preferred_element_type=jnp.float32)
            * score_scale
        )
        scores = jnp.where(allowed[None], scores, -1e30)
        row_top = jnp.max(scores, axis=-1, keepdims=True)
        expd = jnp.exp(scores - row_top)
        row_total = jnp.sum(expd, axis=-1, keepdims=True)
        probs = (expd / row_total).astype(jnp.bfloat16)
        mixed = jnp.einsum("hqk,khd->qhd", probs, value_all, preferred_element_type=jnp.float32)
        return (
            mixed.astype(jnp.bfloat16).reshape(block_rows, local_width),
            (row_top + jnp.log(row_total))[..., 0],
        )

    outputs, log_sums = lax.map(one_block, jnp.arange(block_count, dtype=jnp.int32))
    return (outputs.reshape(length, local_width), log_sums)


def attend_back(query_h, key_h, value_h, grad_h, log_sums, begin, head_dim):
    length, local_width = query_h.shape
    local_heads = local_width // head_dim
    block_rows = min(512, length)
    block_count = length // block_rows
    score_scale = head_dim ** (-0.5)
    query_all = query_h.reshape(length, local_heads, head_dim)
    key_all = key_h.reshape(length, local_heads, head_dim)
    value_all = value_h.reshape(length, local_heads, head_dim)
    grad_all = grad_h.reshape(length, local_heads, head_dim)
    key_places = jnp.arange(length, dtype=jnp.int32)

    def step(carry, inputs):
        key_grad, value_grad = carry
        block_index, block_lse = inputs
        start = block_index * block_rows
        query_block = lax.dynamic_slice_in_dim(query_all, start, block_rows, 0)
        grad_block = lax.dynamic_slice_in_dim(grad_all, start, block_rows, 0)
        rows = start + jnp.arange(block_rows, dtype=jnp.int32)
        row_begin = lax.dynamic_slice_in_dim(begin, start, block_rows, 0)
        allowed = (key_places[None, :] <= rows[:, None]) & (
            key_places[None, :] >= row_begin[:, None]
        )
        scores = (
            jnp.einsum("qhd,khd->hqk", query_block, key_all, preferred_element_type=jnp.float32)
            * score_scale
        )
        probs = jnp.where(allowed[None], jnp.exp(scores - block_lse[..., None]), 0.0)
        probs_low = probs.astype(jnp.bfloat16)
        prob_grad = jnp.einsum(
            "qhd,khd->hqk", grad_block, value_all, preferred_element_type=jnp.float32
        )
        row_delta = jnp.sum(prob_grad * probs, axis=-1, keepdims=True)
        score_grad = (probs * (prob_grad - row_delta)).astype(jnp.bfloat16)
        query_grad = (
            jnp.einsum("hqk,khd->qhd", score_grad, key_all, preferred_element_type=jnp.float32)
            * score_scale
        )
        key_grad = (
            key_grad
            + jnp.einsum(
                "hqk,qhd->khd", score_grad, query_block, preferred_element_type=jnp.float32
            )
            * score_scale
        )
        value_grad = value_grad + jnp.einsum(
            "hqk,qhd->khd", probs_low, grad_block, preferred_element_type=jnp.float32
        )
        return (
            (key_grad, value_grad),
            query_grad.astype(jnp.bfloat16).reshape(block_rows, local_width),
        )

    empty = jnp.zeros((length, local_heads, head_dim), jnp.float32)
    (key_grad, value_grad), query_grad = lax.scan(
        step, (empty, empty), (jnp.arange(block_count, dtype=jnp.int32), log_sums)
    )
    return (
        query_grad.reshape(length, local_width),
        key_grad.astype(jnp.bfloat16).reshape(length, local_width),
        value_grad.astype(jnp.bfloat16).reshape(length, local_width),
    )


def shards(
    tokens,
    cotangent,
    starts,
    adapter_ids,
    w_qkv,
    w_out,
    w_gu,
    w_down,
    a_qkv,
    b_qkv,
    a_out,
    b_out,
    a_gu,
    b_gu,
    a_down,
    b_down,
):
    gathered = (
        lax.all_gather(a_qkv, "fsdp", axis=0, tiled=True),
        lax.all_gather(b_qkv, "fsdp", axis=1, tiled=True),
        lax.all_gather(a_out, "fsdp", axis=0, tiled=True),
        lax.all_gather(b_out, "fsdp", axis=1, tiled=True),
        lax.all_gather(a_gu, "fsdp", axis=0, tiled=True),
        lax.all_gather(b_gu, "fsdp", axis=1, tiled=True),
        lax.all_gather(a_down, "fsdp", axis=0, tiled=True),
        lax.all_gather(b_down, "fsdp", axis=1, tiled=True),
    )
    (
        full_a_qkv,
        full_b_qkv,
        full_a_out,
        full_b_out,
        full_a_gu,
        full_b_gu,
        full_a_down,
        full_b_down,
    ) = gathered
    stream = tokens[0].astype(jnp.float32)
    cot_low = cotangent[0]
    tok_count, width = stream.shape
    seq_count = lax.axis_size("seq")
    seq_place = lax.axis_index("seq")
    stream_len = tok_count * seq_count
    first = starts[0]
    chosen = adapter_ids[0]
    local_places = seq_place * tok_count + jnp.arange(tok_count, dtype=jnp.int32)
    local_begin, which = doc_tables(local_places, first, chosen)
    columns = jnp.arange(full_a_out.shape[1], dtype=jnp.int32) // RANK
    select = (columns[None, :] == which[:, None]).astype(jnp.bfloat16)
    cosine, sine = rope_tables(local_places - local_begin, HEAD_DIM)
    head_count = width // HEAD_DIM
    first_norm, first_factor = layer_norm(stream)
    first_low = first_norm.astype(jnp.bfloat16)
    latent_qkv, extra_qkv = adapter_fwd(first_low, full_a_qkv, full_b_qkv, select, 3)
    qkv_main, held_qkv = frozen_fwd(first_low, w_qkv)
    qkv = qkv_main + extra_qkv
    query_rot = (
        rotate(qkv[:, :width].reshape(tok_count, head_count, HEAD_DIM), cosine, sine)
        .reshape(tok_count, width)
        .astype(jnp.bfloat16)
    )
    key_rot = (
        rotate(qkv[:, width : 2 * width].reshape(tok_count, head_count, HEAD_DIM), cosine, sine)
        .reshape(tok_count, width)
        .astype(jnp.bfloat16)
    )
    value_low = qkv[:, 2 * width :].astype(jnp.bfloat16)
    query_h, key_h, value_h = (
        lax.all_to_all(query_rot, "seq", split_axis=1, concat_axis=0, tiled=True),
        lax.all_to_all(key_rot, "seq", split_axis=1, concat_axis=0, tiled=True),
        lax.all_to_all(value_low, "seq", split_axis=1, concat_axis=0, tiled=True),
    )
    all_begin, all_which = doc_tables(jnp.arange(stream_len, dtype=jnp.int32), first, chosen)
    mixed_h, log_sums = attend(query_h, key_h, value_h, all_begin, HEAD_DIM)
    mixed = lax.all_to_all(mixed_h, "seq", split_axis=0, concat_axis=1, tiled=True)
    latent_out, extra_out = adapter_fwd(mixed, full_a_out, full_b_out, select, 1)
    out_main, held_out = frozen_fwd(mixed, w_out)
    second = stream + (out_main + extra_out)
    second_norm, second_factor = layer_norm(second)
    second_low = second_norm.astype(jnp.bfloat16)
    latent_gu, extra_gu = adapter_fwd(second_low, full_a_gu, full_b_gu, select, 2)
    gu_main, held_gu = frozen_fwd(second_low, w_gu)
    gate_up = gu_main + extra_gu
    ff_width = gate_up.shape[1] // 2
    gate = gate_up[:, :ff_width]
    upper = gate_up[:, ff_width:]
    sigma = jax.nn.sigmoid(gate)
    active = gate * sigma
    hidden = (active * upper).astype(jnp.bfloat16)
    latent_down, extra_down = adapter_fwd(hidden, full_a_down, full_b_down, select, 1)
    down_main, held_down = frozen_fwd(hidden, w_down)
    activations = second + (down_main + extra_down)
    grad_a_down, grad_b_down, hidden_extra = adapter_back(
        hidden, latent_down, cot_low, full_a_down, full_b_down, select, 1
    )
    hidden_grad = frozen_bwd(cot_low, held_down) + hidden_extra
    gate_grad = (hidden_grad * upper * sigma * (1.0 + gate * (1.0 - sigma))).astype(jnp.bfloat16)
    upper_grad = (hidden_grad * active).astype(jnp.bfloat16)
    gate_up_grad = jnp.concatenate([gate_grad, upper_grad], axis=1)
    grad_a_gu, grad_b_gu, second_extra = adapter_back(
        second_low, latent_gu, gate_up_grad, full_a_gu, full_b_gu, select, 2
    )
    second_norm_grad = frozen_bwd(gate_up_grad, held_gu) + second_extra
    second_grad = cot_low.astype(jnp.float32) + norm_back(
        second_norm, second_factor, second_norm_grad
    )
    branch_grad = second_grad.astype(jnp.bfloat16)
    grad_a_out, grad_b_out, mixed_extra = adapter_back(
        mixed, latent_out, branch_grad, full_a_out, full_b_out, select, 1
    )
    mixed_grad = (frozen_bwd(branch_grad, held_out) + mixed_extra).astype(jnp.bfloat16)
    mixed_grad_h = lax.all_to_all(mixed_grad, "seq", split_axis=1, concat_axis=0, tiled=True)
    query_grad_h, key_grad_h, value_grad_h = attend_back(
        query_h, key_h, value_h, mixed_grad_h, log_sums, all_begin, HEAD_DIM
    )
    query_grad, key_grad, value_grad = (
        lax.all_to_all(query_grad_h, "seq", split_axis=0, concat_axis=1, tiled=True),
        lax.all_to_all(key_grad_h, "seq", split_axis=0, concat_axis=1, tiled=True),
        lax.all_to_all(value_grad_h, "seq", split_axis=0, concat_axis=1, tiled=True),
    )
    query_pre = (
        rotate_back(
            query_grad.astype(jnp.float32).reshape(tok_count, head_count, HEAD_DIM), cosine, sine
        )
        .reshape(tok_count, width)
        .astype(jnp.bfloat16)
    )
    key_pre = (
        rotate_back(
            key_grad.astype(jnp.float32).reshape(tok_count, head_count, HEAD_DIM), cosine, sine
        )
        .reshape(tok_count, width)
        .astype(jnp.bfloat16)
    )
    qkv_grad = jnp.concatenate([query_pre, key_pre, value_grad], axis=1)
    grad_a_qkv, grad_b_qkv, first_extra = adapter_back(
        first_low, latent_qkv, qkv_grad, full_a_qkv, full_b_qkv, select, 3
    )
    first_norm_grad = frozen_bwd(qkv_grad, held_qkv) + first_extra
    input_grad = second_grad + norm_back(first_norm, first_factor, first_norm_grad)
    grads = (
        grad_a_qkv,
        grad_b_qkv,
        grad_a_out,
        grad_b_out,
        grad_a_gu,
        grad_b_gu,
        grad_a_down,
        grad_b_down,
    )
    shard_dims = (0, 1, 0, 1, 0, 1, 0, 1)
    summed = lax.psum(
        (grads[0], grads[1], grads[2], grads[3], grads[4], grads[5], grads[6], grads[7]),
        ("seq", "fsdp"),
    )
    fsdp_place = lax.axis_index("fsdp")
    fsdp_count = lax.axis_size("fsdp")
    totals = tuple(
        (
            lax.dynamic_slice_in_dim(
                whole,
                fsdp_place * (whole.shape[along] // fsdp_count),
                whole.shape[along] // fsdp_count,
                along,
            )
            for whole, along in zip(summed, shard_dims)
        )
    )
    return (
        activations[None],
        input_grad[None],
        totals[0],
        totals[1],
        totals[2],
        totals[3],
        totals[4],
        totals[5],
        totals[6],
        totals[7],
    )


BF = jnp.bfloat16
F32 = jnp.float32
CHIPS = 4
PLANE = 8
CHUNKS = 2
LANES = 128


def swap(value, bit):
    return lax.ppermute(value, "seq", [(i, i ^ bit) for i in range(PLANE)])


def plane_gather(block):
    half = block.shape[0] // 2
    over_x = swap(block, 2)
    over_y = swap(block, 4)
    far_a = swap(over_y[:half], 2)
    far_b = swap(over_x[half:], 4)
    return jnp.concatenate([block, over_x, over_y, far_a, far_b], axis=0)


def plane_scatter(partial):
    rows = partial.shape[0] // 4
    half = rows // 2
    low = partial.astype(BF)
    own = partial[:rows].astype(F32)
    to_x = jnp.concatenate([low[rows : rows + half], low[3 * rows : 3 * rows + half]], axis=0)
    to_y = jnp.concatenate([low[2 * rows + half : 3 * rows], low[3 * rows + half :]], axis=0)
    from_x = swap(to_x, 2)
    from_y = swap(to_y, 4)
    pass_y = (partial[2 * rows : 2 * rows + half].astype(F32) + from_x[half:].astype(F32)).astype(BF)
    pass_x = (partial[rows + half : 2 * rows].astype(F32) + from_y[half:].astype(F32)).astype(BF)
    got_y = swap(pass_y, 4)
    got_x = swap(pass_x, 2)
    upper = own[:half] + from_x[:half].astype(F32) + got_y.astype(F32)
    lower = own[half:] + from_y[:half].astype(F32) + got_x.astype(F32)
    return jnp.concatenate([upper, lower], axis=0)


def dot(left, right):
    return jnp.dot(left, right, preferred_element_type=F32)


def lane_blocks(value):
    count = value.shape[1] // LANES
    return jnp.concatenate([value[:, k * LANES : (k + 1) * LANES] for k in range(count)], axis=0)


def in_order(scalars, own, other, whole, blocks, rows):
    chip, core = scalars[0], scalars[1]
    for place in range(blocks):
        start = pl.multiple_of(((place // 2) ^ chip) * rows, rows)

        @pl.when(core == place % 2)
        def _():
            whole[place * rows : (place + 1) * rows, :] = own[pl.ds(start, rows), :]

        @pl.when(core != place % 2)
        def _():
            whole[place * rows : (place + 1) * rows, :] = other[pl.ds(start, rows), :]


def out_of_order(scalars, whole, own, other, blocks, rows):
    chip, core = scalars[0], scalars[1]
    for place in range(blocks):
        start = pl.multiple_of(((place // 2) ^ chip) * rows, rows)

        @pl.when(core == place % 2)
        def _():
            own[pl.ds(start, rows), :] = whole[place * rows : (place + 1) * rows, :]

        @pl.when(core != place % 2)
        def _():
            other[pl.ds(start, rows), :] = whole[place * rows : (place + 1) * rows, :]


def allowed_pairs(scalars, first_row, rows, width):
    row = first_row + lax.broadcasted_iota(jnp.int32, (rows, 1), 0)
    column = lax.broadcasted_iota(jnp.int32, (1, width), 1)
    begin = jnp.zeros((rows, 1), jnp.int32)
    for doc in range(4):
        begin = jnp.where(scalars[2 + doc] <= row, jnp.maximum(begin, scalars[2 + doc]), begin)
    return (column <= row) & (column >= begin)


def inner(left, right, on_left, on_right):
    return lax.dot_general(
        left, right, (((on_left,), (on_right,)), ((), ())), preferred_element_type=F32
    )


def attend_kernel(blocks, rows, scalars, qa, ka, va, qb, kb, vb, out, lse, q_all, k_all, v_all):
    in_order(scalars, qa, qb, q_all, blocks, rows)
    in_order(scalars, ka, kb, k_all, blocks, rows)
    in_order(scalars, va, vb, v_all, blocks, rows)
    scale = HEAD_DIM**-0.5
    for place in range(blocks):
        here = slice(place * rows, (place + 1) * rows)
        width = (place + 1) * rows
        scores = inner(q_all[here, :], k_all[:width, :], 1, 1) * scale
        scores = jnp.where(allowed_pairs(scalars, place * rows, rows, width), scores, -1e30)
        top = jnp.max(scores, axis=1, keepdims=True)
        expd = jnp.exp(scores - top)
        total = jnp.sum(expd, axis=1, keepdims=True)
        probs = (expd * (1.0 / total)).astype(BF)
        out[here, :] = dot(probs, v_all[:width, :]).astype(BF)
        lse[here, :] = jnp.broadcast_to(top + jnp.log(total), (rows, LANES))


def attend_back_kernel(
    blocks, rows, scalars, qa, ka, va, qb, kb, vb, grad, lse,
    own, other, q_all, k_all, v_all, dq_all, dk_sum, dv_sum,
):
    in_order(scalars, qa, qb, q_all, blocks, rows)
    in_order(scalars, ka, kb, k_all, blocks, rows)
    in_order(scalars, va, vb, v_all, blocks, rows)
    dk_sum[...] = jnp.zeros_like(dk_sum)
    dv_sum[...] = jnp.zeros_like(dv_sum)
    scale = HEAD_DIM**-0.5
    for place in range(blocks):
        here = slice(place * rows, (place + 1) * rows)
        width = (place + 1) * rows
        query = q_all[here, :]
        upstream = grad[here, :]
        scores = inner(query, k_all[:width, :], 1, 1) * scale
        probs = jnp.where(
            allowed_pairs(scalars, place * rows, rows, width),
            jnp.exp(scores - lse[here, :1]),
            0.0,
        )
        prob_grad = inner(upstream, v_all[:width, :], 1, 1)
        delta = jnp.sum(prob_grad * probs, axis=1, keepdims=True)
        score_grad = (probs * (prob_grad - delta)).astype(BF)
        dq_all[here, :] = (dot(score_grad, k_all[:width, :]) * scale).astype(BF)
        dk_sum[:width, :] += inner(score_grad, query, 0, 0)
        dv_sum[:width, :] += inner(probs.astype(BF), upstream, 0, 0)
    out_of_order(scalars, dq_all, own.at[0], other.at[0], blocks, rows)
    dq_all[...] = (dk_sum[...] * scale).astype(BF)
    out_of_order(scalars, dq_all, own.at[1], other.at[1], blocks, rows)
    dq_all[...] = dv_sum[...].astype(BF)
    out_of_order(scalars, dq_all, own.at[2], other.at[2], blocks, rows)


def attend_plane(scalars, own, other, rows):
    length = 2 * own.shape[0]
    group = own.shape[0]
    heads = own.shape[1] // (3 * HEAD_DIM)
    blocks = length // rows
    part = lambda k: pl.BlockSpec((group, HEAD_DIM), lambda h, _: (0, k * heads + h))
    return pl.pallas_call(
        functools.partial(attend_kernel, blocks, rows),
        grid_spec=pltpu.PrefetchScalarGridSpec(
            num_scalar_prefetch=1,
            grid=(heads,),
            in_specs=[part(0), part(1), part(2)] * 2,
            out_specs=[
                pl.BlockSpec((length, HEAD_DIM), lambda h, _: (0, h)),
                pl.BlockSpec((length, LANES), lambda h, _: (0, h)),
            ],
            scratch_shapes=[pltpu.VMEM((length, HEAD_DIM), BF)] * 3,
        ),
        out_shape=[
            jax.ShapeDtypeStruct((length, heads * HEAD_DIM), BF),
            jax.ShapeDtypeStruct((length, heads * LANES), F32),
        ],
        compiler_params=pltpu.CompilerParams(vmem_limit_bytes=48 * 2**20),
        cost_estimate=pl.CostEstimate(
            flops=2 * heads * length * length * HEAD_DIM,
            bytes_accessed=8 * length * heads * HEAD_DIM,
            transcendentals=heads * length * length // 2,
        ),
    )(scalars, own, own, own, other, other, other)


def attend_plane_back(scalars, own, other, grad, lse, rows):
    length = 2 * own.shape[0]
    group = own.shape[0]
    heads = own.shape[1] // (3 * HEAD_DIM)
    blocks = length // rows
    part = lambda k: pl.BlockSpec((group, HEAD_DIM), lambda h, _: (0, k * heads + h))
    result = pl.BlockSpec((3, group, HEAD_DIM), lambda h, _: (0, 0, h))
    shape = jax.ShapeDtypeStruct((3, group, heads * HEAD_DIM), BF)
    return pl.pallas_call(
        functools.partial(attend_back_kernel, blocks, rows),
        grid_spec=pltpu.PrefetchScalarGridSpec(
            num_scalar_prefetch=1,
            grid=(heads,),
            in_specs=[part(0), part(1), part(2)] * 2
            + [
                pl.BlockSpec((length, HEAD_DIM), lambda h, _: (0, h)),
                pl.BlockSpec((length, LANES), lambda h, _: (0, h)),
            ],
            out_specs=[result, result],
            scratch_shapes=[pltpu.VMEM((length, HEAD_DIM), BF)] * 4
            + [pltpu.VMEM((length, HEAD_DIM), F32)] * 2,
        ),
        out_shape=[shape, shape],
        compiler_params=pltpu.CompilerParams(vmem_limit_bytes=48 * 2**20),
        cost_estimate=pl.CostEstimate(
            flops=5 * heads * length * length * HEAD_DIM,
            bytes_accessed=20 * length * heads * HEAD_DIM,
            transcendentals=heads * length * length // 2,
        ),
    )(scalars, own, own, own, other, other, other, grad, lse)


def plane_shards(
    tokens, cotangent, starts, adapter_ids,
    w_qkv, w_out, w_gu, w_down, a_qkv, b_qkv, a_out, b_out, a_gu, b_gu, a_down, b_down,
):
    seat = lax.axis_index("seq")
    z_count = lax.axis_size("fsdp")
    core = seat % 2
    chip = seat // 2
    rows, width = tokens.shape[1:]
    length = rows * PLANE
    ff = w_gu.shape[1] // 2
    ff_z = ff // z_count
    ff_dev = ff_z // PLANE
    ff_chunk = ff_dev // CHUNKS
    quarter = w_qkv.shape[0]
    latent = a_out.shape[1]
    heads = width // HEAD_DIM
    heads_dev = heads // PLANE
    span = heads_dev * HEAD_DIM
    first = starts[0]
    chosen = adapter_ids[0]

    def take(value, start, count, axis):
        return lax.dynamic_slice_in_dim(value, start, count, axis)

    head_columns = [
        part * width + (2 * core + i) * quarter + chip * HEAD_DIM
        for part in range(3)
        for i in range(heads_dev)
    ]
    qkv_part = jnp.concatenate([take(w_qkv, at, HEAD_DIM, 1) for at in head_columns], axis=1)
    qkv_own = lax.all_gather(qkv_part, "fsdp", axis=0, tiled=True)
    qkv_oth = swap(qkv_own, 1)

    share = quarter // PLANE
    share_b = latent // PLANE
    packed = jnp.concatenate(
        [
            lane_blocks(take(a_qkv, seat * share, share, 0)),
            lane_blocks(take(a_out, seat * share, share, 0)),
            lane_blocks(take(a_gu, seat * share, share, 0)),
            lane_blocks(take(b_out, seat * share_b, share_b, 0)),
            lane_blocks(take(b_down, seat * share_b, share_b, 0)),
        ],
        axis=0,
    )
    packed = lax.all_gather(packed, ("fsdp", "seq"), axis=0, tiled=False).reshape(
        z_count, PLANE, packed.shape[0], LANES
    )

    def unpack_rows(start, blocks):
        piece = packed[:, :, start : start + blocks * share]
        piece = piece.reshape(z_count, PLANE, blocks, share, LANES).transpose(0, 1, 3, 2, 4)
        return piece.reshape(width, blocks * LANES)

    def unpack_columns(start):
        blocks = width // z_count // LANES
        piece = packed[:, :, start : start + blocks * share_b]
        piece = piece.reshape(z_count, PLANE, blocks, share_b, LANES).transpose(1, 3, 0, 2, 4)
        return piece.reshape(latent, width)

    at = 0
    full_a_qkv = unpack_rows(at, a_qkv.shape[1] // LANES)
    at += a_qkv.shape[1] // LANES * share
    full_a_out = unpack_rows(at, a_out.shape[1] // LANES)
    at += a_out.shape[1] // LANES * share
    full_a_gu = unpack_rows(at, a_gu.shape[1] // LANES)
    at += a_gu.shape[1] // LANES * share
    full_b_out = unpack_columns(at)
    at += width // z_count // LANES * share_b
    full_b_down = unpack_columns(at)

    b_qkv_chip = lax.all_gather(
        take(b_qkv, chip * HEAD_DIM, HEAD_DIM, 1), "fsdp", axis=1, tiled=True
    )
    b_qkv_own = take(b_qkv_chip, core * span, span, 1)
    b_qkv_oth = take(b_qkv_chip, (1 - core) * span, span, 1)

    full_out = lax.all_gather(
        take(w_out, seat * share, share, 0), ("fsdp", "seq"), axis=0, tiled=True
    )

    b_gu_own = lax.all_gather(take(b_gu, seat * ff_dev, ff_dev, 1), "fsdp", axis=0, tiled=True)
    b_gu_oth = swap(b_gu_own, 1)
    gu_pairs = []
    down_pairs = []
    b_gu_pairs = []
    for chunk in range(CHUNKS):
        columns = [
            half * ff + z * ff_z + seat * ff_dev + chunk * ff_chunk
            for half in range(2)
            for z in range(z_count)
        ]
        part = jnp.concatenate([take(w_gu, at, ff_chunk, 1) for at in columns], axis=1)
        own = lax.all_gather(part, "fsdp", axis=0, tiled=True)
        gu_pairs.append((own, swap(own, 1)))
        at = seat * ff_dev + chunk * ff_chunk
        part = jnp.concatenate([take(w_down, at, ff_chunk, 0), take(a_down, at, ff_chunk, 0)], axis=1)
        own = lax.all_gather(part, "fsdp", axis=0, tiled=True)
        down_pairs.append((own, swap(own, 1)))
        pair = []
        for whole in (b_gu_own, b_gu_oth):
            by_z = whole.reshape(z_count, 2 * latent, ff_dev)
            by_z = by_z[:, :, chunk * ff_chunk : (chunk + 1) * ff_chunk]
            pair.append(by_z.transpose(1, 0, 2).reshape(2 * latent, z_count * ff_chunk))
        b_gu_pairs.append(tuple(pair))

    order = jnp.arange(CHIPS, dtype=jnp.int32) ^ chip
    group_places = ((order * 2 + core)[:, None] * rows + jnp.arange(rows, dtype=jnp.int32)).reshape(-1)
    group_begin, group_which = doc_tables(group_places, first, chosen)
    adapters_at = jnp.arange(latent, dtype=jnp.int32) // RANK
    group_select = (adapters_at[None, :] == group_which[:, None]).astype(BF)
    select = group_select[:rows]
    cosine, sine = rope_tables(group_places - group_begin, HEAD_DIM)
    scalars = jnp.concatenate([jnp.stack([chip, core]).astype(jnp.int32), first])

    stream = tokens[0].astype(F32)
    cot_low = cotangent[0]
    first_norm, first_factor = layer_norm(stream)
    norm1 = plane_gather(first_norm.astype(BF))
    z_qkv = dot(norm1, full_a_qkv).astype(BF) * jnp.tile(group_select, (1, 3))
    z_parts = [z_qkv[:, k * latent : (k + 1) * latent] for k in range(3)]
    b_parts_own = [b_qkv_own[k * latent : (k + 1) * latent] for k in range(3)]
    b_parts_oth = [b_qkv_oth[k * latent : (k + 1) * latent] for k in range(3)]

    def project(weight, ups):
        pre = dot(norm1, weight) + jnp.concatenate(
            [dot(z, up) for z, up in zip(z_parts, ups)], axis=1
        )
        turned = rotate(pre[:, : 2 * span].reshape(-1, 2 * heads_dev, HEAD_DIM), cosine, sine)
        return jnp.concatenate([turned.reshape(-1, 2 * span), pre[:, 2 * span :]], axis=1).astype(BF)

    sent = project(qkv_oth, b_parts_oth)
    qkv_a = project(qkv_own, b_parts_own)
    qkv_b = swap(sent, 1)
    mixed_h, log_sums = attend_plane(scalars, qkv_a, qkv_b, rows)
    mixed = lax.all_to_all(mixed_h, "seq", split_axis=0, concat_axis=1, tiled=True)

    def natural(value):
        return jnp.concatenate(
            [
                value[:, (j * z_count + z) * HEAD_DIM : (j * z_count + z + 1) * HEAD_DIM]
                for z in range(z_count)
                for j in range(CHIPS)
            ],
            axis=1,
        )

    def by_device(value):
        return jnp.concatenate(
            [
                value[:, (z * CHIPS + j) * HEAD_DIM : (z * CHIPS + j + 1) * HEAD_DIM]
                for j in range(CHIPS)
                for z in range(z_count)
            ],
            axis=1,
        )

    mixed = natural(mixed)
    z_out = dot(mixed, full_a_out).astype(BF) * select
    second = stream + (dot(mixed, full_out) + dot(z_out, full_b_out))

    second_norm, second_factor = layer_norm(second)
    norm2 = plane_gather(second_norm.astype(BF))
    cot_all = plane_gather(cot_low)
    z_gu = dot(norm2, full_a_gu).astype(BF) * jnp.tile(group_select, (1, 2))
    z_gate, z_up = z_gu[:, :latent], z_gu[:, latent:]
    dz_down = (inner_cols(cot_all, full_b_down) * group_select.astype(F32)).astype(BF)
    cot_wide = jnp.concatenate([cot_all, dz_down], axis=1)
    down_sum = 0.0
    norm_grad_sum = 0.0
    latent_grad_sum = 0.0
    grads_b_gu = []
    grads_a_down = []
    for chunk in range(CHUNKS):
        for side in range(2):
            gu = gu_pairs[chunk][side]
            down = down_pairs[chunk][side]
            ups = b_gu_pairs[chunk][side]
            size = gu.shape[1] // 2
            gate = dot(norm2, gu[:, :size]) + dot(z_gate, ups[:latent])
            upper = dot(norm2, gu[:, size:]) + dot(z_up, ups[latent:])
            sigma = jax.nn.sigmoid(gate)
            active = gate * sigma
            hidden = (active * upper).astype(BF)
            hidden_grad = inner_cols(cot_wide, down)
            gate_grad = (hidden_grad * upper * sigma * (1.0 + gate * (1.0 - sigma))).astype(BF)
            upper_grad = (hidden_grad * active).astype(BF)
            both = jnp.concatenate([gate_grad, upper_grad], axis=1)
            norm_grad_sum = norm_grad_sum + inner_cols(both, gu)
            latent_grad_sum = latent_grad_sum + jnp.concatenate(
                [inner_cols(gate_grad, ups[:latent]), inner_cols(upper_grad, ups[latent:])], axis=1
            )
            down_sum = down_sum + dot(hidden, down)
            grads_b_gu.append(
                jnp.concatenate([inner_rows(z_gate, gate_grad), inner_rows(z_up, upper_grad)], axis=0)
            )
            grads_a_down.append(inner_rows(hidden, dz_down))

    wide = plane_scatter(jnp.concatenate([norm_grad_sum, latent_grad_sum], axis=1))
    dz_gu = (wide[:, width:] * jnp.tile(select, (1, 2)).astype(F32)).astype(BF)
    second_norm_grad = wide[:, :width] + inner_cols(dz_gu, full_a_gu)
    second_grad = cot_low.astype(F32) + norm_back(second_norm, second_factor, second_norm_grad)
    branch_grad = second_grad.astype(BF)
    dz_out = (inner_cols(branch_grad, full_b_out) * select.astype(F32)).astype(BF)
    mixed_grad = (inner_cols(branch_grad, full_out) + inner_cols(dz_out, full_a_out)).astype(BF)
    mixed_grad_h = lax.all_to_all(
        by_device(mixed_grad), "seq", split_axis=1, concat_axis=0, tiled=True
    )

    wide = plane_scatter(down_sum)
    z_down = wide[:, width:].astype(BF) * select
    activations = second + (wide[:, :width] + dot(z_down, full_b_down))

    grads_a, grads_b = attend_plane_back(scalars, qkv_a, qkv_b, mixed_grad_h, log_sums, rows)
    grads_b = swap(grads_b, 1)

    def unturn(parts):
        pre = [
            rotate_back(
                part.astype(F32).reshape(-1, heads_dev, HEAD_DIM), cosine, sine
            ).reshape(-1, span).astype(BF)
            for part in (parts[0], parts[1])
        ]
        return [pre[0], pre[1], parts[2]]

    parts_own = unturn(grads_a)
    parts_oth = unturn(grads_b)
    latent_grad = jnp.concatenate(
        [
            inner_cols(own, up_own) + inner_cols(oth, up_oth)
            for own, up_own, oth, up_oth in zip(parts_own, b_parts_own, parts_oth, b_parts_oth)
        ],
        axis=1,
    )
    norm_grad = inner_cols(jnp.concatenate(parts_own, axis=1), qkv_own) + inner_cols(
        jnp.concatenate(parts_oth, axis=1), qkv_oth
    )
    wide = plane_scatter(jnp.concatenate([norm_grad, latent_grad], axis=1))
    dz_qkv = (wide[:, width:] * jnp.tile(select, (1, 3)).astype(F32)).astype(BF)
    first_norm_grad = wide[:, :width] + inner_cols(dz_qkv, full_a_qkv)
    input_grad = second_grad + norm_back(first_norm, first_factor, first_norm_grad)

    def core_rows(value):
        half = value.shape[1] // 2
        return take(value, core * half, half, 1) + swap(take(value, (1 - core) * half, half, 1), 1)

    def z_lanes(value):
        count = value.shape[2] // LANES
        return jnp.concatenate([value[:, :, k * LANES : (k + 1) * LANES] for k in range(count)], axis=1)

    def chip_columns(value):
        return jnp.concatenate(
            [take(value, z * quarter + chip * LANES, LANES, 1) for z in range(z_count)], axis=1
        )

    def column_split(value):
        size = value.shape[1] // z_count
        return jnp.stack([value[:, z * size : (z + 1) * size] for z in range(z_count)])

    def finish(pieces):
        stacked = jnp.concatenate(pieces, axis=1)
        summed = lax.psum_scatter(stacked, "fsdp", scatter_dimension=0, tiled=True)[0]
        whole = lax.all_gather(summed, "seq", axis=0, tiled=False)
        result = []
        at = 0
        for piece in pieces:
            result.append(whole[:, at : at + piece.shape[1]])
            at += piece.shape[1]
        return result

    slice_b_gu = []
    slice_a_down = []
    for chunk in range(CHUNKS):
        mine, theirs = grads_b_gu[2 * chunk], grads_b_gu[2 * chunk + 1]
        slice_b_gu.append(column_split(mine + swap(theirs, 1)))
        mine, theirs = grads_a_down[2 * chunk], grads_a_down[2 * chunk + 1]
        slice_a_down.append((mine + swap(theirs, 1)).reshape(z_count, ff_chunk, latent))
    dz_gu_all = plane_gather(dz_gu)
    slice_a_gu = inner_rows(chip_columns(norm2), dz_gu_all).reshape(z_count, LANES, 2 * latent)
    slice_a_gu = z_lanes(core_rows(slice_a_gu))
    z_down_all = plane_gather(z_down)
    slice_b_down = core_rows(column_split(inner_rows(z_down_all, chip_columns(cot_all))))
    dz_out_all = lax.all_gather(dz_out, "seq", axis=0, tiled=True)
    rows_out = inner_rows(mixed_h, dz_out_all).reshape(heads_dev, HEAD_DIM, latent)
    half = HEAD_DIM // 2
    kept = take(rows_out, core * half, half, 1)
    brought = swap(take(rows_out, (1 - core) * half, half, 1), 1)
    slice_a_out = jnp.where(
        core == 0,
        jnp.concatenate([kept, brought], axis=0),
        jnp.concatenate([brought, kept], axis=0),
    )
    slice_b_out = lax.psum_scatter(
        inner_rows(z_out, branch_grad), "seq", scatter_dimension=0, tiled=True
    )
    slice_b_out = z_lanes(column_split(slice_b_out))
    got = finish(slice_b_gu + slice_a_down + [slice_a_gu, slice_b_down, slice_a_out, slice_b_out])
    g_b_gu = jnp.stack(got[:CHUNKS], axis=1)
    g_b_gu = g_b_gu.transpose(2, 0, 1, 3).reshape(2 * latent, ff_z)
    g_a_down = jnp.concatenate(got[CHUNKS : 2 * CHUNKS], axis=1).reshape(ff_z, latent)
    g_a_gu, g_b_down, g_a_out, g_b_out = got[2 * CHUNKS :]
    share_rows = LANES // 2

    def from_rows(value, count):
        value = value.reshape(PLANE, count, share_rows, LANES).transpose(0, 2, 1, 3)
        return value.reshape(PLANE * share_rows, count * LANES)

    def from_columns(value):
        value = value.reshape(CHIPS, 2, -1, LANES).transpose(1, 2, 0, 3)
        return value.reshape(-1, CHIPS * LANES)

    g_a_gu = from_rows(g_a_gu, 2)
    g_b_down = from_columns(g_b_down)
    g_a_out = g_a_out.reshape(quarter, latent)
    g_b_out = g_b_out.reshape(PLANE, -1, share_b, LANES).transpose(0, 2, 1, 3).reshape(latent, quarter)

    dz_qkv_all = plane_gather(dz_qkv)
    slice_a_qkv = inner_rows(chip_columns(norm1), dz_qkv_all).reshape(z_count, LANES, 3 * latent)
    slice_a_qkv = z_lanes(core_rows(slice_a_qkv))
    up_own = jnp.concatenate([inner_rows(z, g) for z, g in zip(z_parts, parts_own)], axis=0)
    up_oth = jnp.concatenate([inner_rows(z, g) for z, g in zip(z_parts, parts_oth)], axis=0)
    slice_b_qkv = jnp.where(
        core == 0,
        jnp.concatenate([up_own, up_oth], axis=1),
        jnp.concatenate([up_oth, up_own], axis=1),
    )
    slice_b_qkv = core_rows(column_split(slice_b_qkv))
    g_a_qkv, g_b_qkv = finish([slice_a_qkv, slice_b_qkv])
    g_a_qkv = from_rows(g_a_qkv, 3)
    g_b_qkv = from_columns(g_b_qkv)

    return (
        activations[None], input_grad[None],
        g_a_qkv, g_b_qkv, g_a_out, g_b_out, g_a_gu, g_b_gu, g_a_down, g_b_down,
    )


def solution(mesh):
    placed = (
        P("fsdp", "seq", None),
        P("fsdp", "seq", None),
        P("fsdp", None),
        P("fsdp", None),
        P("fsdp", None),
        P("fsdp", None),
        P("fsdp", None),
        P("fsdp", None),
        P("fsdp", None),
        P(None, "fsdp"),
        P("fsdp", None),
        P(None, "fsdp"),
        P("fsdp", None),
        P(None, "fsdp"),
        P("fsdp", None),
        P(None, "fsdp"),
    )
    on_plane = mesh.shape["seq"] == PLANE and mesh.shape["fsdp"] == 4
    return jax.shard_map(
        plane_shards if on_plane else shards,
        mesh=mesh,
        in_specs=placed,
        out_specs=(
            P("fsdp", "seq", None),
            P("fsdp", "seq", None),
            P("fsdp", None),
            P(None, "fsdp"),
            P("fsdp", None),
            P(None, "fsdp"),
            P("fsdp", None),
            P(None, "fsdp"),
            P("fsdp", None),
            P(None, "fsdp"),
        ),
        check_vma=False,
    )
```

```python
import functools

import jax
import jax.numpy as jnp
from jax import lax
from jax.experimental import pallas as pl
from jax.experimental.pallas import tpu as pltpu
from jax.sharding import PartitionSpec as P

HEAD_DIM = 128
RANK = 16


def layer_norm(values):
    centre = values - jnp.mean(values, axis=-1, keepdims=True)
    spread = jnp.mean(centre * centre, axis=-1, keepdims=True)
    factor = lax.rsqrt(spread + 1e-05)
    return (centre * factor, factor)


def norm_back(normed, factor, upstream):
    upstream_mean = jnp.mean(upstream, axis=-1, keepdims=True)
    cross_mean = jnp.mean(upstream * normed, axis=-1, keepdims=True)
    return factor * (upstream - upstream_mean - normed * cross_mean)


def doc_tables(places, first, chosen):
    within = first[None, :] <= places[:, None]
    begin = jnp.max(jnp.where(within, first[None, :], 0), axis=1)
    latest = jnp.sum(within.astype(jnp.int32), axis=1) - 1
    doc_order = jnp.arange(first.shape[0], dtype=jnp.int32)
    which = jnp.sum(jnp.where(doc_order[None, :] == latest[:, None], chosen[None, :], 0), axis=1)
    return (begin, which)


def rope_tables(position, head_dim):
    freqs = 10000.0 ** (-(jnp.arange(0, head_dim, 2, dtype=jnp.float32) / head_dim))
    angles = position.astype(jnp.float32)[:, None] * freqs[None, :]
    cosine = jnp.concatenate([jnp.cos(angles), jnp.cos(angles)], axis=-1)
    sine = jnp.concatenate([jnp.sin(angles), jnp.sin(angles)], axis=-1)
    return (cosine, sine)


def rotate(values, cosine, sine):
    half_dim = values.shape[-1] // 2
    turned = jnp.concatenate([-values[..., half_dim:], values[..., :half_dim]], axis=-1)
    return values * cosine[:, None, :] + turned * sine[:, None, :]


def rotate_back(upstream, cosine, sine):
    half_dim = upstream.shape[-1] // 2
    scaled = upstream * sine[:, None, :]
    return upstream * cosine[:, None, :] + jnp.concatenate(
        [scaled[..., half_dim:], -scaled[..., :half_dim]], axis=-1
    )


def inner_rows(left, right):
    return lax.dot_general(
        left, right, (((0,), (0,)), ((), ())), preferred_element_type=jnp.float32
    )


def inner_cols(left, right):
    return lax.dot_general(
        left, right, (((1,), (1,)), ((), ())), preferred_element_type=jnp.float32
    )


def adapter_fwd(inputs, down, up, select, segments):
    latent = jnp.dot(inputs, down, preferred_element_type=jnp.float32).astype(
        jnp.bfloat16
    ) * jnp.tile(select, (1, segments))
    span = up.shape[0] // segments
    pieces = [
        jnp.dot(
            latent[:, seg * span : (seg + 1) * span],
            up[seg * span : (seg + 1) * span],
            preferred_element_type=jnp.float32,
        )
        for seg in range(segments)
    ]
    return (latent, jnp.concatenate(pieces, axis=1))


def adapter_back(inputs, latent, upstream, down, up, select, segments):
    span = up.shape[0] // segments
    out_span = up.shape[1]
    grad_up = jnp.concatenate(
        [
            inner_rows(
                latent[:, seg * span : (seg + 1) * span],
                upstream[:, seg * out_span : (seg + 1) * out_span],
            )
            for seg in range(segments)
        ],
        axis=0,
    )
    latent_grad = jnp.concatenate(
        [
            inner_cols(
                upstream[:, seg * out_span : (seg + 1) * out_span],
                up[seg * span : (seg + 1) * span],
            )
            for seg in range(segments)
        ],
        axis=1,
    )
    latent_grad = (latent_grad * jnp.tile(select, (1, segments)).astype(jnp.float32)).astype(
        jnp.bfloat16
    )
    grad_down = inner_rows(inputs, latent_grad)
    back = inner_cols(latent_grad, down)
    return (grad_down, grad_up, back)


def frozen_fwd(inputs, weight):
    return (
        jnp.dot(
            inputs,
            lax.all_gather(weight, "fsdp", axis=0, tiled=True),
            preferred_element_type=jnp.float32,
        ),
        weight,
    )


def frozen_bwd(upstream, weight):
    return inner_cols(upstream, lax.all_gather(weight, "fsdp", axis=0, tiled=True))


def attend(query_h, key_h, value_h, begin, head_dim):
    length, local_width = query_h.shape
    local_heads = local_width // head_dim
    block_rows = min(512, length)
    block_count = length // block_rows
    score_scale = head_dim ** (-0.5)
    query_all = query_h.reshape(length, local_heads, head_dim)
    key_all = key_h.reshape(length, local_heads, head_dim)
    value_all = value_h.reshape(length, local_heads, head_dim)
    key_places = jnp.arange(length, dtype=jnp.int32)

    def one_block(block_index):
        start = block_index * block_rows
        query_block = lax.dynamic_slice_in_dim(query_all, start, block_rows, 0)
        rows = start + jnp.arange(block_rows, dtype=jnp.int32)
        row_begin = lax.dynamic_slice_in_dim(begin, start, block_rows, 0)
        allowed = (key_places[None, :] <= rows[:, None]) & (
            key_places[None, :] >= row_begin[:, None]
        )
        scores = (
            jnp.einsum("qhd,khd->hqk", query_block, key_all, preferred_element_type=jnp.float32)
            * score_scale
        )
        scores = jnp.where(allowed[None], scores, -1e30)
        row_top = jnp.max(scores, axis=-1, keepdims=True)
        expd = jnp.exp(scores - row_top)
        row_total = jnp.sum(expd, axis=-1, keepdims=True)
        probs = (expd / row_total).astype(jnp.bfloat16)
        mixed = jnp.einsum("hqk,khd->qhd", probs, value_all, preferred_element_type=jnp.float32)
        return (
            mixed.astype(jnp.bfloat16).reshape(block_rows, local_width),
            (row_top + jnp.log(row_total))[..., 0],
        )

    outputs, log_sums = lax.map(one_block, jnp.arange(block_count, dtype=jnp.int32))
    return (outputs.reshape(length, local_width), log_sums)


def attend_back(query_h, key_h, value_h, grad_h, log_sums, begin, head_dim):
    length, local_width = query_h.shape
    local_heads = local_width // head_dim
    block_rows = min(512, length)
    block_count = length // block_rows
    score_scale = head_dim ** (-0.5)
    query_all = query_h.reshape(length, local_heads, head_dim)
    key_all = key_h.reshape(length, local_heads, head_dim)
    value_all = value_h.reshape(length, local_heads, head_dim)
    grad_all = grad_h.reshape(length, local_heads, head_dim)
    key_places = jnp.arange(length, dtype=jnp.int32)

    def step(carry, inputs):
        key_grad, value_grad = carry
        block_index, block_lse = inputs
        start = block_index * block_rows
        query_block = lax.dynamic_slice_in_dim(query_all, start, block_rows, 0)
        grad_block = lax.dynamic_slice_in_dim(grad_all, start, block_rows, 0)
        rows = start + jnp.arange(block_rows, dtype=jnp.int32)
        row_begin = lax.dynamic_slice_in_dim(begin, start, block_rows, 0)
        allowed = (key_places[None, :] <= rows[:, None]) & (
            key_places[None, :] >= row_begin[:, None]
        )
        scores = (
            jnp.einsum("qhd,khd->hqk", query_block, key_all, preferred_element_type=jnp.float32)
            * score_scale
        )
        probs = jnp.where(allowed[None], jnp.exp(scores - block_lse[..., None]), 0.0)
        probs_low = probs.astype(jnp.bfloat16)
        prob_grad = jnp.einsum(
            "qhd,khd->hqk", grad_block, value_all, preferred_element_type=jnp.float32
        )
        row_delta = jnp.sum(prob_grad * probs, axis=-1, keepdims=True)
        score_grad = (probs * (prob_grad - row_delta)).astype(jnp.bfloat16)
        query_grad = (
            jnp.einsum("hqk,khd->qhd", score_grad, key_all, preferred_element_type=jnp.float32)
            * score_scale
        )
        key_grad = (
            key_grad
            + jnp.einsum(
                "hqk,qhd->khd", score_grad, query_block, preferred_element_type=jnp.float32
            )
            * score_scale
        )
        value_grad = value_grad + jnp.einsum(
            "hqk,qhd->khd", probs_low, grad_block, preferred_element_type=jnp.float32
        )
        return (
            (key_grad, value_grad),
            query_grad.astype(jnp.bfloat16).reshape(block_rows, local_width),
        )

    empty = jnp.zeros((length, local_heads, head_dim), jnp.float32)
    (key_grad, value_grad), query_grad = lax.scan(
        step, (empty, empty), (jnp.arange(block_count, dtype=jnp.int32), log_sums)
    )
    return (
        query_grad.reshape(length, local_width),
        key_grad.astype(jnp.bfloat16).reshape(length, local_width),
        value_grad.astype(jnp.bfloat16).reshape(length, local_width),
    )


def shards(
    tokens,
    cotangent,
    starts,
    adapter_ids,
    w_qkv,
    w_out,
    w_gu,
    w_down,
    a_qkv,
    b_qkv,
    a_out,
    b_out,
    a_gu,
    b_gu,
    a_down,
    b_down,
):
    gathered = (
        lax.all_gather(a_qkv, "fsdp", axis=0, tiled=True),
        lax.all_gather(b_qkv, "fsdp", axis=1, tiled=True),
        lax.all_gather(a_out, "fsdp", axis=0, tiled=True),
        lax.all_gather(b_out, "fsdp", axis=1, tiled=True),
        lax.all_gather(a_gu, "fsdp", axis=0, tiled=True),
        lax.all_gather(b_gu, "fsdp", axis=1, tiled=True),
        lax.all_gather(a_down, "fsdp", axis=0, tiled=True),
        lax.all_gather(b_down, "fsdp", axis=1, tiled=True),
    )
    (
        full_a_qkv,
        full_b_qkv,
        full_a_out,
        full_b_out,
        full_a_gu,
        full_b_gu,
        full_a_down,
        full_b_down,
    ) = gathered
    stream = tokens[0].astype(jnp.float32)
    cot_low = cotangent[0]
    tok_count, width = stream.shape
    seq_count = lax.axis_size("seq")
    seq_place = lax.axis_index("seq")
    stream_len = tok_count * seq_count
    first = starts[0]
    chosen = adapter_ids[0]
    local_places = seq_place * tok_count + jnp.arange(tok_count, dtype=jnp.int32)
    local_begin, which = doc_tables(local_places, first, chosen)
    columns = jnp.arange(full_a_out.shape[1], dtype=jnp.int32) // RANK
    select = (columns[None, :] == which[:, None]).astype(jnp.bfloat16)
    cosine, sine = rope_tables(local_places - local_begin, HEAD_DIM)
    head_count = width // HEAD_DIM
    first_norm, first_factor = layer_norm(stream)
    first_low = first_norm.astype(jnp.bfloat16)
    latent_qkv, extra_qkv = adapter_fwd(first_low, full_a_qkv, full_b_qkv, select, 3)
    qkv_main, held_qkv = frozen_fwd(first_low, w_qkv)
    qkv = qkv_main + extra_qkv
    query_rot = (
        rotate(qkv[:, :width].reshape(tok_count, head_count, HEAD_DIM), cosine, sine)
        .reshape(tok_count, width)
        .astype(jnp.bfloat16)
    )
    key_rot = (
        rotate(qkv[:, width : 2 * width].reshape(tok_count, head_count, HEAD_DIM), cosine, sine)
        .reshape(tok_count, width)
        .astype(jnp.bfloat16)
    )
    value_low = qkv[:, 2 * width :].astype(jnp.bfloat16)
    query_h, key_h, value_h = (
        lax.all_to_all(query_rot, "seq", split_axis=1, concat_axis=0, tiled=True),
        lax.all_to_all(key_rot, "seq", split_axis=1, concat_axis=0, tiled=True),
        lax.all_to_all(value_low, "seq", split_axis=1, concat_axis=0, tiled=True),
    )
    all_begin, all_which = doc_tables(jnp.arange(stream_len, dtype=jnp.int32), first, chosen)
    mixed_h, log_sums = attend(query_h, key_h, value_h, all_begin, HEAD_DIM)
    mixed = lax.all_to_all(mixed_h, "seq", split_axis=0, concat_axis=1, tiled=True)
    latent_out, extra_out = adapter_fwd(mixed, full_a_out, full_b_out, select, 1)
    out_main, held_out = frozen_fwd(mixed, w_out)
    second = stream + (out_main + extra_out)
    second_norm, second_factor = layer_norm(second)
    second_low = second_norm.astype(jnp.bfloat16)
    latent_gu, extra_gu = adapter_fwd(second_low, full_a_gu, full_b_gu, select, 2)
    gu_main, held_gu = frozen_fwd(second_low, w_gu)
    gate_up = gu_main + extra_gu
    ff_width = gate_up.shape[1] // 2
    gate = gate_up[:, :ff_width]
    upper = gate_up[:, ff_width:]
    sigma = jax.nn.sigmoid(gate)
    active = gate * sigma
    hidden = (active * upper).astype(jnp.bfloat16)
    latent_down, extra_down = adapter_fwd(hidden, full_a_down, full_b_down, select, 1)
    down_main, held_down = frozen_fwd(hidden, w_down)
    activations = second + (down_main + extra_down)
    grad_a_down, grad_b_down, hidden_extra = adapter_back(
        hidden, latent_down, cot_low, full_a_down, full_b_down, select, 1
    )
    hidden_grad = frozen_bwd(cot_low, held_down) + hidden_extra
    gate_grad = (hidden_grad * upper * sigma * (1.0 + gate * (1.0 - sigma))).astype(jnp.bfloat16)
    upper_grad = (hidden_grad * active).astype(jnp.bfloat16)
    gate_up_grad = jnp.concatenate([gate_grad, upper_grad], axis=1)
    grad_a_gu, grad_b_gu, second_extra = adapter_back(
        second_low, latent_gu, gate_up_grad, full_a_gu, full_b_gu, select, 2
    )
    second_norm_grad = frozen_bwd(gate_up_grad, held_gu) + second_extra
    second_grad = cot_low.astype(jnp.float32) + norm_back(
        second_norm, second_factor, second_norm_grad
    )
    branch_grad = second_grad.astype(jnp.bfloat16)
    grad_a_out, grad_b_out, mixed_extra = adapter_back(
        mixed, latent_out, branch_grad, full_a_out, full_b_out, select, 1
    )
    mixed_grad = (frozen_bwd(branch_grad, held_out) + mixed_extra).astype(jnp.bfloat16)
    mixed_grad_h = lax.all_to_all(mixed_grad, "seq", split_axis=1, concat_axis=0, tiled=True)
    query_grad_h, key_grad_h, value_grad_h = attend_back(
        query_h, key_h, value_h, mixed_grad_h, log_sums, all_begin, HEAD_DIM
    )
    query_grad, key_grad, value_grad = (
        lax.all_to_all(query_grad_h, "seq", split_axis=0, concat_axis=1, tiled=True),
        lax.all_to_all(key_grad_h, "seq", split_axis=0, concat_axis=1, tiled=True),
        lax.all_to_all(value_grad_h, "seq", split_axis=0, concat_axis=1, tiled=True),
    )
    query_pre = (
        rotate_back(
            query_grad.astype(jnp.float32).reshape(tok_count, head_count, HEAD_DIM), cosine, sine
        )
        .reshape(tok_count, width)
        .astype(jnp.bfloat16)
    )
    key_pre = (
        rotate_back(
            key_grad.astype(jnp.float32).reshape(tok_count, head_count, HEAD_DIM), cosine, sine
        )
        .reshape(tok_count, width)
        .astype(jnp.bfloat16)
    )
    qkv_grad = jnp.concatenate([query_pre, key_pre, value_grad], axis=1)
    grad_a_qkv, grad_b_qkv, first_extra = adapter_back(
        first_low, latent_qkv, qkv_grad, full_a_qkv, full_b_qkv, select, 3
    )
    first_norm_grad = frozen_bwd(qkv_grad, held_qkv) + first_extra
    input_grad = second_grad + norm_back(first_norm, first_factor, first_norm_grad)
    grads = (
        grad_a_qkv,
        grad_b_qkv,
        grad_a_out,
        grad_b_out,
        grad_a_gu,
        grad_b_gu,
        grad_a_down,
        grad_b_down,
    )
    shard_dims = (0, 1, 0, 1, 0, 1, 0, 1)
    summed = lax.psum(
        (grads[0], grads[1], grads[2], grads[3], grads[4], grads[5], grads[6], grads[7]),
        ("seq", "fsdp"),
    )
    fsdp_place = lax.axis_index("fsdp")
    fsdp_count = lax.axis_size("fsdp")
    totals = tuple(
        (
            lax.dynamic_slice_in_dim(
                whole,
                fsdp_place * (whole.shape[along] // fsdp_count),
                whole.shape[along] // fsdp_count,
                along,
            )
            for whole, along in zip(summed, shard_dims)
        )
    )
    return (
        activations[None],
        input_grad[None],
        totals[0],
        totals[1],
        totals[2],
        totals[3],
        totals[4],
        totals[5],
        totals[6],
        totals[7],
    )


BF = jnp.bfloat16
F32 = jnp.float32
PLANE = 8
CHIPS = 4
LANES = 128
CHUNKS = 2
HALVES = ((1, 0), (3, 0), (2, 1), (3, 1), (2, 0), (1, 1), (0, 0), (0, 1))
ANY = pl.BlockSpec(memory_space=pl.ANY)
ROOMY = 56 * 2**20


def swap(value, bits):
    return lax.ppermute(value, "seq", [(i, i ^ bits) for i in range(PLANE)])


def gather_halves(first, second):
    x_first, y_second = swap(first, 2), swap(second, 4)
    y_first, x_second = swap(first, 4), swap(second, 2)
    far_first, far_second = swap(y_first, 2), swap(x_second, 4)
    return [x_first, far_first, y_second, far_second, y_first, x_second, first, second]


def blocks_of(block):
    return [block, swap(block, 2), swap(block, 4), swap(block, 6)]


def dot(left, right):
    return jnp.dot(left, right, preferred_element_type=F32)


def inner(left, right, on_left, on_right):
    return lax.dot_general(
        left, right, (((on_left,), (on_right,)), ((), ())), preferred_element_type=F32
    )


def take(value, start, count, axis):
    return lax.dynamic_slice_in_dim(value, start, count, axis)


def whole_spec(shape):
    return pl.BlockSpec(shape, lambda *_: (0,) * len(shape))


def call(body, scalars, operands, specs, shapes, out_specs, scratch=(), grid=(1,), cost=None, ties=()):
    count = len(operands)

    def run(*refs):
        inside = refs[: 1 + count] + refs[1 + count + len(ties) :]
        body(*inside)

    return pl.pallas_call(
        run,
        grid_spec=pltpu.PrefetchScalarGridSpec(
            num_scalar_prefetch=1,
            grid=grid,
            in_specs=list(specs) + [ANY] * len(ties),
            out_specs=out_specs,
            scratch_shapes=list(scratch),
        ),
        out_shape=shapes,
        compiler_params=pltpu.CompilerParams(vmem_limit_bytes=ROOMY),
        cost_estimate=None
        if cost is None
        else pl.CostEstimate(flops=cost[0], bytes_accessed=cost[1], transcendentals=0),
    )(scalars, *operands, *ties)


def hold(value, ties):
    return pl.pallas_call(
        lambda *refs: None,
        in_specs=[ANY] * (1 + len(ties)),
        out_specs=ANY,
        out_shape=sds(value.shape, value.dtype),
        input_output_aliases={0: 0},
    )(value, *ties)


def copies(pairs, sems):
    started = [
        pltpu.make_async_copy(source, target, sems.at[k]) for k, (source, target) in enumerate(pairs)
    ]
    for one in started:
        one.start()
    for one in started:
        one.wait()


def sds(shape, dtype=BF):
    return jax.ShapeDtypeStruct(shape, dtype)


def doc_begin(scalars, places):
    begin = jnp.zeros_like(places)
    for doc in range(4):
        begin = jnp.where(scalars[3 + doc] <= places, scalars[3 + doc], begin)
    return begin


def adapter_mask(scalars, places):
    which = jnp.zeros_like(places) + scalars[7]
    for doc in range(1, 4):
        which = jnp.where(scalars[3 + doc] <= places, scalars[7 + doc], which)
    column = lax.broadcasted_iota(jnp.int32, (1, LANES), 1) // RANK
    return (column == which).astype(F32)


def rows_from(first, count):
    return first + lax.broadcasted_iota(jnp.int32, (count, 1), 0)


def normed(values):
    centre = values - jnp.mean(values, axis=-1, keepdims=True)
    factor = lax.rsqrt(jnp.mean(centre * centre, axis=-1, keepdims=True) + 1e-05)
    return centre * factor, factor


def cut_first_kernel(sizes, scalars, w_qkv, w_out, a_qkv, a_out, a_gu, b_out, b_down, b_qkv, out, sems):
    share, quarter, width = sizes
    chip, core = scalars[0], scalars[1]
    seat = chip * 2 + core
    pairs = []
    for part in range(3):
        for i in range(2):
            column = pl.multiple_of(part * width + (2 * core + i) * quarter + chip * LANES, LANES)
            k = part * 2 + i
            pairs.append(
                (w_qkv.at[:, pl.ds(column, LANES)], out.at[:quarter, k * LANES : (k + 1) * LANES])
            )
    rows = pl.ds(pl.multiple_of(seat * share, share), share)
    small = slice(quarter, quarter + share)
    pairs.append((a_qkv.at[rows], out.at[small, :384]))
    pairs.append((a_gu.at[rows], out.at[small, 384:640]))
    pairs.append((a_out.at[rows], out.at[small, 640:768]))
    low = pl.ds(pl.multiple_of(seat * 16, 16), 16)
    at = quarter + share
    pairs.append((b_out.at[low], out.at[at : at + 16, :512]))
    pairs.append((b_down.at[low], out.at[at + 16 : at + 32, :512]))
    column = pl.ds(pl.multiple_of(chip * LANES, LANES), LANES)
    for k in range(12):
        here = pl.ds(pl.multiple_of(core * 192 + k * 16, 16), 16)
        row, lane = up_slot(k)
        row += at
        pairs.append((b_qkv.at[here, column], out.at[row : row + 16, lane : lane + LANES]))
    at += 64
    for k in range(16):
        row, lane = at + (k // 6) * share, (k % 6) * LANES
        pairs.append(
            (w_out.at[rows, k * LANES : (k + 1) * LANES], out.at[row : row + share, lane : lane + LANES])
        )
    copies(pairs, sems)


def up_slot(k):
    if k < 4:
        return (k // 2) * 16, 512 + (k % 2) * LANES
    return 32 + ((k - 4) // 4) * 16, ((k - 4) % 4) * LANES


def cut_rest_kernel(sizes, scalars, w_gu, w_down, a_down, b_gu, down, gu_0, gu_1, sems):
    ff, ff_z, ff_dev, width = sizes
    seat = scalars[0] * 2 + scalars[1]
    rows = pl.ds(pl.multiple_of(seat * ff_dev, ff_dev), ff_dev)
    wide = width + LANES
    pairs = [
        (w_down.at[rows], down.at[:, :width]),
        (a_down.at[rows], down.at[:, width:wide]),
        (b_gu.at[:, rows], down.at[:, wide : wide + ff_dev]),
    ]
    for chunk, gu in enumerate((gu_0, gu_1)):
        for half in range(2):
            for i in range(2):
                column = pl.multiple_of(half * ff + (2 * chunk + i) * ff_z + seat * ff_dev, ff_dev)
                k = half * 2 + i
                pairs.append(
                    (w_gu.at[:, pl.ds(column, ff_dev)], gu.at[:, k * ff_dev : (k + 1) * ff_dev])
                )
    copies(pairs, sems)


def unpack_small_kernel(share, quarter, scalars, *refs):
    pieces = refs[:16]
    a_qkv, a_gu, a_out, b_out, b_down = refs[16:]
    chip, core = scalars[0], scalars[1]
    for k in range(2):
        for at, (rel, half) in enumerate(HALVES):
            piece = pieces[8 * k + at]
            tall = piece.shape[0] // 2
            seat = (chip ^ rel) * 2 + (core if k == 0 else 1 - core)
            for i in range(2):
                z = half * 2 + i
                rows = slice(i * tall, i * tall + share)
                there = pl.ds(pl.multiple_of(z * quarter + seat * share, share), share)
                a_qkv[there, :] = piece[rows, :384]
                a_gu[there, :] = piece[rows, 384:640]
                a_out[there, :] = piece[rows, 640:768]
                there = pl.ds(pl.multiple_of(seat * 16, 16), 16)
                columns = slice(z * quarter, (z + 1) * quarter)
                row = i * tall + share
                b_out[there, columns] = piece[row : row + 16, :512]
                b_down[there, columns] = piece[row + 16 : row + 32, :512]


def unpack_out_kernel(share, quarter, scalars, *refs):
    pieces, out, sems = refs[:16], refs[16], refs[17]
    chip, core = scalars[0], scalars[1]
    pairs = []
    for k in range(2):
        for at, (rel, half) in enumerate(HALVES):
            seat = (chip ^ rel) * 2 + (core if k == 0 else 1 - core)
            for i in range(2):
                there = pl.ds(pl.multiple_of((half * 2 + i) * quarter + seat * share, share), share)
                for block in range(3):
                    row = (i * 3 + block) * share
                    lanes = min(768, out.shape[1] - block * 768)
                    pairs.append(
                        (
                            pieces[8 * k + at].at[row : row + share, :lanes],
                            out.at[there, block * 768 : block * 768 + lanes],
                        )
                    )
    copies(pairs, sems)


def norm_kernel(scalars, tokens, first, second):
    value, _ = normed(tokens[...].astype(F32))
    half = first.shape[0]
    first[...] = value[:half].astype(BF)
    second[...] = value[half:].astype(BF)


def qkv_kernel(scalars, *refs):
    pieces, gathered = refs[:16], refs[16]
    down, up, cosine, sine, out, latents, weight, rows_all, sems = refs[17:]
    chip, core = scalars[0], scalars[1]
    half = pieces[0].shape[0]
    quarter = weight.shape[0] // 4
    tall = gathered.shape[0] // 4
    pairs = [
        (gathered.at[pl.ds(z * tall, quarter)], weight.at[pl.ds(z * quarter, quarter)]) for z in range(4)
    ]
    for k in range(2):
        for at, (rel, part) in enumerate(HALVES):
            seat = (chip ^ rel) * 2 + (core if k == 0 else 1 - core)
            there = pl.ds(pl.multiple_of((seat * 2 + part) * half, half), half)
            pairs.append((pieces[8 * k + at], rows_all.at[there]))
    copies(pairs, sems)
    step = 512
    span = up.shape[1]
    for start in range(0, rows_all.shape[0], step):
        here = slice(start, start + step)
        value = rows_all[here, :]
        mask = adapter_mask(scalars, rows_from(start, step))
        latent = dot(value, down[...]).astype(BF) * jnp.concatenate([mask] * 3, axis=1).astype(BF)
        latents[here, :] = latent
        pre = dot(value, weight[...])
        for part in range(3):
            block = pre[:, part * span : (part + 1) * span] + dot(
                latent[:, part * LANES : (part + 1) * LANES], up[part * LANES : (part + 1) * LANES, :]
            )
            if part < 2:
                heads = []
                for k in range(span // HEAD_DIM):
                    head = block[:, k * HEAD_DIM : (k + 1) * HEAD_DIM]
                    heads.append(
                        head * cosine[here, :] + pltpu.roll(head, HEAD_DIM // 2, 1) * sine[here, :]
                    )
                block = jnp.concatenate(heads, axis=1)
            out[here, part * span : (part + 1) * span] = block.astype(BF)


def allowed_pairs(scalars, first_row, rows, width):
    row = rows_from(first_row, rows)
    column = lax.broadcasted_iota(jnp.int32, (1, width), 1)
    return (column <= row) & (column >= doc_begin(scalars, row))


def attend_kernel(rows, scalars, query, key, value, out, lse):
    scale = HEAD_DIM**-0.5
    for start in range(0, query.shape[0], rows):
        here = slice(start, start + rows)
        width = start + rows
        scores = inner(query[here, :], key[:width, :], 1, 1) * scale
        scores = jnp.where(allowed_pairs(scalars, start, rows, width), scores, -1e30)
        top = jnp.max(scores, axis=1, keepdims=True)
        expd = jnp.exp(scores - top)
        total = jnp.sum(expd, axis=1, keepdims=True)
        probs = (expd * (1.0 / total)).astype(BF)
        out[here, :] = dot(probs, value[:width, :]).astype(BF)
        lse[here, :] = jnp.broadcast_to(top + jnp.log(total), (rows, LANES))


def attend_back_kernel(
    rows, scalars, query, key, value, grad, lse, latents, cosine, sine, own, other, ups,
    dq_all, dk_sum, dv_sum,
):
    dk_sum[...] = jnp.zeros_like(dk_sum)
    dv_sum[...] = jnp.zeros_like(dv_sum)
    scale = HEAD_DIM**-0.5
    length = query.shape[0]
    for start in range(0, length, rows):
        here = slice(start, start + rows)
        width = start + rows
        this_query = query[here, :]
        upstream = grad[here, :]
        scores = inner(this_query, key[:width, :], 1, 1) * scale
        probs = jnp.where(
            allowed_pairs(scalars, start, rows, width), jnp.exp(scores - lse[here, :1]), 0.0
        )
        prob_grad = inner(upstream, value[:width, :], 1, 1)
        delta = jnp.sum(prob_grad * probs, axis=1, keepdims=True)
        score_grad = (probs * (prob_grad - delta)).astype(BF)
        dq_all[here, :] = dot(score_grad, key[:width, :]) * scale
        dk_sum[:width, :] += inner(score_grad, this_query, 0, 0)
        dv_sum[:width, :] += inner(probs.astype(BF), upstream, 0, 0)

    chip, core = scalars[0], scalars[1]
    half = own.shape[1] // 8
    for part, total in enumerate((dq_all, dk_sum, dv_sum)):
        for start in range(0, length, 512):
            here = slice(start, start + 512)
            if part == 0:
                raw = total[here, :].astype(BF).astype(F32)
            elif part == 1:
                raw = (total[here, :] * scale).astype(BF).astype(F32)
            else:
                raw = total[here, :]
            if part < 2:
                raw = raw * cosine[here, :] - pltpu.roll(raw, HEAD_DIM // 2, 1) * sine[here, :]
            total[here, :] = raw.astype(BF).astype(F32)
        low = total[...].astype(BF)
        ups[part] = inner(latents[:, part * LANES : (part + 1) * LANES], low, 0, 0)
        for k, target in enumerate((own, other)):
            for at, (rel, h) in enumerate(HALVES):
                seat = (chip ^ rel) * 2 + (core if k == 0 else 1 - core)
                there = pl.ds(pl.multiple_of((seat * 2 + h) * half, half), half)
                target[part, at * half : (at + 1) * half, :] = total[there, :].astype(BF)


def head_order(k):
    return (k % CHIPS) * CHIPS + k // CHIPS


def out_kernel(scalars, mixed, weight, down, up, tokens, second, first_half, second_half, latents, natural):
    for k in range(16):
        at = head_order(k)
        natural[:, k * LANES : (k + 1) * LANES] = mixed[:, at * LANES : (at + 1) * LANES]
    rows = tokens.shape[0]
    seat = scalars[0] * 2 + scalars[1]
    mask = adapter_mask(scalars, rows_from(seat * rows, rows)).astype(BF)
    value = natural[...]
    latent = dot(value, down[...]).astype(BF) * mask
    latents[...] = latent
    total = tokens[...].astype(F32) + (dot(value, weight[...]) + dot(latent, up[...]))
    second[...] = total
    norm, _ = normed(total)
    first_half[...] = norm[: rows // 2].astype(BF)
    second_half[...] = norm[rows // 2 :].astype(BF)


def ff_kernel(begin, chunk, scalars, *refs):
    select, a_gu, b_down, down_own, down_oth, gu_own, gu_oth = refs[:7]
    norm, cot = refs[7:11], refs[11:15]
    count = 15 if begin else 16
    outs = refs[count : count + (1 if begin else 2)]
    count += len(outs)
    hidden_out, ups, downs = refs[count : count + 3]
    rows_in, cot_in, gu_a, gu_b, down_a, down_b, sums, sems = refs[count + 3 :]
    rows, width = rows_in.shape
    wide = width + LANES
    part = pl.ds(chunk * down_a.shape[0], down_a.shape[0])
    low = rows // 4
    pairs = [(norm[k], rows_in.at[pl.ds(k * low, low)]) for k in range(4)]
    pairs += [(gu_own, gu_a)]
    pairs += [(cot[k], cot_in.at[pl.ds(k * low, low)]) for k in range(4)]
    pairs += [(down_own.at[part], down_a), (gu_oth, gu_b), (down_oth.at[part], down_b)]
    if not begin:
        pairs.append((refs[15], sums))
    loads = [pltpu.make_async_copy(x, y, sems.at[k]) for k, (x, y) in enumerate(pairs)]
    for load in loads:
        load.start()
    mask = select[...]
    for load in loads[:4]:
        load.wait()
    z_gu = dot(rows_in[...], a_gu[...]).astype(BF) * jnp.concatenate([mask, mask], axis=1)
    z_gate, z_up = z_gu[:, :LANES], z_gu[:, LANES:]
    norm_grad = 0.0
    latent_grad = 0.0
    for side, (gu, down) in enumerate(((gu_a, down_a), (gu_b, down_b))):
        size = gu.shape[1] // 2
        own_ff = size // 2
        loads[4 if side == 0 else 10].wait()
        both = dot(rows_in[...], gu[...])
        if side == 0:
            for load in loads[5:9]:
                load.wait()
            dz_down = (inner(cot_in[...], b_down[...], 1, 1) * mask.astype(F32)).astype(BF)
        loads[9 if side == 0 else 11].wait()
        up_gate = jnp.concatenate(
            [down[i * own_ff : i * own_ff + LANES, wide:] for i in range(2)], axis=1
        )
        up_up = jnp.concatenate(
            [down[i * own_ff + LANES : i * own_ff + 2 * LANES, wide:] for i in range(2)], axis=1
        )
        gate = both[:, :size] + dot(z_gate, up_gate)
        upper = both[:, size:] + dot(z_up, up_up)
        sigma = 1.0 / (1.0 + jnp.exp(-gate))
        active = gate * sigma
        hidden = (active * upper).astype(BF)
        hidden_out[:, side * size : (side + 1) * size] = hidden
        hidden_grad = inner(cot_in[...], down[:, :width], 1, 1) + inner(
            dz_down, down[:, width:wide], 1, 1
        )
        gate_grad = (hidden_grad * upper * sigma * (1.0 + gate * (1.0 - sigma))).astype(BF)
        upper_grad = (hidden_grad * active).astype(BF)
        norm_grad += inner(jnp.concatenate([gate_grad, upper_grad], axis=1), gu[...], 1, 1)
        latent_grad += jnp.concatenate(
            [inner(gate_grad, up_gate, 1, 1), inner(upper_grad, up_up, 1, 1)], axis=1
        )
        ups[side] = jnp.concatenate(
            [inner(z_gate, gate_grad, 0, 0), inner(z_up, upper_grad, 0, 0)], axis=0
        )
        downs[side] = inner(hidden, dz_down, 0, 0)
    if begin:
        outs[0][:, :width] = norm_grad
        outs[0][:, width:] = latent_grad
        return
    loads[12].wait()
    low = rows // 2
    for k in range(2):
        at = slice(k * low, (k + 1) * low)
        kind = outs[k].dtype
        outs[k][:, :width] = (norm_grad[at] + sums[at, :width]).astype(kind)
        outs[k][:, width:] = (latent_grad[at] + sums[at, width:]).astype(kind)


def down_kernel(scalars, hidden_0, hidden_1, down_own, down_oth, out_0, out_1):
    wide = out_0.shape[1]
    size = hidden_0.shape[1] // 2
    total = 0.0
    for chunk, hidden in enumerate((hidden_0, hidden_1)):
        part = slice(chunk * size, (chunk + 1) * size)
        total += dot(hidden[:, :size], down_own[part, :wide]) + dot(hidden[:, size:], down_oth[part, :wide])
    for k, out in enumerate((out_0, out_1)):

        @pl.when(pl.program_id(0) == k)
        def _():
            out[...] = total.astype(out.dtype)


def spread_kernel(places, scalars, *refs):
    pieces, outs = refs[:8], refs[8:]
    for k, piece in enumerate(pieces):
        chip = scalars[0] ^ (k % 4)
        core = scalars[1] if k < 4 else 1 - scalars[1]
        seat = chip * 2 + core
        at = 0
        for out, (kind, rows, blocks) in zip(outs, places):
            for block in range(blocks):
                value = piece[at : at + rows, :].astype(F32)
                at += rows
                columns = pl.ds(block * LANES, LANES)
                if kind == "rows":
                    out[pl.ds(pl.multiple_of(seat * rows, rows), rows), columns] = value
                elif kind == "core rows":
                    row = pl.multiple_of(core * (CHIPS * rows) + chip * rows, rows)
                    out[pl.ds(row, rows), columns] = value
                elif kind == "columns":
                    column = pl.multiple_of((seat * blocks + block) * LANES, LANES)
                    out[:, pl.ds(column, LANES)] = value
                else:
                    row = pl.multiple_of(core * rows, rows)
                    out[pl.ds(row, rows), pl.ds(pl.multiple_of(chip * LANES, LANES), LANES)] = value


def ff_grads_kernel(scalars, *refs):
    ups, downs, keep, send = refs[:4], refs[4:8], refs[8], refs[9]
    for side, out in enumerate((keep, send)):
        for chunk in range(CHUNKS):
            up = ups[2 * chunk][side] + ups[2 * chunk + 1][side]
            down = downs[2 * chunk][side] + downs[2 * chunk + 1][side]
            rows = up.shape[0]
            size = up.shape[1] // 2
            for i in range(2):
                z = 2 * chunk + i
                count = size // LANES
                for k in range(count):
                    at = i * size + k * LANES
                    out[z, k * rows : (k + 1) * rows, :] = up[:, at : at + LANES].astype(out.dtype)
                at = count * rows
                out[z, at : at + size, :] = down[i * size : (i + 1) * size].astype(out.dtype)


def other_grads_kernel(quarter, scalars, *refs):
    norm1, norm2, cot, mixed = refs[:8], refs[8:16], refs[16:24], refs[24]
    dz_gu, dz_qkv, z_down, dz_out, up_out = (refs[25 + 4 * k : 29 + 4 * k] for k in range(5))
    up_qkv, keep, send, columns, all_gu, all_qkv, all_down, sems = refs[45:]
    half = norm1[0].shape[0]
    chip, core = scalars[0], scalars[1]
    pairs = []
    for k, source in enumerate((norm1, norm2, cot)):
        for z in range(4):
            column = pl.ds(pl.multiple_of(z * quarter + chip * LANES, LANES), LANES)
            for h in range(8):
                target = columns.at[k, h * half : (h + 1) * half, z * LANES : (z + 1) * LANES]
                pairs.append((source[h].at[:, column], target))
    loads = [pltpu.make_async_copy(x, y, sems.at[k]) for k, (x, y) in enumerate(pairs)]
    for load in loads:
        load.start()
    for pieces, whole in ((dz_gu, all_gu), (dz_qkv, all_qkv), (z_down, all_down)):
        for k, (rel, h) in enumerate(HALVES):
            whole[k * half : (k + 1) * half, :] = pieces[rel][h * half : (h + 1) * half, :]

    def halves(z, at, value):
        rows = value.shape[0] // 2
        for k in range(2):
            piece = value[k * rows : (k + 1) * rows]

            @pl.when(core == k)
            def _():
                keep[z, at : at + rows, :] = piece

            @pl.when(core != k)
            def _():
                send[z, at : at + rows, :] = piece.astype(BF)

    def two_of_four(at, values):
        rows = values[0].shape[0] // 2
        for k in range(2):

            @pl.when(core == k)
            def _():
                for i in range(2):
                    here, there = 2 * k + i, 2 * (1 - k) + i
                    keep[here, at : at + rows, :] = values[i][k * rows : (k + 1) * rows]
                    send[here, at : at + rows, :] = values[i][(1 - k) * rows : (2 - k) * rows].astype(BF)
                    keep[there, at : at + rows, :] = jnp.zeros((rows, LANES), F32)
                    send[there, at : at + rows, :] = jnp.zeros((rows, LANES), BF)

    low = LANES // 2
    at = 3 * low
    total = 0.0
    rows = dz_out[0].shape[1]
    for rel in range(4):
        for k in range(2):
            seat = (chip ^ rel) * 2 + (core if k == 0 else 1 - core)
            here = pl.ds(pl.multiple_of(seat * rows, rows), rows)
            total += inner(mixed[here, :], dz_out[rel][k], 0, 0)
    two_of_four(at, [total[:LANES], total[LANES:]])
    at += low
    value = up_out[0][...]
    for piece in up_out[1:]:
        value = value + piece[...].astype(F32)
    share = value.shape[0] // 2
    for z in range(4):
        for k in range(4):
            block = value[:, (z * 4 + k) * LANES : (z * 4 + k + 1) * LANES]
            halves(z, at + k * share, block)
    at += low
    at_b = at + 3 * low
    heads = [jnp.concatenate([up_qkv[part, :, i * LANES : (i + 1) * LANES] for part in range(3)], axis=0) for i in range(2)]
    two_of_four(at_b, heads)
    for load in loads:
        load.wait()
    value = inner(columns[1], all_gu[...], 0, 0)
    for z in range(4):
        for k in range(2):
            block = value[z * LANES : (z + 1) * LANES, k * LANES : (k + 1) * LANES]
            halves(z, k * low, block)
    value = inner(all_down[...], columns[2], 0, 0)
    for z in range(4):
        halves(z, 2 * low, value[:, z * LANES : (z + 1) * LANES])
    value = inner(columns[0], all_qkv[...], 0, 0)
    for z in range(4):
        for k in range(3):
            block = value[z * LANES : (z + 1) * LANES, k * LANES : (k + 1) * LANES]
            halves(z, at + k * low, block)


def along_line_kernel(scalars, keep, brought, mine, *outs):
    z = scalars[2]
    mine[...] = keep[z] + brought[z].astype(F32)
    for k, out in enumerate(outs):
        hop = k // 2 + 1
        to = jnp.minimum(z + hop, 3) if k % 2 == 0 else jnp.maximum(z - hop, 0)
        out[...] = (keep[to] + brought[to].astype(F32)).astype(BF)


def keep_kernel(scalars, *refs):
    count = len(refs) // 2
    for source, target in zip(refs[:count], refs[count:]):
        target[...] = source[...]


def back_middle_kernel(
    scalars, own, by_x, by_y, got_y, got_x, second, cot, a_gu, w_out, a_out, b_out, z_out,
    grad, dz_gu_out, dz_out_out, mixed_grad, up_own, up_x, up_y, up_far,
):
    rows, width = second.shape
    half = rows // 2
    upper = own[:half] + by_x[...].astype(F32) + got_y[...].astype(F32)
    lower = own[half:] + by_y[...].astype(F32) + got_x[...].astype(F32)
    wide = jnp.concatenate([upper, lower], axis=0)
    seat = scalars[0] * 2 + scalars[1]
    mask = adapter_mask(scalars, rows_from(seat * rows, rows))
    dz_gu = (wide[:, width:] * jnp.concatenate([mask, mask], axis=1)).astype(BF)
    dz_gu_out[...] = dz_gu
    upstream = wide[:, :width] + inner(dz_gu, a_gu[...], 1, 1)
    norm, factor = normed(second[...])
    total = cot[...].astype(F32) + norm_back(norm, factor, upstream)
    grad[...] = total
    low = total.astype(BF)
    dz_out = (inner(low, b_out[...], 1, 1) * mask).astype(BF)
    dz_out_out[...] = dz_out
    back = (inner(low, w_out[...], 1, 1) + inner(dz_out, a_out[...], 1, 1)).astype(BF)
    for k in range(16):
        at = head_order(k)
        mixed_grad[:, at * LANES : (at + 1) * LANES] = back[:, k * LANES : (k + 1) * LANES]
    value = inner(z_out[...], low, 0, 0)
    share = value.shape[0] // PLANE
    for block in range(CHIPS):
        for core in range(2):
            at = (core * CHIPS + block) * share
            piece = value[at : at + share]
            for rel, out in enumerate((up_own, up_x, up_y, up_far)):

                @pl.when((scalars[0] ^ rel) == block)
                def _():
                    out[core * share : (core + 1) * share, :] = piece.astype(out.dtype)


def back_latent_kernel(scalars, own, other, up_own, up_oth, to_x, to_y, to_far, kept):
    half = kept.shape[0] // 2
    targets = {0: kept, 1: to_x, 2: to_y, 3: to_far}
    for part in range(3):
        at = slice(part * LANES, (part + 1) * LANES)
        value = inner(own[part], up_own[at, :], 1, 1) + inner(other[part], up_oth[at, :], 1, 1)
        for k, (rel, h) in enumerate(HALVES):
            target = targets[rel]
            target[h * half : (h + 1) * half, at] = value[k * half : (k + 1) * half].astype(target.dtype)


def back_qkv_kernel(scalars, own, other, w_own, w_oth, out_0, out_1):
    rows = out_0.shape[0]
    mine = jnp.concatenate([own[part] for part in range(3)], axis=1)
    theirs = jnp.concatenate([other[part] for part in range(3)], axis=1)
    value = inner(mine, w_own[...], 1, 1) + inner(theirs, w_oth[...], 1, 1)
    out_0[...] = value[:rows].astype(out_0.dtype)
    out_1[...] = value[rows:].astype(out_1.dtype)


def back_first_kernel(
    scalars, own, by_x, by_y, got_y, got_x, tokens, second_grad, dz_qkv, a_qkv, input_grad
):
    half = tokens.shape[0] // 2
    upper = own[:half] + by_x[...].astype(F32) + got_y[...].astype(F32)
    lower = own[half:] + by_y[...].astype(F32) + got_x[...].astype(F32)
    upstream = jnp.concatenate([upper, lower], axis=0) + inner(dz_qkv[...], a_qkv[...], 1, 1)
    norm, factor = normed(tokens[...].astype(F32))
    input_grad[...] = second_grad[...] + norm_back(norm, factor, upstream)


def scatter_rest(send_x, send_y, onward):
    half = onward.shape[0] // 2
    by_x, by_y = swap(send_x, 2), swap(send_y, 4)
    pass_y = (onward[:half] + by_x[half:].astype(F32)).astype(BF)
    pass_x = (onward[half:] + by_y[half:].astype(F32)).astype(BF)
    got_y, got_x = swap(pass_y, 4), swap(pass_x, 2)
    return by_x, by_y, got_y, got_x, (pass_y, pass_x)


def plane_shards(
    tokens, cotangent, starts, adapter_ids,
    w_qkv, w_out, w_gu, w_down, a_qkv, b_qkv, a_out, b_out, a_gu, b_gu, a_down, b_down,
):
    seat = lax.axis_index("seq")
    z_at = lax.axis_index("fsdp")
    z_count = lax.axis_size("fsdp")
    core = seat % 2
    chip = seat // 2
    rows, width = tokens.shape[1:]
    half = rows // 2
    group = CHIPS * rows
    length = rows * PLANE
    ff = w_gu.shape[1] // 2
    ff_z = ff // z_count
    ff_dev = ff_z // PLANE
    quarter = w_qkv.shape[0]
    latent = a_out.shape[1]
    heads_dev = width // HEAD_DIM // PLANE
    span = heads_dev * HEAD_DIM
    share = quarter // PLANE
    share_b = latent // PLANE
    wide_down = width + latent
    wide_gu = width + 2 * latent
    first = starts[0]
    chosen = adapter_ids[0]
    scalars = jnp.concatenate([jnp.stack([chip, core, z_at]).astype(jnp.int32), first, chosen])
    stream, cot_low = tokens[0], cotangent[0]

    norm_a, norm_b = call(
        norm_kernel, scalars, [stream], [whole_spec((rows, width))],
        [sds((half, width))] * 2, [whole_spec((half, width))] * 2,
    )
    tall_rows = quarter + 2 * share + 3 * share
    first_part = call(
        functools.partial(cut_first_kernel, (share, quarter, width)), scalars,
        [w_qkv, w_out, a_qkv, a_out, a_gu, b_out, b_down, b_qkv], [ANY] * 8,
        sds((tall_rows, 3 * span)), whole_spec((tall_rows, 3 * span)),
        scratch=[pltpu.SemaphoreType.DMA((39,))],
    )
    first_all = lax.all_gather(first_part, "fsdp", axis=0, tiled=True)
    down_part, gu_part_0, gu_part_1 = call(
        functools.partial(cut_rest_kernel, (ff, ff_z, ff_dev, width)), scalars,
        [w_gu, w_down, a_down, b_gu], [ANY] * 4,
        [sds((ff_dev, wide_down + ff_dev))] + [sds((quarter, 4 * ff_dev))] * 2,
        [whole_spec((ff_dev, wide_down + ff_dev))] + [whole_spec((quarter, 4 * ff_dev))] * 2,
        scratch=[pltpu.SemaphoreType.DMA((11,))], ties=[first_part],
    )
    down_own = lax.all_gather(down_part, "fsdp", axis=0, tiled=True)
    gu_own_0 = lax.all_gather(gu_part_0, "fsdp", axis=0, tiled=True)
    gu_own_1 = lax.all_gather(gu_part_1, "fsdp", axis=0, tiled=True)

    pieces1 = gather_halves(norm_a, norm_b)
    pieces1_oth = [swap(piece, 1) for piece in pieces1]


    cot_pieces = gather_halves(cot_low[:half], cot_low[half:])
    first_all = hold(first_all, [pieces1_oth[1], pieces1_oth[3], cot_pieces[1], cot_pieces[3]])
    by_z = first_all.reshape(z_count, tall_rows, 3 * span)

    def rows_of(start, count, z, many):
        return by_z[z : z + many, start : start + count].reshape(many * count, 3 * span)

    pieces_small = gather_halves(rows_of(quarter, share + 32, 0, 2), rows_of(quarter, share + 32, 2, 2))
    pieces_small += [swap(piece, 1) for piece in pieces_small]
    ups_qkv = rows_of(quarter + share, 64, 0, 4)
    full_a_qkv, full_a_gu, full_a_out, full_b_out, full_b_down = call(
        functools.partial(unpack_small_kernel, share, quarter), scalars, pieces_small,
        [whole_spec((2 * share + 64, 3 * span))] * 16,
        [sds((width, 3 * latent)), sds((width, 2 * latent)), sds((width, latent))]
        + [sds((latent, width))] * 2,
        [whole_spec((width, 3 * latent)), whole_spec((width, 2 * latent)), whole_spec((width, latent))]
        + [whole_spec((latent, width))] * 2,
    )
    at = quarter + 2 * share
    out_a, out_b = rows_of(at, 3 * share, 0, 2), rows_of(at, 3 * share, 2, 2)
    pieces_out = gather_halves(hold(out_a, [pieces_small[1]]), hold(out_b, [pieces_small[3]]))
    pieces_out += [swap(piece, 1) for piece in pieces_out]
    full_out = call(
        functools.partial(unpack_out_kernel, share, quarter), scalars, pieces_out, [ANY] * 16,
        sds((width, width)), whole_spec((width, width)), scratch=[pltpu.SemaphoreType.DMA((96,))],
    )
    ups_oth = swap(ups_qkv, 1)

    def qkv_up(piece):
        piece = piece.reshape(z_count, 64, 3 * span)
        parts = []
        for k in range(12):
            row, lane = up_slot(k)
            parts.append(piece[:, row : row + 16, lane : lane + LANES])
        return jnp.concatenate(parts, axis=1).transpose(1, 0, 2).reshape(192, z_count * LANES)

    mine, theirs = qkv_up(ups_qkv), qkv_up(ups_oth)
    up_chip = jnp.where(
        core == 0, jnp.concatenate([mine, theirs], axis=0), jnp.concatenate([theirs, mine], axis=0)
    )
    up_own = take(up_chip, core * span, span, 1)
    up_oth = take(up_chip, (1 - core) * span, span, 1)

    all_places = jnp.arange(length, dtype=jnp.int32)
    all_begin, _ = doc_tables(all_places, first, chosen)
    cosine, sine = rope_tables(all_places - all_begin, HEAD_DIM)
    sign = jnp.where(jnp.arange(HEAD_DIM) < HEAD_DIM // 2, -1.0, 1.0)
    turn = sine * sign[None, :]
    rel = jnp.array([r for r, _ in HALVES], jnp.int32)
    part = jnp.array([h for _, h in HALVES], jnp.int32)
    group_places = ((((rel ^ chip) * 2 + core) * 2 + part) * half)[:, None] + jnp.arange(
        half, dtype=jnp.int32
    )
    _, group_which = doc_tables(group_places.reshape(-1), first, chosen)
    adapters_at = jnp.arange(latent, dtype=jnp.int32) // RANK
    group_select = (adapters_at[None, :] == group_which[:, None]).astype(BF)
    select = group_select[-rows:]

    qkv, z_qkv, qkv_own = call(
        qkv_kernel, scalars,
        pieces1 + pieces1_oth + [first_all, full_a_qkv, up_own, cosine, turn],
        [ANY] * 17
        + [
            whole_spec((width, 3 * latent)),
            whole_spec((3 * latent, span)), whole_spec((length, LANES)), whole_spec((length, LANES)),
        ],
        [sds((length, 3 * span)), sds((length, 3 * latent)), sds((width, 3 * span))],
        [whole_spec((length, 3 * span)), whole_spec((length, 3 * latent)), whole_spec((width, 3 * span))],
        scratch=[pltpu.VMEM((length, width), BF), pltpu.SemaphoreType.DMA((20,))],
        cost=(2 * length * width * (3 * span + 3 * latent), 20 * 2**20),
    )
    column = lambda k: pl.BlockSpec((length, LANES), lambda h, _: (0, k * heads_dev + h))
    mixed_h, log_sums = call(
        functools.partial(attend_kernel, rows), scalars, [qkv] * 3, [column(0), column(1), column(2)],
        [sds((length, span)), sds((length, span), F32)], [column(0), column(0)], grid=(heads_dev,),
        cost=(4 * heads_dev * length * length * HEAD_DIM, 8 * 2**20),
    )
    mixed = lax.all_to_all(mixed_h, "seq", split_axis=0, concat_axis=1, tiled=True)
    square = whole_spec((width, width))
    tall = whole_spec((rows, width))
    second, norm_a, norm_b, z_out = call(
        out_kernel, scalars, [mixed, full_out, full_a_out, full_b_out, stream],
        [tall, square, whole_spec((width, latent)), whole_spec((latent, width)), tall],
        [sds((rows, width), F32), sds((half, width)), sds((half, width)), sds((rows, latent))],
        [tall, whole_spec((half, width)), whole_spec((half, width)), whole_spec((rows, latent))],
        scratch=[pltpu.VMEM((rows, width), BF)],
        cost=(2 * rows * width * width, 12 * 2**20),
    )

    pieces2 = gather_halves(norm_a, norm_b)
    down_own = hold(down_own, [second])
    down_oth = swap(down_own, 1)
    gu_own_0 = hold(gu_own_0, [pieces2[1], pieces2[3]])
    gu_oth_0 = swap(gu_own_0, 1)
    step = group // 2

    def feed(chunk, gu_pair, at, onward, kind):
        operands = [group_select, full_a_gu, full_b_down, down_own, down_oth, *gu_pair]
        operands += pieces2[4 * at : 4 * at + 4] + cot_pieces[4 * at : 4 * at + 4]
        specs = [
            pl.BlockSpec((step, latent), lambda *_: (at, 0)), whole_spec((width, 2 * latent)),
            whole_spec((latent, width)),
        ] + [ANY] * 12
        if onward is None:
            shapes, outs = [sds((step, wide_gu), F32)], [whole_spec((step, wide_gu))]
        else:
            operands.append(onward)
            specs.append(ANY)
            shapes, outs = [sds((rows, wide_gu), kind)] * 2, [whole_spec((rows, wide_gu))] * 2
        shapes += [
            sds((step, 4 * ff_dev)), sds((2, 2 * latent, 2 * ff_dev), F32), sds((2, 2 * ff_dev, latent), F32)
        ]
        outs += [
            whole_spec((step, 4 * ff_dev)), whole_spec((2, 2 * latent, 2 * ff_dev)),
            whole_spec((2, 2 * ff_dev, latent)),
        ]
        return call(
            functools.partial(ff_kernel, onward is None, chunk), scalars, operands, specs,
            shapes, outs,
            scratch=[pltpu.VMEM((step, width), BF)] * 2 + [pltpu.VMEM((width, 4 * ff_dev), BF)] * 2
            + [pltpu.VMEM((2 * ff_dev, wide_down + ff_dev), BF)] * 2
            + [pltpu.VMEM((step, wide_gu) if onward is not None else (8, LANES), F32)]
            + [pltpu.SemaphoreType.DMA((13,))],
            cost=(step * 10 * width * ff_dev * 4, 26 * 2**20),
        )

    gu_pair = (gu_own_0, gu_oth_0)
    sums_0, hidden_00, up_grads_00, down_grads_00 = feed(0, gu_pair, 0, None, F32)
    sums_1, hidden_01, up_grads_01, down_grads_01 = feed(0, gu_pair, 1, None, F32)
    gu_own_1 = hold(gu_own_1, [sums_0, sums_1])
    gu_pair = (gu_own_1, swap(gu_own_1, 1))
    send_x, send_y, hidden_10, up_grads_10, down_grads_10 = feed(1, gu_pair, 0, sums_0, BF)
    pass_on, kept, hidden_11, up_grads_11, down_grads_11 = feed(1, gu_pair, 1, sums_1, F32)

    def after(values, ties):
        specs = [whole_spec(value.shape) for value in values]
        return call(
            keep_kernel, scalars, values, specs, [sds(v.shape, v.dtype) for v in values], specs, ties=ties
        )

    once = pl.Buffered(1)

    def down_half(at, hidden_0, hidden_1, kind, ties):
        row = pl.BlockSpec((rows, 4 * ff_dev), lambda i, _: (i, 0))
        weight = pl.BlockSpec(
            (z_count * ff_dev, wide_down + ff_dev), lambda i, _: (0, 0), pipeline_mode=once
        )
        return call(
            down_kernel, scalars, [hidden_0, hidden_1, down_own, down_oth], [row, row, weight, weight],
            [sds((rows, wide_down), kind)] * 2, [whole_spec((rows, wide_down))] * 2, grid=(2,),
            cost=(2 * step * 8 * ff_dev * width, 16 * 2**20), ties=ties,
        )

    ff_rows = 2 * latent * (ff_dev // LANES) + ff_dev
    ups = [up_grads_00, up_grads_01, up_grads_10, up_grads_11]
    downs = [down_grads_00, down_grads_01, down_grads_10, down_grads_11]
    ff_keep, ff_send = call(
        ff_grads_kernel, scalars, ups + downs,
        [whole_spec(ups[0].shape)] * 4 + [whole_spec(downs[0].shape)] * 4,
        [sds((z_count, ff_rows, LANES), F32), sds((z_count, ff_rows, LANES))],
        [whole_spec((z_count, ff_rows, LANES))] * 2, cost=(2**20, 12 * 2**20),
    )
    by_x, by_y, got_y, got_x, _ = scatter_rest(send_x, send_y, pass_on)
    down_x, down_y = down_half(0, hidden_00, hidden_10, BF, [by_x, by_y])
    halfspec = lambda n: pl.BlockSpec((half, n), lambda *_: (0, 0))
    second_grad, dz_gu, dz_out, mixed_grad, *up_out = call(
        back_middle_kernel, scalars,
        [kept, by_x, by_y, got_y, got_x, second, cot_low, full_a_gu, full_out, full_a_out, full_b_out, z_out],
        [whole_spec((rows, wide_gu))] + [halfspec(wide_gu)] * 4
        + [
            tall, tall, whole_spec((width, 2 * latent)), square, whole_spec((width, latent)),
            whole_spec((latent, width)), whole_spec((rows, latent)),
        ],
        [
            sds((rows, width), F32), sds((rows, 2 * latent)), sds((rows, latent)), sds((rows, width)),
            sds((2 * share_b, width), F32),
        ]
        + [sds((2 * share_b, width))] * 3,
        [tall, whole_spec((rows, 2 * latent)), whole_spec((rows, latent)), tall]
        + [whole_spec((2 * share_b, width))] * 4,
        cost=(2 * rows * width * width, 16 * 2**20), ties=[down_x, ff_send],
    )
    mixed_grad_h = lax.all_to_all(mixed_grad, "seq", split_axis=1, concat_axis=0, tiled=True)
    down_on, down_kept = down_half(1, hidden_01, hidden_11, F32, [mixed_grad])

    def along_line(keep, send, ties):
        shape = keep.shape[1:]
        brought = swap(send, 1)
        mine, *sends = call(
            along_line_kernel, scalars, [keep, brought], [whole_spec(keep.shape)] * 2,
            [sds(shape, F32)] + [sds(shape)] * 6, [whole_spec(shape)] * 7, ties=ties,
            cost=(2**20, 8 * 2**20),
        )
        return mine, sends

    def line_sum(mine, sends, ties):
        total = hold(mine, ties) if ties else mine
        for k, value in enumerate(sends):
            hop = k // 2 + 1
            if k % 2 == 0:
                perm = [(i, i + hop) for i in range(z_count - hop)]
            else:
                perm = [(i + hop, i) for i in range(z_count - hop)]
            total = total + lax.ppermute(value, "fsdp", perm).astype(F32)
        return total.astype(BF)

    def spread(mine, places, shapes, ties):
        plane = blocks_of(mine)
        plane += [swap(piece, 1) for piece in plane]
        return call(
            functools.partial(spread_kernel, places), scalars, plane, [whole_spec(mine.shape)] * 8,
            [sds(shape, F32) for shape in shapes], [whole_spec(shape) for shape in shapes], ties=ties,
        )

    *down_by, down_passed = scatter_rest(down_x, down_y, down_on)
    dz_gu, dz_out, *up_out = after([dz_gu, dz_out] + up_out, [mixed_grad_h])
    all_dz_gu = blocks_of(dz_gu)
    all_dz_out = blocks_of(jnp.stack([dz_out, swap(dz_out, 1)]))
    all_up_out = [up_out[0], swap(up_out[1], 2), swap(up_out[2], 4), swap(up_out[3], 6)]

    result = pl.BlockSpec((3, group, HEAD_DIM), lambda h, _: (0, 0, h))
    grads_a, grads_b, up_qkv = call(
        functools.partial(attend_back_kernel, rows), scalars,
        [qkv, qkv, qkv, mixed_grad_h, log_sums, z_qkv, cosine, turn],
        [column(0), column(1), column(2), column(0), column(0), whole_spec((length, 3 * latent))]
        + [whole_spec((length, LANES))] * 2,
        [sds((3, group, span))] * 2 + [sds((3, latent, span), F32)],
        [result, result, pl.BlockSpec((3, latent, HEAD_DIM), lambda h, _: (0, 0, h))],
        scratch=[pltpu.VMEM((length, HEAD_DIM), F32)] * 3, grid=(heads_dev,),
        cost=(10 * heads_dev * length * length * HEAD_DIM, 16 * 2**20), ties=down_passed,
    )
    grads_b = swap(grads_b, 1)
    qkv_oth = swap(qkv_own, 1)

    down_kept = hold(down_kept, [grads_a])
    upper = down_kept[:half] + down_by[0][:half].astype(F32) + down_by[2].astype(F32)
    lower = down_kept[half:] + down_by[1][:half].astype(F32) + down_by[3].astype(F32)
    wide = jnp.concatenate([upper, lower], axis=0)
    z_down = wide[:, width:].astype(BF) * select
    all_z_down = blocks_of(z_down)
    to_x, to_y, to_far, latent_kept = call(
        back_latent_kernel, scalars, [grads_a, grads_b, up_own, up_oth],
        [whole_spec((3, group, span))] * 2 + [whole_spec((3 * latent, span))] * 2,
        [sds((rows, 3 * latent))] * 3 + [sds((rows, 3 * latent), F32)],
        [whole_spec((rows, 3 * latent))] * 4,
        cost=(4 * group * span * 3 * latent, 4 * 2**20),
    )

    def back_qkv(at, kind, ties):
        part = pl.BlockSpec((3, step, span), lambda *_: (0, at, 0))
        return call(
            back_qkv_kernel, scalars, [grads_a, grads_b, qkv_own, qkv_oth],
            [part, part] + [whole_spec((width, 3 * span))] * 2,
            [sds((rows, width), kind)] * 2, [tall] * 2,
            cost=(2 * group * span * 3 * width, 12 * 2**20), ties=ties,
        )

    send_x, send_y = back_qkv(0, BF, [to_x])
    pass_on, kept = back_qkv(1, F32, [send_x])
    by_x, by_y, got_y, got_x, passed = scatter_rest(send_x, send_y, pass_on)
    latent_kept = hold(latent_kept, passed)
    dz_qkv = latent_kept + swap(to_x, 2).astype(F32) + swap(to_y, 4).astype(F32)
    dz_qkv = (dz_qkv + swap(to_far, 6).astype(F32)) * jnp.tile(select, (1, 3)).astype(F32)
    dz_qkv = dz_qkv.astype(BF)
    ff_mine, ff_sends = along_line(ff_keep, ff_send, [kept])
    ff_total = line_sum(ff_mine, ff_sends, passed)
    other_rows = 11 * LANES // 2
    block = lambda n: [whole_spec((rows, n))] * 4
    keep, send = call(
        functools.partial(other_grads_kernel, quarter), scalars,
        [*pieces1, *pieces2, *cot_pieces, mixed_h, *all_dz_gu, *blocks_of(dz_qkv), *all_z_down, *all_dz_out,
         *all_up_out, up_qkv],
        [ANY] * 24 + [whole_spec((length, span))] + block(2 * latent) + block(3 * latent) + block(latent)
        + [whole_spec((2, rows, latent))] * 4 + [whole_spec((2 * share_b, width))] * 4
        + [whole_spec((3, latent, span))],
        [sds((z_count, other_rows, LANES), F32), sds((z_count, other_rows, LANES))],
        [whole_spec((z_count, other_rows, LANES))] * 2,
        scratch=[
            pltpu.VMEM((3, group, z_count * LANES), BF), pltpu.VMEM((group, 2 * latent), BF),
            pltpu.VMEM((group, 3 * latent), BF), pltpu.VMEM((group, latent), BF),
            pltpu.SemaphoreType.DMA((96,)),
        ],
        cost=(2 * group * 512 * 768, 8 * 2**20), ties=passed,
    )

    g_b_gu, g_a_down = spread(
        ff_total, (("columns", 2 * latent, ff_dev // LANES), ("rows", ff_dev, 1)),
        [(2 * latent, ff_z), (ff_z, latent)], passed,
    )

    input_grad = call(
        back_first_kernel, scalars,
        [kept, by_x, by_y, got_y, got_x, stream, second_grad, dz_qkv, full_a_qkv],
        [tall] + [halfspec(width)] * 4
        + [tall, tall, whole_spec((rows, 3 * latent)), whole_spec((width, 3 * latent))],
        sds((rows, width), F32), tall,
        cost=(2 * rows * width * 3 * latent, 12 * 2**20),
    )
    activations = second + (wide[:, :width] + dot(hold(z_down, passed), full_b_down))
    mine, sends = along_line(keep, send, [input_grad])
    low = LANES // 2
    g_a_gu, g_b_down, g_a_out, g_b_out, g_a_qkv, g_b_qkv = spread(
        line_sum(mine, sends, []),
        (
            ("rows", low, 2), ("both", low, 1), ("rows", low, 1), ("core rows", share_b, z_count),
            ("rows", low, 3), ("both", 3 * low, 1),
        ),
        [
            (quarter, 2 * latent), (latent, quarter), (quarter, latent), (latent, quarter),
            (quarter, 3 * latent), (3 * latent, quarter),
        ],
        [],
    )

    return (
        activations[None], input_grad[None],
        g_a_qkv, g_b_qkv, g_a_out, g_b_out, g_a_gu, g_b_gu, g_a_down, g_b_down,
    )


def solution(mesh):
    placed = (
        P("fsdp", "seq", None),
        P("fsdp", "seq", None),
        P("fsdp", None),
        P("fsdp", None),
        P("fsdp", None),
        P("fsdp", None),
        P("fsdp", None),
        P("fsdp", None),
        P("fsdp", None),
        P(None, "fsdp"),
        P("fsdp", None),
        P(None, "fsdp"),
        P("fsdp", None),
        P(None, "fsdp"),
        P("fsdp", None),
        P(None, "fsdp"),
    )
    on_plane = mesh.shape["seq"] == PLANE and mesh.shape["fsdp"] == 4
    return jax.shard_map(
        plane_shards if on_plane else shards,
        mesh=mesh,
        in_specs=placed,
        out_specs=(
            P("fsdp", "seq", None),
            P("fsdp", "seq", None),
            P("fsdp", None),
            P(None, "fsdp"),
            P("fsdp", None),
            P(None, "fsdp"),
            P("fsdp", None),
            P(None, "fsdp"),
            P("fsdp", None),
            P(None, "fsdp"),
        ),
        check_vma=False,
    )
```

```python
import functools

import jax
import jax.numpy as jnp
from jax import lax
from jax.experimental import pallas as pl
from jax.experimental.pallas import tpu as pltpu
from jax.sharding import PartitionSpec as P

HEAD_DIM = 128
RANK = 16


def layer_norm(values):
    centre = values - jnp.mean(values, axis=-1, keepdims=True)
    spread = jnp.mean(centre * centre, axis=-1, keepdims=True)
    factor = lax.rsqrt(spread + 1e-05)
    return (centre * factor, factor)


def norm_back(normed, factor, upstream):
    upstream_mean = jnp.mean(upstream, axis=-1, keepdims=True)
    cross_mean = jnp.mean(upstream * normed, axis=-1, keepdims=True)
    return factor * (upstream - upstream_mean - normed * cross_mean)


def doc_tables(places, first, chosen):
    within = first[None, :] <= places[:, None]
    begin = jnp.max(jnp.where(within, first[None, :], 0), axis=1)
    latest = jnp.sum(within.astype(jnp.int32), axis=1) - 1
    doc_order = jnp.arange(first.shape[0], dtype=jnp.int32)
    which = jnp.sum(jnp.where(doc_order[None, :] == latest[:, None], chosen[None, :], 0), axis=1)
    return (begin, which)


def rope_tables(position, head_dim):
    freqs = 10000.0 ** (-(jnp.arange(0, head_dim, 2, dtype=jnp.float32) / head_dim))
    angles = position.astype(jnp.float32)[:, None] * freqs[None, :]
    cosine = jnp.concatenate([jnp.cos(angles), jnp.cos(angles)], axis=-1)
    sine = jnp.concatenate([jnp.sin(angles), jnp.sin(angles)], axis=-1)
    return (cosine, sine)


def rotate(values, cosine, sine):
    half_dim = values.shape[-1] // 2
    turned = jnp.concatenate([-values[..., half_dim:], values[..., :half_dim]], axis=-1)
    return values * cosine[:, None, :] + turned * sine[:, None, :]


def rotate_back(upstream, cosine, sine):
    half_dim = upstream.shape[-1] // 2
    scaled = upstream * sine[:, None, :]
    return upstream * cosine[:, None, :] + jnp.concatenate(
        [scaled[..., half_dim:], -scaled[..., :half_dim]], axis=-1
    )


def inner_rows(left, right):
    return lax.dot_general(
        left, right, (((0,), (0,)), ((), ())), preferred_element_type=jnp.float32
    )


def inner_cols(left, right):
    return lax.dot_general(
        left, right, (((1,), (1,)), ((), ())), preferred_element_type=jnp.float32
    )


def adapter_fwd(inputs, down, up, select, segments):
    latent = jnp.dot(inputs, down, preferred_element_type=jnp.float32).astype(
        jnp.bfloat16
    ) * jnp.tile(select, (1, segments))
    span = up.shape[0] // segments
    pieces = [
        jnp.dot(
            latent[:, seg * span : (seg + 1) * span],
            up[seg * span : (seg + 1) * span],
            preferred_element_type=jnp.float32,
        )
        for seg in range(segments)
    ]
    return (latent, jnp.concatenate(pieces, axis=1))


def adapter_back(inputs, latent, upstream, down, up, select, segments):
    span = up.shape[0] // segments
    out_span = up.shape[1]
    grad_up = jnp.concatenate(
        [
            inner_rows(
                latent[:, seg * span : (seg + 1) * span],
                upstream[:, seg * out_span : (seg + 1) * out_span],
            )
            for seg in range(segments)
        ],
        axis=0,
    )
    latent_grad = jnp.concatenate(
        [
            inner_cols(
                upstream[:, seg * out_span : (seg + 1) * out_span],
                up[seg * span : (seg + 1) * span],
            )
            for seg in range(segments)
        ],
        axis=1,
    )
    latent_grad = (latent_grad * jnp.tile(select, (1, segments)).astype(jnp.float32)).astype(
        jnp.bfloat16
    )
    grad_down = inner_rows(inputs, latent_grad)
    back = inner_cols(latent_grad, down)
    return (grad_down, grad_up, back)


def frozen_fwd(inputs, weight):
    return (
        jnp.dot(
            inputs,
            lax.all_gather(weight, "fsdp", axis=0, tiled=True),
            preferred_element_type=jnp.float32,
        ),
        weight,
    )


def frozen_bwd(upstream, weight):
    return inner_cols(upstream, lax.all_gather(weight, "fsdp", axis=0, tiled=True))


def attend(query_h, key_h, value_h, begin, head_dim):
    length, local_width = query_h.shape
    local_heads = local_width // head_dim
    block_rows = min(512, length)
    block_count = length // block_rows
    score_scale = head_dim ** (-0.5)
    query_all = query_h.reshape(length, local_heads, head_dim)
    key_all = key_h.reshape(length, local_heads, head_dim)
    value_all = value_h.reshape(length, local_heads, head_dim)
    key_places = jnp.arange(length, dtype=jnp.int32)

    def one_block(block_index):
        start = block_index * block_rows
        query_block = lax.dynamic_slice_in_dim(query_all, start, block_rows, 0)
        rows = start + jnp.arange(block_rows, dtype=jnp.int32)
        row_begin = lax.dynamic_slice_in_dim(begin, start, block_rows, 0)
        allowed = (key_places[None, :] <= rows[:, None]) & (
            key_places[None, :] >= row_begin[:, None]
        )
        scores = (
            jnp.einsum("qhd,khd->hqk", query_block, key_all, preferred_element_type=jnp.float32)
            * score_scale
        )
        scores = jnp.where(allowed[None], scores, -1e30)
        row_top = jnp.max(scores, axis=-1, keepdims=True)
        expd = jnp.exp(scores - row_top)
        row_total = jnp.sum(expd, axis=-1, keepdims=True)
        probs = (expd / row_total).astype(jnp.bfloat16)
        mixed = jnp.einsum("hqk,khd->qhd", probs, value_all, preferred_element_type=jnp.float32)
        return (
            mixed.astype(jnp.bfloat16).reshape(block_rows, local_width),
            (row_top + jnp.log(row_total))[..., 0],
        )

    outputs, log_sums = lax.map(one_block, jnp.arange(block_count, dtype=jnp.int32))
    return (outputs.reshape(length, local_width), log_sums)


def attend_back(query_h, key_h, value_h, grad_h, log_sums, begin, head_dim):
    length, local_width = query_h.shape
    local_heads = local_width // head_dim
    block_rows = min(512, length)
    block_count = length // block_rows
    score_scale = head_dim ** (-0.5)
    query_all = query_h.reshape(length, local_heads, head_dim)
    key_all = key_h.reshape(length, local_heads, head_dim)
    value_all = value_h.reshape(length, local_heads, head_dim)
    grad_all = grad_h.reshape(length, local_heads, head_dim)
    key_places = jnp.arange(length, dtype=jnp.int32)

    def step(carry, inputs):
        key_grad, value_grad = carry
        block_index, block_lse = inputs
        start = block_index * block_rows
        query_block = lax.dynamic_slice_in_dim(query_all, start, block_rows, 0)
        grad_block = lax.dynamic_slice_in_dim(grad_all, start, block_rows, 0)
        rows = start + jnp.arange(block_rows, dtype=jnp.int32)
        row_begin = lax.dynamic_slice_in_dim(begin, start, block_rows, 0)
        allowed = (key_places[None, :] <= rows[:, None]) & (
            key_places[None, :] >= row_begin[:, None]
        )
        scores = (
            jnp.einsum("qhd,khd->hqk", query_block, key_all, preferred_element_type=jnp.float32)
            * score_scale
        )
        probs = jnp.where(allowed[None], jnp.exp(scores - block_lse[..., None]), 0.0)
        probs_low = probs.astype(jnp.bfloat16)
        prob_grad = jnp.einsum(
            "qhd,khd->hqk", grad_block, value_all, preferred_element_type=jnp.float32
        )
        row_delta = jnp.sum(prob_grad * probs, axis=-1, keepdims=True)
        score_grad = (probs * (prob_grad - row_delta)).astype(jnp.bfloat16)
        query_grad = (
            jnp.einsum("hqk,khd->qhd", score_grad, key_all, preferred_element_type=jnp.float32)
            * score_scale
        )
        key_grad = (
            key_grad
            + jnp.einsum(
                "hqk,qhd->khd", score_grad, query_block, preferred_element_type=jnp.float32
            )
            * score_scale
        )
        value_grad = value_grad + jnp.einsum(
            "hqk,qhd->khd", probs_low, grad_block, preferred_element_type=jnp.float32
        )
        return (
            (key_grad, value_grad),
            query_grad.astype(jnp.bfloat16).reshape(block_rows, local_width),
        )

    empty = jnp.zeros((length, local_heads, head_dim), jnp.float32)
    (key_grad, value_grad), query_grad = lax.scan(
        step, (empty, empty), (jnp.arange(block_count, dtype=jnp.int32), log_sums)
    )
    return (
        query_grad.reshape(length, local_width),
        key_grad.astype(jnp.bfloat16).reshape(length, local_width),
        value_grad.astype(jnp.bfloat16).reshape(length, local_width),
    )


def shards(
    tokens,
    cotangent,
    starts,
    adapter_ids,
    w_qkv,
    w_out,
    w_gu,
    w_down,
    a_qkv,
    b_qkv,
    a_out,
    b_out,
    a_gu,
    b_gu,
    a_down,
    b_down,
):
    gathered = (
        lax.all_gather(a_qkv, "fsdp", axis=0, tiled=True),
        lax.all_gather(b_qkv, "fsdp", axis=1, tiled=True),
        lax.all_gather(a_out, "fsdp", axis=0, tiled=True),
        lax.all_gather(b_out, "fsdp", axis=1, tiled=True),
        lax.all_gather(a_gu, "fsdp", axis=0, tiled=True),
        lax.all_gather(b_gu, "fsdp", axis=1, tiled=True),
        lax.all_gather(a_down, "fsdp", axis=0, tiled=True),
        lax.all_gather(b_down, "fsdp", axis=1, tiled=True),
    )
    (
        full_a_qkv,
        full_b_qkv,
        full_a_out,
        full_b_out,
        full_a_gu,
        full_b_gu,
        full_a_down,
        full_b_down,
    ) = gathered
    stream = tokens[0].astype(jnp.float32)
    cot_low = cotangent[0]
    tok_count, width = stream.shape
    seq_count = lax.axis_size("seq")
    seq_place = lax.axis_index("seq")
    stream_len = tok_count * seq_count
    first = starts[0]
    chosen = adapter_ids[0]
    local_places = seq_place * tok_count + jnp.arange(tok_count, dtype=jnp.int32)
    local_begin, which = doc_tables(local_places, first, chosen)
    columns = jnp.arange(full_a_out.shape[1], dtype=jnp.int32) // RANK
    select = (columns[None, :] == which[:, None]).astype(jnp.bfloat16)
    cosine, sine = rope_tables(local_places - local_begin, HEAD_DIM)
    head_count = width // HEAD_DIM
    first_norm, first_factor = layer_norm(stream)
    first_low = first_norm.astype(jnp.bfloat16)
    latent_qkv, extra_qkv = adapter_fwd(first_low, full_a_qkv, full_b_qkv, select, 3)
    qkv_main, held_qkv = frozen_fwd(first_low, w_qkv)
    qkv = qkv_main + extra_qkv
    query_rot = (
        rotate(qkv[:, :width].reshape(tok_count, head_count, HEAD_DIM), cosine, sine)
        .reshape(tok_count, width)
        .astype(jnp.bfloat16)
    )
    key_rot = (
        rotate(qkv[:, width : 2 * width].reshape(tok_count, head_count, HEAD_DIM), cosine, sine)
        .reshape(tok_count, width)
        .astype(jnp.bfloat16)
    )
    value_low = qkv[:, 2 * width :].astype(jnp.bfloat16)
    query_h, key_h, value_h = (
        lax.all_to_all(query_rot, "seq", split_axis=1, concat_axis=0, tiled=True),
        lax.all_to_all(key_rot, "seq", split_axis=1, concat_axis=0, tiled=True),
        lax.all_to_all(value_low, "seq", split_axis=1, concat_axis=0, tiled=True),
    )
    all_begin, all_which = doc_tables(jnp.arange(stream_len, dtype=jnp.int32), first, chosen)
    mixed_h, log_sums = attend(query_h, key_h, value_h, all_begin, HEAD_DIM)
    mixed = lax.all_to_all(mixed_h, "seq", split_axis=0, concat_axis=1, tiled=True)
    latent_out, extra_out = adapter_fwd(mixed, full_a_out, full_b_out, select, 1)
    out_main, held_out = frozen_fwd(mixed, w_out)
    second = stream + (out_main + extra_out)
    second_norm, second_factor = layer_norm(second)
    second_low = second_norm.astype(jnp.bfloat16)
    latent_gu, extra_gu = adapter_fwd(second_low, full_a_gu, full_b_gu, select, 2)
    gu_main, held_gu = frozen_fwd(second_low, w_gu)
    gate_up = gu_main + extra_gu
    ff_width = gate_up.shape[1] // 2
    gate = gate_up[:, :ff_width]
    upper = gate_up[:, ff_width:]
    sigma = jax.nn.sigmoid(gate)
    active = gate * sigma
    hidden = (active * upper).astype(jnp.bfloat16)
    latent_down, extra_down = adapter_fwd(hidden, full_a_down, full_b_down, select, 1)
    down_main, held_down = frozen_fwd(hidden, w_down)
    activations = second + (down_main + extra_down)
    grad_a_down, grad_b_down, hidden_extra = adapter_back(
        hidden, latent_down, cot_low, full_a_down, full_b_down, select, 1
    )
    hidden_grad = frozen_bwd(cot_low, held_down) + hidden_extra
    gate_grad = (hidden_grad * upper * sigma * (1.0 + gate * (1.0 - sigma))).astype(jnp.bfloat16)
    upper_grad = (hidden_grad * active).astype(jnp.bfloat16)
    gate_up_grad = jnp.concatenate([gate_grad, upper_grad], axis=1)
    grad_a_gu, grad_b_gu, second_extra = adapter_back(
        second_low, latent_gu, gate_up_grad, full_a_gu, full_b_gu, select, 2
    )
    second_norm_grad = frozen_bwd(gate_up_grad, held_gu) + second_extra
    second_grad = cot_low.astype(jnp.float32) + norm_back(
        second_norm, second_factor, second_norm_grad
    )
    branch_grad = second_grad.astype(jnp.bfloat16)
    grad_a_out, grad_b_out, mixed_extra = adapter_back(
        mixed, latent_out, branch_grad, full_a_out, full_b_out, select, 1
    )
    mixed_grad = (frozen_bwd(branch_grad, held_out) + mixed_extra).astype(jnp.bfloat16)
    mixed_grad_h = lax.all_to_all(mixed_grad, "seq", split_axis=1, concat_axis=0, tiled=True)
    query_grad_h, key_grad_h, value_grad_h = attend_back(
        query_h, key_h, value_h, mixed_grad_h, log_sums, all_begin, HEAD_DIM
    )
    query_grad, key_grad, value_grad = (
        lax.all_to_all(query_grad_h, "seq", split_axis=0, concat_axis=1, tiled=True),
        lax.all_to_all(key_grad_h, "seq", split_axis=0, concat_axis=1, tiled=True),
        lax.all_to_all(value_grad_h, "seq", split_axis=0, concat_axis=1, tiled=True),
    )
    query_pre = (
        rotate_back(
            query_grad.astype(jnp.float32).reshape(tok_count, head_count, HEAD_DIM), cosine, sine
        )
        .reshape(tok_count, width)
        .astype(jnp.bfloat16)
    )
    key_pre = (
        rotate_back(
            key_grad.astype(jnp.float32).reshape(tok_count, head_count, HEAD_DIM), cosine, sine
        )
        .reshape(tok_count, width)
        .astype(jnp.bfloat16)
    )
    qkv_grad = jnp.concatenate([query_pre, key_pre, value_grad], axis=1)
    grad_a_qkv, grad_b_qkv, first_extra = adapter_back(
        first_low, latent_qkv, qkv_grad, full_a_qkv, full_b_qkv, select, 3
    )
    first_norm_grad = frozen_bwd(qkv_grad, held_qkv) + first_extra
    input_grad = second_grad + norm_back(first_norm, first_factor, first_norm_grad)
    grads = (
        grad_a_qkv,
        grad_b_qkv,
        grad_a_out,
        grad_b_out,
        grad_a_gu,
        grad_b_gu,
        grad_a_down,
        grad_b_down,
    )
    shard_dims = (0, 1, 0, 1, 0, 1, 0, 1)
    summed = lax.psum(
        (grads[0], grads[1], grads[2], grads[3], grads[4], grads[5], grads[6], grads[7]),
        ("seq", "fsdp"),
    )
    fsdp_place = lax.axis_index("fsdp")
    fsdp_count = lax.axis_size("fsdp")
    totals = tuple(
        (
            lax.dynamic_slice_in_dim(
                whole,
                fsdp_place * (whole.shape[along] // fsdp_count),
                whole.shape[along] // fsdp_count,
                along,
            )
            for whole, along in zip(summed, shard_dims)
        )
    )
    return (
        activations[None],
        input_grad[None],
        totals[0],
        totals[1],
        totals[2],
        totals[3],
        totals[4],
        totals[5],
        totals[6],
        totals[7],
    )


BF = jnp.bfloat16
F32 = jnp.float32
PLANE = 8
CHIPS = 4
LANES = 128
CHUNKS = ((0, 1), (2, 3))
HALVES = ((1, 0), (3, 0), (2, 1), (3, 1), (2, 0), (1, 1), (0, 0), (0, 1))
ANY = pl.BlockSpec(memory_space=pl.ANY)
ROOMY = 60 * 2**20


def swap(value, bits):
    return lax.ppermute(value, "seq", [(i, i ^ bits) for i in range(PLANE)])


def gather_halves(first, second):
    x_first, y_second = swap(first, 2), swap(second, 4)
    y_first, x_second = swap(first, 4), swap(second, 2)
    far_first, far_second = swap(y_first, 2), swap(x_second, 4)
    return [x_first, far_first, y_second, far_second, y_first, x_second, first, second]


def blocks_of(block):
    return [block, swap(block, 2), swap(block, 4), swap(block, 6)]


def dot(left, right):
    return jnp.dot(left, right, preferred_element_type=F32)


def inner(left, right, on_left, on_right):
    return lax.dot_general(
        left, right, (((on_left,), (on_right,)), ((), ())), preferred_element_type=F32
    )


def take(value, start, count, axis):
    return lax.dynamic_slice_in_dim(value, start, count, axis)


def whole_spec(shape):
    return pl.BlockSpec(shape, lambda *_: (0,) * len(shape))


def call(body, scalars, operands, specs, shapes, out_specs, scratch=(), grid=(1,), cost=None, ties=()):
    count = len(operands)

    def run(*refs):
        inside = refs[: 1 + count] + refs[1 + count + len(ties) :]
        body(*inside)

    return pl.pallas_call(
        run,
        grid_spec=pltpu.PrefetchScalarGridSpec(
            num_scalar_prefetch=1,
            grid=grid,
            in_specs=list(specs) + [ANY] * len(ties),
            out_specs=out_specs,
            scratch_shapes=list(scratch),
        ),
        out_shape=shapes,
        compiler_params=pltpu.CompilerParams(vmem_limit_bytes=ROOMY),
        cost_estimate=None
        if cost is None
        else pl.CostEstimate(flops=cost[0], bytes_accessed=cost[1], transcendentals=0),
    )(scalars, *operands, *ties)


def hold(value, ties):
    return pl.pallas_call(
        lambda *refs: None,
        in_specs=[ANY] * (1 + len(ties)),
        out_specs=ANY,
        out_shape=sds(value.shape, value.dtype),
        input_output_aliases={0: 0},
    )(value, *ties)


def copies(pairs, sems):
    started = [
        pltpu.make_async_copy(source, target, sems.at[k]) for k, (source, target) in enumerate(pairs)
    ]
    for one in started:
        one.start()
    for one in started:
        one.wait()


def sds(shape, dtype=BF):
    return jax.ShapeDtypeStruct(shape, dtype)


def doc_begin(scalars, places):
    begin = jnp.zeros_like(places)
    for doc in range(4):
        begin = jnp.where(scalars[3 + doc] <= places, scalars[3 + doc], begin)
    return begin


def adapter_mask(scalars, places):
    which = jnp.zeros_like(places) + scalars[7]
    for doc in range(1, 4):
        which = jnp.where(scalars[3 + doc] <= places, scalars[7 + doc], which)
    column = lax.broadcasted_iota(jnp.int32, (1, LANES), 1) // RANK
    return (column == which).astype(F32)


def rows_from(first, count):
    return first + lax.broadcasted_iota(jnp.int32, (count, 1), 0)


def normed(values):
    centre = values - jnp.mean(values, axis=-1, keepdims=True)
    factor = lax.rsqrt(jnp.mean(centre * centre, axis=-1, keepdims=True) + 1e-05)
    return centre * factor, factor


def cut_first_kernel(sizes, scalars, w_qkv, w_out, a_qkv, a_out, a_gu, b_out, b_down, b_qkv, out, sems):
    share, quarter, width = sizes
    chip, core = scalars[0], scalars[1]
    seat = chip * 2 + core
    pairs = []
    for part in range(3):
        for i in range(2):
            column = pl.multiple_of(part * width + (2 * core + i) * quarter + chip * LANES, LANES)
            k = part * 2 + i
            pairs.append(
                (w_qkv.at[:, pl.ds(column, LANES)], out.at[:quarter, k * LANES : (k + 1) * LANES])
            )
    rows = pl.ds(pl.multiple_of(seat * share, share), share)
    small = slice(quarter, quarter + share)
    pairs.append((a_qkv.at[rows], out.at[small, :384]))
    pairs.append((a_gu.at[rows], out.at[small, 384:640]))
    pairs.append((a_out.at[rows], out.at[small, 640:768]))
    low = pl.ds(pl.multiple_of(seat * 16, 16), 16)
    at = quarter + share
    pairs.append((b_out.at[low], out.at[at : at + 16, :512]))
    pairs.append((b_down.at[low], out.at[at + 16 : at + 32, :512]))
    column = pl.ds(pl.multiple_of(chip * LANES, LANES), LANES)
    for k in range(12):
        here = pl.ds(pl.multiple_of(core * 192 + k * 16, 16), 16)
        row, lane = up_slot(k)
        row += at
        pairs.append((b_qkv.at[here, column], out.at[row : row + 16, lane : lane + LANES]))
    at += 64
    for k in range(16):
        row, lane = at + (k // 6) * share, (k % 6) * LANES
        pairs.append(
            (w_out.at[rows, k * LANES : (k + 1) * LANES], out.at[row : row + share, lane : lane + LANES])
        )
    copies(pairs, sems)


def up_slot(k):
    if k < 4:
        return (k // 2) * 16, 512 + (k % 2) * LANES
    return 32 + ((k - 4) // 4) * 16, ((k - 4) % 4) * LANES


def cut_rest_kernel(sizes, scalars, w_gu, w_down, a_down, b_gu, down, *refs):
    ff, ff_z, ff_dev, width = sizes
    parts, sems = refs[:-1], refs[-1]
    seat = scalars[0] * 2 + scalars[1]
    rows = pl.ds(pl.multiple_of(seat * ff_dev, ff_dev), ff_dev)
    wide = width + LANES
    pairs = [
        (w_down.at[rows], down.at[:, :width]),
        (a_down.at[rows], down.at[:, width:wide]),
        (b_gu.at[:, rows], down.at[:, wide : wide + ff_dev]),
    ]
    for zs, gu in zip(CHUNKS, parts):
        for half in range(2):
            for i, z in enumerate(zs):
                column = pl.multiple_of(half * ff + z * ff_z + seat * ff_dev, ff_dev)
                k = half * len(zs) + i
                pairs.append(
                    (w_gu.at[:, pl.ds(column, ff_dev)], gu.at[:, k * ff_dev : (k + 1) * ff_dev])
                )
    copies(pairs, sems)


def unpack_small_kernel(share, quarter, scalars, *refs):
    pieces = refs[:16]
    a_qkv, a_gu, a_out, b_out, b_down = refs[16:]
    chip, core = scalars[0], scalars[1]
    for k in range(2):
        for at, (rel, half) in enumerate(HALVES):
            piece = pieces[8 * k + at]
            tall = piece.shape[0] // 2
            seat = (chip ^ rel) * 2 + (core if k == 0 else 1 - core)
            for i in range(2):
                z = half * 2 + i
                rows = slice(i * tall, i * tall + share)
                there = pl.ds(pl.multiple_of(z * quarter + seat * share, share), share)
                a_qkv[there, :] = piece[rows, :384]
                a_gu[there, :] = piece[rows, 384:640]
                a_out[there, :] = piece[rows, 640:768]
                there = pl.ds(pl.multiple_of(seat * 16, 16), 16)
                columns = slice(z * quarter, (z + 1) * quarter)
                row = i * tall + share
                b_out[there, columns] = piece[row : row + 16, :512]
                b_down[there, columns] = piece[row + 16 : row + 32, :512]


def unpack_out_kernel(share, quarter, scalars, *refs):
    pieces, out, sems = refs[:16], refs[16], refs[17]
    chip, core = scalars[0], scalars[1]
    pairs = []
    for k in range(2):
        for at, (rel, half) in enumerate(HALVES):
            seat = (chip ^ rel) * 2 + (core if k == 0 else 1 - core)
            for i in range(2):
                there = pl.ds(pl.multiple_of((half * 2 + i) * quarter + seat * share, share), share)
                for block in range(3):
                    row = (i * 3 + block) * share
                    lanes = min(768, out.shape[1] - block * 768)
                    pairs.append(
                        (
                            pieces[8 * k + at].at[row : row + share, :lanes],
                            out.at[there, block * 768 : block * 768 + lanes],
                        )
                    )
    copies(pairs, sems)


def norm_kernel(scalars, tokens, first, second):
    value, _ = normed(tokens[...].astype(F32))
    half = first.shape[0]
    first[...] = value[:half].astype(BF)
    second[...] = value[half:].astype(BF)


def qkv_kernel(scalars, *refs):
    pieces, gathered = refs[:16], refs[16]
    down, up, cosine, sine, out, latents, weight, rows_all, sems = refs[17:]
    chip, core = scalars[0], scalars[1]
    half = pieces[0].shape[0]
    quarter = weight.shape[0] // 4
    tall = gathered.shape[0] // 4
    pairs = [
        (gathered.at[pl.ds(z * tall, quarter)], weight.at[pl.ds(z * quarter, quarter)]) for z in range(4)
    ]
    for k in range(2):
        for at, (rel, part) in enumerate(HALVES):
            seat = (chip ^ rel) * 2 + (core if k == 0 else 1 - core)
            there = pl.ds(pl.multiple_of((seat * 2 + part) * half, half), half)
            pairs.append((pieces[8 * k + at], rows_all.at[there]))
    copies(pairs, sems)
    step = 512
    span = up.shape[1]
    for start in range(0, rows_all.shape[0], step):
        here = slice(start, start + step)
        value = rows_all[here, :]
        mask = adapter_mask(scalars, rows_from(start, step))
        latent = dot(value, down[...]).astype(BF) * jnp.concatenate([mask] * 3, axis=1).astype(BF)
        latents[here, :] = latent
        pre = dot(value, weight[...])
        for part in range(3):
            block = pre[:, part * span : (part + 1) * span] + dot(
                latent[:, part * LANES : (part + 1) * LANES], up[part * LANES : (part + 1) * LANES, :]
            )
            if part < 2:
                heads = []
                for k in range(span // HEAD_DIM):
                    head = block[:, k * HEAD_DIM : (k + 1) * HEAD_DIM]
                    heads.append(
                        head * cosine[here, :] + pltpu.roll(head, HEAD_DIM // 2, 1) * sine[here, :]
                    )
                block = jnp.concatenate(heads, axis=1)
            out[here, part * span : (part + 1) * span] = block.astype(BF)


def allowed_pairs(scalars, first_row, rows, width):
    row = rows_from(first_row, rows)
    column = lax.broadcasted_iota(jnp.int32, (1, width), 1)
    return (column <= row) & (column >= doc_begin(scalars, row))


def attend_kernel(rows, scalars, query, key, value, out, lse):
    scale = HEAD_DIM**-0.5
    for start in range(0, query.shape[0], rows):
        here = slice(start, start + rows)
        width = start + rows
        scores = inner(query[here, :], key[:width, :], 1, 1) * scale
        scores = jnp.where(allowed_pairs(scalars, start, rows, width), scores, -1e30)
        top = jnp.max(scores, axis=1, keepdims=True)
        expd = jnp.exp(scores - top)
        total = jnp.sum(expd, axis=1, keepdims=True)
        probs = (expd * (1.0 / total)).astype(BF)
        out[here, :] = dot(probs, value[:width, :]).astype(BF)
        lse[here, :] = jnp.broadcast_to(top + jnp.log(total), (rows, LANES))


def attend_back_kernel(
    rows, scalars, query, key, value, grad, lse, latents, cosine, sine, own, other, ups,
    dq_all, dk_sum, dv_sum,
):
    dk_sum[...] = jnp.zeros_like(dk_sum)
    dv_sum[...] = jnp.zeros_like(dv_sum)
    scale = HEAD_DIM**-0.5
    length = query.shape[0]
    for start in range(0, length, rows):
        here = slice(start, start + rows)
        width = start + rows
        this_query = query[here, :]
        upstream = grad[here, :]
        scores = inner(this_query, key[:width, :], 1, 1) * scale
        probs = jnp.where(
            allowed_pairs(scalars, start, rows, width), jnp.exp(scores - lse[here, :1]), 0.0
        )
        prob_grad = inner(upstream, value[:width, :], 1, 1)
        delta = jnp.sum(prob_grad * probs, axis=1, keepdims=True)
        score_grad = (probs * (prob_grad - delta)).astype(BF)
        dq_all[here, :] = dot(score_grad, key[:width, :]) * scale
        dk_sum[:width, :] += inner(score_grad, this_query, 0, 0)
        dv_sum[:width, :] += inner(probs.astype(BF), upstream, 0, 0)

    chip, core = scalars[0], scalars[1]
    half = own.shape[1] // 8
    for part, total in enumerate((dq_all, dk_sum, dv_sum)):
        for start in range(0, length, 512):
            here = slice(start, start + 512)
            if part == 0:
                raw = total[here, :].astype(BF).astype(F32)
            elif part == 1:
                raw = (total[here, :] * scale).astype(BF).astype(F32)
            else:
                raw = total[here, :]
            if part < 2:
                raw = raw * cosine[here, :] - pltpu.roll(raw, HEAD_DIM // 2, 1) * sine[here, :]
            total[here, :] = raw.astype(BF).astype(F32)
        low = total[...].astype(BF)
        ups[part] = inner(latents[:, part * LANES : (part + 1) * LANES], low, 0, 0)
        for k, target in enumerate((own, other)):
            for at, (rel, h) in enumerate(HALVES):
                seat = (chip ^ rel) * 2 + (core if k == 0 else 1 - core)
                there = pl.ds(pl.multiple_of((seat * 2 + h) * half, half), half)
                target[part, at * half : (at + 1) * half, :] = total[there, :].astype(BF)


def head_order(k):
    return (k % CHIPS) * CHIPS + k // CHIPS


def out_kernel(scalars, mixed, weight, down, up, tokens, second, first_half, second_half, latents, natural):
    for k in range(16):
        at = head_order(k)
        natural[:, k * LANES : (k + 1) * LANES] = mixed[:, at * LANES : (at + 1) * LANES]
    rows = tokens.shape[0]
    seat = scalars[0] * 2 + scalars[1]
    mask = adapter_mask(scalars, rows_from(seat * rows, rows)).astype(BF)
    value = natural[...]
    latent = dot(value, down[...]).astype(BF) * mask
    latents[...] = latent
    total = tokens[...].astype(F32) + (dot(value, weight[...]) + dot(latent, up[...]))
    second[...] = total
    norm, _ = normed(total)
    first_half[...] = norm[: rows // 2].astype(BF)
    second_half[...] = norm[rows // 2 :].astype(BF)


def ff_kernel(begin, last, sides, first_z, scalars, *refs):
    if begin:
        select, a_gu, b_down = refs[:3]
        count = 3
    else:
        z_gu_in, dz_down_in = refs[:2]
        count = 2
    weights = [refs[count + 2 * k : count + 2 * k + 2] for k in range(sides)]
    count += 2 * sides
    norm, cot = refs[count : count + 4], refs[count + 4 : count + 8]
    count += 8
    if not begin:
        sums_in = refs[count]
        count += 1
    outs = refs[count : count + (2 if last else 1)]
    count += len(outs)
    results = [refs[count + 2 * k : count + 2 * k + 2] for k in range(sides)]
    count += 2 * sides
    if begin:
        z_gu_out, dz_down_out = refs[count : count + 2]
        count += 2
    rows_in, cot_in, sums, sems = refs[count : count + 4]
    held = [refs[count + 4 + 2 * k : count + 6 + 2 * k] for k in range(sides)]
    rows, width = rows_in.shape
    wide = width + LANES
    own_ff = weights[0][1].shape[0] // 4
    many = held[0][1].shape[0] // own_ff
    part = pl.ds(first_z * own_ff, many * own_ff)
    low = rows // 4
    pairs = [(norm[k], rows_in.at[pl.ds(k * low, low)]) for k in range(4)]
    pairs.append((weights[0][0], held[0][0]))
    pairs += [(cot[k], cot_in.at[pl.ds(k * low, low)]) for k in range(4)]
    pairs.append((weights[0][1].at[part], held[0][1]))
    if sides == 2:
        pairs += [(weights[1][0], held[1][0]), (weights[1][1].at[part], held[1][1])]
    if not begin:
        pairs.append((sums_in, sums))
    loads = [pltpu.make_async_copy(x, y, sems.at[k]) for k, (x, y) in enumerate(pairs)]
    for load in loads:
        load.start()
    for load in loads[:4]:
        load.wait()
    if begin:
        mask = select[...]
        z_gu = dot(rows_in[...], a_gu[...]).astype(BF) * jnp.concatenate([mask, mask], axis=1)
        z_gu_out[...] = z_gu
    else:
        z_gu, dz_down = z_gu_in[...], dz_down_in[...]
    z_gate, z_up = z_gu[:, :LANES], z_gu[:, LANES:]
    norm_grad = 0.0
    latent_grad = 0.0
    for side, (gu, down) in enumerate(held):
        size = gu.shape[1] // 2
        loads[4 if side == 0 else 10].wait()
        both = dot(rows_in[...], gu[...])
        if side == 0:
            for load in loads[5:9]:
                load.wait()
            if begin:
                dz_down = (inner(cot_in[...], b_down[...], 1, 1) * mask.astype(F32)).astype(BF)
                dz_down_out[...] = dz_down
        loads[9 if side == 0 else 11].wait()
        up_gate = jnp.concatenate(
            [down[i * own_ff : i * own_ff + LANES, wide:] for i in range(many)], axis=1
        )
        up_up = jnp.concatenate(
            [down[i * own_ff + LANES : i * own_ff + 2 * LANES, wide:] for i in range(many)], axis=1
        )
        gate = both[:, :size] + dot(z_gate, up_gate)
        upper = both[:, size:] + dot(z_up, up_up)
        sigma = 1.0 / (1.0 + jnp.exp(-gate))
        active = gate * sigma
        results[side][0][...] = (active * upper).astype(BF)
        hidden_grad = inner(cot_in[...], down[:, :width], 1, 1) + inner(
            dz_down, down[:, width:wide], 1, 1
        )
        grads = results[side][1]
        grads[:, :size] = (hidden_grad * upper * sigma * (1.0 + gate * (1.0 - sigma))).astype(BF)
        grads[:, size:] = (hidden_grad * active).astype(BF)
        norm_grad += inner(grads[...], gu[...], 1, 1)
        latent_grad += jnp.concatenate(
            [inner(grads[:, :size], up_gate, 1, 1), inner(grads[:, size:], up_up, 1, 1)], axis=1
        )
    if begin:
        outs[0][:, :width] = norm_grad
        outs[0][:, width:] = latent_grad
        return
    loads[-1].wait()
    if not last:
        outs[0][:, :width] = norm_grad + sums[:, :width]
        outs[0][:, width:] = latent_grad + sums[:, width:]
        return
    low = rows // 2
    for k in range(2):
        at = slice(k * low, (k + 1) * low)
        kind = outs[k].dtype
        outs[k][:, :width] = (norm_grad[at] + sums[at, :width]).astype(kind)
        outs[k][:, width:] = (latent_grad[at] + sums[at, width:]).astype(kind)


def down_kernel(begin, scalars, hidden_own, hidden_oth, down_own, down_oth, *refs):
    outs = refs if begin else refs[1:]
    wide = outs[0].shape[1]
    total = dot(hidden_own[...], down_own[:, :wide]) + dot(hidden_oth[...], down_oth[:, :wide])
    if not begin:
        total += refs[0][...]
    rows = outs[0].shape[0]
    for k, out in enumerate(outs):
        out[...] = total[k * rows : (k + 1) * rows].astype(out.dtype)


def spread_kernel(places, scalars, *refs):
    pieces, outs = [*refs[:4], *(refs[4].at[k] for k in range(4))], refs[5:]
    for k, piece in enumerate(pieces):
        chip = scalars[0] ^ (k % 4)
        core = scalars[1] if k < 4 else 1 - scalars[1]
        seat = chip * 2 + core
        at = 0
        for out, (kind, rows, blocks) in zip(outs, places):
            for block in range(blocks):
                value = piece[at : at + rows, :].astype(F32)
                at += rows
                columns = pl.ds(block * LANES, LANES)
                if kind == "rows":
                    out[pl.ds(pl.multiple_of(seat * rows, rows), rows), columns] = value
                elif kind == "core rows":
                    row = pl.multiple_of(core * (CHIPS * rows) + chip * rows, rows)
                    out[pl.ds(row, rows), columns] = value
                elif kind == "columns":
                    column = pl.multiple_of((seat * blocks + block) * LANES, LANES)
                    out[:, pl.ds(column, LANES)] = value
                else:
                    row = pl.multiple_of(core * rows, rows)
                    out[pl.ds(row, rows), pl.ds(pl.multiple_of(chip * LANES, LANES), LANES)] = value


def ff_grads_kernel(scalars, *refs):
    z_gu, dz_down, results, keep, send = refs[:2], refs[2:4], refs[4:-2], refs[-2], refs[-1]
    at = 0
    for zs in CHUNKS:
        for out in (keep, send):
            gate, upper, down = 0.0, 0.0, 0.0
            for half in range(2):
                hidden, grads = results[at], results[at + 1]
                at += 2
                size = hidden.shape[1]
                gate += inner(z_gu[half][:, :LANES], grads[:, :size], 0, 0)
                upper += inner(z_gu[half][:, LANES:], grads[:, size:], 0, 0)
                down += inner(hidden[...], dz_down[half][...], 0, 0)
            own_ff = size // len(zs)
            rows = 2 * LANES
            blocks = own_ff // LANES
            for i, z in enumerate(zs):
                for k in range(blocks):
                    columns = slice(i * own_ff + k * LANES, i * own_ff + (k + 1) * LANES)
                    out[z, k * rows : k * rows + LANES, :] = gate[:, columns].astype(out.dtype)
                    out[z, k * rows + LANES : (k + 1) * rows, :] = upper[:, columns].astype(out.dtype)
                there = slice(blocks * rows, blocks * rows + own_ff)
                out[z, there, :] = down[i * own_ff : (i + 1) * own_ff].astype(out.dtype)


def other_grads_kernel(quarter, scalars, *refs):
    norm1, norm2, cot, mixed = refs[:8], refs[8:16], refs[16:24], refs[24:26]
    middle, last = refs[26:30], refs[30:34]
    up_qkv, keep, send, columns, all_gu, all_qkv, all_down, sems = refs[34:]
    half = norm1[0].shape[0]
    chip, core = scalars[0], scalars[1]
    pairs = []
    for k, source in enumerate((norm1, norm2, cot)):
        for z in range(4):
            column = pl.ds(pl.multiple_of(z * quarter + chip * LANES, LANES), LANES)
            for h in range(8):
                target = columns.at[k, h * half : (h + 1) * half, z * LANES : (z + 1) * LANES]
                pairs.append((source[h].at[:, column], target))
    loads = [pltpu.make_async_copy(x, y, sems.at[k]) for k, (x, y) in enumerate(pairs)]
    for load in loads:
        load.start()
    gu_wide, qkv_wide = all_gu.shape[1], all_qkv.shape[1]
    for k, (rel, h) in enumerate(HALVES):
        here, there = slice(h * half, (h + 1) * half), slice(k * half, (k + 1) * half)
        all_gu[there, :] = middle[rel][here, :gu_wide]
        all_qkv[there, :] = last[rel][here, :qkv_wide]
        all_down[there, :] = last[rel][here, qkv_wide:]

    def halves(z, at, value):
        rows = value.shape[0] // 2
        for k in range(2):
            piece = value[k * rows : (k + 1) * rows]

            @pl.when(core == k)
            def _():
                keep[z, at : at + rows, :] = piece

            @pl.when(core != k)
            def _():
                send[z, at : at + rows, :] = piece.astype(BF)

    def two_of_four(at, values):
        rows = values[0].shape[0] // 2
        for k in range(2):

            @pl.when(core == k)
            def _():
                for i in range(2):
                    here, there = 2 * k + i, 2 * (1 - k) + i
                    keep[here, at : at + rows, :] = values[i][k * rows : (k + 1) * rows]
                    send[here, at : at + rows, :] = values[i][(1 - k) * rows : (2 - k) * rows].astype(BF)
                    keep[there, at : at + rows, :] = jnp.zeros((rows, LANES), F32)
                    send[there, at : at + rows, :] = jnp.zeros((rows, LANES), BF)

    low = LANES // 2
    at = 3 * low
    rows = 2 * half
    for k, source in enumerate(mixed):
        total = 0.0
        for rel in range(4):
            here = pl.ds(pl.multiple_of(((chip ^ rel) * 2 + core) * rows, rows), rows)
            total += inner(source[here, :], middle[rel][:, gu_wide : gu_wide + LANES], 0, 0)
        first = 2 * (core if k == 0 else 1 - core)
        for i in range(2):
            halves(first + i, at, total[i * LANES : (i + 1) * LANES])
    at += low
    share = LANES // PLANE
    for z in range(4):
        for k in range(4):
            block = (z * 4 + k) // 2
            column = gu_wide + LANES + ((z * 4 + k) % 2) * LANES
            value = 0.0
            for rel in range(4):
                piece = middle[rel][block * 2 * share : (block + 1) * 2 * share, column : column + LANES]
                value = value + piece.astype(F32)
            halves(z, at + k * share, value)
    at += low
    at_b = at + 3 * low
    heads = [jnp.concatenate([up_qkv[part, :, i * LANES : (i + 1) * LANES] for part in range(3)], axis=0) for i in range(2)]
    two_of_four(at_b, heads)
    for load in loads:
        load.wait()
    value = inner(columns[1], all_gu[...], 0, 0)
    for z in range(4):
        for k in range(2):
            block = value[z * LANES : (z + 1) * LANES, k * LANES : (k + 1) * LANES]
            halves(z, k * low, block)
    value = inner(all_down[...], columns[2], 0, 0)
    for z in range(4):
        halves(z, 2 * low, value[:, z * LANES : (z + 1) * LANES])
    value = inner(columns[0], all_qkv[...], 0, 0)
    for z in range(4):
        for k in range(3):
            block = value[z * LANES : (z + 1) * LANES, k * LANES : (k + 1) * LANES]
            halves(z, at + k * low, block)


def along_line_kernel(scalars, keep, brought, mine, onward, sent):
    z = scalars[2]
    mine[...] = keep[z] + brought[z].astype(F32)
    onward[...] = keep[z ^ 2] + brought[z ^ 2].astype(F32)
    for k, other in enumerate((1, 3)):
        sent[k] = (keep[z ^ other] + brought[z ^ other].astype(F32)).astype(BF)


def keep_kernel(scalars, *refs):
    count = len(refs) // 2
    for source, target in zip(refs[:count], refs[count:]):
        target[...] = source[...]


def back_middle_kernel(
    scalars, own, by_x, by_y, got_y, got_x, second, cot, a_gu, w_out, a_out, b_out, z_out,
    grad, mixed_grad, pack_0, pack_1, pack_2, pack_3, w_held, sem,
):
    packs = (pack_0, pack_1, pack_2, pack_3)
    load = pltpu.make_async_copy(w_out, w_held, sem)
    load.start()
    rows, width = second.shape
    half = rows // 2
    upper = own[:half] + by_x[...].astype(F32) + got_y[...].astype(F32)
    lower = own[half:] + by_y[...].astype(F32) + got_x[...].astype(F32)
    wide = jnp.concatenate([upper, lower], axis=0)
    seat = scalars[0] * 2 + scalars[1]
    mask = adapter_mask(scalars, rows_from(seat * rows, rows))
    dz_gu = (wide[:, width:] * jnp.concatenate([mask, mask], axis=1)).astype(BF)
    upstream = wide[:, :width] + inner(dz_gu, a_gu[...], 1, 1)
    norm, factor = normed(second[...])
    total = cot[...].astype(F32) + norm_back(norm, factor, upstream)
    grad[...] = total
    low = total.astype(BF)
    dz_out = (inner(low, b_out[...], 1, 1) * mask).astype(BF)
    value = inner(z_out[...], low, 0, 0).astype(BF)
    load.wait()
    back = (inner(low, w_held[...], 1, 1) + inner(dz_out, a_out[...], 1, 1)).astype(BF)
    for k in range(16):
        at = head_order(k)
        mixed_grad[:, at * LANES : (at + 1) * LANES] = back[:, k * LANES : (k + 1) * LANES]
    share = value.shape[0] // PLANE
    at = dz_gu.shape[1] + LANES
    for pack in packs:
        pack[:, : dz_gu.shape[1]] = dz_gu
        pack[:, dz_gu.shape[1] : at] = dz_out
    for block in range(CHIPS):
        for core in range(2):
            row = (core * CHIPS + block) * share
            for rel, pack in enumerate(packs):

                @pl.when((scalars[0] ^ rel) == block)
                def _():
                    for k in range(PLANE):
                        there = slice(k * 2 * share + core * share, k * 2 * share + (core + 1) * share)
                        pack[there, at:] = value[row : row + share, k * 2 * LANES : (k + 1) * 2 * LANES]


def back_latent_kernel(scalars, own, other, up_own, up_oth, to_x, to_y, to_far, kept):
    half = kept.shape[0] // 2
    targets = {0: kept, 1: to_x, 2: to_y, 3: to_far}
    for part in range(3):
        at = slice(part * LANES, (part + 1) * LANES)
        value = inner(own[part], up_own[at, :], 1, 1) + inner(other[part], up_oth[at, :], 1, 1)
        for k, (rel, h) in enumerate(HALVES):
            target = targets[rel]
            target[h * half : (h + 1) * half, at] = value[k * half : (k + 1) * half].astype(target.dtype)


def back_qkv_kernel(scalars, own, other, w_own, w_oth, out_0, out_1):
    rows = out_0.shape[0]
    mine = jnp.concatenate([own[part] for part in range(3)], axis=1)
    theirs = jnp.concatenate([other[part] for part in range(3)], axis=1)
    value = inner(mine, w_own[...], 1, 1) + inner(theirs, w_oth[...], 1, 1)
    out_0[...] = value[:rows].astype(out_0.dtype)
    out_1[...] = value[rows:].astype(out_1.dtype)


def back_first_kernel(
    scalars, own, by_x, by_y, got_y, got_x, tokens, second_grad, dz_qkv, a_qkv, input_grad
):
    half = tokens.shape[0] // 2
    upper = own[:half] + by_x[...].astype(F32) + got_y[...].astype(F32)
    lower = own[half:] + by_y[...].astype(F32) + got_x[...].astype(F32)
    upstream = jnp.concatenate([upper, lower], axis=0) + inner(dz_qkv[...], a_qkv[...], 1, 1)
    norm, factor = normed(tokens[...].astype(F32))
    input_grad[...] = second_grad[...] + norm_back(norm, factor, upstream)


def scatter_rest(send_x, send_y, onward):
    half = onward.shape[0] // 2
    by_x, by_y = swap(send_x, 2), swap(send_y, 4)
    pass_y = (onward[:half] + by_x[half:].astype(F32)).astype(BF)
    pass_x = (onward[half:] + by_y[half:].astype(F32)).astype(BF)
    got_y, got_x = swap(pass_y, 4), swap(pass_x, 2)
    return by_x, by_y, got_y, got_x, (pass_y, pass_x)


def plane_shards(
    tokens, cotangent, starts, adapter_ids,
    w_qkv, w_out, w_gu, w_down, a_qkv, b_qkv, a_out, b_out, a_gu, b_gu, a_down, b_down,
):
    seat = lax.axis_index("seq")
    z_at = lax.axis_index("fsdp")
    z_count = lax.axis_size("fsdp")
    core = seat % 2
    chip = seat // 2
    rows, width = tokens.shape[1:]
    half = rows // 2
    group = CHIPS * rows
    length = rows * PLANE
    ff = w_gu.shape[1] // 2
    ff_z = ff // z_count
    ff_dev = ff_z // PLANE
    quarter = w_qkv.shape[0]
    latent = a_out.shape[1]
    heads_dev = width // HEAD_DIM // PLANE
    span = heads_dev * HEAD_DIM
    share = quarter // PLANE
    share_b = latent // PLANE
    wide_down = width + latent
    wide_gu = width + 2 * latent
    first = starts[0]
    chosen = adapter_ids[0]
    scalars = jnp.concatenate([jnp.stack([chip, core, z_at]).astype(jnp.int32), first, chosen])
    stream, cot_low = tokens[0], cotangent[0]

    norm_a, norm_b = call(
        norm_kernel, scalars, [stream], [whole_spec((rows, width))],
        [sds((half, width))] * 2, [whole_spec((half, width))] * 2,
    )
    tall_rows = quarter + 2 * share + 3 * share
    first_part = call(
        functools.partial(cut_first_kernel, (share, quarter, width)), scalars,
        [w_qkv, w_out, a_qkv, a_out, a_gu, b_out, b_down, b_qkv], [ANY] * 8,
        sds((tall_rows, 3 * span)), whole_spec((tall_rows, 3 * span)),
        scratch=[pltpu.SemaphoreType.DMA((39,))],
    )
    first_all = lax.all_gather(first_part, "fsdp", axis=0, tiled=True)
    gates = [len(zs) * 2 * ff_dev for zs in CHUNKS]
    down_part, *gu_parts = call(
        functools.partial(cut_rest_kernel, (ff, ff_z, ff_dev, width)), scalars,
        [w_gu, w_down, a_down, b_gu], [ANY] * 4,
        [sds((ff_dev, wide_down + ff_dev))] + [sds((quarter, n)) for n in gates],
        [whole_spec((ff_dev, wide_down + ff_dev))] + [whole_spec((quarter, n)) for n in gates],
        scratch=[pltpu.SemaphoreType.DMA((3 + 2 * z_count,))], ties=[first_part],
    )
    down_own = lax.all_gather(down_part, "fsdp", axis=0, tiled=True)
    gu_owns = [lax.all_gather(part, "fsdp", axis=0, tiled=True) for part in gu_parts]

    pieces1 = gather_halves(norm_a, norm_b)
    pieces1_oth = [swap(piece, 1) for piece in pieces1]


    cot_pieces = gather_halves(cot_low[:half], cot_low[half:])
    first_all = hold(first_all, [pieces1_oth[1], pieces1_oth[3], cot_pieces[1], cot_pieces[3]])
    by_z = first_all.reshape(z_count, tall_rows, 3 * span)

    def rows_of(start, count, z, many):
        return by_z[z : z + many, start : start + count].reshape(many * count, 3 * span)

    pieces_small = gather_halves(rows_of(quarter, share + 32, 0, 2), rows_of(quarter, share + 32, 2, 2))
    pieces_small += [swap(piece, 1) for piece in pieces_small]
    ups_qkv = rows_of(quarter + share, 64, 0, 4)
    full_a_qkv, full_a_gu, full_a_out, full_b_out, full_b_down = call(
        functools.partial(unpack_small_kernel, share, quarter), scalars, pieces_small,
        [whole_spec((2 * share + 64, 3 * span))] * 16,
        [sds((width, 3 * latent)), sds((width, 2 * latent)), sds((width, latent))]
        + [sds((latent, width))] * 2,
        [whole_spec((width, 3 * latent)), whole_spec((width, 2 * latent)), whole_spec((width, latent))]
        + [whole_spec((latent, width))] * 2,
    )
    at = quarter + 2 * share
    out_a, out_b = rows_of(at, 3 * share, 0, 2), rows_of(at, 3 * share, 2, 2)
    pieces_out = gather_halves(hold(out_a, [pieces_small[1]]), hold(out_b, [pieces_small[3]]))
    pieces_out += [swap(piece, 1) for piece in pieces_out]
    full_out = call(
        functools.partial(unpack_out_kernel, share, quarter), scalars, pieces_out, [ANY] * 16,
        sds((width, width)), whole_spec((width, width)), scratch=[pltpu.SemaphoreType.DMA((96,))],
    )
    ups_oth = swap(ups_qkv, 1)

    def qkv_up(piece):
        piece = piece.reshape(z_count, 64, 3 * span)
        parts = []
        for k in range(12):
            row, lane = up_slot(k)
            parts.append(piece[:, row : row + 16, lane : lane + LANES])
        return jnp.concatenate(parts, axis=1).transpose(1, 0, 2).reshape(192, z_count * LANES)

    mine, theirs = qkv_up(ups_qkv), qkv_up(ups_oth)
    up_chip = jnp.where(
        core == 0, jnp.concatenate([mine, theirs], axis=0), jnp.concatenate([theirs, mine], axis=0)
    )
    up_own = take(up_chip, core * span, span, 1)
    up_oth = take(up_chip, (1 - core) * span, span, 1)

    all_places = jnp.arange(length, dtype=jnp.int32)
    all_begin, _ = doc_tables(all_places, first, chosen)
    cosine, sine = rope_tables(all_places - all_begin, HEAD_DIM)
    sign = jnp.where(jnp.arange(HEAD_DIM) < HEAD_DIM // 2, -1.0, 1.0)
    turn = sine * sign[None, :]
    rel = jnp.array([r for r, _ in HALVES], jnp.int32)
    part = jnp.array([h for _, h in HALVES], jnp.int32)
    group_places = ((((rel ^ chip) * 2 + core) * 2 + part) * half)[:, None] + jnp.arange(
        half, dtype=jnp.int32
    )
    _, group_which = doc_tables(group_places.reshape(-1), first, chosen)
    adapters_at = jnp.arange(latent, dtype=jnp.int32) // RANK
    group_select = (adapters_at[None, :] == group_which[:, None]).astype(BF)
    select = group_select[-rows:]

    qkv, z_qkv, qkv_own = call(
        qkv_kernel, scalars,
        pieces1 + pieces1_oth + [first_all, full_a_qkv, up_own, cosine, turn],
        [ANY] * 17
        + [
            whole_spec((width, 3 * latent)),
            whole_spec((3 * latent, span)), whole_spec((length, LANES)), whole_spec((length, LANES)),
        ],
        [sds((length, 3 * span)), sds((length, 3 * latent)), sds((width, 3 * span))],
        [whole_spec((length, 3 * span)), whole_spec((length, 3 * latent)), whole_spec((width, 3 * span))],
        scratch=[pltpu.VMEM((length, width), BF), pltpu.SemaphoreType.DMA((20,))],
        cost=(2 * length * width * (3 * span + 3 * latent), 20 * 2**20),
    )
    column = lambda k: pl.BlockSpec((length, LANES), lambda h, _: (0, k * heads_dev + h))
    mixed_h, log_sums = call(
        functools.partial(attend_kernel, rows), scalars, [qkv] * 3, [column(0), column(1), column(2)],
        [sds((length, span)), sds((length, span), F32)], [column(0), column(0)], grid=(heads_dev,),
        cost=(4 * heads_dev * length * length * HEAD_DIM, 8 * 2**20),
    )
    mixed = lax.all_to_all(mixed_h, "seq", split_axis=0, concat_axis=1, tiled=True)
    mixed_oth = swap(mixed_h, 1)
    square = whole_spec((width, width))
    tall = whole_spec((rows, width))
    second, norm_a, norm_b, z_out = call(
        out_kernel, scalars, [mixed, full_out, full_a_out, full_b_out, stream],
        [tall, square, whole_spec((width, latent)), whole_spec((latent, width)), tall],
        [sds((rows, width), F32), sds((half, width)), sds((half, width)), sds((rows, latent))],
        [tall, whole_spec((half, width)), whole_spec((half, width)), whole_spec((rows, latent))],
        scratch=[pltpu.VMEM((rows, width), BF)],
        cost=(2 * rows * width * width, 12 * 2**20), ties=[mixed_oth],
    )

    pieces2 = gather_halves(norm_a, norm_b)
    down_own = hold(down_own, [second])
    down_oth = swap(down_own, 1)
    step = group // 2

    HBM = pl.BlockSpec(memory_space=pltpu.HBM)
    size = len(CHUNKS[0]) * ff_dev
    latents = [None, None]

    def feed(place, weights, at, onward, last):
        begin = onward is None
        if begin:
            operands = [group_select, full_a_gu, full_b_down]
            specs = [
                pl.BlockSpec((step, latent), lambda *_: (at, 0)), whole_spec((width, 2 * latent)),
                whole_spec((latent, width)),
            ]
        else:
            operands = list(latents[at])
            specs = [whole_spec((step, 2 * latent)), whole_spec((step, latent))]
        for pair in weights:
            operands += pair
            specs += [HBM, HBM]
        operands += pieces2[4 * at : 4 * at + 4] + cot_pieces[4 * at : 4 * at + 4]
        specs += [ANY] * 8
        if not begin:
            operands.append(onward)
            specs.append(HBM)
        if last:
            shapes, outs = [sds((rows, wide_gu), (BF, F32)[at])] * 2, [whole_spec((rows, wide_gu))] * 2
        else:
            shapes, outs = [sds((step, wide_gu), F32)], [whole_spec((step, wide_gu))]
        more = [(step, size), (step, 2 * size)] * len(weights)
        if begin:
            more += [(step, 2 * latent), (step, latent)]
        shapes += [sds(shape) for shape in more]
        outs += [whole_spec(shape) for shape in more]
        return call(
            functools.partial(ff_kernel, begin, last, len(weights), CHUNKS[place][0]), scalars, operands,
            specs, shapes, outs,
            scratch=[pltpu.VMEM((step, width), BF)] * 2
            + [pltpu.VMEM((8, LANES) if begin else (step, wide_gu), F32), pltpu.SemaphoreType.DMA((13,))]
            + [pltpu.VMEM((width, 2 * size), BF), pltpu.VMEM((size, wide_down + ff_dev), BF)]
            * len(weights),
            cost=(step * 10 * width * size * len(weights), 26 * 2**20),
        )

    def down_half(place, at, kind, total, ties):
        weight = pl.BlockSpec((size, wide_down + ff_dev), lambda *_: (place, 0))
        begin = total is None
        operands = [results[place][0][at][0], results[place][1][at][0], down_own, down_oth]
        specs = [whole_spec((step, size))] * 2 + [weight] * 2
        if not begin:
            operands.append(total)
            specs.append(whole_spec((step, wide_down)))
        shape = (step, wide_down) if begin else (rows, wide_down)
        count = 1 if begin else 2
        return call(
            functools.partial(down_kernel, begin), scalars, operands, specs,
            [sds(shape, kind)] * count, [whole_spec(shape)] * count,
            cost=(2 * step * 4 * ff_dev * width, 12 * 2**20), ties=ties,
        )

    results = [[[None, None], [None, None]] for _ in CHUNKS]
    gu_own = hold(gu_owns[0], [pieces2[1], pieces2[3]])
    weights = [(gu_own, down_own), (swap(gu_own, 1), down_oth)]
    sums = []
    for at in range(2):
        total, *more = feed(0, weights, at, None, False)
        sums.append(total)
        results[0][0][at], results[0][1][at], latents[at] = more[:2], more[2:4], more[4:]
    down_first = [down_half(0, at, F32, None, [sums[1]])[0] for at in range(2)]
    gu_own = hold(gu_owns[1], sums + down_first)
    weights = [(gu_own, down_own), (swap(gu_own, 1), down_oth)]
    total, *results[1][0][0] = feed(1, weights[:1], 0, sums[0], False)
    send_x, send_y, *results[1][1][0] = feed(1, weights[1:], 0, total, True)
    pass_on, kept, *more = feed(1, weights, 1, sums[1], True)
    results[1][0][1], results[1][1][1] = more[:2], more[2:]
    by_x, by_y, got_y, got_x, passed = scatter_rest(send_x, send_y, pass_on)
    down_x, down_y = down_half(1, 0, BF, down_first[0], passed)
    halfspec = lambda n: pl.BlockSpec((half, n), lambda *_: (0, 0))
    second_grad, mixed_grad, *packs = call(
        back_middle_kernel, scalars,
        [kept, by_x, by_y, got_y, got_x, second, cot_low, full_a_gu, full_out, full_a_out, full_b_out, z_out],
        [whole_spec((rows, wide_gu))] + [halfspec(wide_gu)] * 4
        + [
            tall, tall, whole_spec((width, 2 * latent)), ANY, whole_spec((width, latent)),
            whole_spec((latent, width)), whole_spec((rows, latent)),
        ],
        [
            sds((rows, width), F32), sds((rows, width)),
        ]
        + [sds((rows, 5 * latent))] * 4,
        [tall, tall] + [whole_spec((rows, 5 * latent))] * 4,
        scratch=[pltpu.VMEM((width, width), BF), pltpu.SemaphoreType.DMA],
        cost=(2 * rows * width * width, 16 * 2**20), ties=[down_x],
    )
    mixed_grad_h = lax.all_to_all(mixed_grad, "seq", split_axis=1, concat_axis=0, tiled=True)
    down_on, down_kept = down_half(1, 1, F32, down_first[1], [mixed_grad])

    def along_line(keep, send, ties):
        shape = keep.shape[1:]
        return call(
            along_line_kernel, scalars, [keep, swap(send, 1)], [whole_spec(keep.shape)] * 2,
            [sds(shape, F32)] * 2 + [sds((2, *shape))], [whole_spec(shape)] * 2 + [whole_spec((2, *shape))],
            ties=ties, cost=(2**20, 8 * 2**20),
        )

    def line_sum(mine, onward, sent, ties):
        brought = lax.ppermute(sent, "fsdp", [(i, i ^ 1) for i in range(z_count)])
        onward = (onward + brought[1].astype(F32)).astype(BF)
        far = lax.ppermute(onward, "fsdp", [(i, i ^ 2) for i in range(z_count)])
        mine = hold(mine, ties) if ties else mine
        return (mine + brought[0].astype(F32) + far.astype(F32)).astype(BF)

    def spread(mine, places, shapes, ties):
        plane = blocks_of(mine)
        plane.append(swap(jnp.stack(plane), 1))
        return call(
            functools.partial(spread_kernel, places), scalars, plane,
            [whole_spec(piece.shape) for piece in plane],
            [sds(shape, F32) for shape in shapes], [whole_spec(shape) for shape in shapes], ties=ties,
        )

    *down_by, _ = scatter_rest(
        hold(down_x, [mixed_grad_h]), hold(down_y, [mixed_grad_h]), down_on
    )
    middle = [packs[0]] + [swap(hold(packs[k], [mixed_grad_h]), 2 * k) for k in (1, 2, 3)]

    result = pl.BlockSpec((3, group, HEAD_DIM), lambda h, _: (0, 0, h))
    grads_a, grads_b, up_qkv = call(
        functools.partial(attend_back_kernel, rows), scalars,
        [qkv, qkv, qkv, mixed_grad_h, log_sums, z_qkv, cosine, turn],
        [column(0), column(1), column(2), column(0), column(0), whole_spec((length, 3 * latent))]
        + [whole_spec((length, LANES))] * 2,
        [sds((3, group, span))] * 2 + [sds((3, latent, span), F32)],
        [result, result, pl.BlockSpec((3, latent, HEAD_DIM), lambda h, _: (0, 0, h))],
        scratch=[pltpu.VMEM((length, HEAD_DIM), F32)] * 3, grid=(heads_dev,),
        cost=(10 * heads_dev * length * length * HEAD_DIM, 16 * 2**20), ties=[down_on],
    )
    grads_b = swap(grads_b, 1)
    qkv_oth = swap(qkv_own, 1)

    down_kept = hold(down_kept, [grads_a])
    upper = down_kept[:half] + down_by[0][:half].astype(F32) + down_by[2].astype(F32)
    lower = down_kept[half:] + down_by[1][:half].astype(F32) + down_by[3].astype(F32)
    wide = jnp.concatenate([upper, lower], axis=0)
    z_down = wide[:, width:].astype(BF) * select
    to_x, to_y, to_far, latent_kept = call(
        back_latent_kernel, scalars, [grads_a, grads_b, up_own, up_oth],
        [whole_spec((3, group, span))] * 2 + [whole_spec((3 * latent, span))] * 2,
        [sds((rows, 3 * latent))] * 3 + [sds((rows, 3 * latent), F32)],
        [whole_spec((rows, 3 * latent))] * 4,
        cost=(4 * group * span * 3 * latent, 4 * 2**20),
    )

    def back_qkv(at, kind, ties):
        part = pl.BlockSpec((3, step, span), lambda *_: (0, at, 0))
        return call(
            back_qkv_kernel, scalars, [grads_a, grads_b, qkv_own, qkv_oth],
            [part, part] + [whole_spec((width, 3 * span))] * 2,
            [sds((rows, width), kind)] * 2, [tall] * 2,
            cost=(2 * group * span * 3 * width, 12 * 2**20), ties=ties,
        )

    pass_on, kept = back_qkv(1, F32, [to_x, *middle[1:]])
    dz_qkv = latent_kept + swap(to_x, 2).astype(F32) + swap(to_y, 4).astype(F32)
    dz_qkv = (dz_qkv + swap(to_far, 6).astype(F32)) * jnp.tile(select, (1, 3)).astype(F32)
    both = jnp.concatenate([dz_qkv.astype(BF), z_down], axis=1)
    last = blocks_of(both)
    ff_rows = 2 * latent * (ff_dev // LANES) + ff_dev
    values = [one[k] for one in latents for k in range(1)] + [one[1] for one in latents]
    values += [value for chunk in results for side in chunk for one in side for value in one]
    ff_keep, ff_send = call(
        ff_grads_kernel, scalars, values, [whole_spec(value.shape) for value in values],
        [sds((z_count, ff_rows, LANES), F32), sds((z_count, ff_rows, LANES))],
        [whole_spec((z_count, ff_rows, LANES))] * 2, cost=(2**32, 12 * 2**20), ties=[kept, both],
    )
    send_x, send_y = back_qkv(0, BF, [*last[1:], ff_send])
    other_rows = 11 * LANES // 2
    keep, send = call(
        functools.partial(other_grads_kernel, quarter), scalars,
        [*pieces1, *pieces2, *cot_pieces, mixed_h, mixed_oth, *middle, *last, up_qkv],
        [ANY] * 24 + [whole_spec((length, span))] * 2 + [whole_spec((rows, 5 * latent))] * 4
        + [whole_spec((rows, 4 * latent))] * 4 + [whole_spec((3, latent, span))],
        [sds((z_count, other_rows, LANES), F32), sds((z_count, other_rows, LANES))],
        [whole_spec((z_count, other_rows, LANES))] * 2,
        scratch=[
            pltpu.VMEM((3, group, z_count * LANES), BF), pltpu.VMEM((group, 2 * latent), BF),
            pltpu.VMEM((group, 3 * latent), BF), pltpu.VMEM((group, latent), BF),
            pltpu.SemaphoreType.DMA((96,)),
        ],
        cost=(2 * group * 512 * 768, 8 * 2**20), ties=[send_x],
    )
    ff_mine, *ff_rest = along_line(ff_keep, ff_send, [keep])
    by_x, by_y, got_y, got_x, passed = scatter_rest(send_x, send_y, hold(pass_on, [keep]))
    input_grad = call(
        back_first_kernel, scalars,
        [kept, by_x, by_y, got_y, got_x, stream, second_grad, both, full_a_qkv],
        [tall] + [halfspec(width)] * 4
        + [tall, tall, pl.BlockSpec((rows, 3 * latent), lambda *_: (0, 0)), whole_spec((width, 3 * latent))],
        sds((rows, width), F32), tall,
        cost=(2 * rows * width * 3 * latent, 12 * 2**20),
    )
    ff_total = line_sum(ff_mine, *ff_rest, [])
    total = line_sum(*along_line(keep, send, []), [got_y, got_x])
    activations = second + (wide[:, :width] + dot(hold(z_down, passed), full_b_down))
    g_b_gu, g_a_down = spread(
        ff_total, (("columns", 2 * latent, ff_dev // LANES), ("rows", ff_dev, 1)),
        [(2 * latent, ff_z), (ff_z, latent)], [input_grad],
    )
    low = LANES // 2
    g_a_gu, g_b_down, g_a_out, g_b_out, g_a_qkv, g_b_qkv = spread(
        total,
        (
            ("rows", low, 2), ("both", low, 1), ("rows", low, 1), ("core rows", share_b, z_count),
            ("rows", low, 3), ("both", 3 * low, 1),
        ),
        [
            (quarter, 2 * latent), (latent, quarter), (quarter, latent), (latent, quarter),
            (quarter, 3 * latent), (3 * latent, quarter),
        ],
        [input_grad],
    )

    return (
        activations[None], input_grad[None],
        g_a_qkv, g_b_qkv, g_a_out, g_b_out, g_a_gu, g_b_gu, g_a_down, g_b_down,
    )


def solution(mesh):
    placed = (
        P("fsdp", "seq", None),
        P("fsdp", "seq", None),
        P("fsdp", None),
        P("fsdp", None),
        P("fsdp", None),
        P("fsdp", None),
        P("fsdp", None),
        P("fsdp", None),
        P("fsdp", None),
        P(None, "fsdp"),
        P("fsdp", None),
        P(None, "fsdp"),
        P("fsdp", None),
        P(None, "fsdp"),
        P("fsdp", None),
        P(None, "fsdp"),
    )
    on_plane = mesh.shape["seq"] == PLANE and mesh.shape["fsdp"] == 4
    return jax.shard_map(
        plane_shards if on_plane else shards,
        mesh=mesh,
        in_specs=placed,
        out_specs=(
            P("fsdp", "seq", None),
            P("fsdp", "seq", None),
            P("fsdp", None),
            P(None, "fsdp"),
            P("fsdp", None),
            P(None, "fsdp"),
            P("fsdp", None),
            P(None, "fsdp"),
            P("fsdp", None),
            P(None, "fsdp"),
        ),
        check_vma=False,
    )
```

```python
import functools

import jax
import jax.numpy as jnp
from jax import lax
from jax.experimental import pallas as pl
from jax.experimental.pallas import tpu as pltpu
from jax.sharding import PartitionSpec as P

HEAD_DIM = 128
RANK = 16


def layer_norm(values):
    centre = values - jnp.mean(values, axis=-1, keepdims=True)
    spread = jnp.mean(centre * centre, axis=-1, keepdims=True)
    factor = lax.rsqrt(spread + 1e-05)
    return (centre * factor, factor)


def norm_back(normed, factor, upstream):
    upstream_mean = jnp.mean(upstream, axis=-1, keepdims=True)
    cross_mean = jnp.mean(upstream * normed, axis=-1, keepdims=True)
    return factor * (upstream - upstream_mean - normed * cross_mean)


def doc_tables(places, first, chosen):
    within = first[None, :] <= places[:, None]
    begin = jnp.max(jnp.where(within, first[None, :], 0), axis=1)
    latest = jnp.sum(within.astype(jnp.int32), axis=1) - 1
    doc_order = jnp.arange(first.shape[0], dtype=jnp.int32)
    which = jnp.sum(jnp.where(doc_order[None, :] == latest[:, None], chosen[None, :], 0), axis=1)
    return (begin, which)


def rope_tables(position, head_dim):
    freqs = 10000.0 ** (-(jnp.arange(0, head_dim, 2, dtype=jnp.float32) / head_dim))
    angles = position.astype(jnp.float32)[:, None] * freqs[None, :]
    cosine = jnp.concatenate([jnp.cos(angles), jnp.cos(angles)], axis=-1)
    sine = jnp.concatenate([jnp.sin(angles), jnp.sin(angles)], axis=-1)
    return (cosine, sine)


def rotate(values, cosine, sine):
    half_dim = values.shape[-1] // 2
    turned = jnp.concatenate([-values[..., half_dim:], values[..., :half_dim]], axis=-1)
    return values * cosine[:, None, :] + turned * sine[:, None, :]


def rotate_back(upstream, cosine, sine):
    half_dim = upstream.shape[-1] // 2
    scaled = upstream * sine[:, None, :]
    return upstream * cosine[:, None, :] + jnp.concatenate(
        [scaled[..., half_dim:], -scaled[..., :half_dim]], axis=-1
    )


def inner_rows(left, right):
    return lax.dot_general(
        left, right, (((0,), (0,)), ((), ())), preferred_element_type=jnp.float32
    )


def inner_cols(left, right):
    return lax.dot_general(
        left, right, (((1,), (1,)), ((), ())), preferred_element_type=jnp.float32
    )


def adapter_fwd(inputs, down, up, select, segments):
    latent = jnp.dot(inputs, down, preferred_element_type=jnp.float32).astype(
        jnp.bfloat16
    ) * jnp.tile(select, (1, segments))
    span = up.shape[0] // segments
    pieces = [
        jnp.dot(
            latent[:, seg * span : (seg + 1) * span],
            up[seg * span : (seg + 1) * span],
            preferred_element_type=jnp.float32,
        )
        for seg in range(segments)
    ]
    return (latent, jnp.concatenate(pieces, axis=1))


def adapter_back(inputs, latent, upstream, down, up, select, segments):
    span = up.shape[0] // segments
    out_span = up.shape[1]
    grad_up = jnp.concatenate(
        [
            inner_rows(
                latent[:, seg * span : (seg + 1) * span],
                upstream[:, seg * out_span : (seg + 1) * out_span],
            )
            for seg in range(segments)
        ],
        axis=0,
    )
    latent_grad = jnp.concatenate(
        [
            inner_cols(
                upstream[:, seg * out_span : (seg + 1) * out_span],
                up[seg * span : (seg + 1) * span],
            )
            for seg in range(segments)
        ],
        axis=1,
    )
    latent_grad = (latent_grad * jnp.tile(select, (1, segments)).astype(jnp.float32)).astype(
        jnp.bfloat16
    )
    grad_down = inner_rows(inputs, latent_grad)
    back = inner_cols(latent_grad, down)
    return (grad_down, grad_up, back)


def frozen_fwd(inputs, weight):
    return (
        jnp.dot(
            inputs,
            lax.all_gather(weight, "fsdp", axis=0, tiled=True),
            preferred_element_type=jnp.float32,
        ),
        weight,
    )


def frozen_bwd(upstream, weight):
    return inner_cols(upstream, lax.all_gather(weight, "fsdp", axis=0, tiled=True))


def attend(query_h, key_h, value_h, begin, head_dim):
    length, local_width = query_h.shape
    local_heads = local_width // head_dim
    block_rows = min(512, length)
    block_count = length // block_rows
    score_scale = head_dim ** (-0.5)
    query_all = query_h.reshape(length, local_heads, head_dim)
    key_all = key_h.reshape(length, local_heads, head_dim)
    value_all = value_h.reshape(length, local_heads, head_dim)
    key_places = jnp.arange(length, dtype=jnp.int32)

    def one_block(block_index):
        start = block_index * block_rows
        query_block = lax.dynamic_slice_in_dim(query_all, start, block_rows, 0)
        rows = start + jnp.arange(block_rows, dtype=jnp.int32)
        row_begin = lax.dynamic_slice_in_dim(begin, start, block_rows, 0)
        allowed = (key_places[None, :] <= rows[:, None]) & (
            key_places[None, :] >= row_begin[:, None]
        )
        scores = (
            jnp.einsum("qhd,khd->hqk", query_block, key_all, preferred_element_type=jnp.float32)
            * score_scale
        )
        scores = jnp.where(allowed[None], scores, -1e30)
        row_top = jnp.max(scores, axis=-1, keepdims=True)
        expd = jnp.exp(scores - row_top)
        row_total = jnp.sum(expd, axis=-1, keepdims=True)
        probs = (expd / row_total).astype(jnp.bfloat16)
        mixed = jnp.einsum("hqk,khd->qhd", probs, value_all, preferred_element_type=jnp.float32)
        return (
            mixed.astype(jnp.bfloat16).reshape(block_rows, local_width),
            (row_top + jnp.log(row_total))[..., 0],
        )

    outputs, log_sums = lax.map(one_block, jnp.arange(block_count, dtype=jnp.int32))
    return (outputs.reshape(length, local_width), log_sums)


def attend_back(query_h, key_h, value_h, grad_h, log_sums, begin, head_dim):
    length, local_width = query_h.shape
    local_heads = local_width // head_dim
    block_rows = min(512, length)
    block_count = length // block_rows
    score_scale = head_dim ** (-0.5)
    query_all = query_h.reshape(length, local_heads, head_dim)
    key_all = key_h.reshape(length, local_heads, head_dim)
    value_all = value_h.reshape(length, local_heads, head_dim)
    grad_all = grad_h.reshape(length, local_heads, head_dim)
    key_places = jnp.arange(length, dtype=jnp.int32)

    def step(carry, inputs):
        key_grad, value_grad = carry
        block_index, block_lse = inputs
        start = block_index * block_rows
        query_block = lax.dynamic_slice_in_dim(query_all, start, block_rows, 0)
        grad_block = lax.dynamic_slice_in_dim(grad_all, start, block_rows, 0)
        rows = start + jnp.arange(block_rows, dtype=jnp.int32)
        row_begin = lax.dynamic_slice_in_dim(begin, start, block_rows, 0)
        allowed = (key_places[None, :] <= rows[:, None]) & (
            key_places[None, :] >= row_begin[:, None]
        )
        scores = (
            jnp.einsum("qhd,khd->hqk", query_block, key_all, preferred_element_type=jnp.float32)
            * score_scale
        )
        probs = jnp.where(allowed[None], jnp.exp(scores - block_lse[..., None]), 0.0)
        probs_low = probs.astype(jnp.bfloat16)
        prob_grad = jnp.einsum(
            "qhd,khd->hqk", grad_block, value_all, preferred_element_type=jnp.float32
        )
        row_delta = jnp.sum(prob_grad * probs, axis=-1, keepdims=True)
        score_grad = (probs * (prob_grad - row_delta)).astype(jnp.bfloat16)
        query_grad = (
            jnp.einsum("hqk,khd->qhd", score_grad, key_all, preferred_element_type=jnp.float32)
            * score_scale
        )
        key_grad = (
            key_grad
            + jnp.einsum(
                "hqk,qhd->khd", score_grad, query_block, preferred_element_type=jnp.float32
            )
            * score_scale
        )
        value_grad = value_grad + jnp.einsum(
            "hqk,qhd->khd", probs_low, grad_block, preferred_element_type=jnp.float32
        )
        return (
            (key_grad, value_grad),
            query_grad.astype(jnp.bfloat16).reshape(block_rows, local_width),
        )

    empty = jnp.zeros((length, local_heads, head_dim), jnp.float32)
    (key_grad, value_grad), query_grad = lax.scan(
        step, (empty, empty), (jnp.arange(block_count, dtype=jnp.int32), log_sums)
    )
    return (
        query_grad.reshape(length, local_width),
        key_grad.astype(jnp.bfloat16).reshape(length, local_width),
        value_grad.astype(jnp.bfloat16).reshape(length, local_width),
    )


def shards(
    tokens,
    cotangent,
    starts,
    adapter_ids,
    w_qkv,
    w_out,
    w_gu,
    w_down,
    a_qkv,
    b_qkv,
    a_out,
    b_out,
    a_gu,
    b_gu,
    a_down,
    b_down,
):
    gathered = (
        lax.all_gather(a_qkv, "fsdp", axis=0, tiled=True),
        lax.all_gather(b_qkv, "fsdp", axis=1, tiled=True),
        lax.all_gather(a_out, "fsdp", axis=0, tiled=True),
        lax.all_gather(b_out, "fsdp", axis=1, tiled=True),
        lax.all_gather(a_gu, "fsdp", axis=0, tiled=True),
        lax.all_gather(b_gu, "fsdp", axis=1, tiled=True),
        lax.all_gather(a_down, "fsdp", axis=0, tiled=True),
        lax.all_gather(b_down, "fsdp", axis=1, tiled=True),
    )
    (
        full_a_qkv,
        full_b_qkv,
        full_a_out,
        full_b_out,
        full_a_gu,
        full_b_gu,
        full_a_down,
        full_b_down,
    ) = gathered
    stream = tokens[0].astype(jnp.float32)
    cot_low = cotangent[0]
    tok_count, width = stream.shape
    seq_count = lax.axis_size("seq")
    seq_place = lax.axis_index("seq")
    stream_len = tok_count * seq_count
    first = starts[0]
    chosen = adapter_ids[0]
    local_places = seq_place * tok_count + jnp.arange(tok_count, dtype=jnp.int32)
    local_begin, which = doc_tables(local_places, first, chosen)
    columns = jnp.arange(full_a_out.shape[1], dtype=jnp.int32) // RANK
    select = (columns[None, :] == which[:, None]).astype(jnp.bfloat16)
    cosine, sine = rope_tables(local_places - local_begin, HEAD_DIM)
    head_count = width // HEAD_DIM
    first_norm, first_factor = layer_norm(stream)
    first_low = first_norm.astype(jnp.bfloat16)
    latent_qkv, extra_qkv = adapter_fwd(first_low, full_a_qkv, full_b_qkv, select, 3)
    qkv_main, held_qkv = frozen_fwd(first_low, w_qkv)
    qkv = qkv_main + extra_qkv
    query_rot = (
        rotate(qkv[:, :width].reshape(tok_count, head_count, HEAD_DIM), cosine, sine)
        .reshape(tok_count, width)
        .astype(jnp.bfloat16)
    )
    key_rot = (
        rotate(qkv[:, width : 2 * width].reshape(tok_count, head_count, HEAD_DIM), cosine, sine)
        .reshape(tok_count, width)
        .astype(jnp.bfloat16)
    )
    value_low = qkv[:, 2 * width :].astype(jnp.bfloat16)
    query_h, key_h, value_h = (
        lax.all_to_all(query_rot, "seq", split_axis=1, concat_axis=0, tiled=True),
        lax.all_to_all(key_rot, "seq", split_axis=1, concat_axis=0, tiled=True),
        lax.all_to_all(value_low, "seq", split_axis=1, concat_axis=0, tiled=True),
    )
    all_begin, all_which = doc_tables(jnp.arange(stream_len, dtype=jnp.int32), first, chosen)
    mixed_h, log_sums = attend(query_h, key_h, value_h, all_begin, HEAD_DIM)
    mixed = lax.all_to_all(mixed_h, "seq", split_axis=0, concat_axis=1, tiled=True)
    latent_out, extra_out = adapter_fwd(mixed, full_a_out, full_b_out, select, 1)
    out_main, held_out = frozen_fwd(mixed, w_out)
    second = stream + (out_main + extra_out)
    second_norm, second_factor = layer_norm(second)
    second_low = second_norm.astype(jnp.bfloat16)
    latent_gu, extra_gu = adapter_fwd(second_low, full_a_gu, full_b_gu, select, 2)
    gu_main, held_gu = frozen_fwd(second_low, w_gu)
    gate_up = gu_main + extra_gu
    ff_width = gate_up.shape[1] // 2
    gate = gate_up[:, :ff_width]
    upper = gate_up[:, ff_width:]
    sigma = jax.nn.sigmoid(gate)
    active = gate * sigma
    hidden = (active * upper).astype(jnp.bfloat16)
    latent_down, extra_down = adapter_fwd(hidden, full_a_down, full_b_down, select, 1)
    down_main, held_down = frozen_fwd(hidden, w_down)
    activations = second + (down_main + extra_down)
    grad_a_down, grad_b_down, hidden_extra = adapter_back(
        hidden, latent_down, cot_low, full_a_down, full_b_down, select, 1
    )
    hidden_grad = frozen_bwd(cot_low, held_down) + hidden_extra
    gate_grad = (hidden_grad * upper * sigma * (1.0 + gate * (1.0 - sigma))).astype(jnp.bfloat16)
    upper_grad = (hidden_grad * active).astype(jnp.bfloat16)
    gate_up_grad = jnp.concatenate([gate_grad, upper_grad], axis=1)
    grad_a_gu, grad_b_gu, second_extra = adapter_back(
        second_low, latent_gu, gate_up_grad, full_a_gu, full_b_gu, select, 2
    )
    second_norm_grad = frozen_bwd(gate_up_grad, held_gu) + second_extra
    second_grad = cot_low.astype(jnp.float32) + norm_back(
        second_norm, second_factor, second_norm_grad
    )
    branch_grad = second_grad.astype(jnp.bfloat16)
    grad_a_out, grad_b_out, mixed_extra = adapter_back(
        mixed, latent_out, branch_grad, full_a_out, full_b_out, select, 1
    )
    mixed_grad = (frozen_bwd(branch_grad, held_out) + mixed_extra).astype(jnp.bfloat16)
    mixed_grad_h = lax.all_to_all(mixed_grad, "seq", split_axis=1, concat_axis=0, tiled=True)
    query_grad_h, key_grad_h, value_grad_h = attend_back(
        query_h, key_h, value_h, mixed_grad_h, log_sums, all_begin, HEAD_DIM
    )
    query_grad, key_grad, value_grad = (
        lax.all_to_all(query_grad_h, "seq", split_axis=0, concat_axis=1, tiled=True),
        lax.all_to_all(key_grad_h, "seq", split_axis=0, concat_axis=1, tiled=True),
        lax.all_to_all(value_grad_h, "seq", split_axis=0, concat_axis=1, tiled=True),
    )
    query_pre = (
        rotate_back(
            query_grad.astype(jnp.float32).reshape(tok_count, head_count, HEAD_DIM), cosine, sine
        )
        .reshape(tok_count, width)
        .astype(jnp.bfloat16)
    )
    key_pre = (
        rotate_back(
            key_grad.astype(jnp.float32).reshape(tok_count, head_count, HEAD_DIM), cosine, sine
        )
        .reshape(tok_count, width)
        .astype(jnp.bfloat16)
    )
    qkv_grad = jnp.concatenate([query_pre, key_pre, value_grad], axis=1)
    grad_a_qkv, grad_b_qkv, first_extra = adapter_back(
        first_low, latent_qkv, qkv_grad, full_a_qkv, full_b_qkv, select, 3
    )
    first_norm_grad = frozen_bwd(qkv_grad, held_qkv) + first_extra
    input_grad = second_grad + norm_back(first_norm, first_factor, first_norm_grad)
    grads = (
        grad_a_qkv,
        grad_b_qkv,
        grad_a_out,
        grad_b_out,
        grad_a_gu,
        grad_b_gu,
        grad_a_down,
        grad_b_down,
    )
    shard_dims = (0, 1, 0, 1, 0, 1, 0, 1)
    summed = lax.psum(
        (grads[0], grads[1], grads[2], grads[3], grads[4], grads[5], grads[6], grads[7]),
        ("seq", "fsdp"),
    )
    fsdp_place = lax.axis_index("fsdp")
    fsdp_count = lax.axis_size("fsdp")
    totals = tuple(
        (
            lax.dynamic_slice_in_dim(
                whole,
                fsdp_place * (whole.shape[along] // fsdp_count),
                whole.shape[along] // fsdp_count,
                along,
            )
            for whole, along in zip(summed, shard_dims)
        )
    )
    return (
        activations[None],
        input_grad[None],
        totals[0],
        totals[1],
        totals[2],
        totals[3],
        totals[4],
        totals[5],
        totals[6],
        totals[7],
    )


BF = jnp.bfloat16
F32 = jnp.float32
PLANE = 8
CHIPS = 4
LANES = 128
CHUNKS = ((0, 1), (2, 3))
HALVES = ((1, 0), (3, 0), (2, 1), (3, 1), (2, 0), (1, 1), (0, 0), (0, 1))
ANY = pl.BlockSpec(memory_space=pl.ANY)
ROOMY = 60 * 2**20


def swap(value, bits):
    return lax.ppermute(value, "seq", [(i, i ^ bits) for i in range(PLANE)])


def gather_halves(first, second):
    x_first, y_second = swap(first, 2), swap(second, 4)
    y_first, x_second = swap(first, 4), swap(second, 2)
    far_first, far_second = swap(y_first, 2), swap(x_second, 4)
    return [x_first, far_first, y_second, far_second, y_first, x_second, first, second]


def blocks_of(block):
    return [block, swap(block, 2), swap(block, 4), swap(block, 6)]


def dot(left, right):
    return jnp.dot(left, right, preferred_element_type=F32)


def inner(left, right, on_left, on_right):
    return lax.dot_general(
        left, right, (((on_left,), (on_right,)), ((), ())), preferred_element_type=F32
    )


def take(value, start, count, axis):
    return lax.dynamic_slice_in_dim(value, start, count, axis)


def whole_spec(shape):
    return pl.BlockSpec(shape, lambda *_: (0,) * len(shape))


def call(body, scalars, operands, specs, shapes, out_specs, scratch=(), grid=(1,), cost=None, ties=()):
    count = len(operands)

    def run(*refs):
        inside = refs[: 1 + count] + refs[1 + count + len(ties) :]
        body(*inside)

    return pl.pallas_call(
        run,
        grid_spec=pltpu.PrefetchScalarGridSpec(
            num_scalar_prefetch=1,
            grid=grid,
            in_specs=list(specs) + [ANY] * len(ties),
            out_specs=out_specs,
            scratch_shapes=list(scratch),
        ),
        out_shape=shapes,
        compiler_params=pltpu.CompilerParams(vmem_limit_bytes=ROOMY),
        cost_estimate=None
        if cost is None
        else pl.CostEstimate(flops=cost[0], bytes_accessed=cost[1], transcendentals=0),
    )(scalars, *operands, *ties)


def hold(value, ties):
    return pl.pallas_call(
        lambda *refs: None,
        in_specs=[ANY] * (1 + len(ties)),
        out_specs=ANY,
        out_shape=sds(value.shape, value.dtype),
        input_output_aliases={0: 0},
    )(value, *ties)


def copies(pairs, sems):
    started = [
        pltpu.make_async_copy(source, target, sems.at[k]) for k, (source, target) in enumerate(pairs)
    ]
    for one in started:
        one.start()
    for one in started:
        one.wait()


def sds(shape, dtype=BF):
    return jax.ShapeDtypeStruct(shape, dtype)


def doc_begin(scalars, places):
    begin = jnp.zeros_like(places)
    for doc in range(4):
        begin = jnp.where(scalars[3 + doc] <= places, scalars[3 + doc], begin)
    return begin


def adapter_mask(scalars, places):
    which = jnp.zeros_like(places) + scalars[7]
    for doc in range(1, 4):
        which = jnp.where(scalars[3 + doc] <= places, scalars[7 + doc], which)
    column = lax.broadcasted_iota(jnp.int32, (1, LANES), 1) // RANK
    return (column == which).astype(F32)


def rows_from(first, count):
    return first + lax.broadcasted_iota(jnp.int32, (count, 1), 0)


def normed(values):
    centre = values - jnp.mean(values, axis=-1, keepdims=True)
    factor = lax.rsqrt(jnp.mean(centre * centre, axis=-1, keepdims=True) + 1e-05)
    return centre * factor, factor


def cut_first_kernel(sizes, scalars, w_qkv, w_out, a_qkv, a_out, a_gu, b_out, b_down, b_qkv, out, sems):
    share, quarter, width = sizes
    chip, core = scalars[0], scalars[1]
    seat = chip * 2 + core
    pairs = []
    for part in range(3):
        for i in range(2):
            column = pl.multiple_of(part * width + (2 * core + i) * quarter + chip * LANES, LANES)
            k = part * 2 + i
            pairs.append(
                (w_qkv.at[:, pl.ds(column, LANES)], out.at[:quarter, k * LANES : (k + 1) * LANES])
            )
    rows = pl.ds(pl.multiple_of(seat * share, share), share)
    small = slice(quarter, quarter + share)
    pairs.append((a_qkv.at[rows], out.at[small, :384]))
    pairs.append((a_gu.at[rows], out.at[small, 384:640]))
    pairs.append((a_out.at[rows], out.at[small, 640:768]))
    low = pl.ds(pl.multiple_of(seat * 16, 16), 16)
    at = quarter + share
    pairs.append((b_out.at[low], out.at[at : at + 16, :512]))
    pairs.append((b_down.at[low], out.at[at + 16 : at + 32, :512]))
    column = pl.ds(pl.multiple_of(chip * LANES, LANES), LANES)
    for k in range(12):
        here = pl.ds(pl.multiple_of(core * 192 + k * 16, 16), 16)
        row, lane = up_slot(k)
        row += at
        pairs.append((b_qkv.at[here, column], out.at[row : row + 16, lane : lane + LANES]))
    at += 32
    for k in range(16):
        row, lane = at + (k // 6) * share, (k % 6) * LANES
        pairs.append(
            (w_out.at[rows, k * LANES : (k + 1) * LANES], out.at[row : row + share, lane : lane + LANES])
        )
    copies(pairs, sems)


def up_slot(k):
    row = (k // 2) * 16 if k < 4 else 32 + 2 * 64 + ((k - 4) // 2) * 16
    return row, 512 + (k % 2) * LANES


def cut_rest_kernel(sizes, scalars, w_gu, w_down, a_down, b_gu, down, *refs):
    ff, ff_z, ff_dev, width = sizes
    parts, sems = refs[:-1], refs[-1]
    seat = scalars[0] * 2 + scalars[1]
    rows = pl.ds(pl.multiple_of(seat * ff_dev, ff_dev), ff_dev)
    wide = width + LANES
    pairs = [
        (w_down.at[rows], down.at[:, :width]),
        (a_down.at[rows], down.at[:, width:wide]),
        (b_gu.at[:, rows], down.at[:, wide : wide + ff_dev]),
    ]
    for zs, gu in zip(CHUNKS, parts):
        for half in range(2):
            for i, z in enumerate(zs):
                column = pl.multiple_of(half * ff + z * ff_z + seat * ff_dev, ff_dev)
                k = half * len(zs) + i
                pairs.append(
                    (w_gu.at[:, pl.ds(column, ff_dev)], gu.at[:, k * ff_dev : (k + 1) * ff_dev])
                )
    copies(pairs, sems)


def unpack_small_kernel(share, quarter, scalars, *refs):
    pieces = refs[:16]
    a_qkv, a_gu, a_out, b_out, b_down = refs[16:]
    chip, core = scalars[0], scalars[1]
    for k in range(2):
        for at, (rel, half) in enumerate(HALVES):
            piece = pieces[8 * k + at]
            tall = piece.shape[0] // 2
            seat = (chip ^ rel) * 2 + (core if k == 0 else 1 - core)
            for i in range(2):
                z = half * 2 + i
                rows = slice(i * tall, i * tall + share)
                there = pl.ds(pl.multiple_of(z * quarter + seat * share, share), share)
                a_qkv[there, :] = piece[rows, :384]
                a_gu[there, :] = piece[rows, 384:640]
                a_out[there, :] = piece[rows, 640:768]
                there = pl.ds(pl.multiple_of(seat * 16, 16), 16)
                columns = slice(z * quarter, (z + 1) * quarter)
                row = i * tall + share
                b_out[there, columns] = piece[row : row + 16, :512]
                b_down[there, columns] = piece[row + 16 : row + 32, :512]


def unpack_out_kernel(share, quarter, scalars, *refs):
    pieces, out, sems = refs[:16], refs[16], refs[17]
    chip, core = scalars[0], scalars[1]
    pairs = []
    for k in range(2):
        for at, (rel, half) in enumerate(HALVES):
            seat = (chip ^ rel) * 2 + (core if k == 0 else 1 - core)
            for i in range(2):
                there = pl.ds(pl.multiple_of((half * 2 + i) * quarter + seat * share, share), share)
                for block in range(3):
                    row = (i * 3 + block) * share
                    lanes = min(768, out.shape[1] - block * 768)
                    pairs.append(
                        (
                            pieces[8 * k + at].at[row : row + share, :lanes],
                            out.at[there, block * 768 : block * 768 + lanes],
                        )
                    )
    copies(pairs, sems)


def norm_kernel(scalars, tokens, first, second):
    value, _ = normed(tokens[...].astype(F32))
    half = first.shape[0]
    first[...] = value[:half].astype(BF)
    second[...] = value[half:].astype(BF)


def qkv_kernel(scalars, *refs):
    pieces, gathered = refs[:16], refs[16]
    down, up, cosine, sine, out, latents, weight, rows_all, sems = refs[17:]
    chip, core = scalars[0], scalars[1]
    half = pieces[0].shape[0]
    quarter = weight.shape[0] // 4
    tall = gathered.shape[0] // 4
    pairs = [
        (gathered.at[pl.ds(z * tall, quarter)], weight.at[pl.ds(z * quarter, quarter)]) for z in range(4)
    ]
    for k in range(2):
        for at, (rel, part) in enumerate(HALVES):
            seat = (chip ^ rel) * 2 + (core if k == 0 else 1 - core)
            there = pl.ds(pl.multiple_of((seat * 2 + part) * half, half), half)
            pairs.append((pieces[8 * k + at], rows_all.at[there]))
    copies(pairs, sems)
    step = 512
    span = up.shape[1]
    for start in range(0, rows_all.shape[0], step):
        here = slice(start, start + step)
        value = rows_all[here, :]
        mask = adapter_mask(scalars, rows_from(start, step))
        latent = dot(value, down[...]).astype(BF) * jnp.concatenate([mask] * 3, axis=1).astype(BF)
        latents[here, :] = latent
        pre = dot(value, weight[...])
        for part in range(3):
            block = pre[:, part * span : (part + 1) * span] + dot(
                latent[:, part * LANES : (part + 1) * LANES], up[part * LANES : (part + 1) * LANES, :]
            )
            if part < 2:
                heads = []
                for k in range(span // HEAD_DIM):
                    head = block[:, k * HEAD_DIM : (k + 1) * HEAD_DIM]
                    heads.append(
                        head * cosine[here, :] + pltpu.roll(head, HEAD_DIM // 2, 1) * sine[here, :]
                    )
                block = jnp.concatenate(heads, axis=1)
            out[here, part * span : (part + 1) * span] = block.astype(BF)


def allowed_pairs(scalars, first_row, rows, width):
    row = rows_from(first_row, rows)
    column = lax.broadcasted_iota(jnp.int32, (1, width), 1)
    return (column <= row) & (column >= doc_begin(scalars, row))


def attend_kernel(rows, scalars, query, key, value, out, lse):
    scale = HEAD_DIM**-0.5
    for start in range(0, query.shape[0], rows):
        here = slice(start, start + rows)
        width = start + rows
        scores = inner(query[here, :], key[:width, :], 1, 1) * scale
        scores = jnp.where(allowed_pairs(scalars, start, rows, width), scores, -1e30)
        top = jnp.max(scores, axis=1, keepdims=True)
        expd = jnp.exp(scores - top)
        total = jnp.sum(expd, axis=1, keepdims=True)
        probs = (expd * (1.0 / total)).astype(BF)
        out[here, :] = dot(probs, value[:width, :]).astype(BF)
        lse[here, :] = jnp.broadcast_to(top + jnp.log(total), (rows, LANES))


def attend_back_kernel(
    rows, scalars, query, key, value, grad, lse, latents, cosine, sine, own, other, ups,
    dq_all, dk_sum, dv_sum,
):
    dk_sum[...] = jnp.zeros_like(dk_sum)
    dv_sum[...] = jnp.zeros_like(dv_sum)
    scale = HEAD_DIM**-0.5
    length = query.shape[0]
    for start in range(0, length, rows):
        here = slice(start, start + rows)
        width = start + rows
        this_query = query[here, :]
        upstream = grad[here, :]
        scores = inner(this_query, key[:width, :], 1, 1) * scale
        probs = jnp.where(
            allowed_pairs(scalars, start, rows, width), jnp.exp(scores - lse[here, :1]), 0.0
        )
        prob_grad = inner(upstream, value[:width, :], 1, 1)
        delta = jnp.sum(prob_grad * probs, axis=1, keepdims=True)
        score_grad = (probs * (prob_grad - delta)).astype(BF)
        dq_all[here, :] = dot(score_grad, key[:width, :]) * scale
        dk_sum[:width, :] += inner(score_grad, this_query, 0, 0)
        dv_sum[:width, :] += inner(probs.astype(BF), upstream, 0, 0)

    chip, core = scalars[0], scalars[1]
    half = own.shape[1] // 8
    for part, total in enumerate((dq_all, dk_sum, dv_sum)):
        for start in range(0, length, 512):
            here = slice(start, start + 512)
            if part == 0:
                raw = total[here, :].astype(BF).astype(F32)
            elif part == 1:
                raw = (total[here, :] * scale).astype(BF).astype(F32)
            else:
                raw = total[here, :]
            if part < 2:
                raw = raw * cosine[here, :] - pltpu.roll(raw, HEAD_DIM // 2, 1) * sine[here, :]
            total[here, :] = raw.astype(BF).astype(F32)
        low = total[...].astype(BF)
        ups[part] = inner(latents[:, part * LANES : (part + 1) * LANES], low, 0, 0)
        for k, target in enumerate((own, other)):
            for at, (rel, h) in enumerate(HALVES):
                seat = (chip ^ rel) * 2 + (core if k == 0 else 1 - core)
                there = pl.ds(pl.multiple_of((seat * 2 + h) * half, half), half)
                target[part, at * half : (at + 1) * half, :] = total[there, :].astype(BF)


def head_order(k):
    return (k % CHIPS) * CHIPS + k // CHIPS


def out_kernel(scalars, mixed, weight, down, up, tokens, second, first_half, second_half, latents, natural):
    for k in range(16):
        at = head_order(k)
        natural[:, k * LANES : (k + 1) * LANES] = mixed[:, at * LANES : (at + 1) * LANES]
    rows = tokens.shape[0]
    seat = scalars[0] * 2 + scalars[1]
    mask = adapter_mask(scalars, rows_from(seat * rows, rows)).astype(BF)
    value = natural[...]
    latent = dot(value, down[...]).astype(BF) * mask
    latents[...] = latent
    total = tokens[...].astype(F32) + (dot(value, weight[...]) + dot(latent, up[...]))
    second[...] = total
    norm, _ = normed(total)
    first_half[...] = norm[: rows // 2].astype(BF)
    second_half[...] = norm[rows // 2 :].astype(BF)


def ff_kernel(begin, last, sides, first_z, scalars, *refs):
    if begin:
        select, a_gu, b_down = refs[:3]
        count = 3
    else:
        z_gu_in, dz_down_in = refs[:2]
        count = 2
    weights = [refs[count + 2 * k : count + 2 * k + 2] for k in range(sides)]
    count += 2 * sides
    norm, cot = refs[count : count + 4], refs[count + 4 : count + 8]
    count += 8
    if not begin:
        sums_in = refs[count]
        count += 1
    outs = refs[count : count + (2 if last else 1)]
    count += len(outs)
    results = [refs[count + 2 * k : count + 2 * k + 2] for k in range(sides)]
    count += 2 * sides
    if begin:
        z_gu_out, dz_down_out = refs[count : count + 2]
        count += 2
    rows_in, cot_in, sums, sems = refs[count : count + 4]
    held = [refs[count + 4 + 2 * k : count + 6 + 2 * k] for k in range(sides)]
    rows, width = rows_in.shape
    wide = width + LANES
    own_ff = weights[0][1].shape[0] // 4
    many = held[0][1].shape[0] // own_ff
    part = pl.ds(first_z * own_ff, many * own_ff)
    low = rows // 4
    pairs = [(norm[k], rows_in.at[pl.ds(k * low, low)]) for k in range(4)]
    pairs.append((weights[0][0], held[0][0]))
    pairs += [(cot[k], cot_in.at[pl.ds(k * low, low)]) for k in range(4)]
    pairs.append((weights[0][1].at[part], held[0][1]))
    if sides == 2:
        pairs += [(weights[1][0], held[1][0]), (weights[1][1].at[part], held[1][1])]
    if not begin:
        pairs.append((sums_in, sums))
    loads = [pltpu.make_async_copy(x, y, sems.at[k]) for k, (x, y) in enumerate(pairs)]
    for load in loads:
        load.start()
    for load in loads[:4]:
        load.wait()
    if begin:
        mask = select[...]
        z_gu = dot(rows_in[...], a_gu[...]).astype(BF) * jnp.concatenate([mask, mask], axis=1)
        z_gu_out[...] = z_gu
    else:
        z_gu, dz_down = z_gu_in[...], dz_down_in[...]
    z_gate, z_up = z_gu[:, :LANES], z_gu[:, LANES:]
    norm_grad = 0.0
    latent_grad = 0.0
    for side, (gu, down) in enumerate(held):
        size = gu.shape[1] // 2
        loads[4 if side == 0 else 10].wait()
        both = dot(rows_in[...], gu[...])
        if side == 0:
            for load in loads[5:9]:
                load.wait()
            if begin:
                dz_down = (inner(cot_in[...], b_down[...], 1, 1) * mask.astype(F32)).astype(BF)
                dz_down_out[...] = dz_down
        loads[9 if side == 0 else 11].wait()
        up_gate = jnp.concatenate(
            [down[i * own_ff : i * own_ff + LANES, wide:] for i in range(many)], axis=1
        )
        up_up = jnp.concatenate(
            [down[i * own_ff + LANES : i * own_ff + 2 * LANES, wide:] for i in range(many)], axis=1
        )
        gate = both[:, :size] + dot(z_gate, up_gate)
        upper = both[:, size:] + dot(z_up, up_up)
        sigma = 1.0 / (1.0 + jnp.exp(-gate))
        active = gate * sigma
        results[side][0][...] = (active * upper).astype(BF)
        hidden_grad = inner(cot_in[...], down[:, :width], 1, 1) + inner(
            dz_down, down[:, width:wide], 1, 1
        )
        grads = results[side][1]
        grads[:, :size] = (hidden_grad * upper * sigma * (1.0 + gate * (1.0 - sigma))).astype(BF)
        grads[:, size:] = (hidden_grad * active).astype(BF)
        norm_grad += inner(grads[...], gu[...], 1, 1)
        latent_grad += jnp.concatenate(
            [inner(grads[:, :size], up_gate, 1, 1), inner(grads[:, size:], up_up, 1, 1)], axis=1
        )
    if begin:
        outs[0][:, :width] = norm_grad
        outs[0][:, width:] = latent_grad
        return
    loads[-1].wait()
    if not last:
        outs[0][:, :width] = norm_grad + sums[:, :width]
        outs[0][:, width:] = latent_grad + sums[:, width:]
        return
    low = rows // 2
    for k in range(2):
        at = slice(k * low, (k + 1) * low)
        kind = outs[k].dtype
        outs[k][:, :width] = (norm_grad[at] + sums[at, :width]).astype(kind)
        outs[k][:, width:] = (latent_grad[at] + sums[at, width:]).astype(kind)


def down_kernel(begin, scalars, hidden_own, hidden_oth, down_own, down_oth, *refs):
    outs = refs if begin else refs[1:]
    wide = outs[0].shape[1]
    total = dot(hidden_own[...], down_own[:, :wide]) + dot(hidden_oth[...], down_oth[:, :wide])
    if not begin:
        total += refs[0][...]
    rows = outs[0].shape[0]
    for k, out in enumerate(outs):
        out[...] = total[k * rows : (k + 1) * rows].astype(out.dtype)


def spread_kernel(places, scalars, *refs):
    pieces, outs = [*refs[:4], *(refs[4].at[k] for k in range(4))], refs[5:]
    for k, piece in enumerate(pieces):
        chip = scalars[0] ^ (k % 4)
        core = scalars[1] if k < 4 else 1 - scalars[1]
        seat = chip * 2 + core
        at = 0
        for out, (kind, rows, blocks) in zip(outs, places):
            for block in range(blocks):
                value = piece[at : at + rows, :].astype(F32)
                at += rows
                columns = pl.ds(block * LANES, LANES)
                if kind == "rows":
                    out[pl.ds(pl.multiple_of(seat * rows, rows), rows), columns] = value
                elif kind == "core rows":
                    row = pl.multiple_of(core * (CHIPS * rows) + chip * rows, rows)
                    out[pl.ds(row, rows), columns] = value
                elif kind == "columns":
                    column = pl.multiple_of((seat * blocks + block) * LANES, LANES)
                    out[:, pl.ds(column, LANES)] = value
                else:
                    row = pl.multiple_of(core * rows, rows)
                    out[pl.ds(row, rows), pl.ds(pl.multiple_of(chip * LANES, LANES), LANES)] = value


def ff_grads_kernel(scalars, *refs):
    z_gu, dz_down, results, keep, send = refs[:2], refs[2:4], refs[4:-2], refs[-2], refs[-1]
    at = 0
    for zs in CHUNKS:
        for out in (keep, send):
            gate, upper, down = 0.0, 0.0, 0.0
            for half in range(2):
                hidden, grads = results[at], results[at + 1]
                at += 2
                size = hidden.shape[1]
                gate += inner(z_gu[half][:, :LANES], grads[:, :size], 0, 0)
                upper += inner(z_gu[half][:, LANES:], grads[:, size:], 0, 0)
                down += inner(hidden[...], dz_down[half][...], 0, 0)
            own_ff = size // len(zs)
            rows = 2 * LANES
            blocks = own_ff // LANES
            for i, z in enumerate(zs):
                for k in range(blocks):
                    columns = slice(i * own_ff + k * LANES, i * own_ff + (k + 1) * LANES)
                    out[z, k * rows : k * rows + LANES, :] = gate[:, columns].astype(out.dtype)
                    out[z, k * rows + LANES : (k + 1) * rows, :] = upper[:, columns].astype(out.dtype)
                there = slice(blocks * rows, blocks * rows + own_ff)
                out[z, there, :] = down[i * own_ff : (i + 1) * own_ff].astype(out.dtype)


def other_grads_kernel(quarter, scalars, *refs):
    norm1, norm2, cot, mixed = refs[:8], refs[8:16], refs[16:24], refs[24:26]
    middle, last = refs[26:30], refs[30:34]
    up_qkv, keep, send, columns, all_gu, all_qkv, all_down, sems = refs[34:]
    half = norm1[0].shape[0]
    chip, core = scalars[0], scalars[1]
    pairs = []
    for k, source in enumerate((norm1, norm2, cot)):
        for z in range(4):
            column = pl.ds(pl.multiple_of(z * quarter + chip * LANES, LANES), LANES)
            for h in range(8):
                target = columns.at[k, h * half : (h + 1) * half, z * LANES : (z + 1) * LANES]
                pairs.append((source[h].at[:, column], target))
    loads = [pltpu.make_async_copy(x, y, sems.at[k]) for k, (x, y) in enumerate(pairs)]
    for load in loads:
        load.start()
    gu_wide, qkv_wide = all_gu.shape[1], all_qkv.shape[1]
    for k, (rel, h) in enumerate(HALVES):
        here, there = slice(h * half, (h + 1) * half), slice(k * half, (k + 1) * half)
        all_gu[there, :] = middle[rel][here, :gu_wide]
        all_qkv[there, :] = last[rel][here, :qkv_wide]
        all_down[there, :] = last[rel][here, qkv_wide:]

    def halves(z, at, value):
        rows = value.shape[0] // 2
        for k in range(2):
            piece = value[k * rows : (k + 1) * rows]

            @pl.when(core == k)
            def _():
                keep[z, at : at + rows, :] = piece

            @pl.when(core != k)
            def _():
                send[z, at : at + rows, :] = piece.astype(BF)

    def two_of_four(at, values):
        rows = values[0].shape[0] // 2
        for k in range(2):

            @pl.when(core == k)
            def _():
                for i in range(2):
                    here, there = 2 * k + i, 2 * (1 - k) + i
                    keep[here, at : at + rows, :] = values[i][k * rows : (k + 1) * rows]
                    send[here, at : at + rows, :] = values[i][(1 - k) * rows : (2 - k) * rows].astype(BF)
                    keep[there, at : at + rows, :] = jnp.zeros((rows, LANES), F32)
                    send[there, at : at + rows, :] = jnp.zeros((rows, LANES), BF)

    low = LANES // 2
    at = 3 * low
    rows = 2 * half
    for k, source in enumerate(mixed):
        total = 0.0
        for rel in range(4):
            here = pl.ds(pl.multiple_of(((chip ^ rel) * 2 + core) * rows, rows), rows)
            total += inner(source[here, :], middle[rel][:, gu_wide : gu_wide + LANES], 0, 0)
        first = 2 * (core if k == 0 else 1 - core)
        for i in range(2):
            halves(first + i, at, total[i * LANES : (i + 1) * LANES])
    at += low
    share = LANES // PLANE
    for z in range(4):
        for k in range(4):
            block = (z * 4 + k) // 2
            column = gu_wide + LANES + ((z * 4 + k) % 2) * LANES
            value = 0.0
            for rel in range(4):
                piece = middle[rel][block * 2 * share : (block + 1) * 2 * share, column : column + LANES]
                value = value + piece.astype(F32)
            halves(z, at + k * share, value)
    at += low
    at_b = at + 3 * low
    heads = [jnp.concatenate([up_qkv[part, :, i * LANES : (i + 1) * LANES] for part in range(3)], axis=0) for i in range(2)]
    two_of_four(at_b, heads)
    for load in loads:
        load.wait()
    value = inner(columns[1], all_gu[...], 0, 0)
    for z in range(4):
        for k in range(2):
            block = value[z * LANES : (z + 1) * LANES, k * LANES : (k + 1) * LANES]
            halves(z, k * low, block)
    value = inner(all_down[...], columns[2], 0, 0)
    for z in range(4):
        halves(z, 2 * low, value[:, z * LANES : (z + 1) * LANES])
    value = inner(columns[0], all_qkv[...], 0, 0)
    for z in range(4):
        for k in range(3):
            block = value[z * LANES : (z + 1) * LANES, k * LANES : (k + 1) * LANES]
            halves(z, at + k * low, block)


def along_line_kernel(scalars, keep, brought, mine, onward, sent):
    z = scalars[2]
    mine[...] = keep[z] + brought[z].astype(F32)
    onward[...] = keep[z ^ 2] + brought[z ^ 2].astype(F32)
    for k, other in enumerate((1, 3)):
        sent[k] = (keep[z ^ other] + brought[z ^ other].astype(F32)).astype(BF)


def keep_kernel(scalars, *refs):
    count = len(refs) // 2
    for source, target in zip(refs[:count], refs[count:]):
        target[...] = source[...]


def back_middle_kernel(
    scalars, own, by_x, by_y, got_y, got_x, second, cot, a_gu, w_out, a_out, b_out, z_out,
    grad, mixed_grad, pack_0, pack_1, pack_2, pack_3, w_held, sem,
):
    packs = (pack_0, pack_1, pack_2, pack_3)
    load = pltpu.make_async_copy(w_out, w_held, sem)
    load.start()
    rows, width = second.shape
    half = rows // 2
    upper = own[:half] + by_x[...].astype(F32) + got_y[...].astype(F32)
    lower = own[half:] + by_y[...].astype(F32) + got_x[...].astype(F32)
    wide = jnp.concatenate([upper, lower], axis=0)
    seat = scalars[0] * 2 + scalars[1]
    mask = adapter_mask(scalars, rows_from(seat * rows, rows))
    dz_gu = (wide[:, width:] * jnp.concatenate([mask, mask], axis=1)).astype(BF)
    upstream = wide[:, :width] + inner(dz_gu, a_gu[...], 1, 1)
    norm, factor = normed(second[...])
    total = cot[...].astype(F32) + norm_back(norm, factor, upstream)
    grad[...] = total
    low = total.astype(BF)
    dz_out = (inner(low, b_out[...], 1, 1) * mask).astype(BF)
    value = inner(z_out[...], low, 0, 0).astype(BF)
    load.wait()
    back = (inner(low, w_held[...], 1, 1) + inner(dz_out, a_out[...], 1, 1)).astype(BF)
    for k in range(16):
        at = head_order(k)
        mixed_grad[:, at * LANES : (at + 1) * LANES] = back[:, k * LANES : (k + 1) * LANES]
    share = value.shape[0] // PLANE
    at = dz_gu.shape[1] + LANES
    for pack in packs:
        pack[:, : dz_gu.shape[1]] = dz_gu
        pack[:, dz_gu.shape[1] : at] = dz_out
    for block in range(CHIPS):
        for core in range(2):
            row = (core * CHIPS + block) * share
            for rel, pack in enumerate(packs):

                @pl.when((scalars[0] ^ rel) == block)
                def _():
                    for k in range(PLANE):
                        there = slice(k * 2 * share + core * share, k * 2 * share + (core + 1) * share)
                        pack[there, at:] = value[row : row + share, k * 2 * LANES : (k + 1) * 2 * LANES]


def back_latent_kernel(scalars, own, other, up_own, up_oth, to_x, to_y, to_far, kept):
    half = kept.shape[0] // 2
    targets = {0: kept, 1: to_x, 2: to_y, 3: to_far}
    for part in range(3):
        at = slice(part * LANES, (part + 1) * LANES)
        value = inner(own[part], up_own[at, :], 1, 1) + inner(other[part], up_oth[at, :], 1, 1)
        for k, (rel, h) in enumerate(HALVES):
            target = targets[rel]
            target[h * half : (h + 1) * half, at] = value[k * half : (k + 1) * half].astype(target.dtype)


def back_qkv_kernel(scalars, own, other, w_own, w_oth, out_0, out_1):
    rows = out_0.shape[0]
    mine = jnp.concatenate([own[part] for part in range(3)], axis=1)
    theirs = jnp.concatenate([other[part] for part in range(3)], axis=1)
    value = inner(mine, w_own[...], 1, 1) + inner(theirs, w_oth[...], 1, 1)
    out_0[...] = value[:rows].astype(out_0.dtype)
    out_1[...] = value[rows:].astype(out_1.dtype)


def back_first_kernel(
    scalars, own, by_x, by_y, got_y, got_x, tokens, second_grad, dz_qkv, a_qkv, input_grad
):
    half = tokens.shape[0] // 2
    upper = own[:half] + by_x[...].astype(F32) + got_y[...].astype(F32)
    lower = own[half:] + by_y[...].astype(F32) + got_x[...].astype(F32)
    upstream = jnp.concatenate([upper, lower], axis=0) + inner(dz_qkv[...], a_qkv[...], 1, 1)
    norm, factor = normed(tokens[...].astype(F32))
    input_grad[...] = second_grad[...] + norm_back(norm, factor, upstream)


def scatter_rest(send_x, send_y, onward):
    half = onward.shape[0] // 2
    by_x, by_y = swap(send_x, 2), swap(send_y, 4)
    pass_y = (onward[:half] + by_x[half:].astype(F32)).astype(BF)
    pass_x = (onward[half:] + by_y[half:].astype(F32)).astype(BF)
    got_y, got_x = swap(pass_y, 4), swap(pass_x, 2)
    return by_x, by_y, got_y, got_x, (pass_y, pass_x)


def plane_shards(
    tokens, cotangent, starts, adapter_ids,
    w_qkv, w_out, w_gu, w_down, a_qkv, b_qkv, a_out, b_out, a_gu, b_gu, a_down, b_down,
):
    seat = lax.axis_index("seq")
    z_at = lax.axis_index("fsdp")
    z_count = lax.axis_size("fsdp")
    core = seat % 2
    chip = seat // 2
    rows, width = tokens.shape[1:]
    half = rows // 2
    group = CHIPS * rows
    length = rows * PLANE
    ff = w_gu.shape[1] // 2
    ff_z = ff // z_count
    ff_dev = ff_z // PLANE
    quarter = w_qkv.shape[0]
    latent = a_out.shape[1]
    heads_dev = width // HEAD_DIM // PLANE
    span = heads_dev * HEAD_DIM
    share = quarter // PLANE
    share_b = latent // PLANE
    wide_down = width + latent
    wide_gu = width + 2 * latent
    first = starts[0]
    chosen = adapter_ids[0]
    scalars = jnp.concatenate([jnp.stack([chip, core, z_at]).astype(jnp.int32), first, chosen])
    stream, cot_low = tokens[0], cotangent[0]

    norm_a, norm_b = call(
        norm_kernel, scalars, [stream], [whole_spec((rows, width))],
        [sds((half, width))] * 2, [whole_spec((half, width))] * 2,
    )
    tall_rows = quarter + share + 32 + 3 * share
    first_part = call(
        functools.partial(cut_first_kernel, (share, quarter, width)), scalars,
        [w_qkv, w_out, a_qkv, a_out, a_gu, b_out, b_down, b_qkv], [ANY] * 8,
        sds((tall_rows, 3 * span)), whole_spec((tall_rows, 3 * span)),
        scratch=[pltpu.SemaphoreType.DMA((39,))],
    )
    first_all = lax.all_gather(first_part, "fsdp", axis=0, tiled=True)
    gates = [len(zs) * 2 * ff_dev for zs in CHUNKS]
    down_part, *gu_parts = call(
        functools.partial(cut_rest_kernel, (ff, ff_z, ff_dev, width)), scalars,
        [w_gu, w_down, a_down, b_gu], [ANY] * 4,
        [sds((ff_dev, wide_down + ff_dev))] + [sds((quarter, n)) for n in gates],
        [whole_spec((ff_dev, wide_down + ff_dev))] + [whole_spec((quarter, n)) for n in gates],
        scratch=[pltpu.SemaphoreType.DMA((3 + 2 * z_count,))], ties=[first_part],
    )
    down_own = lax.all_gather(down_part, "fsdp", axis=0, tiled=True)
    gu_owns = [lax.all_gather(part, "fsdp", axis=0, tiled=True) for part in gu_parts]

    pieces1 = gather_halves(norm_a, norm_b)
    pieces1_oth = [swap(piece, 1) for piece in pieces1]


    cot_pieces = gather_halves(cot_low[:half], cot_low[half:])
    first_all = hold(first_all, [pieces1_oth[1], pieces1_oth[3], cot_pieces[1], cot_pieces[3]])
    by_z = first_all.reshape(z_count, tall_rows, 3 * span)

    def rows_of(start, count, z, many):
        return by_z[z : z + many, start : start + count].reshape(many * count, 3 * span)

    pieces_small = gather_halves(rows_of(quarter, share + 32, 0, 2), rows_of(quarter, share + 32, 2, 2))
    pieces_small += [swap(piece, 1) for piece in pieces_small]
    ups_qkv = jnp.concatenate(
        [by_z[:, quarter + share + row : quarter + share + row + 16, lane : lane + LANES] for row, lane in map(up_slot, range(12))],
        axis=1,
    )
    full_a_qkv, full_a_gu, full_a_out, full_b_out, full_b_down = call(
        functools.partial(unpack_small_kernel, share, quarter), scalars, pieces_small,
        [whole_spec((2 * share + 64, 3 * span))] * 16,
        [sds((width, 3 * latent)), sds((width, 2 * latent)), sds((width, latent))]
        + [sds((latent, width))] * 2,
        [whole_spec((width, 3 * latent)), whole_spec((width, 2 * latent)), whole_spec((width, latent))]
        + [whole_spec((latent, width))] * 2,
    )
    at = quarter + share + 32
    out_a, out_b = rows_of(at, 3 * share, 0, 2), rows_of(at, 3 * share, 2, 2)
    pieces_out = gather_halves(hold(out_a, [pieces_small[1]]), hold(out_b, [pieces_small[3]]))
    pieces_out += [swap(piece, 1) for piece in pieces_out]
    full_out = call(
        functools.partial(unpack_out_kernel, share, quarter), scalars, pieces_out, [ANY] * 16,
        sds((width, width)), whole_spec((width, width)), scratch=[pltpu.SemaphoreType.DMA((96,))],
    )
    ups_oth = swap(ups_qkv, 1)

    def qkv_up(piece):
        return piece.transpose(1, 0, 2).reshape(192, z_count * LANES)

    mine, theirs = qkv_up(ups_qkv), qkv_up(ups_oth)
    up_chip = jnp.where(
        core == 0, jnp.concatenate([mine, theirs], axis=0), jnp.concatenate([theirs, mine], axis=0)
    )
    up_own = take(up_chip, core * span, span, 1)
    up_oth = take(up_chip, (1 - core) * span, span, 1)

    all_places = jnp.arange(length, dtype=jnp.int32)
    all_begin, _ = doc_tables(all_places, first, chosen)
    cosine, sine = rope_tables(all_places - all_begin, HEAD_DIM)
    sign = jnp.where(jnp.arange(HEAD_DIM) < HEAD_DIM // 2, -1.0, 1.0)
    turn = sine * sign[None, :]
    rel = jnp.array([r for r, _ in HALVES], jnp.int32)
    part = jnp.array([h for _, h in HALVES], jnp.int32)
    group_places = ((((rel ^ chip) * 2 + core) * 2 + part) * half)[:, None] + jnp.arange(
        half, dtype=jnp.int32
    )
    _, group_which = doc_tables(group_places.reshape(-1), first, chosen)
    adapters_at = jnp.arange(latent, dtype=jnp.int32) // RANK
    group_select = (adapters_at[None, :] == group_which[:, None]).astype(BF)
    select = group_select[-rows:]

    qkv, z_qkv, qkv_own = call(
        qkv_kernel, scalars,
        pieces1 + pieces1_oth + [first_all, full_a_qkv, up_own, cosine, turn],
        [ANY] * 17
        + [
            whole_spec((width, 3 * latent)),
            whole_spec((3 * latent, span)), whole_spec((length, LANES)), whole_spec((length, LANES)),
        ],
        [sds((length, 3 * span)), sds((length, 3 * latent)), sds((width, 3 * span))],
        [whole_spec((length, 3 * span)), whole_spec((length, 3 * latent)), whole_spec((width, 3 * span))],
        scratch=[pltpu.VMEM((length, width), BF), pltpu.SemaphoreType.DMA((20,))],
        cost=(2 * length * width * (3 * span + 3 * latent), 20 * 2**20),
    )
    column = lambda k: pl.BlockSpec((length, LANES), lambda h, _: (0, k * heads_dev + h))
    mixed_h, log_sums = call(
        functools.partial(attend_kernel, rows), scalars, [qkv] * 3, [column(0), column(1), column(2)],
        [sds((length, span)), sds((length, span), F32)], [column(0), column(0)], grid=(heads_dev,),
        cost=(4 * heads_dev * length * length * HEAD_DIM, 8 * 2**20),
    )
    mixed = lax.all_to_all(mixed_h, "seq", split_axis=0, concat_axis=1, tiled=True)
    mixed_oth = swap(mixed_h, 1)
    square = whole_spec((width, width))
    tall = whole_spec((rows, width))
    second, norm_a, norm_b, z_out = call(
        out_kernel, scalars, [mixed, full_out, full_a_out, full_b_out, stream],
        [tall, square, whole_spec((width, latent)), whole_spec((latent, width)), tall],
        [sds((rows, width), F32), sds((half, width)), sds((half, width)), sds((rows, latent))],
        [tall, whole_spec((half, width)), whole_spec((half, width)), whole_spec((rows, latent))],
        scratch=[pltpu.VMEM((rows, width), BF)],
        cost=(2 * rows * width * width, 12 * 2**20), ties=[mixed_oth],
    )

    pieces2 = gather_halves(norm_a, norm_b)
    down_own = hold(down_own, [second])
    down_oth = swap(down_own, 1)
    step = group // 2

    HBM = pl.BlockSpec(memory_space=pltpu.HBM)
    size = len(CHUNKS[0]) * ff_dev
    latents = [None, None]

    def feed(place, weights, at, onward, last):
        begin = onward is None
        if begin:
            operands = [group_select, full_a_gu, full_b_down]
            specs = [
                pl.BlockSpec((step, latent), lambda *_: (at, 0)), whole_spec((width, 2 * latent)),
                whole_spec((latent, width)),
            ]
        else:
            operands = list(latents[at])
            specs = [whole_spec((step, 2 * latent)), whole_spec((step, latent))]
        for pair in weights:
            operands += pair
            specs += [HBM, HBM]
        operands += pieces2[4 * at : 4 * at + 4] + cot_pieces[4 * at : 4 * at + 4]
        specs += [ANY] * 8
        if not begin:
            operands.append(onward)
            specs.append(HBM)
        if last:
            shapes, outs = [sds((rows, wide_gu), (BF, F32)[at])] * 2, [whole_spec((rows, wide_gu))] * 2
        else:
            shapes, outs = [sds((step, wide_gu), F32)], [whole_spec((step, wide_gu))]
        more = [(step, size), (step, 2 * size)] * len(weights)
        if begin:
            more += [(step, 2 * latent), (step, latent)]
        shapes += [sds(shape) for shape in more]
        outs += [whole_spec(shape) for shape in more]
        return call(
            functools.partial(ff_kernel, begin, last, len(weights), CHUNKS[place][0]), scalars, operands,
            specs, shapes, outs,
            scratch=[pltpu.VMEM((step, width), BF)] * 2
            + [pltpu.VMEM((8, LANES) if begin else (step, wide_gu), F32), pltpu.SemaphoreType.DMA((13,))]
            + [pltpu.VMEM((width, 2 * size), BF), pltpu.VMEM((size, wide_down + ff_dev), BF)]
            * len(weights),
            cost=(step * 10 * width * size * len(weights), 26 * 2**20),
        )

    def down_half(place, at, kind, total, ties):
        weight = pl.BlockSpec((size, wide_down + ff_dev), lambda *_: (place, 0))
        begin = total is None
        operands = [results[place][0][at][0], results[place][1][at][0], down_own, down_oth]
        specs = [whole_spec((step, size))] * 2 + [weight] * 2
        if not begin:
            operands.append(total)
            specs.append(whole_spec((step, wide_down)))
        shape = (step, wide_down) if begin else (rows, wide_down)
        count = 1 if begin else 2
        return call(
            functools.partial(down_kernel, begin), scalars, operands, specs,
            [sds(shape, kind)] * count, [whole_spec(shape)] * count,
            cost=(2 * step * 4 * ff_dev * width, 12 * 2**20), ties=ties,
        )

    results = [[[None, None], [None, None]] for _ in CHUNKS]
    gu_own = hold(gu_owns[0], [pieces2[1], pieces2[3]])
    weights = [(gu_own, down_own), (swap(gu_own, 1), down_oth)]
    sums = []
    for at in range(2):
        total, *more = feed(0, weights, at, None, False)
        sums.append(total)
        results[0][0][at], results[0][1][at], latents[at] = more[:2], more[2:4], more[4:]
    down_first = [down_half(0, at, F32, None, [sums[1]])[0] for at in range(2)]
    gu_own = hold(gu_owns[1], sums + down_first)
    weights = [(gu_own, down_own), (swap(gu_own, 1), down_oth)]
    total, *results[1][0][0] = feed(1, weights[:1], 0, sums[0], False)
    send_x, send_y, *results[1][1][0] = feed(1, weights[1:], 0, total, True)
    pass_on, kept, *more = feed(1, weights, 1, sums[1], True)
    results[1][0][1], results[1][1][1] = more[:2], more[2:]
    by_x, by_y, got_y, got_x, passed = scatter_rest(send_x, send_y, pass_on)
    down_x, down_y = (hold(x, [got_y, got_x]) for x in down_half(1, 0, BF, down_first[0], passed))
    halfspec = lambda n: pl.BlockSpec((half, n), lambda *_: (0, 0))
    second_grad, mixed_grad, *packs = call(
        back_middle_kernel, scalars,
        [kept, by_x, by_y, got_y, got_x, second, cot_low, full_a_gu, full_out, full_a_out, full_b_out, z_out],
        [whole_spec((rows, wide_gu))] + [halfspec(wide_gu)] * 4
        + [
            tall, tall, whole_spec((width, 2 * latent)), ANY, whole_spec((width, latent)),
            whole_spec((latent, width)), whole_spec((rows, latent)),
        ],
        [
            sds((rows, width), F32), sds((rows, width)),
        ]
        + [sds((rows, 5 * latent))] * 4,
        [tall, tall] + [whole_spec((rows, 5 * latent))] * 4,
        scratch=[pltpu.VMEM((width, width), BF), pltpu.SemaphoreType.DMA],
        cost=(2 * rows * width * width, 16 * 2**20), ties=[down_x],
    )
    mixed_grad_h = lax.all_to_all(mixed_grad, "seq", split_axis=1, concat_axis=0, tiled=True)
    down_on, down_kept = down_half(1, 1, F32, down_first[1], [mixed_grad])

    def along_line(keep, send, ties):
        shape = keep.shape[1:]
        return call(
            along_line_kernel, scalars, [keep, swap(send, 1)], [whole_spec(keep.shape)] * 2,
            [sds(shape, F32)] * 2 + [sds((2, *shape))], [whole_spec(shape)] * 2 + [whole_spec((2, *shape))],
            ties=ties, cost=(2**20, 8 * 2**20),
        )

    def line_sum(mine, onward, sent, ties):
        brought = lax.ppermute(sent, "fsdp", [(i, i ^ 1) for i in range(z_count)])
        onward = (onward + brought[1].astype(F32)).astype(BF)
        far = lax.ppermute(onward, "fsdp", [(i, i ^ 2) for i in range(z_count)])
        mine = hold(mine, ties) if ties else mine
        return (mine + brought[0].astype(F32) + far.astype(F32)).astype(BF)

    def spread(mine, places, shapes, ties):
        plane = blocks_of(mine)
        plane.append(swap(jnp.stack(plane), 1))
        return call(
            functools.partial(spread_kernel, places), scalars, plane,
            [whole_spec(piece.shape) for piece in plane],
            [sds(shape, F32) for shape in shapes], [whole_spec(shape) for shape in shapes], ties=ties,
        )

    *down_by, down_passed = scatter_rest(down_x, down_y, down_on)
    middle = [packs[0]] + [swap(hold(packs[k], [mixed_grad_h]), 2 * k) for k in (1, 2, 3)]

    result = pl.BlockSpec((3, group, HEAD_DIM), lambda h, _: (0, 0, h))
    grads_a, grads_b, up_qkv = call(
        functools.partial(attend_back_kernel, rows), scalars,
        [qkv, qkv, qkv, mixed_grad_h, log_sums, z_qkv, cosine, turn],
        [column(0), column(1), column(2), column(0), column(0), whole_spec((length, 3 * latent))]
        + [whole_spec((length, LANES))] * 2,
        [sds((3, group, span))] * 2 + [sds((3, latent, span), F32)],
        [result, result, pl.BlockSpec((3, latent, HEAD_DIM), lambda h, _: (0, 0, h))],
        scratch=[pltpu.VMEM((length, HEAD_DIM), F32)] * 3, grid=(heads_dev,),
        cost=(10 * heads_dev * length * length * HEAD_DIM, 16 * 2**20), ties=down_passed,
    )
    grads_b = swap(grads_b, 1)
    qkv_oth = swap(qkv_own, 1)

    down_kept = hold(down_kept, [grads_a])
    upper = down_kept[:half] + down_by[0][:half].astype(F32) + down_by[2].astype(F32)
    lower = down_kept[half:] + down_by[1][:half].astype(F32) + down_by[3].astype(F32)
    wide = jnp.concatenate([upper, lower], axis=0)
    z_down = wide[:, width:].astype(BF) * select
    to_x, to_y, to_far, latent_kept = call(
        back_latent_kernel, scalars, [grads_a, grads_b, up_own, up_oth],
        [whole_spec((3, group, span))] * 2 + [whole_spec((3 * latent, span))] * 2,
        [sds((rows, 3 * latent))] * 3 + [sds((rows, 3 * latent), F32)],
        [whole_spec((rows, 3 * latent))] * 4,
        cost=(4 * group * span * 3 * latent, 4 * 2**20), ties=[z_down],
    )

    def back_qkv(at, kind, ties):
        part = pl.BlockSpec((3, step, span), lambda *_: (0, at, 0))
        return call(
            back_qkv_kernel, scalars, [grads_a, grads_b, qkv_own, qkv_oth],
            [part, part] + [whole_spec((width, 3 * span))] * 2,
            [sds((rows, width), kind)] * 2, [tall] * 2,
            cost=(2 * group * span * 3 * width, 12 * 2**20), ties=ties,
        )

    pass_on, kept = back_qkv(1, F32, [to_x, *middle[1:]])
    dz_qkv = latent_kept + swap(to_x, 2).astype(F32) + swap(to_y, 4).astype(F32)
    dz_qkv = (dz_qkv + swap(to_far, 6).astype(F32)) * jnp.tile(select, (1, 3)).astype(F32)
    both = jnp.concatenate([dz_qkv.astype(BF), z_down], axis=1)
    last = blocks_of(both)
    ff_rows = 2 * latent * (ff_dev // LANES) + ff_dev
    values = [one[k] for one in latents for k in range(1)] + [one[1] for one in latents]
    values += [value for chunk in results for side in chunk for one in side for value in one]
    ff_keep, ff_send = call(
        ff_grads_kernel, scalars, values, [whole_spec(value.shape) for value in values],
        [sds((z_count, ff_rows, LANES), F32), sds((z_count, ff_rows, LANES))],
        [whole_spec((z_count, ff_rows, LANES))] * 2, cost=(2**32, 12 * 2**20), ties=[kept, both],
    )
    send_x, send_y = back_qkv(0, BF, [*last[1:], ff_send])
    other_rows = 11 * LANES // 2
    keep, send = call(
        functools.partial(other_grads_kernel, quarter), scalars,
        [*pieces1, *pieces2, *cot_pieces, mixed_h, mixed_oth, *middle, *last, up_qkv],
        [ANY] * 24 + [whole_spec((length, span))] * 2 + [whole_spec((rows, 5 * latent))] * 4
        + [whole_spec((rows, 4 * latent))] * 4 + [whole_spec((3, latent, span))],
        [sds((z_count, other_rows, LANES), F32), sds((z_count, other_rows, LANES))],
        [whole_spec((z_count, other_rows, LANES))] * 2,
        scratch=[
            pltpu.VMEM((3, group, z_count * LANES), BF), pltpu.VMEM((group, 2 * latent), BF),
            pltpu.VMEM((group, 3 * latent), BF), pltpu.VMEM((group, latent), BF),
            pltpu.SemaphoreType.DMA((96,)),
        ],
        cost=(2 * group * 512 * 768, 8 * 2**20), ties=[send_x],
    )
    ff_mine, *ff_rest = along_line(ff_keep, ff_send, [keep])
    by_x, by_y, got_y, got_x, passed = scatter_rest(send_x, send_y, hold(pass_on, [keep]))
    input_grad = call(
        back_first_kernel, scalars,
        [kept, by_x, by_y, got_y, got_x, stream, second_grad, both, full_a_qkv],
        [tall] + [halfspec(width)] * 4
        + [tall, tall, pl.BlockSpec((rows, 3 * latent), lambda *_: (0, 0)), whole_spec((width, 3 * latent))],
        sds((rows, width), F32), tall,
        cost=(2 * rows * width * 3 * latent, 12 * 2**20),
    )
    activations = second + (wide[:, :width] + dot(hold(z_down, passed), full_b_down))
    ff_total = line_sum(ff_mine, *ff_rest, [activations])
    total = line_sum(*along_line(keep, send, []), [input_grad])
    g_b_gu, g_a_down = spread(
        ff_total, (("columns", 2 * latent, ff_dev // LANES), ("rows", ff_dev, 1)),
        [(2 * latent, ff_z), (ff_z, latent)], [],
    )
    low = LANES // 2
    g_a_gu, g_b_down, g_a_out, g_b_out, g_a_qkv, g_b_qkv = spread(
        total,
        (
            ("rows", low, 2), ("both", low, 1), ("rows", low, 1), ("core rows", share_b, z_count),
            ("rows", low, 3), ("both", 3 * low, 1),
        ),
        [
            (quarter, 2 * latent), (latent, quarter), (quarter, latent), (latent, quarter),
            (quarter, 3 * latent), (3 * latent, quarter),
        ],
        [g_b_gu],
    )

    return (
        activations[None], input_grad[None],
        g_a_qkv, g_b_qkv, g_a_out, g_b_out, g_a_gu, g_b_gu, g_a_down, g_b_down,
    )


def solution(mesh):
    placed = (
        P("fsdp", "seq", None),
        P("fsdp", "seq", None),
        P("fsdp", None),
        P("fsdp", None),
        P("fsdp", None),
        P("fsdp", None),
        P("fsdp", None),
        P("fsdp", None),
        P("fsdp", None),
        P(None, "fsdp"),
        P("fsdp", None),
        P(None, "fsdp"),
        P("fsdp", None),
        P(None, "fsdp"),
        P("fsdp", None),
        P(None, "fsdp"),
    )
    on_plane = mesh.shape["seq"] == PLANE and mesh.shape["fsdp"] == 4
    return jax.shard_map(
        plane_shards if on_plane else shards,
        mesh=mesh,
        in_specs=placed,
        out_specs=(
            P("fsdp", "seq", None),
            P("fsdp", "seq", None),
            P("fsdp", None),
            P(None, "fsdp"),
            P("fsdp", None),
            P(None, "fsdp"),
            P("fsdp", None),
            P(None, "fsdp"),
            P("fsdp", None),
            P(None, "fsdp"),
        ),
        check_vma=False,
    )
```

```python
import functools

import jax
import jax.numpy as jnp
from jax import lax
from jax.experimental import pallas as pl
from jax.experimental.pallas import tpu as pltpu
from jax.sharding import PartitionSpec as P

HEAD_DIM = 128
RANK = 16


def layer_norm(values):
    centre = values - jnp.mean(values, axis=-1, keepdims=True)
    spread = jnp.mean(centre * centre, axis=-1, keepdims=True)
    factor = lax.rsqrt(spread + 1e-05)
    return (centre * factor, factor)


def norm_back(normed, factor, upstream):
    upstream_mean = jnp.mean(upstream, axis=-1, keepdims=True)
    cross_mean = jnp.mean(upstream * normed, axis=-1, keepdims=True)
    return factor * (upstream - upstream_mean - normed * cross_mean)


def doc_tables(places, first, chosen):
    within = first[None, :] <= places[:, None]
    begin = jnp.max(jnp.where(within, first[None, :], 0), axis=1)
    latest = jnp.sum(within.astype(jnp.int32), axis=1) - 1
    doc_order = jnp.arange(first.shape[0], dtype=jnp.int32)
    which = jnp.sum(jnp.where(doc_order[None, :] == latest[:, None], chosen[None, :], 0), axis=1)
    return (begin, which)


def rope_tables(position, head_dim):
    freqs = 10000.0 ** (-(jnp.arange(0, head_dim, 2, dtype=jnp.float32) / head_dim))
    angles = position.astype(jnp.float32)[:, None] * freqs[None, :]
    cosine = jnp.concatenate([jnp.cos(angles), jnp.cos(angles)], axis=-1)
    sine = jnp.concatenate([jnp.sin(angles), jnp.sin(angles)], axis=-1)
    return (cosine, sine)


def rotate(values, cosine, sine):
    half_dim = values.shape[-1] // 2
    turned = jnp.concatenate([-values[..., half_dim:], values[..., :half_dim]], axis=-1)
    return values * cosine[:, None, :] + turned * sine[:, None, :]


def rotate_back(upstream, cosine, sine):
    half_dim = upstream.shape[-1] // 2
    scaled = upstream * sine[:, None, :]
    return upstream * cosine[:, None, :] + jnp.concatenate(
        [scaled[..., half_dim:], -scaled[..., :half_dim]], axis=-1
    )


def inner_rows(left, right):
    return lax.dot_general(
        left, right, (((0,), (0,)), ((), ())), preferred_element_type=jnp.float32
    )


def inner_cols(left, right):
    return lax.dot_general(
        left, right, (((1,), (1,)), ((), ())), preferred_element_type=jnp.float32
    )


def adapter_fwd(inputs, down, up, select, segments):
    latent = jnp.dot(inputs, down, preferred_element_type=jnp.float32).astype(
        jnp.bfloat16
    ) * jnp.tile(select, (1, segments))
    span = up.shape[0] // segments
    pieces = [
        jnp.dot(
            latent[:, seg * span : (seg + 1) * span],
            up[seg * span : (seg + 1) * span],
            preferred_element_type=jnp.float32,
        )
        for seg in range(segments)
    ]
    return (latent, jnp.concatenate(pieces, axis=1))


def adapter_back(inputs, latent, upstream, down, up, select, segments):
    span = up.shape[0] // segments
    out_span = up.shape[1]
    grad_up = jnp.concatenate(
        [
            inner_rows(
                latent[:, seg * span : (seg + 1) * span],
                upstream[:, seg * out_span : (seg + 1) * out_span],
            )
            for seg in range(segments)
        ],
        axis=0,
    )
    latent_grad = jnp.concatenate(
        [
            inner_cols(
                upstream[:, seg * out_span : (seg + 1) * out_span],
                up[seg * span : (seg + 1) * span],
            )
            for seg in range(segments)
        ],
        axis=1,
    )
    latent_grad = (latent_grad * jnp.tile(select, (1, segments)).astype(jnp.float32)).astype(
        jnp.bfloat16
    )
    grad_down = inner_rows(inputs, latent_grad)
    back = inner_cols(latent_grad, down)
    return (grad_down, grad_up, back)


def frozen_fwd(inputs, weight):
    return (
        jnp.dot(
            inputs,
            lax.all_gather(weight, "fsdp", axis=0, tiled=True),
            preferred_element_type=jnp.float32,
        ),
        weight,
    )


def frozen_bwd(upstream, weight):
    return inner_cols(upstream, lax.all_gather(weight, "fsdp", axis=0, tiled=True))


def attend(query_h, key_h, value_h, begin, head_dim):
    length, local_width = query_h.shape
    local_heads = local_width // head_dim
    block_rows = min(512, length)
    block_count = length // block_rows
    score_scale = head_dim ** (-0.5)
    query_all = query_h.reshape(length, local_heads, head_dim)
    key_all = key_h.reshape(length, local_heads, head_dim)
    value_all = value_h.reshape(length, local_heads, head_dim)
    key_places = jnp.arange(length, dtype=jnp.int32)

    def one_block(block_index):
        start = block_index * block_rows
        query_block = lax.dynamic_slice_in_dim(query_all, start, block_rows, 0)
        rows = start + jnp.arange(block_rows, dtype=jnp.int32)
        row_begin = lax.dynamic_slice_in_dim(begin, start, block_rows, 0)
        allowed = (key_places[None, :] <= rows[:, None]) & (
            key_places[None, :] >= row_begin[:, None]
        )
        scores = (
            jnp.einsum("qhd,khd->hqk", query_block, key_all, preferred_element_type=jnp.float32)
            * score_scale
        )
        scores = jnp.where(allowed[None], scores, -1e30)
        row_top = jnp.max(scores, axis=-1, keepdims=True)
        expd = jnp.exp(scores - row_top)
        row_total = jnp.sum(expd, axis=-1, keepdims=True)
        probs = (expd / row_total).astype(jnp.bfloat16)
        mixed = jnp.einsum("hqk,khd->qhd", probs, value_all, preferred_element_type=jnp.float32)
        return (
            mixed.astype(jnp.bfloat16).reshape(block_rows, local_width),
            (row_top + jnp.log(row_total))[..., 0],
        )

    outputs, log_sums = lax.map(one_block, jnp.arange(block_count, dtype=jnp.int32))
    return (outputs.reshape(length, local_width), log_sums)


def attend_back(query_h, key_h, value_h, grad_h, log_sums, begin, head_dim):
    length, local_width = query_h.shape
    local_heads = local_width // head_dim
    block_rows = min(512, length)
    block_count = length // block_rows
    score_scale = head_dim ** (-0.5)
    query_all = query_h.reshape(length, local_heads, head_dim)
    key_all = key_h.reshape(length, local_heads, head_dim)
    value_all = value_h.reshape(length, local_heads, head_dim)
    grad_all = grad_h.reshape(length, local_heads, head_dim)
    key_places = jnp.arange(length, dtype=jnp.int32)

    def step(carry, inputs):
        key_grad, value_grad = carry
        block_index, block_lse = inputs
        start = block_index * block_rows
        query_block = lax.dynamic_slice_in_dim(query_all, start, block_rows, 0)
        grad_block = lax.dynamic_slice_in_dim(grad_all, start, block_rows, 0)
        rows = start + jnp.arange(block_rows, dtype=jnp.int32)
        row_begin = lax.dynamic_slice_in_dim(begin, start, block_rows, 0)
        allowed = (key_places[None, :] <= rows[:, None]) & (
            key_places[None, :] >= row_begin[:, None]
        )
        scores = (
            jnp.einsum("qhd,khd->hqk", query_block, key_all, preferred_element_type=jnp.float32)
            * score_scale
        )
        probs = jnp.where(allowed[None], jnp.exp(scores - block_lse[..., None]), 0.0)
        probs_low = probs.astype(jnp.bfloat16)
        prob_grad = jnp.einsum(
            "qhd,khd->hqk", grad_block, value_all, preferred_element_type=jnp.float32
        )
        row_delta = jnp.sum(prob_grad * probs, axis=-1, keepdims=True)
        score_grad = (probs * (prob_grad - row_delta)).astype(jnp.bfloat16)
        query_grad = (
            jnp.einsum("hqk,khd->qhd", score_grad, key_all, preferred_element_type=jnp.float32)
            * score_scale
        )
        key_grad = (
            key_grad
            + jnp.einsum(
                "hqk,qhd->khd", score_grad, query_block, preferred_element_type=jnp.float32
            )
            * score_scale
        )
        value_grad = value_grad + jnp.einsum(
            "hqk,qhd->khd", probs_low, grad_block, preferred_element_type=jnp.float32
        )
        return (
            (key_grad, value_grad),
            query_grad.astype(jnp.bfloat16).reshape(block_rows, local_width),
        )

    empty = jnp.zeros((length, local_heads, head_dim), jnp.float32)
    (key_grad, value_grad), query_grad = lax.scan(
        step, (empty, empty), (jnp.arange(block_count, dtype=jnp.int32), log_sums)
    )
    return (
        query_grad.reshape(length, local_width),
        key_grad.astype(jnp.bfloat16).reshape(length, local_width),
        value_grad.astype(jnp.bfloat16).reshape(length, local_width),
    )


def shards(
    tokens,
    cotangent,
    starts,
    adapter_ids,
    w_qkv,
    w_out,
    w_gu,
    w_down,
    a_qkv,
    b_qkv,
    a_out,
    b_out,
    a_gu,
    b_gu,
    a_down,
    b_down,
):
    gathered = (
        lax.all_gather(a_qkv, "fsdp", axis=0, tiled=True),
        lax.all_gather(b_qkv, "fsdp", axis=1, tiled=True),
        lax.all_gather(a_out, "fsdp", axis=0, tiled=True),
        lax.all_gather(b_out, "fsdp", axis=1, tiled=True),
        lax.all_gather(a_gu, "fsdp", axis=0, tiled=True),
        lax.all_gather(b_gu, "fsdp", axis=1, tiled=True),
        lax.all_gather(a_down, "fsdp", axis=0, tiled=True),
        lax.all_gather(b_down, "fsdp", axis=1, tiled=True),
    )
    (
        full_a_qkv,
        full_b_qkv,
        full_a_out,
        full_b_out,
        full_a_gu,
        full_b_gu,
        full_a_down,
        full_b_down,
    ) = gathered
    stream = tokens[0].astype(jnp.float32)
    cot_low = cotangent[0]
    tok_count, width = stream.shape
    seq_count = lax.axis_size("seq")
    seq_place = lax.axis_index("seq")
    stream_len = tok_count * seq_count
    first = starts[0]
    chosen = adapter_ids[0]
    local_places = seq_place * tok_count + jnp.arange(tok_count, dtype=jnp.int32)
    local_begin, which = doc_tables(local_places, first, chosen)
    columns = jnp.arange(full_a_out.shape[1], dtype=jnp.int32) // RANK
    select = (columns[None, :] == which[:, None]).astype(jnp.bfloat16)
    cosine, sine = rope_tables(local_places - local_begin, HEAD_DIM)
    head_count = width // HEAD_DIM
    first_norm, first_factor = layer_norm(stream)
    first_low = first_norm.astype(jnp.bfloat16)
    latent_qkv, extra_qkv = adapter_fwd(first_low, full_a_qkv, full_b_qkv, select, 3)
    qkv_main, held_qkv = frozen_fwd(first_low, w_qkv)
    qkv = qkv_main + extra_qkv
    query_rot = (
        rotate(qkv[:, :width].reshape(tok_count, head_count, HEAD_DIM), cosine, sine)
        .reshape(tok_count, width)
        .astype(jnp.bfloat16)
    )
    key_rot = (
        rotate(qkv[:, width : 2 * width].reshape(tok_count, head_count, HEAD_DIM), cosine, sine)
        .reshape(tok_count, width)
        .astype(jnp.bfloat16)
    )
    value_low = qkv[:, 2 * width :].astype(jnp.bfloat16)
    query_h, key_h, value_h = (
        lax.all_to_all(query_rot, "seq", split_axis=1, concat_axis=0, tiled=True),
        lax.all_to_all(key_rot, "seq", split_axis=1, concat_axis=0, tiled=True),
        lax.all_to_all(value_low, "seq", split_axis=1, concat_axis=0, tiled=True),
    )
    all_begin, all_which = doc_tables(jnp.arange(stream_len, dtype=jnp.int32), first, chosen)
    mixed_h, log_sums = attend(query_h, key_h, value_h, all_begin, HEAD_DIM)
    mixed = lax.all_to_all(mixed_h, "seq", split_axis=0, concat_axis=1, tiled=True)
    latent_out, extra_out = adapter_fwd(mixed, full_a_out, full_b_out, select, 1)
    out_main, held_out = frozen_fwd(mixed, w_out)
    second = stream + (out_main + extra_out)
    second_norm, second_factor = layer_norm(second)
    second_low = second_norm.astype(jnp.bfloat16)
    latent_gu, extra_gu = adapter_fwd(second_low, full_a_gu, full_b_gu, select, 2)
    gu_main, held_gu = frozen_fwd(second_low, w_gu)
    gate_up = gu_main + extra_gu
    ff_width = gate_up.shape[1] // 2
    gate = gate_up[:, :ff_width]
    upper = gate_up[:, ff_width:]
    sigma = jax.nn.sigmoid(gate)
    active = gate * sigma
    hidden = (active * upper).astype(jnp.bfloat16)
    latent_down, extra_down = adapter_fwd(hidden, full_a_down, full_b_down, select, 1)
    down_main, held_down = frozen_fwd(hidden, w_down)
    activations = second + (down_main + extra_down)
    grad_a_down, grad_b_down, hidden_extra = adapter_back(
        hidden, latent_down, cot_low, full_a_down, full_b_down, select, 1
    )
    hidden_grad = frozen_bwd(cot_low, held_down) + hidden_extra
    gate_grad = (hidden_grad * upper * sigma * (1.0 + gate * (1.0 - sigma))).astype(jnp.bfloat16)
    upper_grad = (hidden_grad * active).astype(jnp.bfloat16)
    gate_up_grad = jnp.concatenate([gate_grad, upper_grad], axis=1)
    grad_a_gu, grad_b_gu, second_extra = adapter_back(
        second_low, latent_gu, gate_up_grad, full_a_gu, full_b_gu, select, 2
    )
    second_norm_grad = frozen_bwd(gate_up_grad, held_gu) + second_extra
    second_grad = cot_low.astype(jnp.float32) + norm_back(
        second_norm, second_factor, second_norm_grad
    )
    branch_grad = second_grad.astype(jnp.bfloat16)
    grad_a_out, grad_b_out, mixed_extra = adapter_back(
        mixed, latent_out, branch_grad, full_a_out, full_b_out, select, 1
    )
    mixed_grad = (frozen_bwd(branch_grad, held_out) + mixed_extra).astype(jnp.bfloat16)
    mixed_grad_h = lax.all_to_all(mixed_grad, "seq", split_axis=1, concat_axis=0, tiled=True)
    query_grad_h, key_grad_h, value_grad_h = attend_back(
        query_h, key_h, value_h, mixed_grad_h, log_sums, all_begin, HEAD_DIM
    )
    query_grad, key_grad, value_grad = (
        lax.all_to_all(query_grad_h, "seq", split_axis=0, concat_axis=1, tiled=True),
        lax.all_to_all(key_grad_h, "seq", split_axis=0, concat_axis=1, tiled=True),
        lax.all_to_all(value_grad_h, "seq", split_axis=0, concat_axis=1, tiled=True),
    )
    query_pre = (
        rotate_back(
            query_grad.astype(jnp.float32).reshape(tok_count, head_count, HEAD_DIM), cosine, sine
        )
        .reshape(tok_count, width)
        .astype(jnp.bfloat16)
    )
    key_pre = (
        rotate_back(
            key_grad.astype(jnp.float32).reshape(tok_count, head_count, HEAD_DIM), cosine, sine
        )
        .reshape(tok_count, width)
        .astype(jnp.bfloat16)
    )
    qkv_grad = jnp.concatenate([query_pre, key_pre, value_grad], axis=1)
    grad_a_qkv, grad_b_qkv, first_extra = adapter_back(
        first_low, latent_qkv, qkv_grad, full_a_qkv, full_b_qkv, select, 3
    )
    first_norm_grad = frozen_bwd(qkv_grad, held_qkv) + first_extra
    input_grad = second_grad + norm_back(first_norm, first_factor, first_norm_grad)
    grads = (
        grad_a_qkv,
        grad_b_qkv,
        grad_a_out,
        grad_b_out,
        grad_a_gu,
        grad_b_gu,
        grad_a_down,
        grad_b_down,
    )
    shard_dims = (0, 1, 0, 1, 0, 1, 0, 1)
    summed = lax.psum(
        (grads[0], grads[1], grads[2], grads[3], grads[4], grads[5], grads[6], grads[7]),
        ("seq", "fsdp"),
    )
    fsdp_place = lax.axis_index("fsdp")
    fsdp_count = lax.axis_size("fsdp")
    totals = tuple(
        (
            lax.dynamic_slice_in_dim(
                whole,
                fsdp_place * (whole.shape[along] // fsdp_count),
                whole.shape[along] // fsdp_count,
                along,
            )
            for whole, along in zip(summed, shard_dims)
        )
    )
    return (
        activations[None],
        input_grad[None],
        totals[0],
        totals[1],
        totals[2],
        totals[3],
        totals[4],
        totals[5],
        totals[6],
        totals[7],
    )


BF = jnp.bfloat16
F32 = jnp.float32
PLANE = 8
CHIPS = 4
LANES = 128
CHUNKS = ((0, 1), (2, 3))
HALVES = ((1, 0), (3, 0), (2, 1), (3, 1), (2, 0), (1, 1), (0, 0), (0, 1))
ANY = pl.BlockSpec(memory_space=pl.ANY)
ROOMY = 60 * 2**20
SMALL = 28 * 2**20


def swap(value, bits):
    return lax.ppermute(value, "seq", [(i, i ^ bits) for i in range(PLANE)])


def gather_halves(first, second):
    x_first, y_second = swap(first, 2), swap(second, 4)
    y_first, x_second = swap(first, 4), swap(second, 2)
    far_first, far_second = swap(y_first, 2), swap(x_second, 4)
    return [x_first, far_first, y_second, far_second, y_first, x_second, first, second]


def blocks_of(block):
    return [block, swap(block, 2), swap(block, 4), swap(block, 6)]


def dot(left, right):
    return jnp.dot(left, right, preferred_element_type=F32)


def inner(left, right, on_left, on_right):
    return lax.dot_general(
        left, right, (((on_left,), (on_right,)), ((), ())), preferred_element_type=F32
    )


def take(value, start, count, axis):
    return lax.dynamic_slice_in_dim(value, start, count, axis)


def whole_spec(shape):
    return pl.BlockSpec(shape, lambda *_: (0,) * len(shape))


def call(
    body, scalars, operands, specs, shapes, out_specs, scratch=(), grid=(1,), cost=None, ties=(), room=ROOMY
):
    count = len(operands)

    def run(*refs):
        inside = refs[: 1 + count] + refs[1 + count + len(ties) :]
        body(*inside)

    return pl.pallas_call(
        run,
        grid_spec=pltpu.PrefetchScalarGridSpec(
            num_scalar_prefetch=1,
            grid=grid,
            in_specs=list(specs) + [ANY] * len(ties),
            out_specs=out_specs,
            scratch_shapes=list(scratch),
        ),
        out_shape=shapes,
        compiler_params=pltpu.CompilerParams(vmem_limit_bytes=room),
        cost_estimate=None
        if cost is None
        else pl.CostEstimate(flops=cost[0], bytes_accessed=cost[1], transcendentals=0),
    )(scalars, *operands, *ties)


def hold(value, ties):
    return pl.pallas_call(
        lambda *refs: None,
        in_specs=[ANY] * (1 + len(ties)),
        out_specs=ANY,
        out_shape=sds(value.shape, value.dtype),
        input_output_aliases={0: 0},
    )(value, *ties)


def copies(pairs, sems):
    started = [
        pltpu.make_async_copy(source, target, sems.at[k]) for k, (source, target) in enumerate(pairs)
    ]
    for one in started:
        one.start()
    for one in started:
        one.wait()


def sds(shape, dtype=BF):
    return jax.ShapeDtypeStruct(shape, dtype)


def doc_begin(scalars, places):
    begin = jnp.zeros_like(places)
    for doc in range(4):
        begin = jnp.where(scalars[3 + doc] <= places, scalars[3 + doc], begin)
    return begin


def adapter_mask(scalars, places):
    which = jnp.zeros_like(places) + scalars[7]
    for doc in range(1, 4):
        which = jnp.where(scalars[3 + doc] <= places, scalars[7 + doc], which)
    column = lax.broadcasted_iota(jnp.int32, (1, LANES), 1) // RANK
    return (column == which).astype(F32)


def rows_from(first, count):
    return first + lax.broadcasted_iota(jnp.int32, (count, 1), 0)


def normed(values):
    centre = values - jnp.mean(values, axis=-1, keepdims=True)
    factor = lax.rsqrt(jnp.mean(centre * centre, axis=-1, keepdims=True) + 1e-05)
    return centre * factor, factor


def cut_first_kernel(sizes, scalars, w_qkv, w_out, a_qkv, a_out, a_gu, b_out, b_down, b_qkv, out, sems):
    share, quarter, width = sizes
    chip, core = scalars[0], scalars[1]
    seat = chip * 2 + core
    pairs = []
    for part in range(3):
        for i in range(2):
            column = pl.multiple_of(part * width + (2 * core + i) * quarter + chip * LANES, LANES)
            k = part * 2 + i
            pairs.append(
                (w_qkv.at[:, pl.ds(column, LANES)], out.at[:quarter, k * LANES : (k + 1) * LANES])
            )
    rows = pl.ds(pl.multiple_of(seat * share, share), share)
    small = slice(quarter, quarter + share)
    pairs.append((a_qkv.at[rows], out.at[small, :384]))
    pairs.append((a_gu.at[rows], out.at[small, 384:640]))
    pairs.append((a_out.at[rows], out.at[small, 640:768]))
    low = pl.ds(pl.multiple_of(seat * 16, 16), 16)
    at = quarter + share
    pairs.append((b_out.at[low], out.at[at : at + 16, :512]))
    pairs.append((b_down.at[low], out.at[at + 16 : at + 32, :512]))
    column = pl.ds(pl.multiple_of(chip * LANES, LANES), LANES)
    for k in range(12):
        here = pl.ds(pl.multiple_of(core * 192 + k * 16, 16), 16)
        row, lane = up_slot(k)
        row += at
        pairs.append((b_qkv.at[here, column], out.at[row : row + 16, lane : lane + LANES]))
    at += 32
    for k in range(16):
        row, lane = at + (k // 6) * share, (k % 6) * LANES
        pairs.append(
            (w_out.at[rows, k * LANES : (k + 1) * LANES], out.at[row : row + share, lane : lane + LANES])
        )
    copies(pairs, sems)


def up_slot(k):
    row = (k // 2) * 16 if k < 4 else 32 + 2 * 64 + ((k - 4) // 2) * 16
    return row, 512 + (k % 2) * LANES


def cut_rest_kernel(sizes, scalars, w_gu, w_down, a_down, b_gu, down, *refs):
    ff, ff_z, ff_dev, width = sizes
    parts, sems = refs[:-1], refs[-1]
    seat = scalars[0] * 2 + scalars[1]
    rows = pl.ds(pl.multiple_of(seat * ff_dev, ff_dev), ff_dev)
    wide = width + LANES
    pairs = [
        (w_down.at[rows], down.at[:, :width]),
        (a_down.at[rows], down.at[:, width:wide]),
        (b_gu.at[:, rows], down.at[:, wide : wide + ff_dev]),
    ]
    for zs, gu in zip(CHUNKS, parts):
        for half in range(2):
            for i, z in enumerate(zs):
                column = pl.multiple_of(half * ff + z * ff_z + seat * ff_dev, ff_dev)
                k = half * len(zs) + i
                pairs.append(
                    (w_gu.at[:, pl.ds(column, ff_dev)], gu.at[:, k * ff_dev : (k + 1) * ff_dev])
                )
    copies(pairs, sems)


def unpack_small_kernel(share, quarter, scalars, *refs):
    pieces = refs[:16]
    a_qkv, a_gu, a_out, b_out, b_down = refs[16:]
    chip, core = scalars[0], scalars[1]
    for k in range(2):
        for at, (rel, half) in enumerate(HALVES):
            piece = pieces[8 * k + at]
            tall = piece.shape[0] // 2
            seat = (chip ^ rel) * 2 + (core if k == 0 else 1 - core)
            for i in range(2):
                z = half * 2 + i
                rows = slice(i * tall, i * tall + share)
                there = pl.ds(pl.multiple_of(z * quarter + seat * share, share), share)
                a_qkv[there, :] = piece[rows, :384]
                a_gu[there, :] = piece[rows, 384:640]
                a_out[there, :] = piece[rows, 640:768]
                there = pl.ds(pl.multiple_of(seat * 16, 16), 16)
                columns = slice(z * quarter, (z + 1) * quarter)
                row = i * tall + share
                b_out[there, columns] = piece[row : row + 16, :512]
                b_down[there, columns] = piece[row + 16 : row + 32, :512]


def unpack_out_kernel(share, quarter, scalars, *refs):
    pieces, out, sems = refs[:16], refs[16], refs[17]
    chip, core = scalars[0], scalars[1]
    pairs = []
    for k in range(2):
        for at, (rel, half) in enumerate(HALVES):
            seat = (chip ^ rel) * 2 + (core if k == 0 else 1 - core)
            for i in range(2):
                there = pl.ds(pl.multiple_of((half * 2 + i) * quarter + seat * share, share), share)
                for block in range(3):
                    row = (i * 3 + block) * share
                    lanes = min(768, out.shape[1] - block * 768)
                    pairs.append(
                        (
                            pieces[8 * k + at].at[row : row + share, :lanes],
                            out.at[there, block * 768 : block * 768 + lanes],
                        )
                    )
    copies(pairs, sems)


def norm_kernel(scalars, tokens, first, second):
    value, _ = normed(tokens[...].astype(F32))
    half = first.shape[0]
    first[...] = value[:half].astype(BF)
    second[...] = value[half:].astype(BF)


def qkv_kernel(scalars, *refs):
    pieces, gathered = refs[:16], refs[16]
    down, up, cosine, sine, out, latents, weight, rows_all, sems = refs[17:]
    chip, core = scalars[0], scalars[1]
    half = pieces[0].shape[0]
    quarter = weight.shape[0] // 4
    tall = gathered.shape[0] // 4
    pairs = [
        (gathered.at[pl.ds(z * tall, quarter)], weight.at[pl.ds(z * quarter, quarter)]) for z in range(4)
    ]
    for k in range(2):
        for at, (rel, part) in enumerate(HALVES):
            seat = (chip ^ rel) * 2 + (core if k == 0 else 1 - core)
            there = pl.ds(pl.multiple_of((seat * 2 + part) * half, half), half)
            pairs.append((pieces[8 * k + at], rows_all.at[there]))
    copies(pairs, sems)
    step = 512
    span = up.shape[1]
    for start in range(0, rows_all.shape[0], step):
        here = slice(start, start + step)
        value = rows_all[here, :]
        mask = adapter_mask(scalars, rows_from(start, step))
        latent = dot(value, down[...]).astype(BF) * jnp.concatenate([mask] * 3, axis=1).astype(BF)
        latents[here, :] = latent
        pre = dot(value, weight[...])
        for part in range(3):
            block = pre[:, part * span : (part + 1) * span] + dot(
                latent[:, part * LANES : (part + 1) * LANES], up[part * LANES : (part + 1) * LANES, :]
            )
            if part < 2:
                heads = []
                for k in range(span // HEAD_DIM):
                    head = block[:, k * HEAD_DIM : (k + 1) * HEAD_DIM]
                    heads.append(
                        head * cosine[here, :] + pltpu.roll(head, HEAD_DIM // 2, 1) * sine[here, :]
                    )
                block = jnp.concatenate(heads, axis=1)
            out[here, part * span : (part + 1) * span] = block.astype(BF)


def allowed_pairs(scalars, first_row, rows, width):
    row = rows_from(first_row, rows)
    column = lax.broadcasted_iota(jnp.int32, (1, width), 1)
    return (column <= row) & (column >= doc_begin(scalars, row))


def attend_kernel(rows, scalars, query, key, value, out, lse):
    scale = HEAD_DIM**-0.5
    for start in range(0, query.shape[0], rows):
        here = slice(start, start + rows)
        width = start + rows
        scores = inner(query[here, :], key[:width, :], 1, 1) * scale
        scores = jnp.where(allowed_pairs(scalars, start, rows, width), scores, -1e30)
        top = jnp.max(scores, axis=1, keepdims=True)
        expd = jnp.exp(scores - top)
        total = jnp.sum(expd, axis=1, keepdims=True)
        probs = (expd * (1.0 / total)).astype(BF)
        out[here, :] = dot(probs, value[:width, :]).astype(BF)
        lse[here, :] = jnp.broadcast_to(top + jnp.log(total), (rows, LANES))


def attend_back_kernel(
    rows, scalars, query, key, value, grad, lse, latents, cosine, sine, own, other, ups,
    dq_all, dk_sum, dv_sum,
):
    dk_sum[...] = jnp.zeros_like(dk_sum)
    dv_sum[...] = jnp.zeros_like(dv_sum)
    scale = HEAD_DIM**-0.5
    length = query.shape[0]
    for start in range(0, length, rows):
        here = slice(start, start + rows)
        width = start + rows
        this_query = query[here, :]
        upstream = grad[here, :]
        scores = inner(this_query, key[:width, :], 1, 1) * scale
        probs = jnp.where(
            allowed_pairs(scalars, start, rows, width), jnp.exp(scores - lse[here, :1]), 0.0
        )
        prob_grad = inner(upstream, value[:width, :], 1, 1)
        delta = jnp.sum(prob_grad * probs, axis=1, keepdims=True)
        score_grad = (probs * (prob_grad - delta)).astype(BF)
        dq_all[here, :] = dot(score_grad, key[:width, :]) * scale
        dk_sum[:width, :] += inner(score_grad, this_query, 0, 0)
        dv_sum[:width, :] += inner(probs.astype(BF), upstream, 0, 0)

    chip, core = scalars[0], scalars[1]
    half = own.shape[1] // 8
    for part, total in enumerate((dq_all, dk_sum, dv_sum)):
        for start in range(0, length, 512):
            here = slice(start, start + 512)
            if part == 0:
                raw = total[here, :].astype(BF).astype(F32)
            elif part == 1:
                raw = (total[here, :] * scale).astype(BF).astype(F32)
            else:
                raw = total[here, :]
            if part < 2:
                raw = raw * cosine[here, :] - pltpu.roll(raw, HEAD_DIM // 2, 1) * sine[here, :]
            total[here, :] = raw.astype(BF).astype(F32)
        low = total[...].astype(BF)
        ups[part] = inner(latents[:, part * LANES : (part + 1) * LANES], low, 0, 0)
        for k, target in enumerate((own, other)):
            for at, (rel, h) in enumerate(HALVES):
                seat = (chip ^ rel) * 2 + (core if k == 0 else 1 - core)
                there = pl.ds(pl.multiple_of((seat * 2 + h) * half, half), half)
                target[part, at * half : (at + 1) * half, :] = total[there, :].astype(BF)


def head_order(k):
    return (k % CHIPS) * CHIPS + k // CHIPS


def out_kernel(scalars, mixed, weight, down, up, tokens, second, first_half, second_half, latents, natural):
    for k in range(16):
        at = head_order(k)
        natural[:, k * LANES : (k + 1) * LANES] = mixed[:, at * LANES : (at + 1) * LANES]
    rows = tokens.shape[0]
    seat = scalars[0] * 2 + scalars[1]
    mask = adapter_mask(scalars, rows_from(seat * rows, rows)).astype(BF)
    value = natural[...]
    latent = dot(value, down[...]).astype(BF) * mask
    latents[...] = latent
    total = tokens[...].astype(F32) + (dot(value, weight[...]) + dot(latent, up[...]))
    second[...] = total
    norm, _ = normed(total)
    first_half[...] = norm[: rows // 2].astype(BF)
    second_half[...] = norm[rows // 2 :].astype(BF)


def ff_kernel(begin, last, sides, first_z, scalars, *refs):
    if begin:
        select, a_gu, b_down = refs[:3]
        count = 3
    else:
        z_gu_in, dz_down_in = refs[:2]
        count = 2
    weights = [refs[count + 2 * k : count + 2 * k + 2] for k in range(sides)]
    count += 2 * sides
    norm, cot = refs[count : count + 4], refs[count + 4 : count + 8]
    count += 8
    if not begin:
        sums_in = refs[count]
        count += 1
    outs = refs[count : count + (2 if last else 1)]
    count += len(outs)
    results = [refs[count + 2 * k : count + 2 * k + 2] for k in range(sides)]
    count += 2 * sides
    if begin:
        z_gu_out, dz_down_out = refs[count : count + 2]
        count += 2
    rows_in, cot_in, sums, sems = refs[count : count + 4]
    held = [refs[count + 4 + 2 * k : count + 6 + 2 * k] for k in range(sides)]
    rows, width = rows_in.shape
    wide = width + LANES
    own_ff = weights[0][1].shape[0] // 4
    many = held[0][1].shape[0] // own_ff
    part = pl.ds(first_z * own_ff, many * own_ff)
    low = rows // 4
    pairs = [(norm[k], rows_in.at[pl.ds(k * low, low)]) for k in range(4)]
    pairs.append((weights[0][0], held[0][0]))
    pairs += [(cot[k], cot_in.at[pl.ds(k * low, low)]) for k in range(4)]
    pairs.append((weights[0][1].at[part], held[0][1]))
    if sides == 2:
        pairs += [(weights[1][0], held[1][0]), (weights[1][1].at[part], held[1][1])]
    if not begin:
        pairs.append((sums_in, sums))
    loads = [pltpu.make_async_copy(x, y, sems.at[k]) for k, (x, y) in enumerate(pairs)]
    for load in loads:
        load.start()
    for load in loads[:4]:
        load.wait()
    if begin:
        mask = select[...]
        z_gu = dot(rows_in[...], a_gu[...]).astype(BF) * jnp.concatenate([mask, mask], axis=1)
        z_gu_out[...] = z_gu
    else:
        z_gu, dz_down = z_gu_in[...], dz_down_in[...]
    z_gate, z_up = z_gu[:, :LANES], z_gu[:, LANES:]
    norm_grad = 0.0
    latent_grad = 0.0
    for side, (gu, down) in enumerate(held):
        size = gu.shape[1] // 2
        loads[4 if side == 0 else 10].wait()
        both = dot(rows_in[...], gu[...])
        if side == 0:
            for load in loads[5:9]:
                load.wait()
            if begin:
                dz_down = (inner(cot_in[...], b_down[...], 1, 1) * mask.astype(F32)).astype(BF)
                dz_down_out[...] = dz_down
        loads[9 if side == 0 else 11].wait()
        up_gate = jnp.concatenate(
            [down[i * own_ff : i * own_ff + LANES, wide:] for i in range(many)], axis=1
        )
        up_up = jnp.concatenate(
            [down[i * own_ff + LANES : i * own_ff + 2 * LANES, wide:] for i in range(many)], axis=1
        )
        gate = both[:, :size] + dot(z_gate, up_gate)
        upper = both[:, size:] + dot(z_up, up_up)
        sigma = 1.0 / (1.0 + jnp.exp(-gate))
        active = gate * sigma
        results[side][0][...] = (active * upper).astype(BF)
        hidden_grad = inner(cot_in[...], down[:, :width], 1, 1) + inner(
            dz_down, down[:, width:wide], 1, 1
        )
        grads = results[side][1]
        grads[:, :size] = (hidden_grad * upper * sigma * (1.0 + gate * (1.0 - sigma))).astype(BF)
        grads[:, size:] = (hidden_grad * active).astype(BF)
        norm_grad += inner(grads[...], gu[...], 1, 1)
        latent_grad += jnp.concatenate(
            [inner(grads[:, :size], up_gate, 1, 1), inner(grads[:, size:], up_up, 1, 1)], axis=1
        )
    if begin:
        outs[0][:, :width] = norm_grad
        outs[0][:, width:] = latent_grad
        return
    loads[-1].wait()
    if not last:
        outs[0][:, :width] = norm_grad + sums[:, :width]
        outs[0][:, width:] = latent_grad + sums[:, width:]
        return
    low = rows // 2
    for k in range(2):
        at = slice(k * low, (k + 1) * low)
        kind = outs[k].dtype
        outs[k][:, :width] = (norm_grad[at] + sums[at, :width]).astype(kind)
        outs[k][:, width:] = (latent_grad[at] + sums[at, width:]).astype(kind)


def down_kernel(begin, scalars, hidden_own, hidden_oth, down_own, down_oth, *refs):
    outs = refs if begin else refs[1:]
    wide = outs[0].shape[1]
    total = dot(hidden_own[...], down_own[:, :wide]) + dot(hidden_oth[...], down_oth[:, :wide])
    if not begin:
        total += refs[0][...]
    rows = outs[0].shape[0]
    for k, out in enumerate(outs):
        out[...] = total[k * rows : (k + 1) * rows].astype(out.dtype)


def spread_kernel(places, scalars, *refs):
    pieces, outs = [*refs[:4], *(refs[4].at[k] for k in range(4))], refs[5:]
    for k, piece in enumerate(pieces):
        chip = scalars[0] ^ (k % 4)
        core = scalars[1] if k < 4 else 1 - scalars[1]
        seat = chip * 2 + core
        at = 0
        for out, (kind, rows, blocks) in zip(outs, places):
            for block in range(blocks):
                value = piece[at : at + rows, :].astype(F32)
                at += rows
                columns = pl.ds(block * LANES, LANES)
                if kind == "rows":
                    out[pl.ds(pl.multiple_of(seat * rows, rows), rows), columns] = value
                elif kind == "core rows":
                    row = pl.multiple_of(core * (CHIPS * rows) + chip * rows, rows)
                    out[pl.ds(row, rows), columns] = value
                elif kind == "columns":
                    column = pl.multiple_of((seat * blocks + block) * LANES, LANES)
                    out[:, pl.ds(column, LANES)] = value
                else:
                    row = pl.multiple_of(core * rows, rows)
                    out[pl.ds(row, rows), pl.ds(pl.multiple_of(chip * LANES, LANES), LANES)] = value


def ff_grads_kernel(scalars, *refs):
    z_gu, dz_down, results, keep, send = refs[:2], refs[2:4], refs[4:-2], refs[-2], refs[-1]
    at = 0
    for zs in CHUNKS:
        for out in (keep, send):
            gate, upper, down = 0.0, 0.0, 0.0
            for half in range(2):
                hidden, grads = results[at], results[at + 1]
                at += 2
                size = hidden.shape[1]
                gate += inner(z_gu[half][:, :LANES], grads[:, :size], 0, 0)
                upper += inner(z_gu[half][:, LANES:], grads[:, size:], 0, 0)
                down += inner(hidden[...], dz_down[half][...], 0, 0)
            own_ff = size // len(zs)
            rows = 2 * LANES
            blocks = own_ff // LANES
            for i, z in enumerate(zs):
                for k in range(blocks):
                    columns = slice(i * own_ff + k * LANES, i * own_ff + (k + 1) * LANES)
                    out[z, k * rows : k * rows + LANES, :] = gate[:, columns].astype(out.dtype)
                    out[z, k * rows + LANES : (k + 1) * rows, :] = upper[:, columns].astype(out.dtype)
                there = slice(blocks * rows, blocks * rows + own_ff)
                out[z, there, :] = down[i * own_ff : (i + 1) * own_ff].astype(out.dtype)


def other_grads_kernel(quarter, scalars, *refs):
    norm1, norm2, cot, mixed = refs[:8], refs[8:16], refs[16:24], refs[24:26]
    middle, last = refs[26:30], refs[30:34]
    up_qkv, keep, send, columns, all_gu, all_qkv, all_down, sems = refs[34:]
    half = norm1[0].shape[0]
    chip, core = scalars[0], scalars[1]
    pairs = []
    for k, source in enumerate((norm1, norm2, cot)):
        for z in range(4):
            column = pl.ds(pl.multiple_of(z * quarter + chip * LANES, LANES), LANES)
            for h in range(8):
                target = columns.at[k, h * half : (h + 1) * half, z * LANES : (z + 1) * LANES]
                pairs.append((source[h].at[:, column], target))
    loads = [pltpu.make_async_copy(x, y, sems.at[k]) for k, (x, y) in enumerate(pairs)]
    for load in loads:
        load.start()
    gu_wide, qkv_wide = all_gu.shape[1], all_qkv.shape[1]
    for k, (rel, h) in enumerate(HALVES):
        here, there = slice(h * half, (h + 1) * half), slice(k * half, (k + 1) * half)
        all_gu[there, :] = middle[rel][here, :gu_wide]
        all_qkv[there, :] = last[rel][here, :qkv_wide]
        all_down[there, :] = last[rel][here, qkv_wide:]

    def halves(z, at, value):
        rows = value.shape[0] // 2
        for k in range(2):
            piece = value[k * rows : (k + 1) * rows]

            @pl.when(core == k)
            def _():
                keep[z, at : at + rows, :] = piece

            @pl.when(core != k)
            def _():
                send[z, at : at + rows, :] = piece.astype(BF)

    def two_of_four(at, values):
        rows = values[0].shape[0] // 2
        for k in range(2):

            @pl.when(core == k)
            def _():
                for i in range(2):
                    here, there = 2 * k + i, 2 * (1 - k) + i
                    keep[here, at : at + rows, :] = values[i][k * rows : (k + 1) * rows]
                    send[here, at : at + rows, :] = values[i][(1 - k) * rows : (2 - k) * rows].astype(BF)
                    keep[there, at : at + rows, :] = jnp.zeros((rows, LANES), F32)
                    send[there, at : at + rows, :] = jnp.zeros((rows, LANES), BF)

    low = LANES // 2
    at = 3 * low
    rows = 2 * half
    for k, source in enumerate(mixed):
        total = 0.0
        for rel in range(4):
            here = pl.ds(pl.multiple_of(((chip ^ rel) * 2 + core) * rows, rows), rows)
            total += inner(source[here, :], middle[rel][:, gu_wide : gu_wide + LANES], 0, 0)
        first = 2 * (core if k == 0 else 1 - core)
        for i in range(2):
            halves(first + i, at, total[i * LANES : (i + 1) * LANES])
    at += low
    share = LANES // PLANE
    for z in range(4):
        for k in range(4):
            block = (z * 4 + k) // 2
            column = gu_wide + LANES + ((z * 4 + k) % 2) * LANES
            value = 0.0
            for rel in range(4):
                piece = middle[rel][block * 2 * share : (block + 1) * 2 * share, column : column + LANES]
                value = value + piece.astype(F32)
            halves(z, at + k * share, value)
    at += low
    at_b = at + 3 * low
    heads = [jnp.concatenate([up_qkv[part, :, i * LANES : (i + 1) * LANES] for part in range(3)], axis=0) for i in range(2)]
    two_of_four(at_b, heads)
    for load in loads:
        load.wait()
    value = inner(columns[1], all_gu[...], 0, 0)
    for z in range(4):
        for k in range(2):
            block = value[z * LANES : (z + 1) * LANES, k * LANES : (k + 1) * LANES]
            halves(z, k * low, block)
    value = inner(all_down[...], columns[2], 0, 0)
    for z in range(4):
        halves(z, 2 * low, value[:, z * LANES : (z + 1) * LANES])
    value = inner(columns[0], all_qkv[...], 0, 0)
    for z in range(4):
        for k in range(3):
            block = value[z * LANES : (z + 1) * LANES, k * LANES : (k + 1) * LANES]
            halves(z, at + k * low, block)


def along_line_kernel(scalars, keep, brought, mine, onward, sent):
    z = scalars[2]
    mine[...] = keep[z] + brought[z].astype(F32)
    onward[...] = keep[z ^ 2] + brought[z ^ 2].astype(F32)
    for k, other in enumerate((1, 3)):
        sent[k] = (keep[z ^ other] + brought[z ^ other].astype(F32)).astype(BF)


def keep_kernel(scalars, *refs):
    count = len(refs) // 2
    for source, target in zip(refs[:count], refs[count:]):
        target[...] = source[...]


def back_middle_kernel(
    scalars, own, by_x, by_y, got_y, got_x, second, cot, a_gu, w_out, a_out, b_out, z_out,
    grad, mixed_grad, pack_0, pack_1, pack_2, pack_3, w_held, sem,
):
    packs = (pack_0, pack_1, pack_2, pack_3)
    load = pltpu.make_async_copy(w_out, w_held, sem)
    load.start()
    rows, width = second.shape
    half = rows // 2
    upper = own[:half] + by_x[...].astype(F32) + got_y[...].astype(F32)
    lower = own[half:] + by_y[...].astype(F32) + got_x[...].astype(F32)
    wide = jnp.concatenate([upper, lower], axis=0)
    seat = scalars[0] * 2 + scalars[1]
    mask = adapter_mask(scalars, rows_from(seat * rows, rows))
    dz_gu = (wide[:, width:] * jnp.concatenate([mask, mask], axis=1)).astype(BF)
    upstream = wide[:, :width] + inner(dz_gu, a_gu[...], 1, 1)
    norm, factor = normed(second[...])
    total = cot[...].astype(F32) + norm_back(norm, factor, upstream)
    grad[...] = total
    low = total.astype(BF)
    dz_out = (inner(low, b_out[...], 1, 1) * mask).astype(BF)
    value = inner(z_out[...], low, 0, 0).astype(BF)
    load.wait()
    back = (inner(low, w_held[...], 1, 1) + inner(dz_out, a_out[...], 1, 1)).astype(BF)
    for k in range(16):
        at = head_order(k)
        mixed_grad[:, at * LANES : (at + 1) * LANES] = back[:, k * LANES : (k + 1) * LANES]
    share = value.shape[0] // PLANE
    at = dz_gu.shape[1] + LANES
    for pack in packs:
        pack[:, : dz_gu.shape[1]] = dz_gu
        pack[:, dz_gu.shape[1] : at] = dz_out
    for block in range(CHIPS):
        for core in range(2):
            row = (core * CHIPS + block) * share
            for rel, pack in enumerate(packs):

                @pl.when((scalars[0] ^ rel) == block)
                def _():
                    for k in range(PLANE):
                        there = slice(k * 2 * share + core * share, k * 2 * share + (core + 1) * share)
                        pack[there, at:] = value[row : row + share, k * 2 * LANES : (k + 1) * 2 * LANES]


def back_latent_kernel(scalars, own, other, up_own, up_oth, to_x, to_y, to_far, kept):
    half = kept.shape[0] // 2
    targets = {0: kept, 1: to_x, 2: to_y, 3: to_far}
    for part in range(3):
        at = slice(part * LANES, (part + 1) * LANES)
        value = inner(own[part], up_own[at, :], 1, 1) + inner(other[part], up_oth[at, :], 1, 1)
        for k, (rel, h) in enumerate(HALVES):
            target = targets[rel]
            target[h * half : (h + 1) * half, at] = value[k * half : (k + 1) * half].astype(target.dtype)


def back_qkv_kernel(scalars, own, other, w_own, w_oth, out_0, out_1):
    rows = out_0.shape[0]
    mine = jnp.concatenate([own[part] for part in range(3)], axis=1)
    theirs = jnp.concatenate([other[part] for part in range(3)], axis=1)
    value = inner(mine, w_own[...], 1, 1) + inner(theirs, w_oth[...], 1, 1)
    out_0[...] = value[:rows].astype(out_0.dtype)
    out_1[...] = value[rows:].astype(out_1.dtype)


def back_first_kernel(
    scalars, own, by_x, by_y, got_y, got_x, tokens, second_grad, dz_qkv, a_qkv, input_grad
):
    half = tokens.shape[0] // 2
    upper = own[:half] + by_x[...].astype(F32) + got_y[...].astype(F32)
    lower = own[half:] + by_y[...].astype(F32) + got_x[...].astype(F32)
    upstream = jnp.concatenate([upper, lower], axis=0) + inner(dz_qkv[...], a_qkv[...], 1, 1)
    norm, factor = normed(tokens[...].astype(F32))
    input_grad[...] = second_grad[...] + norm_back(norm, factor, upstream)


def scatter_rest(send_x, send_y, onward):
    half = onward.shape[0] // 2
    by_x, by_y = swap(send_x, 2), swap(send_y, 4)
    pass_y = (onward[:half] + by_x[half:].astype(F32)).astype(BF)
    pass_x = (onward[half:] + by_y[half:].astype(F32)).astype(BF)
    got_y, got_x = swap(pass_y, 4), swap(pass_x, 2)
    return by_x, by_y, got_y, got_x, (pass_y, pass_x)


def plane_shards(
    tokens, cotangent, starts, adapter_ids,
    w_qkv, w_out, w_gu, w_down, a_qkv, b_qkv, a_out, b_out, a_gu, b_gu, a_down, b_down,
):
    seat = lax.axis_index("seq")
    z_at = lax.axis_index("fsdp")
    z_count = lax.axis_size("fsdp")
    core = seat % 2
    chip = seat // 2
    rows, width = tokens.shape[1:]
    half = rows // 2
    group = CHIPS * rows
    length = rows * PLANE
    ff = w_gu.shape[1] // 2
    ff_z = ff // z_count
    ff_dev = ff_z // PLANE
    quarter = w_qkv.shape[0]
    latent = a_out.shape[1]
    heads_dev = width // HEAD_DIM // PLANE
    span = heads_dev * HEAD_DIM
    share = quarter // PLANE
    share_b = latent // PLANE
    wide_down = width + latent
    wide_gu = width + 2 * latent
    first = starts[0]
    chosen = adapter_ids[0]
    scalars = jnp.concatenate([jnp.stack([chip, core, z_at]).astype(jnp.int32), first, chosen])
    stream, cot_low = tokens[0], cotangent[0]

    norm_a, norm_b = call(
        norm_kernel, scalars, [stream], [whole_spec((rows, width))],
        [sds((half, width))] * 2, [whole_spec((half, width))] * 2,
    )
    tall_rows = quarter + share + 32 + 3 * share
    first_part = call(
        functools.partial(cut_first_kernel, (share, quarter, width)), scalars,
        [w_qkv, w_out, a_qkv, a_out, a_gu, b_out, b_down, b_qkv], [ANY] * 8,
        sds((tall_rows, 3 * span)), whole_spec((tall_rows, 3 * span)),
        scratch=[pltpu.SemaphoreType.DMA((39,))],
    )
    first_all = lax.all_gather(first_part, "fsdp", axis=0, tiled=True)
    gates = [len(zs) * 2 * ff_dev for zs in CHUNKS]
    down_part, *gu_parts = call(
        functools.partial(cut_rest_kernel, (ff, ff_z, ff_dev, width)), scalars,
        [w_gu, w_down, a_down, b_gu], [ANY] * 4,
        [sds((ff_dev, wide_down + ff_dev))] + [sds((quarter, n)) for n in gates],
        [whole_spec((ff_dev, wide_down + ff_dev))] + [whole_spec((quarter, n)) for n in gates],
        scratch=[pltpu.SemaphoreType.DMA((3 + 2 * z_count,))], ties=[first_part],
    )
    down_own = lax.all_gather(down_part, "fsdp", axis=0, tiled=True)
    gu_owns = [lax.all_gather(part, "fsdp", axis=0, tiled=True) for part in gu_parts]

    pieces1 = gather_halves(norm_a, norm_b)
    pieces1_oth = [swap(piece, 1) for piece in pieces1]


    cot_pieces = gather_halves(cot_low[:half], cot_low[half:])
    first_all = hold(first_all, [pieces1_oth[1], pieces1_oth[3], cot_pieces[1], cot_pieces[3]])
    by_z = first_all.reshape(z_count, tall_rows, 3 * span)

    def rows_of(start, count, z, many):
        return by_z[z : z + many, start : start + count].reshape(many * count, 3 * span)

    pieces_small = gather_halves(rows_of(quarter, share + 32, 0, 2), rows_of(quarter, share + 32, 2, 2))
    pieces_small += [swap(piece, 1) for piece in pieces_small]
    ups_qkv = jnp.concatenate(
        [by_z[:, quarter + share + row : quarter + share + row + 16, lane : lane + LANES] for row, lane in map(up_slot, range(12))],
        axis=1,
    )
    full_a_qkv, full_a_gu, full_a_out, full_b_out, full_b_down = call(
        functools.partial(unpack_small_kernel, share, quarter), scalars, pieces_small,
        [whole_spec((2 * share + 64, 3 * span))] * 16,
        [sds((width, 3 * latent)), sds((width, 2 * latent)), sds((width, latent))]
        + [sds((latent, width))] * 2,
        [whole_spec((width, 3 * latent)), whole_spec((width, 2 * latent)), whole_spec((width, latent))]
        + [whole_spec((latent, width))] * 2,
    )
    at = quarter + share + 32
    out_a, out_b = rows_of(at, 3 * share, 0, 2), rows_of(at, 3 * share, 2, 2)
    pieces_out = gather_halves(hold(out_a, [pieces_small[1]]), hold(out_b, [pieces_small[3]]))
    pieces_out += [swap(piece, 1) for piece in pieces_out]
    full_out = call(
        functools.partial(unpack_out_kernel, share, quarter), scalars, pieces_out, [ANY] * 16,
        sds((width, width)), whole_spec((width, width)), scratch=[pltpu.SemaphoreType.DMA((96,))],
    )
    ups_oth = swap(ups_qkv, 1)

    def qkv_up(piece):
        return piece.transpose(1, 0, 2).reshape(192, z_count * LANES)

    mine, theirs = qkv_up(ups_qkv), qkv_up(ups_oth)
    up_chip = jnp.where(
        core == 0, jnp.concatenate([mine, theirs], axis=0), jnp.concatenate([theirs, mine], axis=0)
    )
    up_own = take(up_chip, core * span, span, 1)
    up_oth = take(up_chip, (1 - core) * span, span, 1)

    all_places = jnp.arange(length, dtype=jnp.int32)
    all_begin, _ = doc_tables(all_places, first, chosen)
    cosine, sine = rope_tables(all_places - all_begin, HEAD_DIM)
    sign = jnp.where(jnp.arange(HEAD_DIM) < HEAD_DIM // 2, -1.0, 1.0)
    turn = sine * sign[None, :]
    rel = jnp.array([r for r, _ in HALVES], jnp.int32)
    part = jnp.array([h for _, h in HALVES], jnp.int32)
    group_places = ((((rel ^ chip) * 2 + core) * 2 + part) * half)[:, None] + jnp.arange(
        half, dtype=jnp.int32
    )
    _, group_which = doc_tables(group_places.reshape(-1), first, chosen)
    adapters_at = jnp.arange(latent, dtype=jnp.int32) // RANK
    group_select = (adapters_at[None, :] == group_which[:, None]).astype(BF)
    select = group_select[-rows:]

    qkv, z_qkv, qkv_own = call(
        qkv_kernel, scalars,
        pieces1 + pieces1_oth + [first_all, full_a_qkv, up_own, cosine, turn],
        [ANY] * 17
        + [
            whole_spec((width, 3 * latent)),
            whole_spec((3 * latent, span)), whole_spec((length, LANES)), whole_spec((length, LANES)),
        ],
        [sds((length, 3 * span)), sds((length, 3 * latent)), sds((width, 3 * span))],
        [whole_spec((length, 3 * span)), whole_spec((length, 3 * latent)), whole_spec((width, 3 * span))],
        scratch=[pltpu.VMEM((length, width), BF), pltpu.SemaphoreType.DMA((20,))],
        cost=(2 * length * width * (3 * span + 3 * latent), 20 * 2**20),
    )
    column = lambda k: pl.BlockSpec((length, LANES), lambda h, _: (0, k * heads_dev + h))
    mixed_h, log_sums = call(
        functools.partial(attend_kernel, rows), scalars, [qkv] * 3, [column(0), column(1), column(2)],
        [sds((length, span)), sds((length, span), F32)], [column(0), column(0)], grid=(heads_dev,),
        cost=(4 * heads_dev * length * length * HEAD_DIM, 8 * 2**20),
    )
    mixed = lax.all_to_all(mixed_h, "seq", split_axis=0, concat_axis=1, tiled=True)
    mixed_oth = swap(mixed_h, 1)
    square = whole_spec((width, width))
    tall = whole_spec((rows, width))
    second, norm_a, norm_b, z_out = call(
        out_kernel, scalars, [mixed, full_out, full_a_out, full_b_out, stream],
        [tall, square, whole_spec((width, latent)), whole_spec((latent, width)), tall],
        [sds((rows, width), F32), sds((half, width)), sds((half, width)), sds((rows, latent))],
        [tall, whole_spec((half, width)), whole_spec((half, width)), whole_spec((rows, latent))],
        scratch=[pltpu.VMEM((rows, width), BF)],
        cost=(2 * rows * width * width, 12 * 2**20), ties=[mixed_oth],
    )

    pieces2 = gather_halves(norm_a, norm_b)
    down_own = hold(down_own, [second])
    down_oth = swap(down_own, 1)
    step = group // 2

    HBM = pl.BlockSpec(memory_space=pltpu.HBM)
    size = len(CHUNKS[0]) * ff_dev
    latents = [None, None]

    def feed(place, weights, at, onward, last):
        begin = onward is None
        if begin:
            operands = [group_select, full_a_gu, full_b_down]
            specs = [
                pl.BlockSpec((step, latent), lambda *_: (at, 0)), whole_spec((width, 2 * latent)),
                whole_spec((latent, width)),
            ]
        else:
            operands = list(latents[at])
            specs = [whole_spec((step, 2 * latent)), whole_spec((step, latent))]
        for pair in weights:
            operands += pair
            specs += [HBM, HBM]
        operands += pieces2[4 * at : 4 * at + 4] + cot_pieces[4 * at : 4 * at + 4]
        specs += [ANY] * 8
        if not begin:
            operands.append(onward)
            specs.append(HBM)
        if last:
            shapes, outs = [sds((rows, wide_gu), (BF, F32)[at])] * 2, [whole_spec((rows, wide_gu))] * 2
        else:
            shapes, outs = [sds((step, wide_gu), F32)], [whole_spec((step, wide_gu))]
        more = [(step, size), (step, 2 * size)] * len(weights)
        if begin:
            more += [(step, 2 * latent), (step, latent)]
        shapes += [sds(shape) for shape in more]
        outs += [whole_spec(shape) for shape in more]
        return call(
            functools.partial(ff_kernel, begin, last, len(weights), CHUNKS[place][0]), scalars, operands,
            specs, shapes, outs,
            scratch=[pltpu.VMEM((step, width), BF)] * 2
            + [pltpu.VMEM((8, LANES) if begin else (step, wide_gu), F32), pltpu.SemaphoreType.DMA((13,))]
            + [pltpu.VMEM((width, 2 * size), BF), pltpu.VMEM((size, wide_down + ff_dev), BF)]
            * len(weights),
            cost=(step * 10 * width * size * len(weights), 26 * 2**20),
        )

    def down_half(place, at, kind, total, ties):
        weight = pl.BlockSpec((size, wide_down + ff_dev), lambda *_: (place, 0))
        begin = total is None
        operands = [results[place][0][at][0], results[place][1][at][0], down_own, down_oth]
        specs = [whole_spec((step, size))] * 2 + [weight] * 2
        if not begin:
            operands.append(total)
            specs.append(whole_spec((step, wide_down)))
        shape = (step, wide_down) if begin else (rows, wide_down)
        count = 1 if begin else 2
        return call(
            functools.partial(down_kernel, begin), scalars, operands, specs,
            [sds(shape, kind)] * count, [whole_spec(shape)] * count,
            cost=(2 * step * 4 * ff_dev * width, 12 * 2**20), ties=ties,
        )

    results = [[[None, None], [None, None]] for _ in CHUNKS]
    gu_own = hold(gu_owns[0], [pieces2[1], pieces2[3]])
    weights = [(gu_own, down_own), (swap(gu_own, 1), down_oth)]
    sums = []
    for at in range(2):
        total, *more = feed(0, weights, at, None, False)
        sums.append(total)
        results[0][0][at], results[0][1][at], latents[at] = more[:2], more[2:4], more[4:]
    down_first = [down_half(0, at, F32, None, [sums[1]])[0] for at in range(2)]
    gu_own = hold(gu_owns[1], sums + down_first)
    weights = [(gu_own, down_own), (swap(gu_own, 1), down_oth)]
    total, *results[1][0][0] = feed(1, weights[:1], 0, sums[0], False)
    send_x, send_y, *results[1][1][0] = feed(1, weights[1:], 0, total, True)
    pass_on, kept, *more = feed(1, weights, 1, sums[1], True)
    results[1][0][1], results[1][1][1] = more[:2], more[2:]
    by_x, by_y, got_y, got_x, passed = scatter_rest(send_x, send_y, pass_on)
    down_x, down_y = (hold(x, [got_y, got_x]) for x in down_half(1, 0, BF, down_first[0], passed))
    halfspec = lambda n: pl.BlockSpec((half, n), lambda *_: (0, 0))
    second_grad, mixed_grad, *packs = call(
        back_middle_kernel, scalars,
        [kept, by_x, by_y, got_y, got_x, second, cot_low, full_a_gu, full_out, full_a_out, full_b_out, z_out],
        [whole_spec((rows, wide_gu))] + [halfspec(wide_gu)] * 4
        + [
            tall, tall, whole_spec((width, 2 * latent)), ANY, whole_spec((width, latent)),
            whole_spec((latent, width)), whole_spec((rows, latent)),
        ],
        [
            sds((rows, width), F32), sds((rows, width)),
        ]
        + [sds((rows, 5 * latent))] * 4,
        [tall, tall] + [whole_spec((rows, 5 * latent))] * 4,
        scratch=[pltpu.VMEM((width, width), BF), pltpu.SemaphoreType.DMA],
        cost=(2 * rows * width * width, 16 * 2**20), ties=[down_x],
    )
    mixed_grad_h = lax.all_to_all(mixed_grad, "seq", split_axis=1, concat_axis=0, tiled=True)
    down_on, down_kept = down_half(1, 1, F32, down_first[1], [mixed_grad])

    def along_line(keep, send, ties):
        shape = keep.shape[1:]
        return call(
            along_line_kernel, scalars, [keep, swap(send, 1)], [whole_spec(keep.shape)] * 2,
            [sds(shape, F32)] * 2 + [sds((2, *shape))], [whole_spec(shape)] * 2 + [whole_spec((2, *shape))],
            ties=ties, cost=(2**20, 8 * 2**20), room=SMALL,
        )

    def line_sum(mine, onward, sent, ties):
        brought = lax.ppermute(sent, "fsdp", [(i, i ^ 1) for i in range(z_count)])
        onward = (onward + brought[1].astype(F32)).astype(BF)
        far = lax.ppermute(onward, "fsdp", [(i, i ^ 2) for i in range(z_count)])
        mine = hold(mine, ties) if ties else mine
        return (mine + brought[0].astype(F32) + far.astype(F32)).astype(BF)

    def spread(mine, places, shapes, ties):
        plane = blocks_of(mine)
        plane.append(swap(jnp.stack(plane), 1))
        return call(
            functools.partial(spread_kernel, places), scalars, plane,
            [whole_spec(piece.shape) for piece in plane],
            [sds(shape, F32) for shape in shapes], [whole_spec(shape) for shape in shapes], ties=ties,
            room=SMALL,
        )

    *down_by, down_passed = scatter_rest(down_x, down_y, down_on)
    middle = [packs[0]] + [swap(hold(packs[k], [mixed_grad_h]), 2 * k) for k in (1, 2, 3)]

    result = pl.BlockSpec((3, group, HEAD_DIM), lambda h, _: (0, 0, h))
    grads_a, grads_b, up_qkv = call(
        functools.partial(attend_back_kernel, rows), scalars,
        [qkv, qkv, qkv, mixed_grad_h, log_sums, z_qkv, cosine, turn],
        [column(0), column(1), column(2), column(0), column(0), whole_spec((length, 3 * latent))]
        + [whole_spec((length, LANES))] * 2,
        [sds((3, group, span))] * 2 + [sds((3, latent, span), F32)],
        [result, result, pl.BlockSpec((3, latent, HEAD_DIM), lambda h, _: (0, 0, h))],
        scratch=[pltpu.VMEM((length, HEAD_DIM), F32)] * 3, grid=(heads_dev,),
        cost=(10 * heads_dev * length * length * HEAD_DIM, 16 * 2**20), ties=down_passed,
    )
    grads_b = swap(grads_b, 1)
    qkv_oth = swap(qkv_own, 1)

    down_kept = hold(down_kept, [grads_a])
    upper = down_kept[:half] + down_by[0][:half].astype(F32) + down_by[2].astype(F32)
    lower = down_kept[half:] + down_by[1][:half].astype(F32) + down_by[3].astype(F32)
    wide = jnp.concatenate([upper, lower], axis=0)
    z_down = wide[:, width:].astype(BF) * select
    to_x, to_y, to_far, latent_kept = call(
        back_latent_kernel, scalars, [grads_a, grads_b, up_own, up_oth],
        [whole_spec((3, group, span))] * 2 + [whole_spec((3 * latent, span))] * 2,
        [sds((rows, 3 * latent))] * 3 + [sds((rows, 3 * latent), F32)],
        [whole_spec((rows, 3 * latent))] * 4,
        cost=(4 * group * span * 3 * latent, 4 * 2**20), room=SMALL, ties=[z_down],
    )

    def back_qkv(at, kind, ties):
        part = pl.BlockSpec((3, step, span), lambda *_: (0, at, 0))
        return call(
            back_qkv_kernel, scalars, [grads_a, grads_b, qkv_own, qkv_oth],
            [part, part] + [whole_spec((width, 3 * span))] * 2,
            [sds((rows, width), kind)] * 2, [tall] * 2,
            cost=(2 * group * span * 3 * width, 12 * 2**20), room=SMALL, ties=ties,
        )

    pass_on, kept = back_qkv(1, F32, [to_x, *middle[1:]])
    dz_qkv = latent_kept + swap(to_x, 2).astype(F32) + swap(to_y, 4).astype(F32)
    dz_qkv = (dz_qkv + swap(to_far, 6).astype(F32)) * jnp.tile(select, (1, 3)).astype(F32)
    both = jnp.concatenate([dz_qkv.astype(BF), z_down], axis=1)
    last = blocks_of(both)
    ff_rows = 2 * latent * (ff_dev // LANES) + ff_dev
    values = [one[k] for one in latents for k in range(1)] + [one[1] for one in latents]
    values += [value for chunk in results for side in chunk for one in side for value in one]
    ff_keep, ff_send = call(
        ff_grads_kernel, scalars, values, [whole_spec(value.shape) for value in values],
        [sds((z_count, ff_rows, LANES), F32), sds((z_count, ff_rows, LANES))],
        [whole_spec((z_count, ff_rows, LANES))] * 2, cost=(2**32, 12 * 2**20), ties=[kept, both],
    )
    send_x, send_y = back_qkv(0, BF, [*last[1:], ff_send])
    other_rows = 11 * LANES // 2
    keep, send = call(
        functools.partial(other_grads_kernel, quarter), scalars,
        [*pieces1, *pieces2, *cot_pieces, mixed_h, mixed_oth, *middle, *last, up_qkv],
        [ANY] * 24 + [whole_spec((length, span))] * 2 + [whole_spec((rows, 5 * latent))] * 4
        + [whole_spec((rows, 4 * latent))] * 4 + [whole_spec((3, latent, span))],
        [sds((z_count, other_rows, LANES), F32), sds((z_count, other_rows, LANES))],
        [whole_spec((z_count, other_rows, LANES))] * 2,
        scratch=[
            pltpu.VMEM((3, group, z_count * LANES), BF), pltpu.VMEM((group, 2 * latent), BF),
            pltpu.VMEM((group, 3 * latent), BF), pltpu.VMEM((group, latent), BF),
            pltpu.SemaphoreType.DMA((96,)),
        ],
        cost=(2 * group * 512 * 768, 8 * 2**20), ties=[send_x],
    )
    ff_mine, *ff_rest = along_line(ff_keep, ff_send, [keep])
    by_x, by_y, got_y, got_x, passed = scatter_rest(send_x, send_y, hold(pass_on, [keep]))
    input_grad = call(
        back_first_kernel, scalars,
        [kept, by_x, by_y, got_y, got_x, stream, second_grad, both, full_a_qkv],
        [tall] + [halfspec(width)] * 4
        + [tall, tall, pl.BlockSpec((rows, 3 * latent), lambda *_: (0, 0)), whole_spec((width, 3 * latent))],
        sds((rows, width), F32), tall,
        cost=(2 * rows * width * 3 * latent, 12 * 2**20), room=SMALL,
    )
    activations = second + (wide[:, :width] + dot(hold(z_down, passed), full_b_down))
    ff_total = line_sum(ff_mine, *ff_rest, [activations])
    total = line_sum(*along_line(keep, send, []), [input_grad])
    g_b_gu, g_a_down = spread(
        ff_total, (("columns", 2 * latent, ff_dev // LANES), ("rows", ff_dev, 1)),
        [(2 * latent, ff_z), (ff_z, latent)], [],
    )
    low = LANES // 2
    g_a_gu, g_b_down, g_a_out, g_b_out, g_a_qkv, g_b_qkv = spread(
        total,
        (
            ("rows", low, 2), ("both", low, 1), ("rows", low, 1), ("core rows", share_b, z_count),
            ("rows", low, 3), ("both", 3 * low, 1),
        ),
        [
            (quarter, 2 * latent), (latent, quarter), (quarter, latent), (latent, quarter),
            (quarter, 3 * latent), (3 * latent, quarter),
        ],
        [g_b_gu],
    )

    return (
        activations[None], input_grad[None],
        g_a_qkv, g_b_qkv, g_a_out, g_b_out, g_a_gu, g_b_gu, g_a_down, g_b_down,
    )


def solution(mesh):
    placed = (
        P("fsdp", "seq", None),
        P("fsdp", "seq", None),
        P("fsdp", None),
        P("fsdp", None),
        P("fsdp", None),
        P("fsdp", None),
        P("fsdp", None),
        P("fsdp", None),
        P("fsdp", None),
        P(None, "fsdp"),
        P("fsdp", None),
        P(None, "fsdp"),
        P("fsdp", None),
        P(None, "fsdp"),
        P("fsdp", None),
        P(None, "fsdp"),
    )
    on_plane = mesh.shape["seq"] == PLANE and mesh.shape["fsdp"] == 4
    return jax.shard_map(
        plane_shards if on_plane else shards,
        mesh=mesh,
        in_specs=placed,
        out_specs=(
            P("fsdp", "seq", None),
            P("fsdp", "seq", None),
            P("fsdp", None),
            P(None, "fsdp"),
            P("fsdp", None),
            P(None, "fsdp"),
            P("fsdp", None),
            P(None, "fsdp"),
            P("fsdp", None),
            P(None, "fsdp"),
        ),
        check_vma=False,
    )
```

```python
import functools

import jax
import jax.numpy as jnp
from jax import lax
from jax.experimental import pallas as pl
from jax.experimental.pallas import tpu as pltpu
from jax.sharding import PartitionSpec as P

HEAD_DIM = 128
RANK = 16


def layer_norm(values):
    centre = values - jnp.mean(values, axis=-1, keepdims=True)
    spread = jnp.mean(centre * centre, axis=-1, keepdims=True)
    factor = lax.rsqrt(spread + 1e-05)
    return (centre * factor, factor)


def norm_back(normed, factor, upstream):
    upstream_mean = jnp.mean(upstream, axis=-1, keepdims=True)
    cross_mean = jnp.mean(upstream * normed, axis=-1, keepdims=True)
    return factor * (upstream - upstream_mean - normed * cross_mean)


def doc_tables(places, first, chosen):
    within = first[None, :] <= places[:, None]
    begin = jnp.max(jnp.where(within, first[None, :], 0), axis=1)
    latest = jnp.sum(within.astype(jnp.int32), axis=1) - 1
    doc_order = jnp.arange(first.shape[0], dtype=jnp.int32)
    which = jnp.sum(jnp.where(doc_order[None, :] == latest[:, None], chosen[None, :], 0), axis=1)
    return (begin, which)


def rope_tables(position, head_dim):
    freqs = 10000.0 ** (-(jnp.arange(0, head_dim, 2, dtype=jnp.float32) / head_dim))
    angles = position.astype(jnp.float32)[:, None] * freqs[None, :]
    cosine = jnp.concatenate([jnp.cos(angles), jnp.cos(angles)], axis=-1)
    sine = jnp.concatenate([jnp.sin(angles), jnp.sin(angles)], axis=-1)
    return (cosine, sine)


def rotate(values, cosine, sine):
    half_dim = values.shape[-1] // 2
    turned = jnp.concatenate([-values[..., half_dim:], values[..., :half_dim]], axis=-1)
    return values * cosine[:, None, :] + turned * sine[:, None, :]


def rotate_back(upstream, cosine, sine):
    half_dim = upstream.shape[-1] // 2
    scaled = upstream * sine[:, None, :]
    return upstream * cosine[:, None, :] + jnp.concatenate(
        [scaled[..., half_dim:], -scaled[..., :half_dim]], axis=-1
    )


def inner_rows(left, right):
    return lax.dot_general(
        left, right, (((0,), (0,)), ((), ())), preferred_element_type=jnp.float32
    )


def inner_cols(left, right):
    return lax.dot_general(
        left, right, (((1,), (1,)), ((), ())), preferred_element_type=jnp.float32
    )


def adapter_fwd(inputs, down, up, select, segments):
    latent = jnp.dot(inputs, down, preferred_element_type=jnp.float32).astype(
        jnp.bfloat16
    ) * jnp.tile(select, (1, segments))
    span = up.shape[0] // segments
    pieces = [
        jnp.dot(
            latent[:, seg * span : (seg + 1) * span],
            up[seg * span : (seg + 1) * span],
            preferred_element_type=jnp.float32,
        )
        for seg in range(segments)
    ]
    return (latent, jnp.concatenate(pieces, axis=1))


def adapter_back(inputs, latent, upstream, down, up, select, segments):
    span = up.shape[0] // segments
    out_span = up.shape[1]
    grad_up = jnp.concatenate(
        [
            inner_rows(
                latent[:, seg * span : (seg + 1) * span],
                upstream[:, seg * out_span : (seg + 1) * out_span],
            )
            for seg in range(segments)
        ],
        axis=0,
    )
    latent_grad = jnp.concatenate(
        [
            inner_cols(
                upstream[:, seg * out_span : (seg + 1) * out_span],
                up[seg * span : (seg + 1) * span],
            )
            for seg in range(segments)
        ],
        axis=1,
    )
    latent_grad = (latent_grad * jnp.tile(select, (1, segments)).astype(jnp.float32)).astype(
        jnp.bfloat16
    )
    grad_down = inner_rows(inputs, latent_grad)
    back = inner_cols(latent_grad, down)
    return (grad_down, grad_up, back)


def frozen_fwd(inputs, weight):
    return (
        jnp.dot(
            inputs,
            lax.all_gather(weight, "fsdp", axis=0, tiled=True),
            preferred_element_type=jnp.float32,
        ),
        weight,
    )


def frozen_bwd(upstream, weight):
    return inner_cols(upstream, lax.all_gather(weight, "fsdp", axis=0, tiled=True))


def attend(query_h, key_h, value_h, begin, head_dim):
    length, local_width = query_h.shape
    local_heads = local_width // head_dim
    block_rows = min(512, length)
    block_count = length // block_rows
    score_scale = head_dim ** (-0.5)
    query_all = query_h.reshape(length, local_heads, head_dim)
    key_all = key_h.reshape(length, local_heads, head_dim)
    value_all = value_h.reshape(length, local_heads, head_dim)
    key_places = jnp.arange(length, dtype=jnp.int32)

    def one_block(block_index):
        start = block_index * block_rows
        query_block = lax.dynamic_slice_in_dim(query_all, start, block_rows, 0)
        rows = start + jnp.arange(block_rows, dtype=jnp.int32)
        row_begin = lax.dynamic_slice_in_dim(begin, start, block_rows, 0)
        allowed = (key_places[None, :] <= rows[:, None]) & (
            key_places[None, :] >= row_begin[:, None]
        )
        scores = (
            jnp.einsum("qhd,khd->hqk", query_block, key_all, preferred_element_type=jnp.float32)
            * score_scale
        )
        scores = jnp.where(allowed[None], scores, -1e30)
        row_top = jnp.max(scores, axis=-1, keepdims=True)
        expd = jnp.exp(scores - row_top)
        row_total = jnp.sum(expd, axis=-1, keepdims=True)
        probs = (expd / row_total).astype(jnp.bfloat16)
        mixed = jnp.einsum("hqk,khd->qhd", probs, value_all, preferred_element_type=jnp.float32)
        return (
            mixed.astype(jnp.bfloat16).reshape(block_rows, local_width),
            (row_top + jnp.log(row_total))[..., 0],
        )

    outputs, log_sums = lax.map(one_block, jnp.arange(block_count, dtype=jnp.int32))
    return (outputs.reshape(length, local_width), log_sums)


def attend_back(query_h, key_h, value_h, grad_h, log_sums, begin, head_dim):
    length, local_width = query_h.shape
    local_heads = local_width // head_dim
    block_rows = min(512, length)
    block_count = length // block_rows
    score_scale = head_dim ** (-0.5)
    query_all = query_h.reshape(length, local_heads, head_dim)
    key_all = key_h.reshape(length, local_heads, head_dim)
    value_all = value_h.reshape(length, local_heads, head_dim)
    grad_all = grad_h.reshape(length, local_heads, head_dim)
    key_places = jnp.arange(length, dtype=jnp.int32)

    def step(carry, inputs):
        key_grad, value_grad = carry
        block_index, block_lse = inputs
        start = block_index * block_rows
        query_block = lax.dynamic_slice_in_dim(query_all, start, block_rows, 0)
        grad_block = lax.dynamic_slice_in_dim(grad_all, start, block_rows, 0)
        rows = start + jnp.arange(block_rows, dtype=jnp.int32)
        row_begin = lax.dynamic_slice_in_dim(begin, start, block_rows, 0)
        allowed = (key_places[None, :] <= rows[:, None]) & (
            key_places[None, :] >= row_begin[:, None]
        )
        scores = (
            jnp.einsum("qhd,khd->hqk", query_block, key_all, preferred_element_type=jnp.float32)
            * score_scale
        )
        probs = jnp.where(allowed[None], jnp.exp(scores - block_lse[..., None]), 0.0)
        probs_low = probs.astype(jnp.bfloat16)
        prob_grad = jnp.einsum(
            "qhd,khd->hqk", grad_block, value_all, preferred_element_type=jnp.float32
        )
        row_delta = jnp.sum(prob_grad * probs, axis=-1, keepdims=True)
        score_grad = (probs * (prob_grad - row_delta)).astype(jnp.bfloat16)
        query_grad = (
            jnp.einsum("hqk,khd->qhd", score_grad, key_all, preferred_element_type=jnp.float32)
            * score_scale
        )
        key_grad = (
            key_grad
            + jnp.einsum(
                "hqk,qhd->khd", score_grad, query_block, preferred_element_type=jnp.float32
            )
            * score_scale
        )
        value_grad = value_grad + jnp.einsum(
            "hqk,qhd->khd", probs_low, grad_block, preferred_element_type=jnp.float32
        )
        return (
            (key_grad, value_grad),
            query_grad.astype(jnp.bfloat16).reshape(block_rows, local_width),
        )

    empty = jnp.zeros((length, local_heads, head_dim), jnp.float32)
    (key_grad, value_grad), query_grad = lax.scan(
        step, (empty, empty), (jnp.arange(block_count, dtype=jnp.int32), log_sums)
    )
    return (
        query_grad.reshape(length, local_width),
        key_grad.astype(jnp.bfloat16).reshape(length, local_width),
        value_grad.astype(jnp.bfloat16).reshape(length, local_width),
    )


def shards(
    tokens,
    cotangent,
    starts,
    adapter_ids,
    w_qkv,
    w_out,
    w_gu,
    w_down,
    a_qkv,
    b_qkv,
    a_out,
    b_out,
    a_gu,
    b_gu,
    a_down,
    b_down,
):
    gathered = (
        lax.all_gather(a_qkv, "fsdp", axis=0, tiled=True),
        lax.all_gather(b_qkv, "fsdp", axis=1, tiled=True),
        lax.all_gather(a_out, "fsdp", axis=0, tiled=True),
        lax.all_gather(b_out, "fsdp", axis=1, tiled=True),
        lax.all_gather(a_gu, "fsdp", axis=0, tiled=True),
        lax.all_gather(b_gu, "fsdp", axis=1, tiled=True),
        lax.all_gather(a_down, "fsdp", axis=0, tiled=True),
        lax.all_gather(b_down, "fsdp", axis=1, tiled=True),
    )
    (
        full_a_qkv,
        full_b_qkv,
        full_a_out,
        full_b_out,
        full_a_gu,
        full_b_gu,
        full_a_down,
        full_b_down,
    ) = gathered
    stream = tokens[0].astype(jnp.float32)
    cot_low = cotangent[0]
    tok_count, width = stream.shape
    seq_count = lax.axis_size("seq")
    seq_place = lax.axis_index("seq")
    stream_len = tok_count * seq_count
    first = starts[0]
    chosen = adapter_ids[0]
    local_places = seq_place * tok_count + jnp.arange(tok_count, dtype=jnp.int32)
    local_begin, which = doc_tables(local_places, first, chosen)
    columns = jnp.arange(full_a_out.shape[1], dtype=jnp.int32) // RANK
    select = (columns[None, :] == which[:, None]).astype(jnp.bfloat16)
    cosine, sine = rope_tables(local_places - local_begin, HEAD_DIM)
    head_count = width // HEAD_DIM
    first_norm, first_factor = layer_norm(stream)
    first_low = first_norm.astype(jnp.bfloat16)
    latent_qkv, extra_qkv = adapter_fwd(first_low, full_a_qkv, full_b_qkv, select, 3)
    qkv_main, held_qkv = frozen_fwd(first_low, w_qkv)
    qkv = qkv_main + extra_qkv
    query_rot = (
        rotate(qkv[:, :width].reshape(tok_count, head_count, HEAD_DIM), cosine, sine)
        .reshape(tok_count, width)
        .astype(jnp.bfloat16)
    )
    key_rot = (
        rotate(qkv[:, width : 2 * width].reshape(tok_count, head_count, HEAD_DIM), cosine, sine)
        .reshape(tok_count, width)
        .astype(jnp.bfloat16)
    )
    value_low = qkv[:, 2 * width :].astype(jnp.bfloat16)
    query_h, key_h, value_h = (
        lax.all_to_all(query_rot, "seq", split_axis=1, concat_axis=0, tiled=True),
        lax.all_to_all(key_rot, "seq", split_axis=1, concat_axis=0, tiled=True),
        lax.all_to_all(value_low, "seq", split_axis=1, concat_axis=0, tiled=True),
    )
    all_begin, all_which = doc_tables(jnp.arange(stream_len, dtype=jnp.int32), first, chosen)
    mixed_h, log_sums = attend(query_h, key_h, value_h, all_begin, HEAD_DIM)
    mixed = lax.all_to_all(mixed_h, "seq", split_axis=0, concat_axis=1, tiled=True)
    latent_out, extra_out = adapter_fwd(mixed, full_a_out, full_b_out, select, 1)
    out_main, held_out = frozen_fwd(mixed, w_out)
    second = stream + (out_main + extra_out)
    second_norm, second_factor = layer_norm(second)
    second_low = second_norm.astype(jnp.bfloat16)
    latent_gu, extra_gu = adapter_fwd(second_low, full_a_gu, full_b_gu, select, 2)
    gu_main, held_gu = frozen_fwd(second_low, w_gu)
    gate_up = gu_main + extra_gu
    ff_width = gate_up.shape[1] // 2
    gate = gate_up[:, :ff_width]
    upper = gate_up[:, ff_width:]
    sigma = jax.nn.sigmoid(gate)
    active = gate * sigma
    hidden = (active * upper).astype(jnp.bfloat16)
    latent_down, extra_down = adapter_fwd(hidden, full_a_down, full_b_down, select, 1)
    down_main, held_down = frozen_fwd(hidden, w_down)
    activations = second + (down_main + extra_down)
    grad_a_down, grad_b_down, hidden_extra = adapter_back(
        hidden, latent_down, cot_low, full_a_down, full_b_down, select, 1
    )
    hidden_grad = frozen_bwd(cot_low, held_down) + hidden_extra
    gate_grad = (hidden_grad * upper * sigma * (1.0 + gate * (1.0 - sigma))).astype(jnp.bfloat16)
    upper_grad = (hidden_grad * active).astype(jnp.bfloat16)
    gate_up_grad = jnp.concatenate([gate_grad, upper_grad], axis=1)
    grad_a_gu, grad_b_gu, second_extra = adapter_back(
        second_low, latent_gu, gate_up_grad, full_a_gu, full_b_gu, select, 2
    )
    second_norm_grad = frozen_bwd(gate_up_grad, held_gu) + second_extra
    second_grad = cot_low.astype(jnp.float32) + norm_back(
        second_norm, second_factor, second_norm_grad
    )
    branch_grad = second_grad.astype(jnp.bfloat16)
    grad_a_out, grad_b_out, mixed_extra = adapter_back(
        mixed, latent_out, branch_grad, full_a_out, full_b_out, select, 1
    )
    mixed_grad = (frozen_bwd(branch_grad, held_out) + mixed_extra).astype(jnp.bfloat16)
    mixed_grad_h = lax.all_to_all(mixed_grad, "seq", split_axis=1, concat_axis=0, tiled=True)
    query_grad_h, key_grad_h, value_grad_h = attend_back(
        query_h, key_h, value_h, mixed_grad_h, log_sums, all_begin, HEAD_DIM
    )
    query_grad, key_grad, value_grad = (
        lax.all_to_all(query_grad_h, "seq", split_axis=0, concat_axis=1, tiled=True),
        lax.all_to_all(key_grad_h, "seq", split_axis=0, concat_axis=1, tiled=True),
        lax.all_to_all(value_grad_h, "seq", split_axis=0, concat_axis=1, tiled=True),
    )
    query_pre = (
        rotate_back(
            query_grad.astype(jnp.float32).reshape(tok_count, head_count, HEAD_DIM), cosine, sine
        )
        .reshape(tok_count, width)
        .astype(jnp.bfloat16)
    )
    key_pre = (
        rotate_back(
            key_grad.astype(jnp.float32).reshape(tok_count, head_count, HEAD_DIM), cosine, sine
        )
        .reshape(tok_count, width)
        .astype(jnp.bfloat16)
    )
    qkv_grad = jnp.concatenate([query_pre, key_pre, value_grad], axis=1)
    grad_a_qkv, grad_b_qkv, first_extra = adapter_back(
        first_low, latent_qkv, qkv_grad, full_a_qkv, full_b_qkv, select, 3
    )
    first_norm_grad = frozen_bwd(qkv_grad, held_qkv) + first_extra
    input_grad = second_grad + norm_back(first_norm, first_factor, first_norm_grad)
    grads = (
        grad_a_qkv,
        grad_b_qkv,
        grad_a_out,
        grad_b_out,
        grad_a_gu,
        grad_b_gu,
        grad_a_down,
        grad_b_down,
    )
    shard_dims = (0, 1, 0, 1, 0, 1, 0, 1)
    summed = lax.psum(
        (grads[0], grads[1], grads[2], grads[3], grads[4], grads[5], grads[6], grads[7]),
        ("seq", "fsdp"),
    )
    fsdp_place = lax.axis_index("fsdp")
    fsdp_count = lax.axis_size("fsdp")
    totals = tuple(
        (
            lax.dynamic_slice_in_dim(
                whole,
                fsdp_place * (whole.shape[along] // fsdp_count),
                whole.shape[along] // fsdp_count,
                along,
            )
            for whole, along in zip(summed, shard_dims)
        )
    )
    return (
        activations[None],
        input_grad[None],
        totals[0],
        totals[1],
        totals[2],
        totals[3],
        totals[4],
        totals[5],
        totals[6],
        totals[7],
    )


BF = jnp.bfloat16
F32 = jnp.float32
PLANE = 8
CHIPS = 4
LANES = 128
CHUNKS = ((0, 1), (2, 3))
HALVES = ((1, 0), (3, 0), (2, 1), (3, 1), (2, 0), (1, 1), (0, 0), (0, 1))
ANY = pl.BlockSpec(memory_space=pl.ANY)
ROOMY = 60 * 2**20
SMALL = 28 * 2**20


def swap(value, bits):
    return lax.ppermute(value, "seq", [(i, i ^ bits) for i in range(PLANE)])


def gather_halves(first, second):
    x_first, y_second = swap(first, 2), swap(second, 4)
    y_first, x_second = swap(first, 4), swap(second, 2)
    far_first, far_second = swap(y_first, 2), swap(x_second, 4)
    return [x_first, far_first, y_second, far_second, y_first, x_second, first, second]


def blocks_of(block):
    return [block, swap(block, 2), swap(block, 4), swap(block, 6)]


def dot(left, right):
    return jnp.dot(left, right, preferred_element_type=F32)


def inner(left, right, on_left, on_right):
    return lax.dot_general(
        left, right, (((on_left,), (on_right,)), ((), ())), preferred_element_type=F32
    )


def take(value, start, count, axis):
    return lax.dynamic_slice_in_dim(value, start, count, axis)


def whole_spec(shape):
    return pl.BlockSpec(shape, lambda *_: (0,) * len(shape))


def call(
    body, scalars, operands, specs, shapes, out_specs, scratch=(), grid=(1,), cost=None, ties=(), room=ROOMY
):
    count = len(operands)

    def run(*refs):
        inside = refs[: 1 + count] + refs[1 + count + len(ties) :]
        body(*inside)

    return pl.pallas_call(
        run,
        grid_spec=pltpu.PrefetchScalarGridSpec(
            num_scalar_prefetch=1,
            grid=grid,
            in_specs=list(specs) + [ANY] * len(ties),
            out_specs=out_specs,
            scratch_shapes=list(scratch),
        ),
        out_shape=shapes,
        compiler_params=pltpu.CompilerParams(vmem_limit_bytes=room),
        cost_estimate=None
        if cost is None
        else pl.CostEstimate(flops=cost[0], bytes_accessed=cost[1], transcendentals=0),
    )(scalars, *operands, *ties)


def hold(value, ties):
    return pl.pallas_call(
        lambda *refs: None,
        in_specs=[ANY] * (1 + len(ties)),
        out_specs=ANY,
        out_shape=sds(value.shape, value.dtype),
        input_output_aliases={0: 0},
    )(value, *ties)


def copies(pairs, sems):
    started = [
        pltpu.make_async_copy(source, target, sems.at[k]) for k, (source, target) in enumerate(pairs)
    ]
    for one in started:
        one.start()
    for one in started:
        one.wait()


def sds(shape, dtype=BF):
    return jax.ShapeDtypeStruct(shape, dtype)


def doc_begin(scalars, places):
    begin = jnp.zeros_like(places)
    for doc in range(4):
        begin = jnp.where(scalars[3 + doc] <= places, scalars[3 + doc], begin)
    return begin


def adapter_mask(scalars, places):
    which = jnp.zeros_like(places) + scalars[7]
    for doc in range(1, 4):
        which = jnp.where(scalars[3 + doc] <= places, scalars[7 + doc], which)
    column = lax.broadcasted_iota(jnp.int32, (1, LANES), 1) // RANK
    return (column == which).astype(F32)


def rows_from(first, count):
    return first + lax.broadcasted_iota(jnp.int32, (count, 1), 0)


def normed(values):
    centre = values - jnp.mean(values, axis=-1, keepdims=True)
    factor = lax.rsqrt(jnp.mean(centre * centre, axis=-1, keepdims=True) + 1e-05)
    return centre * factor, factor


def cut_first_kernel(sizes, scalars, w_qkv, w_out, a_qkv, a_out, a_gu, b_out, b_down, b_qkv, out, sems):
    share, quarter, width = sizes
    chip, core = scalars[0], scalars[1]
    seat = chip * 2 + core
    pairs = []
    for part in range(3):
        for i in range(2):
            column = pl.multiple_of(part * width + (2 * core + i) * quarter + chip * LANES, LANES)
            k = part * 2 + i
            pairs.append(
                (w_qkv.at[:, pl.ds(column, LANES)], out.at[:quarter, k * LANES : (k + 1) * LANES])
            )
    rows = pl.ds(pl.multiple_of(seat * share, share), share)
    small = slice(quarter, quarter + share)
    pairs.append((a_qkv.at[rows], out.at[small, :384]))
    pairs.append((a_gu.at[rows], out.at[small, 384:640]))
    pairs.append((a_out.at[rows], out.at[small, 640:768]))
    low = pl.ds(pl.multiple_of(seat * 16, 16), 16)
    at = quarter + share
    pairs.append((b_out.at[low], out.at[at : at + 16, :512]))
    pairs.append((b_down.at[low], out.at[at + 16 : at + 32, :512]))
    column = pl.ds(pl.multiple_of(chip * LANES, LANES), LANES)
    for k in range(12):
        here = pl.ds(pl.multiple_of(core * 192 + k * 16, 16), 16)
        row, lane = up_slot(k)
        row += at
        pairs.append((b_qkv.at[here, column], out.at[row : row + 16, lane : lane + LANES]))
    at += 32
    for k in range(16):
        row, lane = at + (k // 6) * share, (k % 6) * LANES
        pairs.append(
            (w_out.at[rows, k * LANES : (k + 1) * LANES], out.at[row : row + share, lane : lane + LANES])
        )
    copies(pairs, sems)


def up_slot(k):
    row = (k // 2) * 16 if k < 4 else 32 + 2 * 64 + ((k - 4) // 2) * 16
    return row, 512 + (k % 2) * LANES


def cut_rest_kernel(sizes, scalars, w_gu, w_down, a_down, b_gu, down, *refs):
    ff, ff_z, ff_dev, width = sizes
    parts, sems = refs[:-1], refs[-1]
    seat = scalars[0] * 2 + scalars[1]
    rows = pl.ds(pl.multiple_of(seat * ff_dev, ff_dev), ff_dev)
    wide = width + LANES
    pairs = [
        (w_down.at[rows], down.at[:, :width]),
        (a_down.at[rows], down.at[:, width:wide]),
        (b_gu.at[:, rows], down.at[:, wide : wide + ff_dev]),
    ]
    for zs, gu in zip(CHUNKS, parts):
        for half in range(2):
            for i, z in enumerate(zs):
                column = pl.multiple_of(half * ff + z * ff_z + seat * ff_dev, ff_dev)
                k = half * len(zs) + i
                pairs.append(
                    (w_gu.at[:, pl.ds(column, ff_dev)], gu.at[:, k * ff_dev : (k + 1) * ff_dev])
                )
    copies(pairs, sems)


def unpack_small_kernel(share, quarter, scalars, *refs):
    pieces = refs[:16]
    a_qkv, a_gu, a_out, b_out, b_down = refs[16:]
    chip, core = scalars[0], scalars[1]
    for k in range(2):
        for at, (rel, half) in enumerate(HALVES):
            piece = pieces[8 * k + at]
            tall = piece.shape[0] // 2
            seat = (chip ^ rel) * 2 + (core if k == 0 else 1 - core)
            for i in range(2):
                z = half * 2 + i
                rows = slice(i * tall, i * tall + share)
                there = pl.ds(pl.multiple_of(z * quarter + seat * share, share), share)
                a_qkv[there, :] = piece[rows, :384]
                a_gu[there, :] = piece[rows, 384:640]
                a_out[there, :] = piece[rows, 640:768]
                there = pl.ds(pl.multiple_of(seat * 16, 16), 16)
                columns = slice(z * quarter, (z + 1) * quarter)
                row = i * tall + share
                b_out[there, columns] = piece[row : row + 16, :512]
                b_down[there, columns] = piece[row + 16 : row + 32, :512]


def unpack_out_kernel(share, quarter, scalars, *refs):
    pieces, out, sems = refs[:16], refs[16], refs[17]
    chip, core = scalars[0], scalars[1]
    pairs = []
    for k in range(2):
        for at, (rel, half) in enumerate(HALVES):
            seat = (chip ^ rel) * 2 + (core if k == 0 else 1 - core)
            for i in range(2):
                there = pl.ds(pl.multiple_of((half * 2 + i) * quarter + seat * share, share), share)
                for block in range(3):
                    row = (i * 3 + block) * share
                    lanes = min(768, out.shape[1] - block * 768)
                    pairs.append(
                        (
                            pieces[8 * k + at].at[row : row + share, :lanes],
                            out.at[there, block * 768 : block * 768 + lanes],
                        )
                    )
    copies(pairs, sems)


def norm_kernel(scalars, tokens, first, second):
    value, _ = normed(tokens[...].astype(F32))
    half = first.shape[0]
    first[...] = value[:half].astype(BF)
    second[...] = value[half:].astype(BF)


def qkv_kernel(scalars, *refs):
    pieces, gathered = refs[:16], refs[16]
    down, up, cosine, sine, out, latents, weight, rows_all, sems = refs[17:]
    chip, core = scalars[0], scalars[1]
    half = pieces[0].shape[0]
    quarter = weight.shape[0] // 4
    tall = gathered.shape[0] // 4
    pairs = [
        (gathered.at[pl.ds(z * tall, quarter)], weight.at[pl.ds(z * quarter, quarter)]) for z in range(4)
    ]
    for k in range(2):
        for at, (rel, part) in enumerate(HALVES):
            seat = (chip ^ rel) * 2 + (core if k == 0 else 1 - core)
            there = pl.ds(pl.multiple_of((seat * 2 + part) * half, half), half)
            pairs.append((pieces[8 * k + at], rows_all.at[there]))
    copies(pairs, sems)
    step = 512
    span = up.shape[1]
    for start in range(0, rows_all.shape[0], step):
        here = slice(start, start + step)
        value = rows_all[here, :]
        mask = adapter_mask(scalars, rows_from(start, step))
        latent = dot(value, down[...]).astype(BF) * jnp.concatenate([mask] * 3, axis=1).astype(BF)
        latents[here, :] = latent
        pre = dot(value, weight[...])
        for part in range(3):
            block = pre[:, part * span : (part + 1) * span] + dot(
                latent[:, part * LANES : (part + 1) * LANES], up[part * LANES : (part + 1) * LANES, :]
            )
            if part < 2:
                heads = []
                for k in range(span // HEAD_DIM):
                    head = block[:, k * HEAD_DIM : (k + 1) * HEAD_DIM]
                    heads.append(
                        head * cosine[here, :] + pltpu.roll(head, HEAD_DIM // 2, 1) * sine[here, :]
                    )
                block = jnp.concatenate(heads, axis=1)
            out[here, part * span : (part + 1) * span] = block.astype(BF)


def allowed_pairs(scalars, first_row, rows, width):
    row = rows_from(first_row, rows)
    column = lax.broadcasted_iota(jnp.int32, (1, width), 1)
    return (column <= row) & (column >= doc_begin(scalars, row))


def attend_kernel(rows, scalars, query, key, value, out, lse):
    scale = HEAD_DIM**-0.5
    for start in range(0, query.shape[0], rows):
        here = slice(start, start + rows)
        width = start + rows
        scores = inner(query[here, :], key[:width, :], 1, 1) * scale
        scores = jnp.where(allowed_pairs(scalars, start, rows, width), scores, -1e30)
        top = jnp.max(scores, axis=1, keepdims=True)
        expd = jnp.exp(scores - top)
        total = jnp.sum(expd, axis=1, keepdims=True)
        probs = (expd * (1.0 / total)).astype(BF)
        out[here, :] = dot(probs, value[:width, :]).astype(BF)
        lse[here, :] = jnp.broadcast_to(top + jnp.log(total), (rows, LANES))


def attend_back_kernel(
    rows, scalars, query, key, value, grad, lse, latents, cosine, sine, own, other, ups,
    dq_all, dk_sum, dv_sum,
):
    dk_sum[...] = jnp.zeros_like(dk_sum)
    dv_sum[...] = jnp.zeros_like(dv_sum)
    scale = HEAD_DIM**-0.5
    length = query.shape[0]
    for start in range(0, length, rows):
        here = slice(start, start + rows)
        width = start + rows
        this_query = query[here, :]
        upstream = grad[here, :]
        scores = inner(this_query, key[:width, :], 1, 1) * scale
        probs = jnp.where(
            allowed_pairs(scalars, start, rows, width), jnp.exp(scores - lse[here, :1]), 0.0
        )
        prob_grad = inner(upstream, value[:width, :], 1, 1)
        delta = jnp.sum(prob_grad * probs, axis=1, keepdims=True)
        score_grad = (probs * (prob_grad - delta)).astype(BF)
        dq_all[here, :] = dot(score_grad, key[:width, :]) * scale
        dk_sum[:width, :] += inner(score_grad, this_query, 0, 0)
        dv_sum[:width, :] += inner(probs.astype(BF), upstream, 0, 0)

    chip, core = scalars[0], scalars[1]
    half = own.shape[1] // 8
    for part, total in enumerate((dq_all, dk_sum, dv_sum)):
        for start in range(0, length, 512):
            here = slice(start, start + 512)
            if part == 0:
                raw = total[here, :].astype(BF).astype(F32)
            elif part == 1:
                raw = (total[here, :] * scale).astype(BF).astype(F32)
            else:
                raw = total[here, :]
            if part < 2:
                raw = raw * cosine[here, :] - pltpu.roll(raw, HEAD_DIM // 2, 1) * sine[here, :]
            total[here, :] = raw.astype(BF).astype(F32)
        low = total[...].astype(BF)
        ups[part] = inner(latents[:, part * LANES : (part + 1) * LANES], low, 0, 0)
        for k, target in enumerate((own, other)):
            for at, (rel, h) in enumerate(HALVES):
                seat = (chip ^ rel) * 2 + (core if k == 0 else 1 - core)
                there = pl.ds(pl.multiple_of((seat * 2 + h) * half, half), half)
                target[part, at * half : (at + 1) * half, :] = total[there, :].astype(BF)


def head_order(k):
    return (k % CHIPS) * CHIPS + k // CHIPS


def out_kernel(scalars, mixed, weight, down, up, tokens, second, first_half, second_half, latents, natural):
    for k in range(16):
        at = head_order(k)
        natural[:, k * LANES : (k + 1) * LANES] = mixed[:, at * LANES : (at + 1) * LANES]
    rows = tokens.shape[0]
    seat = scalars[0] * 2 + scalars[1]
    mask = adapter_mask(scalars, rows_from(seat * rows, rows)).astype(BF)
    value = natural[...]
    latent = dot(value, down[...]).astype(BF) * mask
    latents[...] = latent
    total = tokens[...].astype(F32) + (dot(value, weight[...]) + dot(latent, up[...]))
    second[...] = total
    norm, _ = normed(total)
    first_half[...] = norm[: rows // 2].astype(BF)
    second_half[...] = norm[rows // 2 :].astype(BF)


def ff_kernel(begin, last, sides, first_z, scalars, *refs):
    if begin:
        select, a_gu, b_down = refs[:3]
        count = 3
    else:
        z_gu_in, dz_down_in = refs[:2]
        count = 2
    weights = [refs[count + 2 * k : count + 2 * k + 2] for k in range(sides)]
    count += 2 * sides
    norm, cot = refs[count : count + 4], refs[count + 4 : count + 8]
    count += 8
    if not begin:
        sums_in = refs[count]
        count += 1
    outs = refs[count : count + (2 if last else 1)]
    count += len(outs)
    results = [refs[count + 2 * k : count + 2 * k + 2] for k in range(sides)]
    count += 2 * sides
    if begin:
        z_gu_out, dz_down_out = refs[count : count + 2]
        count += 2
    rows_in, cot_in, sums, sems = refs[count : count + 4]
    held = [refs[count + 4 + 2 * k : count + 6 + 2 * k] for k in range(sides)]
    rows, width = rows_in.shape
    wide = width + LANES
    own_ff = weights[0][1].shape[0] // 4
    many = held[0][1].shape[0] // own_ff
    part = pl.ds(first_z * own_ff, many * own_ff)
    low = rows // 4
    pairs = [(norm[k], rows_in.at[pl.ds(k * low, low)]) for k in range(4)]
    pairs.append((weights[0][0], held[0][0]))
    pairs += [(cot[k], cot_in.at[pl.ds(k * low, low)]) for k in range(4)]
    pairs.append((weights[0][1].at[part], held[0][1]))
    if sides == 2:
        pairs += [(weights[1][0], held[1][0]), (weights[1][1].at[part], held[1][1])]
    if not begin:
        pairs.append((sums_in, sums))
    loads = [pltpu.make_async_copy(x, y, sems.at[k]) for k, (x, y) in enumerate(pairs)]
    for load in loads:
        load.start()
    for load in loads[:4]:
        load.wait()
    if begin:
        mask = select[...]
        z_gu = dot(rows_in[...], a_gu[...]).astype(BF) * jnp.concatenate([mask, mask], axis=1)
        z_gu_out[...] = z_gu
    else:
        z_gu, dz_down = z_gu_in[...], dz_down_in[...]
    z_gate, z_up = z_gu[:, :LANES], z_gu[:, LANES:]
    norm_grad = 0.0
    latent_grad = 0.0
    for side, (gu, down) in enumerate(held):
        size = gu.shape[1] // 2
        loads[4 if side == 0 else 10].wait()
        both = dot(rows_in[...], gu[...])
        if side == 0:
            for load in loads[5:9]:
                load.wait()
            if begin:
                dz_down = (inner(cot_in[...], b_down[...], 1, 1) * mask.astype(F32)).astype(BF)
                dz_down_out[...] = dz_down
        loads[9 if side == 0 else 11].wait()
        up_gate = jnp.concatenate(
            [down[i * own_ff : i * own_ff + LANES, wide:] for i in range(many)], axis=1
        )
        up_up = jnp.concatenate(
            [down[i * own_ff + LANES : i * own_ff + 2 * LANES, wide:] for i in range(many)], axis=1
        )
        gate = both[:, :size] + dot(z_gate, up_gate)
        upper = both[:, size:] + dot(z_up, up_up)
        sigma = 1.0 / (1.0 + jnp.exp(-gate))
        active = gate * sigma
        results[side][0][...] = (active * upper).astype(BF)
        hidden_grad = inner(cot_in[...], down[:, :width], 1, 1) + inner(
            dz_down, down[:, width:wide], 1, 1
        )
        grads = results[side][1]
        grads[:, :size] = (hidden_grad * upper * sigma * (1.0 + gate * (1.0 - sigma))).astype(BF)
        grads[:, size:] = (hidden_grad * active).astype(BF)
        norm_grad += inner(grads[...], gu[...], 1, 1)
        latent_grad += jnp.concatenate(
            [inner(grads[:, :size], up_gate, 1, 1), inner(grads[:, size:], up_up, 1, 1)], axis=1
        )
    if begin:
        outs[0][:, :width] = norm_grad
        outs[0][:, width:] = latent_grad
        return
    loads[-1].wait()
    if not last:
        outs[0][:, :width] = norm_grad + sums[:, :width]
        outs[0][:, width:] = latent_grad + sums[:, width:]
        return
    low = rows // 2
    for k in range(2):
        at = slice(k * low, (k + 1) * low)
        kind = outs[k].dtype
        outs[k][:, :width] = (norm_grad[at] + sums[at, :width]).astype(kind)
        outs[k][:, width:] = (latent_grad[at] + sums[at, width:]).astype(kind)


def down_kernel(begin, scalars, hidden_own, hidden_oth, down_own, down_oth, *refs):
    outs = refs if begin else refs[1:]
    wide = outs[0].shape[1]
    total = dot(hidden_own[...], down_own[:, :wide]) + dot(hidden_oth[...], down_oth[:, :wide])
    if not begin:
        total += refs[0][...]
    rows = outs[0].shape[0]
    for k, out in enumerate(outs):
        out[...] = total[k * rows : (k + 1) * rows].astype(out.dtype)


def spread_kernel(places, scalars, *refs):
    pieces, outs = [*refs[:4], *(refs[4].at[k] for k in range(4))], refs[5:]
    for k, piece in enumerate(pieces):
        chip = scalars[0] ^ (k % 4)
        core = scalars[1] if k < 4 else 1 - scalars[1]
        seat = chip * 2 + core
        at = 0
        for out, (kind, rows, blocks) in zip(outs, places):
            for block in range(blocks):
                value = piece[at : at + rows, :].astype(F32)
                at += rows
                columns = pl.ds(block * LANES, LANES)
                if kind == "rows":
                    out[pl.ds(pl.multiple_of(seat * rows, rows), rows), columns] = value
                elif kind == "core rows":
                    row = pl.multiple_of(core * (CHIPS * rows) + chip * rows, rows)
                    out[pl.ds(row, rows), columns] = value
                elif kind == "columns":
                    column = pl.multiple_of((seat * blocks + block) * LANES, LANES)
                    out[:, pl.ds(column, LANES)] = value
                else:
                    row = pl.multiple_of(core * rows, rows)
                    out[pl.ds(row, rows), pl.ds(pl.multiple_of(chip * LANES, LANES), LANES)] = value


def ff_grads_kernel(scalars, *refs):
    z_gu, dz_down, results, keep, send = refs[:2], refs[2:4], refs[4:-2], refs[-2], refs[-1]
    at = 0
    for zs in CHUNKS:
        for out in (keep, send):
            gate, upper, down = 0.0, 0.0, 0.0
            for half in range(2):
                hidden, grads = results[at], results[at + 1]
                at += 2
                size = hidden.shape[1]
                gate += inner(z_gu[half][:, :LANES], grads[:, :size], 0, 0)
                upper += inner(z_gu[half][:, LANES:], grads[:, size:], 0, 0)
                down += inner(hidden[...], dz_down[half][...], 0, 0)
            own_ff = size // len(zs)
            rows = 2 * LANES
            blocks = own_ff // LANES
            for i, z in enumerate(zs):
                for k in range(blocks):
                    columns = slice(i * own_ff + k * LANES, i * own_ff + (k + 1) * LANES)
                    out[z, k * rows : k * rows + LANES, :] = gate[:, columns].astype(out.dtype)
                    out[z, k * rows + LANES : (k + 1) * rows, :] = upper[:, columns].astype(out.dtype)
                there = slice(blocks * rows, blocks * rows + own_ff)
                out[z, there, :] = down[i * own_ff : (i + 1) * own_ff].astype(out.dtype)


def other_grads_kernel(quarter, scalars, *refs):
    norm1, norm2, cot, mixed = refs[:8], refs[8:16], refs[16:24], refs[24:26]
    middle, last = refs[26:30], refs[30:34]
    up_qkv, keep, send, columns, all_gu, all_qkv, all_down, sems = refs[34:]
    half = norm1[0].shape[0]
    chip, core = scalars[0], scalars[1]
    pairs = []
    for k, source in enumerate((norm1, norm2, cot)):
        for z in range(4):
            column = pl.ds(pl.multiple_of(z * quarter + chip * LANES, LANES), LANES)
            for h in range(8):
                target = columns.at[k, h * half : (h + 1) * half, z * LANES : (z + 1) * LANES]
                pairs.append((source[h].at[:, column], target))
    loads = [pltpu.make_async_copy(x, y, sems.at[k]) for k, (x, y) in enumerate(pairs)]
    for load in loads:
        load.start()
    gu_wide, qkv_wide = all_gu.shape[1], all_qkv.shape[1]
    for k, (rel, h) in enumerate(HALVES):
        here, there = slice(h * half, (h + 1) * half), slice(k * half, (k + 1) * half)
        all_gu[there, :] = middle[rel][here, :gu_wide]
        all_qkv[there, :] = last[rel][here, :qkv_wide]
        all_down[there, :] = last[rel][here, qkv_wide:]

    def halves(z, at, value):
        rows = value.shape[0] // 2
        for k in range(2):
            piece = value[k * rows : (k + 1) * rows]

            @pl.when(core == k)
            def _():
                keep[z, at : at + rows, :] = piece

            @pl.when(core != k)
            def _():
                send[z, at : at + rows, :] = piece.astype(BF)

    def two_of_four(at, values):
        rows = values[0].shape[0] // 2
        for k in range(2):

            @pl.when(core == k)
            def _():
                for i in range(2):
                    here, there = 2 * k + i, 2 * (1 - k) + i
                    keep[here, at : at + rows, :] = values[i][k * rows : (k + 1) * rows]
                    send[here, at : at + rows, :] = values[i][(1 - k) * rows : (2 - k) * rows].astype(BF)
                    keep[there, at : at + rows, :] = jnp.zeros((rows, LANES), F32)
                    send[there, at : at + rows, :] = jnp.zeros((rows, LANES), BF)

    low = LANES // 2
    at = 3 * low
    rows = 2 * half
    for k, source in enumerate(mixed):
        total = 0.0
        for rel in range(4):
            here = pl.ds(pl.multiple_of(((chip ^ rel) * 2 + core) * rows, rows), rows)
            total += inner(source[here, :], middle[rel][:, gu_wide : gu_wide + LANES], 0, 0)
        first = 2 * (core if k == 0 else 1 - core)
        for i in range(2):
            halves(first + i, at, total[i * LANES : (i + 1) * LANES])
    at += low
    share = LANES // PLANE
    for z in range(4):
        for k in range(4):
            block = (z * 4 + k) // 2
            column = gu_wide + LANES + ((z * 4 + k) % 2) * LANES
            value = 0.0
            for rel in range(4):
                piece = middle[rel][block * 2 * share : (block + 1) * 2 * share, column : column + LANES]
                value = value + piece.astype(F32)
            halves(z, at + k * share, value)
    at += low
    at_b = at + 3 * low
    heads = [jnp.concatenate([up_qkv[part, :, i * LANES : (i + 1) * LANES] for part in range(3)], axis=0) for i in range(2)]
    two_of_four(at_b, heads)
    for load in loads:
        load.wait()
    value = inner(columns[1], all_gu[...], 0, 0)
    for z in range(4):
        for k in range(2):
            block = value[z * LANES : (z + 1) * LANES, k * LANES : (k + 1) * LANES]
            halves(z, k * low, block)
    value = inner(all_down[...], columns[2], 0, 0)
    for z in range(4):
        halves(z, 2 * low, value[:, z * LANES : (z + 1) * LANES])
    value = inner(columns[0], all_qkv[...], 0, 0)
    for z in range(4):
        for k in range(3):
            block = value[z * LANES : (z + 1) * LANES, k * LANES : (k + 1) * LANES]
            halves(z, at + k * low, block)


def along_line_kernel(scalars, keep, brought, mine, onward, sent):
    z = scalars[2]
    mine[...] = keep[z] + brought[z].astype(F32)
    onward[...] = keep[z ^ 2] + brought[z ^ 2].astype(F32)
    for k, other in enumerate((1, 3)):
        sent[k] = (keep[z ^ other] + brought[z ^ other].astype(F32)).astype(BF)


def keep_kernel(scalars, *refs):
    count = len(refs) // 2
    for source, target in zip(refs[:count], refs[count:]):
        target[...] = source[...]


def back_middle_kernel(
    scalars, own, by_x, by_y, got_y, got_x, second, cot, a_gu, w_out, a_out, b_out, z_out,
    grad, mixed_grad, pack_0, pack_1, pack_2, pack_3, w_held, sem,
):
    packs = (pack_0, pack_1, pack_2, pack_3)
    load = pltpu.make_async_copy(w_out, w_held, sem)
    load.start()
    rows, width = second.shape
    half = rows // 2
    upper = own[:half] + by_x[...].astype(F32) + got_y[...].astype(F32)
    lower = own[half:] + by_y[...].astype(F32) + got_x[...].astype(F32)
    wide = jnp.concatenate([upper, lower], axis=0)
    seat = scalars[0] * 2 + scalars[1]
    mask = adapter_mask(scalars, rows_from(seat * rows, rows))
    dz_gu = (wide[:, width:] * jnp.concatenate([mask, mask], axis=1)).astype(BF)
    upstream = wide[:, :width] + inner(dz_gu, a_gu[...], 1, 1)
    norm, factor = normed(second[...])
    total = cot[...].astype(F32) + norm_back(norm, factor, upstream)
    grad[...] = total
    low = total.astype(BF)
    dz_out = (inner(low, b_out[...], 1, 1) * mask).astype(BF)
    value = inner(z_out[...], low, 0, 0).astype(BF)
    load.wait()
    back = (inner(low, w_held[...], 1, 1) + inner(dz_out, a_out[...], 1, 1)).astype(BF)
    for k in range(16):
        at = head_order(k)
        mixed_grad[:, at * LANES : (at + 1) * LANES] = back[:, k * LANES : (k + 1) * LANES]
    share = value.shape[0] // PLANE
    at = dz_gu.shape[1] + LANES
    for pack in packs:
        pack[:, : dz_gu.shape[1]] = dz_gu
        pack[:, dz_gu.shape[1] : at] = dz_out
    for block in range(CHIPS):
        for core in range(2):
            row = (core * CHIPS + block) * share
            for rel, pack in enumerate(packs):

                @pl.when((scalars[0] ^ rel) == block)
                def _():
                    for k in range(PLANE):
                        there = slice(k * 2 * share + core * share, k * 2 * share + (core + 1) * share)
                        pack[there, at:] = value[row : row + share, k * 2 * LANES : (k + 1) * 2 * LANES]


def back_latent_kernel(scalars, own, other, up_own, up_oth, to_x, to_y, to_far, kept):
    half = kept.shape[0] // 2
    targets = {0: kept, 1: to_x, 2: to_y, 3: to_far}
    for part in range(3):
        at = slice(part * LANES, (part + 1) * LANES)
        value = inner(own[part], up_own[at, :], 1, 1) + inner(other[part], up_oth[at, :], 1, 1)
        for k, (rel, h) in enumerate(HALVES):
            target = targets[rel]
            target[h * half : (h + 1) * half, at] = value[k * half : (k + 1) * half].astype(target.dtype)


def back_qkv_kernel(scalars, own, other, w_own, w_oth, out_0, out_1):
    rows = out_0.shape[0]
    mine = jnp.concatenate([own[part] for part in range(3)], axis=1)
    theirs = jnp.concatenate([other[part] for part in range(3)], axis=1)
    value = inner(mine, w_own[...], 1, 1) + inner(theirs, w_oth[...], 1, 1)
    out_0[...] = value[:rows].astype(out_0.dtype)
    out_1[...] = value[rows:].astype(out_1.dtype)


def back_first_kernel(
    scalars, own, by_x, by_y, got_y, got_x, tokens, second_grad, dz_qkv, a_qkv, input_grad
):
    half = tokens.shape[0] // 2
    upper = own[:half] + by_x[...].astype(F32) + got_y[...].astype(F32)
    lower = own[half:] + by_y[...].astype(F32) + got_x[...].astype(F32)
    upstream = jnp.concatenate([upper, lower], axis=0) + inner(dz_qkv[...], a_qkv[...], 1, 1)
    norm, factor = normed(tokens[...].astype(F32))
    input_grad[...] = second_grad[...] + norm_back(norm, factor, upstream)


def scatter_rest(send_x, send_y, onward):
    half = onward.shape[0] // 2
    by_x, by_y = swap(send_x, 2), swap(send_y, 4)
    pass_y = (onward[:half] + by_x[half:].astype(F32)).astype(BF)
    pass_x = (onward[half:] + by_y[half:].astype(F32)).astype(BF)
    got_y, got_x = swap(pass_y, 4), swap(pass_x, 2)
    return by_x, by_y, got_y, got_x, (pass_y, pass_x)


def plane_shards(
    tokens, cotangent, starts, adapter_ids,
    w_qkv, w_out, w_gu, w_down, a_qkv, b_qkv, a_out, b_out, a_gu, b_gu, a_down, b_down,
):
    seat = lax.axis_index("seq")
    z_at = lax.axis_index("fsdp")
    z_count = lax.axis_size("fsdp")
    core = seat % 2
    chip = seat // 2
    rows, width = tokens.shape[1:]
    half = rows // 2
    group = CHIPS * rows
    length = rows * PLANE
    ff = w_gu.shape[1] // 2
    ff_z = ff // z_count
    ff_dev = ff_z // PLANE
    quarter = w_qkv.shape[0]
    latent = a_out.shape[1]
    heads_dev = width // HEAD_DIM // PLANE
    span = heads_dev * HEAD_DIM
    share = quarter // PLANE
    share_b = latent // PLANE
    wide_down = width + latent
    wide_gu = width + 2 * latent
    first = starts[0]
    chosen = adapter_ids[0]
    scalars = jnp.concatenate([jnp.stack([chip, core, z_at]).astype(jnp.int32), first, chosen])
    stream, cot_low = tokens[0], cotangent[0]

    norm_a, norm_b = call(
        norm_kernel, scalars, [stream], [whole_spec((rows, width))],
        [sds((half, width))] * 2, [whole_spec((half, width))] * 2,
    )
    tall_rows = quarter + share + 32 + 3 * share
    first_part = call(
        functools.partial(cut_first_kernel, (share, quarter, width)), scalars,
        [w_qkv, w_out, a_qkv, a_out, a_gu, b_out, b_down, b_qkv], [ANY] * 8,
        sds((tall_rows, 3 * span)), whole_spec((tall_rows, 3 * span)),
        scratch=[pltpu.SemaphoreType.DMA((39,))],
    )
    first_all = lax.all_gather(first_part, "fsdp", axis=0, tiled=True)
    gates = [len(zs) * 2 * ff_dev for zs in CHUNKS]
    down_part, *gu_parts = call(
        functools.partial(cut_rest_kernel, (ff, ff_z, ff_dev, width)), scalars,
        [w_gu, w_down, a_down, b_gu], [ANY] * 4,
        [sds((ff_dev, wide_down + ff_dev))] + [sds((quarter, n)) for n in gates],
        [whole_spec((ff_dev, wide_down + ff_dev))] + [whole_spec((quarter, n)) for n in gates],
        scratch=[pltpu.SemaphoreType.DMA((3 + 2 * z_count,))], ties=[first_part],
    )
    down_own = lax.all_gather(down_part, "fsdp", axis=0, tiled=True)
    gu_owns = [lax.all_gather(part, "fsdp", axis=0, tiled=True) for part in gu_parts]

    pieces1 = gather_halves(norm_a, norm_b)
    pieces1_oth = [swap(piece, 1) for piece in pieces1]


    cot_pieces = gather_halves(cot_low[:half], cot_low[half:])
    first_all = hold(first_all, [pieces1_oth[1], pieces1_oth[3], cot_pieces[1], cot_pieces[3]])
    by_z = first_all.reshape(z_count, tall_rows, 3 * span)

    def rows_of(start, count, z, many):
        return by_z[z : z + many, start : start + count].reshape(many * count, 3 * span)

    pieces_small = gather_halves(rows_of(quarter, share + 32, 0, 2), rows_of(quarter, share + 32, 2, 2))
    pieces_small += [swap(piece, 1) for piece in pieces_small]
    ups_qkv = jnp.concatenate(
        [by_z[:, quarter + share + row : quarter + share + row + 16, lane : lane + LANES] for row, lane in map(up_slot, range(12))],
        axis=1,
    )
    full_a_qkv, full_a_gu, full_a_out, full_b_out, full_b_down = call(
        functools.partial(unpack_small_kernel, share, quarter), scalars, pieces_small,
        [whole_spec((2 * share + 64, 3 * span))] * 16,
        [sds((width, 3 * latent)), sds((width, 2 * latent)), sds((width, latent))]
        + [sds((latent, width))] * 2,
        [whole_spec((width, 3 * latent)), whole_spec((width, 2 * latent)), whole_spec((width, latent))]
        + [whole_spec((latent, width))] * 2,
    )
    at = quarter + share + 32
    out_a, out_b = rows_of(at, 3 * share, 0, 2), rows_of(at, 3 * share, 2, 2)
    pieces_out = gather_halves(hold(out_a, [pieces_small[1]]), hold(out_b, [pieces_small[3]]))
    pieces_out += [swap(piece, 1) for piece in pieces_out]
    full_out = call(
        functools.partial(unpack_out_kernel, share, quarter), scalars, pieces_out, [ANY] * 16,
        sds((width, width)), whole_spec((width, width)), scratch=[pltpu.SemaphoreType.DMA((96,))],
    )
    ups_oth = swap(ups_qkv, 1)

    def qkv_up(piece):
        return piece.transpose(1, 0, 2).reshape(192, z_count * LANES)

    mine, theirs = qkv_up(ups_qkv), qkv_up(ups_oth)
    up_chip = jnp.where(
        core == 0, jnp.concatenate([mine, theirs], axis=0), jnp.concatenate([theirs, mine], axis=0)
    )
    up_own = take(up_chip, core * span, span, 1)
    up_oth = take(up_chip, (1 - core) * span, span, 1)

    all_places = jnp.arange(length, dtype=jnp.int32)
    all_begin, _ = doc_tables(all_places, first, chosen)
    cosine, sine = rope_tables(all_places - all_begin, HEAD_DIM)
    sign = jnp.where(jnp.arange(HEAD_DIM) < HEAD_DIM // 2, -1.0, 1.0)
    turn = sine * sign[None, :]
    rel = jnp.array([r for r, _ in HALVES], jnp.int32)
    part = jnp.array([h for _, h in HALVES], jnp.int32)
    group_places = ((((rel ^ chip) * 2 + core) * 2 + part) * half)[:, None] + jnp.arange(
        half, dtype=jnp.int32
    )
    _, group_which = doc_tables(group_places.reshape(-1), first, chosen)
    adapters_at = jnp.arange(latent, dtype=jnp.int32) // RANK
    group_select = (adapters_at[None, :] == group_which[:, None]).astype(BF)
    select = group_select[-rows:]

    qkv, z_qkv, qkv_own = call(
        qkv_kernel, scalars,
        pieces1 + pieces1_oth + [first_all, full_a_qkv, up_own, cosine, turn],
        [ANY] * 17
        + [
            whole_spec((width, 3 * latent)),
            whole_spec((3 * latent, span)), whole_spec((length, LANES)), whole_spec((length, LANES)),
        ],
        [sds((length, 3 * span)), sds((length, 3 * latent)), sds((width, 3 * span))],
        [whole_spec((length, 3 * span)), whole_spec((length, 3 * latent)), whole_spec((width, 3 * span))],
        scratch=[pltpu.VMEM((length, width), BF), pltpu.SemaphoreType.DMA((20,))],
        cost=(2 * length * width * (3 * span + 3 * latent), 20 * 2**20),
    )
    column = lambda k: pl.BlockSpec((length, LANES), lambda h, _: (0, k * heads_dev + h))
    mixed_h, log_sums = call(
        functools.partial(attend_kernel, rows), scalars, [qkv] * 3, [column(0), column(1), column(2)],
        [sds((length, span)), sds((length, span), F32)], [column(0), column(0)], grid=(heads_dev,),
        cost=(4 * heads_dev * length * length * HEAD_DIM, 8 * 2**20),
    )
    mixed = lax.all_to_all(mixed_h, "seq", split_axis=0, concat_axis=1, tiled=True)
    mixed_oth = swap(mixed_h, 1)
    square = whole_spec((width, width))
    tall = whole_spec((rows, width))
    second, norm_a, norm_b, z_out = call(
        out_kernel, scalars, [mixed, full_out, full_a_out, full_b_out, stream],
        [tall, square, whole_spec((width, latent)), whole_spec((latent, width)), tall],
        [sds((rows, width), F32), sds((half, width)), sds((half, width)), sds((rows, latent))],
        [tall, whole_spec((half, width)), whole_spec((half, width)), whole_spec((rows, latent))],
        scratch=[pltpu.VMEM((rows, width), BF)],
        cost=(2 * rows * width * width, 12 * 2**20), ties=[mixed_oth],
    )

    pieces2 = gather_halves(norm_a, norm_b)
    down_own = hold(down_own, [second])
    down_oth = swap(down_own, 1)
    step = group // 2

    HBM = pl.BlockSpec(memory_space=pltpu.HBM)
    size = len(CHUNKS[0]) * ff_dev
    latents = [None, None]

    def feed(place, weights, at, onward, last):
        begin = onward is None
        if begin:
            operands = [group_select, full_a_gu, full_b_down]
            specs = [
                pl.BlockSpec((step, latent), lambda *_: (at, 0)), whole_spec((width, 2 * latent)),
                whole_spec((latent, width)),
            ]
        else:
            operands = list(latents[at])
            specs = [whole_spec((step, 2 * latent)), whole_spec((step, latent))]
        for pair in weights:
            operands += pair
            specs += [HBM, HBM]
        operands += pieces2[4 * at : 4 * at + 4] + cot_pieces[4 * at : 4 * at + 4]
        specs += [ANY] * 8
        if not begin:
            operands.append(onward)
            specs.append(HBM)
        if last:
            shapes, outs = [sds((rows, wide_gu), (BF, F32)[at])] * 2, [whole_spec((rows, wide_gu))] * 2
        else:
            shapes, outs = [sds((step, wide_gu), F32)], [whole_spec((step, wide_gu))]
        more = [(step, size), (step, 2 * size)] * len(weights)
        if begin:
            more += [(step, 2 * latent), (step, latent)]
        shapes += [sds(shape) for shape in more]
        outs += [whole_spec(shape) for shape in more]
        return call(
            functools.partial(ff_kernel, begin, last, len(weights), CHUNKS[place][0]), scalars, operands,
            specs, shapes, outs,
            scratch=[pltpu.VMEM((step, width), BF)] * 2
            + [pltpu.VMEM((8, LANES) if begin else (step, wide_gu), F32), pltpu.SemaphoreType.DMA((13,))]
            + [pltpu.VMEM((width, 2 * size), BF), pltpu.VMEM((size, wide_down + ff_dev), BF)]
            * len(weights),
            cost=(step * 10 * width * size * len(weights), 26 * 2**20),
        )

    def down_half(place, at, kind, total, ties):
        weight = pl.BlockSpec((size, wide_down + ff_dev), lambda *_: (place, 0))
        begin = total is None
        operands = [results[place][0][at][0], results[place][1][at][0], down_own, down_oth]
        specs = [whole_spec((step, size))] * 2 + [weight] * 2
        if not begin:
            operands.append(total)
            specs.append(whole_spec((step, wide_down)))
        shape = (step, wide_down) if begin else (rows, wide_down)
        count = 1 if begin else 2
        return call(
            functools.partial(down_kernel, begin), scalars, operands, specs,
            [sds(shape, kind)] * count, [whole_spec(shape)] * count,
            cost=(2 * step * 4 * ff_dev * width, 12 * 2**20), ties=ties,
        )

    results = [[[None, None], [None, None]] for _ in CHUNKS]
    gu_own = hold(gu_owns[0], [pieces2[1], pieces2[3]])
    weights = [(gu_own, down_own), (swap(gu_own, 1), down_oth)]
    sums = []
    for at in range(2):
        total, *more = feed(0, weights, at, None, False)
        sums.append(total)
        results[0][0][at], results[0][1][at], latents[at] = more[:2], more[2:4], more[4:]
    down_first = [down_half(0, at, F32, None, [sums[1]])[0] for at in range(2)]
    gu_own = hold(gu_owns[1], sums + down_first)
    weights = [(gu_own, down_own), (swap(gu_own, 1), down_oth)]
    total, *results[1][0][0] = feed(1, weights[:1], 0, sums[0], False)
    send_x, send_y, *results[1][1][0] = feed(1, weights[1:], 0, total, True)
    pass_on, kept, *more = feed(1, weights, 1, sums[1], True)
    results[1][0][1], results[1][1][1] = more[:2], more[2:]
    by_x, by_y, got_y, got_x, passed = scatter_rest(send_x, send_y, pass_on)
    down_x, down_y = (hold(x, [got_y, got_x]) for x in down_half(1, 0, BF, down_first[0], passed))
    halfspec = lambda n: pl.BlockSpec((half, n), lambda *_: (0, 0))
    second_grad, mixed_grad, *packs = call(
        back_middle_kernel, scalars,
        [kept, by_x, by_y, got_y, got_x, second, cot_low, full_a_gu, full_out, full_a_out, full_b_out, z_out],
        [whole_spec((rows, wide_gu))] + [halfspec(wide_gu)] * 4
        + [
            tall, tall, whole_spec((width, 2 * latent)), ANY, whole_spec((width, latent)),
            whole_spec((latent, width)), whole_spec((rows, latent)),
        ],
        [
            sds((rows, width), F32), sds((rows, width)),
        ]
        + [sds((rows, 5 * latent))] * 4,
        [tall, tall] + [whole_spec((rows, 5 * latent))] * 4,
        scratch=[pltpu.VMEM((width, width), BF), pltpu.SemaphoreType.DMA],
        cost=(2 * rows * width * width, 16 * 2**20), ties=[down_x],
    )
    mixed_grad_h = lax.all_to_all(mixed_grad, "seq", split_axis=1, concat_axis=0, tiled=True)
    down_on, down_kept = down_half(1, 1, F32, down_first[1], [mixed_grad])

    def along_line(keep, send, ties):
        shape = keep.shape[1:]
        return call(
            along_line_kernel, scalars, [keep, swap(send, 1)], [whole_spec(keep.shape)] * 2,
            [sds(shape, F32)] * 2 + [sds((2, *shape))], [whole_spec(shape)] * 2 + [whole_spec((2, *shape))],
            ties=ties, cost=(2**20, 8 * 2**20), room=SMALL,
        )

    def line_sum(mine, onward, sent, ties):
        brought = lax.ppermute(sent, "fsdp", [(i, i ^ 1) for i in range(z_count)])
        onward = (onward + brought[1].astype(F32)).astype(BF)
        far = lax.ppermute(onward, "fsdp", [(i, i ^ 2) for i in range(z_count)])
        mine = hold(mine, ties) if ties else mine
        return (mine + brought[0].astype(F32) + far.astype(F32)).astype(BF)

    def spread(mine, places, shapes, ties):
        plane = blocks_of(mine)
        plane.append(swap(jnp.stack(plane), 1))
        return call(
            functools.partial(spread_kernel, places), scalars, plane,
            [whole_spec(piece.shape) for piece in plane],
            [sds(shape, F32) for shape in shapes], [whole_spec(shape) for shape in shapes], ties=ties,
            room=SMALL,
        )

    *down_by, down_passed = scatter_rest(down_x, down_y, down_on)
    middle = [packs[0]] + [swap(hold(packs[k], [mixed_grad_h]), 2 * k) for k in (1, 2, 3)]

    result = pl.BlockSpec((3, group, HEAD_DIM), lambda h, _: (0, 0, h))
    grads_a, grads_b, up_qkv = call(
        functools.partial(attend_back_kernel, rows), scalars,
        [qkv, qkv, qkv, mixed_grad_h, log_sums, z_qkv, cosine, turn],
        [column(0), column(1), column(2), column(0), column(0), whole_spec((length, 3 * latent))]
        + [whole_spec((length, LANES))] * 2,
        [sds((3, group, span))] * 2 + [sds((3, latent, span), F32)],
        [result, result, pl.BlockSpec((3, latent, HEAD_DIM), lambda h, _: (0, 0, h))],
        scratch=[pltpu.VMEM((length, HEAD_DIM), F32)] * 3, grid=(heads_dev,),
        cost=(10 * heads_dev * length * length * HEAD_DIM, 16 * 2**20), ties=down_passed,
    )
    grads_b = swap(grads_b, 1)
    qkv_oth = swap(qkv_own, 1)

    down_kept = hold(down_kept, [grads_a])
    upper = down_kept[:half] + down_by[0][:half].astype(F32) + down_by[2].astype(F32)
    lower = down_kept[half:] + down_by[1][:half].astype(F32) + down_by[3].astype(F32)
    wide = jnp.concatenate([upper, lower], axis=0)
    z_down = wide[:, width:].astype(BF) * select
    to_x, to_y, to_far, latent_kept = call(
        back_latent_kernel, scalars, [grads_a, grads_b, up_own, up_oth],
        [whole_spec((3, group, span))] * 2 + [whole_spec((3 * latent, span))] * 2,
        [sds((rows, 3 * latent))] * 3 + [sds((rows, 3 * latent), F32)],
        [whole_spec((rows, 3 * latent))] * 4,
        cost=(4 * group * span * 3 * latent, 4 * 2**20), room=SMALL, ties=[z_down],
    )

    def back_qkv(at, kind, ties):
        part = pl.BlockSpec((3, step, span), lambda *_: (0, at, 0))
        return call(
            back_qkv_kernel, scalars, [grads_a, grads_b, qkv_own, qkv_oth],
            [part, part] + [whole_spec((width, 3 * span))] * 2,
            [sds((rows, width), kind)] * 2, [tall] * 2,
            cost=(2 * group * span * 3 * width, 12 * 2**20), room=SMALL, ties=ties,
        )

    pass_on, kept = back_qkv(1, F32, [to_x, *middle[1:]])
    dz_qkv = latent_kept + swap(to_x, 2).astype(F32) + swap(to_y, 4).astype(F32)
    dz_qkv = (dz_qkv + swap(to_far, 6).astype(F32)) * jnp.concatenate([select] * 3, axis=1).astype(F32)
    both = jnp.concatenate([dz_qkv.astype(BF), z_down], axis=1)
    last = blocks_of(both)
    ff_rows = 2 * latent * (ff_dev // LANES) + ff_dev
    values = [one[k] for one in latents for k in range(1)] + [one[1] for one in latents]
    values += [value for chunk in results for side in chunk for one in side for value in one]
    ff_keep, ff_send = call(
        ff_grads_kernel, scalars, values, [whole_spec(value.shape) for value in values],
        [sds((z_count, ff_rows, LANES), F32), sds((z_count, ff_rows, LANES))],
        [whole_spec((z_count, ff_rows, LANES))] * 2, cost=(2**32, 12 * 2**20), ties=[kept, both],
    )
    send_x, send_y = back_qkv(0, BF, [*last[1:], ff_send])
    other_rows = 11 * LANES // 2
    keep, send = call(
        functools.partial(other_grads_kernel, quarter), scalars,
        [*pieces1, *pieces2, *cot_pieces, mixed_h, mixed_oth, *middle, *last, up_qkv],
        [ANY] * 24 + [whole_spec((length, span))] * 2 + [whole_spec((rows, 5 * latent))] * 4
        + [whole_spec((rows, 4 * latent))] * 4 + [whole_spec((3, latent, span))],
        [sds((z_count, other_rows, LANES), F32), sds((z_count, other_rows, LANES))],
        [whole_spec((z_count, other_rows, LANES))] * 2,
        scratch=[
            pltpu.VMEM((3, group, z_count * LANES), BF), pltpu.VMEM((group, 2 * latent), BF),
            pltpu.VMEM((group, 3 * latent), BF), pltpu.VMEM((group, latent), BF),
            pltpu.SemaphoreType.DMA((96,)),
        ],
        cost=(2 * group * 512 * 768, 8 * 2**20), ties=[send_x],
    )
    ff_mine, *ff_rest = along_line(ff_keep, ff_send, [keep])
    by_x, by_y, got_y, got_x, passed = scatter_rest(send_x, send_y, hold(pass_on, [keep]))
    input_grad = call(
        back_first_kernel, scalars,
        [kept, by_x, by_y, got_y, got_x, stream, second_grad, both, full_a_qkv],
        [tall] + [halfspec(width)] * 4
        + [tall, tall, pl.BlockSpec((rows, 3 * latent), lambda *_: (0, 0)), whole_spec((width, 3 * latent))],
        sds((rows, width), F32), tall,
        cost=(2 * rows * width * 3 * latent, 12 * 2**20), room=SMALL,
    )
    activations = second + (wide[:, :width] + dot(hold(z_down, passed), full_b_down))
    ff_total = line_sum(ff_mine, *ff_rest, [activations])
    total = line_sum(*along_line(keep, send, []), [input_grad])
    g_b_gu, g_a_down = spread(
        ff_total, (("columns", 2 * latent, ff_dev // LANES), ("rows", ff_dev, 1)),
        [(2 * latent, ff_z), (ff_z, latent)], [],
    )
    low = LANES // 2
    g_a_gu, g_b_down, g_a_out, g_b_out, g_a_qkv, g_b_qkv = spread(
        total,
        (
            ("rows", low, 2), ("both", low, 1), ("rows", low, 1), ("core rows", share_b, z_count),
            ("rows", low, 3), ("both", 3 * low, 1),
        ),
        [
            (quarter, 2 * latent), (latent, quarter), (quarter, latent), (latent, quarter),
            (quarter, 3 * latent), (3 * latent, quarter),
        ],
        [g_b_gu],
    )

    return (
        activations[None], input_grad[None],
        g_a_qkv, g_b_qkv, g_a_out, g_b_out, g_a_gu, g_b_gu, g_a_down, g_b_down,
    )


def solution(mesh):
    placed = (
        P("fsdp", "seq", None),
        P("fsdp", "seq", None),
        P("fsdp", None),
        P("fsdp", None),
        P("fsdp", None),
        P("fsdp", None),
        P("fsdp", None),
        P("fsdp", None),
        P("fsdp", None),
        P(None, "fsdp"),
        P("fsdp", None),
        P(None, "fsdp"),
        P("fsdp", None),
        P(None, "fsdp"),
        P("fsdp", None),
        P(None, "fsdp"),
    )
    on_plane = mesh.shape["seq"] == PLANE and mesh.shape["fsdp"] == 4
    return jax.shard_map(
        plane_shards if on_plane else shards,
        mesh=mesh,
        in_specs=placed,
        out_specs=(
            P("fsdp", "seq", None),
            P("fsdp", "seq", None),
            P("fsdp", None),
            P(None, "fsdp"),
            P("fsdp", None),
            P(None, "fsdp"),
            P("fsdp", None),
            P(None, "fsdp"),
            P("fsdp", None),
            P(None, "fsdp"),
        ),
        check_vma=False,
    )
```
